32 devices in a mesh: dp: 8 (over z, core), mp: 4 (over y, x).
Axes of the slice: x: 2, y: 2, z: 4, core: 2. Of those that a mesh axis runs over, the one named last changes fastest.
Arguments:
- block_in: bfloat16 [16, 1024, 2048], P('dp', 'mp'), may hold values from -6 to 6
- norm1_gain: float32 [2048], replicated, may hold values from 0.25 to 1.75
- w_branch: bfloat16 [2048, 2560], P(None, 'mp'), may hold values from -0.125 to 0.125
- w_input: bfloat16 [2048, 2560], P(None, 'mp'), may hold values from -0.125 to 0.125
- conv_weight: float32 [4, 2560], P(None, 'mp'), may hold values from -3 to 3
- conv_bias: float32 [2560], P('mp'), may hold values from -3 to 3
- gate_a_weight: bfloat16 [16, 160, 160], P('mp'), may hold values from -0.5 to 0.5
- gate_a_bias: float32 [2560], P('mp'), may hold values from -4 to 4
- gate_i_weight: bfloat16 [16, 160, 160], P('mp'), may hold values from -0.5 to 0.5
- gate_i_bias: float32 [2560], P('mp'), may hold values from -4 to 4
- decay_param: float32 [2560], P('mp'), may hold values from 4 to 9
- w_out: bfloat16 [2560, 2048], P('mp'), may hold values from -0.3125 to 0.3125
- norm2_gain: float32 [2048], replicated, may hold values from 0.25 to 1.75
- w_gate: bfloat16 [2048, 6144], P(None, 'mp'), may hold values from -0.125 to 0.125
- w_up: bfloat16 [2048, 6144], P(None, 'mp'), may hold values from -0.125 to 0.125
- w_down: bfloat16 [6144, 2048], P('mp'), may hold values from -0.109375 to 0.109375
- lengths: int32 [16], P('dp'), may hold values from 256 to 1024, as said below
- cotangent: bfloat16 [16, 1024, 2048], P('dp', 'mp'), may hold values from -6 to 6
Outputs:
- block_out: bfloat16 [16, 1024, 2048], P('dp', 'mp')
- input_grad: bfloat16 [16, 1024, 2048], P('dp', 'mp')
- grad_norm1_gain: float32 [2048], replicated
- grad_w_branch: float32 [2048, 2560], P(None, 'mp')
- grad_w_input: float32 [2048, 2560], P(None, 'mp')
- grad_conv_weight: float32 [4, 2560], P(None, 'mp')
- grad_conv_bias: float32 [2560], P('mp')
- grad_gate_a_weight: float32 [16, 160, 160], P('mp')
- grad_gate_a_bias: float32 [2560], P('mp')
- grad_gate_i_weight: float32 [16, 160, 160], P('mp')
- grad_gate_i_bias: float32 [2560], P('mp')
- grad_decay_param: float32 [2560], P('mp')
- grad_w_out: float32 [2560, 2048], P('mp')
- grad_norm2_gain: float32 [2048], replicated
- grad_w_gate: float32 [2048, 6144], P(None, 'mp')
- grad_w_up: float32 [2048, 6144], P(None, 'mp')
- grad_w_down: float32 [6144, 2048], P('mp')
- final_state: float32 [16, 2560], P('dp', 'mp')
The draws below stay inside these ranges and needn't reach their ends.
Inputs may be any that keep to these rules, and one draw needn't show every extreme that they name: `lengths`: in each aligned block of 2 sequences, one sequence drawn from the seed has length 1024; every length is at least 256.
All inputs are finite; a program needn't handle non-finite values.
Results may differ from the reference program's by a relative error of at most 0.019.
Values may be sent and summed in bfloat16 or wider, within the bound.
A program may use at most 448 MiB of HBM per device.

```python
import math
import jax
import jax.numpy as jnp
from jax import lax

D = 2048
NB = 16
BW = 160
F = 6144
CONV = 4
DECAY_EXP = 8
L = 1024
ROWS_DEV = 2
ROWS = 16
R = 2560


def draw_lengths(key, part):
    key = jax.random.fold_in(key, 7)
    first, second = jax.random.split(key)
    groups = ROWS // ROWS_DEV
    base = jax.random.randint(first, (groups, ROWS_DEV), L // 4, L + 1)
    chosen = jax.random.randint(second, (groups, 1), 0, ROWS_DEV)
    slots = jnp.arange(ROWS_DEV, dtype=jnp.int32)[None, :]
    full = jnp.where(slots == chosen, L, base)
    return full.reshape(ROWS).astype(jnp.int32)


def steps_of(rng, dims, cuts, smallest, high):
    def one(position, shards_of):
        steps = jax.random.uniform(jax.random.fold_in(jax.random.fold_in(rng, 6), position), (shards_of,), jnp.float32, smallest / len(cuts), high / len(cuts))
        return jnp.repeat(jnp.exp(steps), dims[position] // shards_of).reshape((-1,) + (1,) * (len(dims) - position - 1))

    loudness = one(*cuts[0])
    for cut in cuts[1:]:
        loudness = loudness * one(*cut)
    return loudness


def normal_values(key, dims, scale, limit, cuts=(), held_as=jnp.bfloat16):
    drawn = jax.random.normal(key, dims, jnp.float32) * scale
    if len(cuts) > 0:
        drawn = steps_of(key, dims, cuts, -0.22, 0.18) * drawn
    return jnp.clip(drawn, min=-limit, max=limit).astype(held_as)


def setup_inputs(seed: int = 0) -> dict:
    keys = jax.random.split(jax.random.key(seed), 19)
    block_in = normal_values(keys[0], (ROWS, L, D), 1.0, 6.0, ((0, 8), (1, 4)))
    norm1_gain = jnp.clip(1.0 + 0.15 * jax.random.normal(keys[1], (D,), jnp.float32), 0.25, 1.75)
    w_branch = normal_values(keys[2], (D, R), D ** -0.5, 0.125, ((1, 4),))
    w_input = normal_values(keys[3], (D, R), D ** -0.5, 0.125, ((1, 4),))
    conv_weight = normal_values(keys[4], (CONV, R), CONV ** -0.5, 3.0, ((1, 4),), jnp.float32)
    conv_bias = normal_values(keys[5], (R,), 0.5, 3.0, ((0, 4),), jnp.float32)
    gate_a_weight = normal_values(keys[6], (NB, BW, BW), BW ** -0.5, 0.5, ((0, 4),))
    gate_a_bias = normal_values(keys[7], (R,), 1.0, 4.0, ((0, 4),), jnp.float32)
    gate_i_weight = normal_values(keys[8], (NB, BW, BW), BW ** -0.5, 0.5, ((0, 4),))
    gate_i_bias = normal_values(keys[9], (R,), 1.0, 4.0, ((0, 4),), jnp.float32)
    decay_param = jnp.clip(4.0 + 5.0 * jax.random.uniform(keys[10], (R,), jnp.float32) ** steps_of(keys[10], (R,), ((0, 4),), -0.2, 0.2), 4.0, 9.0)
    w_out = normal_values(keys[11], (R, D), (R // 8) ** -0.5, 0.3125, ((0, 4),))
    norm2_gain = jnp.clip(1.0 + 0.15 * jax.random.normal(keys[12], (D,), jnp.float32), 0.25, 1.75)
    w_gate = normal_values(keys[13], (D, F), D ** -0.5, 0.125, ((1, 4),))
    w_up = normal_values(keys[14], (D, F), D ** -0.5, 0.125, ((1, 4),))
    w_down = normal_values(keys[15], (F, D), (F // 2) ** -0.5, 0.109375, ((0, 4),))
    lengths = draw_lengths(jax.random.fold_in(keys[18], 71), 0)
    cotangent = normal_values(keys[17], (ROWS, L, D), 1.0, 6.0, ((0, 8), (1, 4)))
    return {"block_in": block_in, "norm1_gain": norm1_gain, "w_branch": w_branch, "w_input": w_input, "conv_weight": conv_weight, "conv_bias": conv_bias, "gate_a_weight": gate_a_weight, "gate_a_bias": gate_a_bias, "gate_i_weight": gate_i_weight, "gate_i_bias": gate_i_bias, "decay_param": decay_param, "w_out": w_out, "norm2_gain": norm2_gain, "w_gate": w_gate, "w_up": w_up, "w_down": w_down, "lengths": lengths, "cotangent": cotangent}


@jax.custom_vjp
def low(v):
    return lax.optimization_barrier(v.astype(jnp.bfloat16)).astype(jnp.float32)

@jax.custom_vjp
def low_back(v):
    return v

def low_keep(v):
    return (low(v), None)

def low_pass(kept, grad):
    return (grad,)

def back_keep(v):
    return (v, None)

def back_low(kept, grad):
    return (low(grad),)
low.defvjp(low_keep, low_pass)
low_back.defvjp(back_keep, back_low)
eps = 1e-06

def rms_norm(values, gain):
    return values * lax.rsqrt(lax.optimization_barrier(jnp.mean(values * values, axis=-1, keepdims=True)) + eps) * gain

def project(left, right):
    return jnp.einsum('rtd,dc->rtc', left, right, precision=lax.Precision.HIGHEST)

def causal_conv(seq, conv_weight, conv_bias):
    span = seq.shape[1]
    total = conv_bias + conv_weight[0] * seq
    for shift in range(1, CONV):
        moved = jnp.pad(seq, ((0, 0), (shift, 0), (0, 0)))[:, :span]
        total = total + conv_weight[shift] * moved
    return total

def recurrence(gated_a, gated_in):
    count, span, width = gated_a.shape
    stretch = math.gcd(span, 128)

    def block(state, pieces):

        def advance(carry, item):
            carry = item[0] * carry + item[1]
            return (carry, carry)
        return lax.scan(advance, state, pieces)

    def arrange(values):
        return jnp.transpose(values, (1, 0, 2)).reshape(span // stretch, stretch, count, width)
    start = jnp.zeros((count, width), jnp.float32)
    final, states = lax.scan(jax.checkpoint(block), start, (arrange(gated_a), arrange(gated_in)))
    states = jnp.transpose(states.reshape(span, count, width), (1, 0, 2))
    return (states, final)

def forward(values, params, live):
    norm1_gain, w_branch, w_input, conv_weight, conv_bias, gate_a_weight, gate_a_bias, gate_i_weight, gate_i_bias, decay_param, w_out, norm2_gain, w_gate, w_up, w_down = params
    count = values.shape[0]
    normed_in = low(rms_norm(values, norm1_gain))
    branch_pre = low_back(project(normed_in, w_branch))
    input_pre = low_back(project(normed_in, w_input))
    conv_out = low(causal_conv(input_pre, conv_weight, conv_bias))
    blocks = conv_out.reshape(count, L, NB, BW)
    gate_a_pre = low_back(jnp.einsum('rtnb,nbc->rtnc', blocks, gate_a_weight, precision=lax.Precision.HIGHEST).reshape(count, L, NB * BW) + gate_a_bias)
    gate_i_pre = low_back(jnp.einsum('rtnb,nbc->rtnc', blocks, gate_i_weight, precision=lax.Precision.HIGHEST).reshape(count, L, NB * BW) + gate_i_bias)
    gate_a = jax.nn.sigmoid(gate_a_pre)
    gate_i = jax.nn.sigmoid(gate_i_pre)
    log_a = -DECAY_EXP * jax.nn.softplus(-decay_param) * gate_a
    decay = jnp.exp(log_a)
    scaled = jnp.sqrt(-jnp.expm1(2.0 * log_a)) * gate_i * conv_out
    gated_a = jnp.where(live, decay, 1.0)
    gated_in = jnp.where(live, scaled, 0.0)
    states, final = recurrence(gated_a, gated_in)
    mixed = low(states * jax.nn.gelu(branch_pre))
    resid_mid = values + low_back(project(mixed, w_out))
    normed_mid = low(rms_norm(resid_mid, norm2_gain))
    mlp_gate = low_back(project(normed_mid, w_gate))
    mlp_up = low_back(project(normed_mid, w_up))
    hidden = low(jax.nn.gelu(mlp_gate) * mlp_up)
    return (resid_mid + project(hidden, w_down), final)

def reference(block_in, norm1_gain, w_branch, w_input, conv_weight, conv_bias, gate_a_weight, gate_a_bias, gate_i_weight, gate_i_bias, decay_param, w_out, norm2_gain, w_gate, w_up, w_down, lengths, cotangent):
    params = tuple((v.astype(jnp.float32) for v in (norm1_gain, w_branch, w_input, conv_weight, conv_bias, gate_a_weight, gate_a_bias, gate_i_weight, gate_i_bias, decay_param, w_out, norm2_gain, w_gate, w_up, w_down)))
    rows_per = math.gcd(ROWS, max(1, 4096 // L))
    count = ROWS // rows_per
    inputs = block_in.astype(jnp.float32).reshape(count, rows_per, L, D)
    cots = cotangent.astype(jnp.float32).reshape(count, rows_per, L, D)
    lens = lengths.reshape(count, rows_per)

    def visit(total, item):
        values, lens_group, cot = item
        live = (jnp.arange(L, dtype=jnp.int32)[None, :] < lens_group[:, None])[..., None]

        def run(values, params):
            return forward(values, params, live)
        result, pull, final = jax.vjp(run, values, params, has_aux=True)
        d_values, d_params = pull(cot)
        total = jax.tree.map(lambda first, second: first + second, total, d_params)
        return (total, (result.astype(jnp.bfloat16), d_values.astype(jnp.bfloat16), final))
    zeros = jax.tree.map(jnp.zeros_like, params)
    grads, (outputs, d_inputs, finals) = lax.scan(visit, zeros, (inputs, lens, cots))
    return (outputs.reshape(ROWS, L, D), d_inputs.reshape(ROWS, L, D), grads[0], grads[1], grads[2], grads[3], grads[4], grads[5], grads[6], grads[7], grads[8], grads[9], grads[10], grads[11], grads[12], grads[13], grads[14], finals.reshape(ROWS, NB * BW))
```

```python
import functools
import math

import jax
import jax.numpy as jnp
from jax import lax
from jax.experimental import pallas as pl
from jax.experimental.pallas import tpu as pltpu
from jax.sharding import PartitionSpec as P

DECAY_EXP = 8.0
EPS = 1e-06
GELU_C = math.sqrt(2.0 / math.pi)
GELU_K = 0.044715
LANES = 128
SUB = 8
VMEM_BYTES = 56 * 1024 * 1024

f32 = jnp.float32
bf16 = jnp.bfloat16


def dot_nn(left, right):
    return lax.dot_general(left, right, (((1,), (0,)), ((), ())), preferred_element_type=f32)


def dot_nt(left, right):
    return lax.dot_general(left, right, (((1,), (1,)), ((), ())), preferred_element_type=f32)


def one_minus_square(log_a, decay):
    x = 2.0 * log_a
    tail = 1.0 + x * (1.0 / 7.0)
    for k in (6.0, 5.0, 4.0, 3.0, 2.0):
        tail = 1.0 + x * (1.0 / k) * tail
    return jnp.where(x > -0.4, -x * tail, 1.0 - decay * decay)


def gelu_parts(x):
    square = x * x
    th = jnp.tanh(GELU_C * x * (1.0 + GELU_K * square))
    half = 0.5 * (1.0 + th)
    value = x * half
    slope = half + 0.5 * x * (1.0 - th * th) * (GELU_C * (1.0 + 3.0 * GELU_K * square))
    return value, slope


def row_index(shape):
    return lax.broadcasted_iota(jnp.int32, shape, 0)


def shift_down(prev, cur, k, row):
    return jnp.where(row < k, pltpu.roll(prev, k, 0), pltpu.roll(cur, k, 0))


def shift_up(cur, following, k, row):
    return jnp.where(row < SUB - k, pltpu.roll(cur, SUB - k, 0), pltpu.roll(following, SUB - k, 0))


def rec_forward_kernel(
    info, x, w_branch, w_input, taps, conv_bias, w_ga, w_gi, ga_bias, gi_bias, decay_param,
    mixed, pre, branch, conv, ga, gi, prev_state, final,
    ga_pre, gi_pre, tail, carry,
):
    step = pl.program_id(0)
    rows, width = mixed.shape[1:]
    pieces = rows // 16
    lanes = [pl.ds(at, LANES) for at in range(0, width, LANES)]
    row = row_index((SUB, LANES))

    @pl.when(step == 0)
    def _():
        tail[...] = jnp.zeros_like(tail)
        carry[...] = jnp.zeros_like(carry)

    pre[0] = dot_nn(x[0], w_input[...])

    def conv_piece(i, _):
        base = pl.multiple_of(i * 16, 16)
        for lane in lanes:
            bias = conv_bias[:, lane]
            before = tail[:, lane]
            parts = []
            for half in range(2):
                cur = pre[0, pl.ds(base + SUB * half, SUB), lane]
                total = bias + taps[0:1, lane] * cur
                for k in range(1, 4):
                    total = total + taps[k : k + 1, lane] * shift_down(before, cur, k, row)
                parts.append(total)
                before = cur
            tail[:, lane] = before
            conv[0, pl.ds(base, 16), lane] = jnp.concatenate(parts, axis=0).astype(bf16)
        return 0

    lax.fori_loop(0, pieces, conv_piece, 0)
    ga_pre[...] = dot_nn(conv[0], w_ga[...])
    gi_pre[...] = dot_nn(conv[0], w_gi[...])
    branch[0] = dot_nn(x[0], w_branch[...])
    length = info[1]

    def scan_piece(i, _):
        base = pl.multiple_of(i * 16, 16)
        start = step * rows + base
        for lane in lanes:
            rate = -DECAY_EXP * jax.nn.softplus(-decay_param[:, lane])
            conv_two = conv[0, pl.ds(base, 16), lane].astype(f32)
            state = carry[:, lane]
            outs = []
            for half in range(2):
                at = pl.ds(base + SUB * half, SUB)
                live = (row + (start + SUB * half)) < length
                gate_a = jax.nn.sigmoid(ga_pre[at, lane] + ga_bias[:, lane])
                gate_i = jax.nn.sigmoid(gi_pre[at, lane] + gi_bias[:, lane])
                ga[0, at, lane] = gate_a
                gi[0, at, lane] = gate_i
                log_a = rate * gate_a
                decay = jnp.exp(log_a)
                scaled = jnp.sqrt(one_minus_square(log_a, decay)) * gate_i * conv_two[SUB * half : SUB * half + SUB]
                mul = jnp.where(live, decay, 1.0)
                add = jnp.where(live, scaled, 0.0)
                for shift in (1, 2, 4):
                    inside = row >= shift
                    add = add + mul * jnp.where(inside, pltpu.roll(add, shift, 0), 0.0)
                    mul = mul * jnp.where(inside, pltpu.roll(mul, shift, 0), 1.0)
                states = mul * state + add
                prev_state[0, at, lane] = jnp.where(row == 0, state, pltpu.roll(states, 1, 0))
                state = jnp.broadcast_to(states[SUB - 1 : SUB], (SUB, LANES))
                value, _ = gelu_parts(branch[0, at, lane])
                outs.append(states * value)
            carry[:, lane] = state
            mixed[0, pl.ds(base, 16), lane] = jnp.concatenate(outs, axis=0).astype(bf16)
        return 0

    lax.fori_loop(0, pieces, scan_piece, 0)
    final[...] = carry[...]


def rec_backward_kernel(
    info, d_resid, w_out, w_branch, w_input, taps, w_ga, w_gi, decay_param,
    pre, branch, conv, ga, gi, prev_state,
    d_in, d_branch, d_input, d_ga, d_gi, sums,
    d_mixed, d_conv, flow, later,
):
    step = pl.program_id(0)
    rows, width = d_branch.shape[1:]
    pieces = rows // 16
    lanes = [pl.ds(at, LANES) for at in range(0, width, LANES)]
    row = row_index((SUB, LANES))
    first = (pl.num_programs(0) - 1 - step) * rows
    length = info[1]

    @pl.when(step == 0)
    def _():
        flow[...] = jnp.zeros_like(flow)
        later[...] = jnp.zeros_like(later)
        sums[...] = jnp.zeros_like(sums)

    d_mixed[...] = dot_nt(d_resid[0], w_out[...])

    def scan_piece(j, _):
        base = pl.multiple_of((pieces - 1 - j) * 16, 16)
        for lane in lanes:
            rate = -DECAY_EXP * jax.nn.softplus(-decay_param[:, lane])
            conv_two = conv[0, pl.ds(base, 16), lane].astype(f32)
            carried = flow[:, lane]
            outs = [None, None]
            sum_log = sums[0, :, lane]
            for half in (1, 0):
                at = pl.ds(base + SUB * half, SUB)
                live = (row + (first + base + SUB * half)) < length
                conv_val = conv_two[SUB * half : SUB * half + SUB]
                gate_a = ga[0, at, lane]
                gate_i = gi[0, at, lane]
                before = prev_state[0, at, lane]
                d_mix = d_mixed[at, lane]
                log_a = rate * gate_a
                decay = jnp.exp(log_a)
                space = one_minus_square(log_a, decay)
                inverse = lax.rsqrt(jnp.maximum(space, 1e-37))
                root = space * inverse
                gated = gate_i * conv_val
                mul = jnp.where(live, decay, 1.0)
                states = mul * before + jnp.where(live, root * gated, 0.0)
                value, slope = gelu_parts(branch[0, at, lane])
                d_br = d_mix * states * slope
                direct = d_mix * value
                add = mul * direct
                for shift in (1, 2, 4):
                    inside = row < SUB - shift
                    add = add + mul * jnp.where(inside, pltpu.roll(add, SUB - shift, 0), 0.0)
                    mul = mul * jnp.where(inside, pltpu.roll(mul, SUB - shift, 0), 1.0)
                moved = add + mul * carried
                d_state = direct + jnp.where(row == SUB - 1, carried, pltpu.roll(moved, SUB - 1, 0))
                carried = jnp.broadcast_to(moved[0:1], (SUB, LANES))
                d_state = jnp.where(live, d_state, 0.0)
                d_log = d_state * decay * (before - gated * decay * inverse)
                sum_log = sum_log + d_log * gate_a
                d_gate_a = d_log * rate * gate_a * (1.0 - gate_a)
                d_rooted = d_state * root
                d_conv_rec = d_rooted * gate_i
                d_gate_i = d_rooted * conv_val * gate_i * (1.0 - gate_i)
                d_conv[at, lane] = d_conv_rec
                outs[half] = (d_br, d_gate_a, d_gate_i)
            flow[:, lane] = carried
            sums[0, :, lane] = sum_log
            for target, which in ((d_branch, 0), (d_ga, 1), (d_gi, 2)):
                both = jnp.concatenate([outs[0][which], outs[1][which]], axis=0).astype(bf16)
                target[0, pl.ds(base, 16), lane] = both
                if which > 0:
                    wide = both.astype(f32)
                    sums[which, :, lane] += wide[:SUB] + wide[SUB:]
        return 0

    lax.fori_loop(0, pieces, scan_piece, 0)
    d_conv[...] += dot_nt(d_ga[0], w_ga[...]) + dot_nt(d_gi[0], w_gi[...])

    def conv_piece(j, _):
        base = pl.multiple_of((pieces - 1 - j) * 16, 16)
        for lane in lanes:
            following = later[:, lane]
            totals = [None, None]
            tap_sums = [sums[3 + k, :, lane] for k in range(5)]
            for half in (1, 0):
                at = pl.ds(base + SUB * half, SUB)
                cur = d_conv[at, lane]
                seen = pre[0, at, lane]
                tap_sums[0] = tap_sums[0] + cur
                tap_sums[1] = tap_sums[1] + cur * seen
                total = taps[0:1, lane] * cur
                for k in range(1, 4):
                    ahead = shift_up(cur, following, k, row)
                    tap_sums[1 + k] = tap_sums[1 + k] + ahead * seen
                    total = total + taps[k : k + 1, lane] * ahead
                totals[half] = total
                following = cur
            later[:, lane] = following
            for k in range(5):
                sums[3 + k, :, lane] = tap_sums[k]
            d_input[0, pl.ds(base, 16), lane] = jnp.concatenate(totals, axis=0).astype(bf16)
        return 0

    lax.fori_loop(0, pieces, conv_piece, 0)
    d_in[0] = (dot_nt(d_branch[0], w_branch[...]) + dot_nt(d_input[0], w_input[...])).astype(bf16)


def mlp_kernel(x, cot, w_gate, w_up, w_down, hidden, d_gate, d_up, gate_pre, up_pre, d_hidden):
    rows = x.shape[1]
    gate_pre[...] = dot_nn(x[0], w_gate[...])
    up_pre[...] = dot_nn(x[0], w_up[...])
    d_hidden[...] = dot_nt(cot[0], w_down[...])

    def piece(i, _):
        at = pl.ds(pl.multiple_of(i * 16, 16), 16)
        for lane in range(0, hidden.shape[2], LANES):
            lane = pl.ds(lane, LANES)
            up = up_pre[at, lane]
            back = d_hidden[at, lane]
            value, slope = gelu_parts(gate_pre[at, lane])
            hidden[0, at, lane] = (value * up).astype(bf16)
            d_gate[0, at, lane] = (back * up * slope).astype(bf16)
            d_up[0, at, lane] = (back * value).astype(bf16)
        return 0

    lax.fori_loop(0, rows // 16, piece, 0)


def whole(array):
    zeros = (0,) * array.ndim
    return pl.BlockSpec(array.shape, lambda *_: zeros, pipeline_mode=pl.Buffered(1))


def rec_forward(info, x, params):
    blocks, rows, model = x.shape
    width = params[0].shape[1]

    def at(step, info):
        return (step ^ info[0], 0, 0)

    wide = pl.BlockSpec((1, rows, width), at)
    out = jax.ShapeDtypeStruct((blocks, rows, width), f32)
    low = jax.ShapeDtypeStruct((blocks, rows, width), bf16)
    return pl.pallas_call(
        rec_forward_kernel,
        out_shape=(low, out, out, low, out, out, out, jax.ShapeDtypeStruct((SUB, width), f32)),
        grid_spec=pltpu.PrefetchScalarGridSpec(
            num_scalar_prefetch=1,
            grid=(blocks,),
            in_specs=[pl.BlockSpec((1, rows, model), at)] + [whole(p) for p in params],
            out_specs=(wide,) * 7 + (pl.BlockSpec((SUB, width), lambda *_: (0, 0)),),
            scratch_shapes=[
                pltpu.VMEM((rows, width), f32),
                pltpu.VMEM((rows, width), f32),
                pltpu.VMEM((SUB, width), f32),
                pltpu.VMEM((SUB, width), f32),
            ],
        ),
        compiler_params=pltpu.CompilerParams(vmem_limit_bytes=VMEM_BYTES),
        cost_estimate=pl.CostEstimate(
            flops=20 * blocks * rows * model * width, bytes_accessed=blocks * rows * (2 * model + 24 * width), transcendentals=0
        ),
        name="rec_forward",
    )(info, x, *params)


def rec_backward(info, d_resid, params, saved):
    blocks, rows, model = d_resid.shape
    width = saved[0].shape[2]

    def at(step, info):
        return ((blocks - 1 - step) ^ info[0], 0, 0)

    wide = pl.BlockSpec((1, rows, width), at)
    long = pl.BlockSpec((1, rows, model), at)
    low = jax.ShapeDtypeStruct((blocks, rows, width), bf16)
    return pl.pallas_call(
        rec_backward_kernel,
        out_shape=(
            jax.ShapeDtypeStruct((blocks, rows, model), bf16),
            low,
            low,
            low,
            low,
            jax.ShapeDtypeStruct((8, SUB, width), f32),
        ),
        grid_spec=pltpu.PrefetchScalarGridSpec(
            num_scalar_prefetch=1,
            grid=(blocks,),
            in_specs=[long] + [whole(p) for p in params] + [wide] * len(saved),
            out_specs=(long, wide, wide, wide, wide, pl.BlockSpec((8, SUB, width), lambda *_: (0, 0, 0))),
            scratch_shapes=[
                pltpu.VMEM((rows, width), f32),
                pltpu.VMEM((rows, width), f32),
                pltpu.VMEM((SUB, width), f32),
                pltpu.VMEM((SUB, width), f32),
            ],
        ),
        compiler_params=pltpu.CompilerParams(vmem_limit_bytes=VMEM_BYTES),
        cost_estimate=pl.CostEstimate(
            flops=30 * blocks * rows * model * width, bytes_accessed=blocks * rows * (4 * model + 32 * width), transcendentals=0
        ),
        name="rec_backward",
    )(info, d_resid, *params, *saved)


def mlp_core(x, cot, w_gate, w_up, w_down):
    blocks, rows, model = x.shape
    units = w_gate.shape[1]
    tile = max(t for t in range(LANES, 512 + 1, LANES) if units % t == 0)
    low = jax.ShapeDtypeStruct((blocks, rows, units), bf16)
    long = pl.BlockSpec((1, rows, model), lambda j, r: (r, 0, 0))
    column = pl.BlockSpec((model, tile), lambda j, r: (0, j))
    part = pl.BlockSpec((1, rows, tile), lambda j, r: (r, 0, j))
    return pl.pallas_call(
        mlp_kernel,
        out_shape=(low, low, low),
        grid=(units // tile, blocks),
        in_specs=[long, long, column, column, pl.BlockSpec((tile, model), lambda j, r: (j, 0))],
        out_specs=(part, part, part),
        scratch_shapes=[pltpu.VMEM((rows, tile), f32)] * 3,
        compiler_params=pltpu.CompilerParams(vmem_limit_bytes=VMEM_BYTES),
        cost_estimate=pl.CostEstimate(
            flops=9 * blocks * rows * model * units, bytes_accessed=blocks * rows * 16 * model, transcendentals=0
        ),
        name="mlp_core",
    )(x, cot, w_gate, w_up, w_down)


def swap(value, axis, bit):
    size = lax.axis_size(axis)
    return lax.ppermute(value, axis, [(i, i ^ bit) for i in range(size)])


def gather(shard):
    size = lax.axis_size("mp")
    if size != 4:
        return jnp.stack([shard] + [swap(shard, "mp", r) for r in range(1, size)])
    half = shard.shape[0] // 2
    by_x = swap(shard, "mp", 1)
    by_y = swap(shard, "mp", 2)
    far = jnp.concatenate([swap(by_x[:half], "mp", 2), swap(by_y[half:], "mp", 1)], axis=0)
    return jnp.stack([shard, by_x, by_y, far])


def scatter(parts):
    size = lax.axis_size("mp")
    if size != 4:
        total = parts[0].astype(f32)
        for r in range(1, size):
            total = total + swap(parts[r], "mp", r).astype(f32)
        return total
    half = parts.shape[1] // 2
    from_x = swap(parts[3, :half], "mp", 1)
    from_y = swap(parts[3, half:], "mp", 2)
    for_y = jnp.concatenate(
        [(parts[2, :half].astype(f32) + from_x.astype(f32)).astype(bf16), parts[2, half:]], axis=0
    )
    for_x = jnp.concatenate(
        [parts[1, :half], (parts[1, half:].astype(f32) + from_y.astype(f32)).astype(bf16)], axis=0
    )
    return parts[0].astype(f32) + swap(for_y, "mp", 2).astype(f32) + swap(for_x, "mp", 1).astype(f32)


def add_low(left, right):
    return (left.astype(f32) + right.astype(f32)).astype(bf16)


def sum_over_dp(part):
    size = lax.axis_size("dp")
    rows = part.shape[0]
    if size != 8 or rows % 64 != 0:
        return lax.psum(part, "dp").astype(f32)
    me = lax.axis_index("dp")
    core = me % 2
    chip = me // 2
    outer = jnp.where((chip == 0) | (chip == 3), 0, 1)

    def split(value, mine):
        half = value.shape[0] // 2
        keep = lax.dynamic_slice_in_dim(value, mine * half, half, 0)
        give = lax.dynamic_slice_in_dim(value, (1 - mine) * half, half, 0)
        return keep, give

    def join(kept, other, mine):
        return jnp.concatenate(
            [jnp.where(mine == 0, kept, other), jnp.where(mine == 0, other, kept)], axis=0
        )

    keep, give = split(part, core)
    total = add_low(keep, swap(give, "dp", 1))
    keep, give = split(total, outer)
    total = add_low(keep, swap(give, "dp", 2))
    total = add_low(total, lax.ppermute(total, "dp", [(i, (3 - i // 2) * 2 + i % 2) for i in range(8)]))
    total = join(total, swap(total, "dp", 2), outer)
    return join(total, swap(total, "dp", 1), core).astype(f32)


def normalize(values, gain):
    return values * lax.rsqrt(jnp.mean(values * values, axis=-1, keepdims=True) + EPS) * gain


def normalize_back(values, gain, grad):
    inverse = lax.rsqrt(jnp.mean(values * values, axis=-1, keepdims=True) + EPS)
    scaled = grad * gain
    unit = values * inverse
    return inverse * (scaled - unit * jnp.mean(scaled * unit, axis=-1, keepdims=True))


def dense_blocks(weight):
    blocks, inner, outer = weight.shape
    rows = [
        jnp.pad(weight[n], ((0, 0), (n * outer, (blocks - 1 - n) * outer))) for n in range(blocks)
    ]
    return jnp.concatenate(rows, axis=0)


def diagonal_blocks(full, blocks):
    inner = full.shape[0] // blocks
    return jnp.stack([full[n * inner : (n + 1) * inner, n * inner : (n + 1) * inner] for n in range(blocks)])


def weight_grad(lefts, rights):
    total = None
    for left, right in zip(lefts, rights):
        term = jnp.einsum("rtd,rtc->dc", left, right, preferred_element_type=f32)
        total = term if total is None else total + term
    return total


def per_device(
    block_in,
    norm1_gain,
    w_branch,
    w_input,
    conv_weight,
    conv_bias,
    gate_a_weight,
    gate_a_bias,
    gate_i_weight,
    gate_i_bias,
    decay_param,
    w_out,
    norm2_gain,
    w_gate,
    w_up,
    w_down,
    lengths,
    cotangent,
):
    count = block_in.shape[0]
    nblocks = gate_a_weight.shape[0]
    true_width = w_branch.shape[1]
    extra = -true_width % LANES
    me = lax.axis_index("mp")

    def pad_last(value):
        return jnp.pad(value, [(0, 0)] * (value.ndim - 1) + [(0, extra)]) if extra else value

    def line(value):
        return pad_last(value)[None, :]

    wb, wi = pad_last(w_branch), pad_last(w_input)
    wo = jnp.pad(w_out, ((0, extra), (0, 0))) if extra else w_out
    w_ga, w_gi = dense_blocks(gate_a_weight), dense_blocks(gate_i_weight)
    if extra:
        w_ga, w_gi = (jnp.pad(v, ((0, extra), (0, extra))) for v in (w_ga, w_gi))
    taps = pad_last(conv_weight)
    decay_line = line(decay_param)
    forward_params = (
        wb, wi, taps, line(conv_bias), w_ga, w_gi, line(gate_a_bias), line(gate_i_bias), decay_line
    )
    backward_params = (wo, wb, wi, taps, w_ga, w_gi, decay_line)
    seqs = range(count)
    infos = [jnp.stack([me.astype(jnp.int32), lengths[s]]) for s in seqs]

    resid = [block_in[s].astype(f32) for s in seqs]
    seq_in = [gather(normalize(resid[s], norm1_gain).astype(bf16)) for s in seqs]
    cot_seq = [gather(cotangent[s]) for s in seqs]

    mixed, saved, finals, resid_mid, seq_mid = [], [], [], [], []
    for s in seqs:
        out = rec_forward(infos[s], seq_in[s], forward_params)
        mixed.append(out[0])
        saved.append(out[1:7])
        finals.append(out[7][:1, :true_width])
        part = jnp.einsum("rtc,cd->rtd", out[0], wo, preferred_element_type=f32).astype(bf16)
        resid_mid.append(resid[s] + scatter(part))
        seq_mid.append(gather(normalize(resid_mid[s], norm2_gain).astype(bf16)))

    hidden, d_gate, d_up, d_resid, d_resid_seq, mlp_part = [], [], [], [], [], []
    for s in seqs:
        low_hidden, low_gate, low_up = mlp_core(seq_mid[s], cot_seq[s], w_gate, w_up, w_down)
        hidden.append(low_hidden)
        d_gate.append(low_gate)
        d_up.append(low_up)
        part = jnp.einsum("rtc,dc->rtd", low_gate, w_gate, preferred_element_type=f32)
        part = (part + jnp.einsum("rtc,dc->rtd", low_up, w_up, preferred_element_type=f32)).astype(bf16)
        d_mid = scatter(part)
        d_resid.append(cotangent[s].astype(f32) + normalize_back(resid_mid[s], norm2_gain, d_mid))
        d_resid_seq.append(gather(d_resid[s].astype(bf16)))
        mlp_part.append(jnp.einsum("rtc,cd->rtd", low_hidden, w_down, preferred_element_type=f32).astype(bf16))

    block_out = jnp.stack([(resid_mid[s] + scatter(mlp_part[s])).astype(bf16) for s in seqs])

    grad_w_down = sum_over_dp(weight_grad(hidden, cot_seq).astype(bf16))
    grad_w_gate = sum_over_dp(weight_grad(seq_mid, d_gate).astype(bf16))
    grad_w_up = sum_over_dp(weight_grad(seq_mid, d_up).astype(bf16))

    d_branch, d_input, d_ga, d_gi, sums, input_grad = [], [], [], [], [], []
    for s in seqs:
        out = rec_backward(infos[s], d_resid_seq[s], backward_params, saved[s])
        d_branch.append(out[1])
        d_input.append(out[2])
        d_ga.append(out[3])
        d_gi.append(out[4])
        sums.append(out[5])
        d_in = scatter(out[0])
        input_grad.append((d_resid[s] + normalize_back(resid[s], norm1_gain, d_in)).astype(bf16))
    input_grad = jnp.stack(input_grad)

    grad_w_out = sum_over_dp(weight_grad(mixed, d_resid_seq).astype(bf16)[:true_width])
    grad_w_branch = sum_over_dp(weight_grad(seq_in, d_branch).astype(bf16)[:, :true_width])
    grad_w_input = sum_over_dp(weight_grad(seq_in, d_input).astype(bf16)[:, :true_width])

    conv = [part[2] for part in saved]
    full_ga = diagonal_blocks(weight_grad(conv, d_ga)[:true_width, :true_width], nblocks)
    full_gi = diagonal_blocks(weight_grad(conv, d_gi)[:true_width, :true_width], nblocks)
    vectors = jnp.sum(sum(sums), axis=1)[:, :true_width]
    decay_grad = vectors[0] * DECAY_EXP * jax.nn.sigmoid(-decay_param)
    vectors = jnp.concatenate([decay_grad[None, :], vectors[1:]], axis=0)
    small = jnp.concatenate([full_ga.reshape(-1), full_gi.reshape(-1), vectors.reshape(-1)]).astype(bf16)
    used = small.shape[0]
    columns = 640
    padded = -(-used // (64 * columns)) * 64 * columns
    small = sum_over_dp(jnp.pad(small, (0, padded - used)).reshape(-1, columns)).reshape(-1)[:used]
    many = full_ga.size
    grad_gate_a_weight = small[:many].reshape(full_ga.shape)
    grad_gate_i_weight = small[many : 2 * many].reshape(full_gi.shape)
    vectors = small[2 * many :].reshape(8, true_width)

    gain1 = jnp.sum(w_branch.astype(f32) * grad_w_branch + w_input.astype(f32) * grad_w_input, axis=1) / norm1_gain
    gain2 = jnp.sum(w_gate.astype(f32) * grad_w_gate + w_up.astype(f32) * grad_w_up, axis=1) / norm2_gain
    gains = jnp.stack([gain1, gain2])
    if lax.axis_size("mp") == 4:
        gains = gains + swap(gains, "mp", 1)
        gains = gains + swap(gains, "mp", 2)
    else:
        gains = lax.psum(gains, "mp")

    return (
        block_out,
        input_grad,
        gains[0],
        grad_w_branch,
        grad_w_input,
        vectors[4:8],
        vectors[3],
        grad_gate_a_weight,
        vectors[1],
        grad_gate_i_weight,
        vectors[2],
        vectors[0],
        grad_w_out,
        gains[1],
        grad_w_gate,
        grad_w_up,
        grad_w_down,
        jnp.concatenate(finals, axis=0),
    )


def solution(mesh):
    placed = (
        P("dp", "mp", None),
        P(),
        P(None, "mp"),
        P(None, "mp"),
        P(None, "mp"),
        P("mp"),
        P("mp", None, None),
        P("mp"),
        P("mp", None, None),
        P("mp"),
        P("mp"),
        P("mp", None),
        P(),
        P(None, "mp"),
        P(None, "mp"),
        P("mp", None),
        P("dp"),
        P("dp", "mp", None),
    )
    return jax.shard_map(
        per_device,
        mesh=mesh,
        in_specs=placed,
        out_specs=(
            P("dp", "mp", None),
            P("dp", "mp", None),
            P(),
            P(None, "mp"),
            P(None, "mp"),
            P(None, "mp"),
            P("mp"),
            P("mp", None, None),
            P("mp"),
            P("mp", None, None),
            P("mp"),
            P("mp"),
            P("mp", None),
            P(),
            P(None, "mp"),
            P(None, "mp"),
            P("mp", None),
            P("dp", "mp"),
        ),
        check_vma=False,
    )
```

```python
import functools
import math

import jax
import jax.numpy as jnp
from jax import lax
from jax.experimental import pallas as pl
from jax.experimental.pallas import tpu as pltpu
from jax.sharding import PartitionSpec as P

DECAY_EXP = 8.0
EPS = 1e-06
GELU_C = math.sqrt(2.0 / math.pi)
GELU_K = 0.044715
LANES = 128
SUB = 8
UNIT_TILE = 256
COST_SCALE = 0.5
MODEL_TILE = 512
VMEM_BYTES = 56 * 1024 * 1024

f32 = jnp.float32
bf16 = jnp.bfloat16


def dot_nn(left, right):
    return lax.dot_general(left, right, (((1,), (0,)), ((), ())), preferred_element_type=f32)


def dot_nt(left, right):
    return lax.dot_general(left, right, (((1,), (1,)), ((), ())), preferred_element_type=f32)


def one_minus_square(log_a, decay):
    x = 2.0 * log_a
    tail = 1.0 + x * (1.0 / 7.0)
    for k in (6.0, 5.0, 4.0, 3.0, 2.0):
        tail = 1.0 + x * (1.0 / k) * tail
    return jnp.where(x > -0.4, -x * tail, 1.0 - decay * decay)


def gelu_parts(x):
    square = x * x
    th = jnp.tanh(GELU_C * x * (1.0 + GELU_K * square))
    half = 0.5 * (1.0 + th)
    value = x * half
    slope = half + 0.5 * x * (1.0 - th * th) * (GELU_C * (1.0 + 3.0 * GELU_K * square))
    return value, slope


def row_index(shape):
    return lax.broadcasted_iota(jnp.int32, shape, 0)


def shift_down(prev, cur, k, row):
    return jnp.where(row < k, pltpu.roll(prev, k, 0), pltpu.roll(cur, k, 0))


def shift_up(cur, following, k, row):
    return jnp.where(row < SUB - k, pltpu.roll(cur, SUB - k, 0), pltpu.roll(following, SUB - k, 0))


def load_block(pieces, layout, block, target):
    for ref, (owner, start, count) in zip(pieces, layout):

        @pl.when(block == owner)
        def _(ref=ref, start=start, count=count):
            target[pl.ds(start, count), :] = ref[...]


def store_block(pieces, layout, block, column, value):
    for ref, (owner, start, count) in zip(pieces, layout):

        @pl.when(block == owner)
        def _(ref=ref, start=start, count=count):
            ref[:, column] = value[start : start + count]


def rec_forward_kernel(layout, length, *refs):
    x_pieces, refs = refs[: len(layout)], refs[len(layout) :]
    w_both, taps, conv_bias, w_gates, ga_bias, gi_bias, decay_param, w_out = refs[:8]
    gates_pre, tail, carry, x = refs[-4:]
    outs = refs[-4 - 8 - len(layout) : -4]
    mixed, pre, branch, conv, ga, gi, prev_state, final = outs[:8]
    parts = outs[8:]
    step = pl.program_id(0)
    block = flip(step, lax.axis_index("mp"), 4 if len(layout) == 5 else len(layout))
    rows, width = mixed.shape[1:]
    load_block(x_pieces, layout, block, x)
    pieces = rows // 16
    lanes = [pl.ds(at, LANES) for at in range(0, width, LANES)]
    row = row_index((SUB, LANES))

    @pl.when(step == 0)
    def _():
        tail[...] = jnp.zeros_like(tail)
        carry[...] = jnp.zeros_like(carry)

    both = dot_nn(x[...], w_both[...])
    branch[0] = both[:, :width]
    pre[0] = both[:, width:]

    def conv_piece(i, _):
        base = pl.multiple_of(i * 16, 16)
        for lane in lanes:
            bias = conv_bias[:, lane]
            before = tail[:, lane]
            parts = []
            for half in range(2):
                cur = pre[0, pl.ds(base + SUB * half, SUB), lane]
                total = bias + taps[0:1, lane] * cur
                for k in range(1, 4):
                    total = total + taps[k : k + 1, lane] * shift_down(before, cur, k, row)
                parts.append(total)
                before = cur
            tail[:, lane] = before
            conv[0, pl.ds(base, 16), lane] = jnp.concatenate(parts, axis=0).astype(bf16)
        return 0

    lax.fori_loop(0, pieces, conv_piece, 0)
    gates_pre[...] = dot_nn(conv[0], w_gates[...])
    limit = length[...]

    def scan_piece(i, _):
        base = pl.multiple_of(i * 16, 16)
        start = step * rows + base
        for lane in lanes:
            second = pl.ds(width + lane.start, LANES)
            rate = -DECAY_EXP * jax.nn.softplus(-decay_param[:, lane])
            conv_two = conv[0, pl.ds(base, 16), lane].astype(f32)
            state = carry[:, lane]
            outs = []
            for half in range(2):
                at = pl.ds(base + SUB * half, SUB)
                live = (row + (start + SUB * half)) < limit
                gate_a = jax.nn.sigmoid(gates_pre[at, lane] + ga_bias[:, lane])
                gate_i = jax.nn.sigmoid(gates_pre[at, second] + gi_bias[:, lane])
                ga[0, at, lane] = gate_a
                gi[0, at, lane] = gate_i
                log_a = rate * gate_a
                decay = jnp.exp(log_a)
                scaled = jnp.sqrt(one_minus_square(log_a, decay)) * gate_i * conv_two[SUB * half : SUB * half + SUB]
                mul = jnp.where(live, decay, 1.0)
                add = jnp.where(live, scaled, 0.0)
                for shift in (1, 2, 4):
                    inside = row >= shift
                    add = add + mul * jnp.where(inside, pltpu.roll(add, shift, 0), 0.0)
                    mul = mul * jnp.where(inside, pltpu.roll(mul, shift, 0), 1.0)
                states = mul * state + add
                prev_state[0, at, lane] = jnp.where(row == 0, state, pltpu.roll(states, 1, 0))
                state = jnp.broadcast_to(states[SUB - 1 : SUB], (SUB, LANES))
                value, _ = gelu_parts(branch[0, at, lane])
                outs.append(states * value)
            carry[:, lane] = state
            mixed[0, pl.ds(base, 16), lane] = jnp.concatenate(outs, axis=0).astype(bf16)
        return 0

    lax.fori_loop(0, pieces, scan_piece, 0)
    final[...] = carry[...]
    for at in range(0, w_out.shape[1], MODEL_TILE):
        column = pl.ds(at, MODEL_TILE)
        x[:, column] = dot_nn(mixed[0], w_out[:, column]).astype(bf16)
    store_block(parts, layout, block, slice(None), x[...])


def rec_backward_kernel(layout, nshared, length, *refs):
    many = len(layout)
    d_resid_pieces, x_pieces, refs = refs[:many], refs[many : 2 * many], refs[2 * many :]
    w_out, w_both, taps, w_gates, decay_param = refs[:5]
    pre, branch, conv, ga, gi, prev_state = refs[5:11]
    d_mixed, d_conv, flow, later, x, d_resid = refs[-6:]
    outs = refs[-6 - 4 - many : -6]
    d_both, d_gates, sums, gain_sums = outs[:4]
    parts = outs[4:]
    step = pl.program_id(0)
    rows, width = pre.shape[1:]
    pieces = rows // 16
    lanes = [pl.ds(at, LANES) for at in range(0, width, LANES)]
    row = row_index((SUB, LANES))
    first = (pl.num_programs(0) - 1 - step) * rows
    limit = length[...]

    @pl.when(step == 0)
    def _():
        flow[...] = jnp.zeros_like(flow)
        later[...] = jnp.zeros_like(later)
        sums[...] = jnp.zeros_like(sums)
        gain_sums[...] = jnp.zeros_like(gain_sums)

    block = flip(pl.num_programs(0) - 1 - step, lax.axis_index("mp"), 4 if len(layout) == 5 else len(layout))
    load_block(d_resid_pieces, layout, block, d_resid)
    load_block(x_pieces, layout, block, x)
    d_mixed[...] = dot_nt(d_resid[...], w_out[...])

    def scan_piece(j, _):
        base = pl.multiple_of((pieces - 1 - j) * 16, 16)
        for lane in lanes:
            rate = -DECAY_EXP * jax.nn.softplus(-decay_param[:, lane])
            conv_two = conv[0, pl.ds(base, 16), lane].astype(f32)
            carried = flow[:, lane]
            outs = [None, None]
            sum_log = sums[0, :, lane]
            for half in (1, 0):
                at = pl.ds(base + SUB * half, SUB)
                live = (row + (first + base + SUB * half)) < limit
                conv_val = conv_two[SUB * half : SUB * half + SUB]
                gate_a = ga[0, at, lane]
                gate_i = gi[0, at, lane]
                before = prev_state[0, at, lane]
                d_mix = d_mixed[at, lane]
                log_a = rate * gate_a
                decay = jnp.exp(log_a)
                space = one_minus_square(log_a, decay)
                inverse = lax.rsqrt(jnp.maximum(space, 1e-37))
                root = space * inverse
                gated = gate_i * conv_val
                mul = jnp.where(live, decay, 1.0)
                states = mul * before + jnp.where(live, root * gated, 0.0)
                value, slope = gelu_parts(branch[0, at, lane])
                d_br = d_mix * states * slope
                direct = d_mix * value
                add = mul * direct
                for shift in (1, 2, 4):
                    inside = row < SUB - shift
                    add = add + mul * jnp.where(inside, pltpu.roll(add, SUB - shift, 0), 0.0)
                    mul = mul * jnp.where(inside, pltpu.roll(mul, SUB - shift, 0), 1.0)
                moved = add + mul * carried
                d_state = direct + jnp.where(row == SUB - 1, carried, pltpu.roll(moved, SUB - 1, 0))
                carried = jnp.broadcast_to(moved[0:1], (SUB, LANES))
                d_state = jnp.where(live, d_state, 0.0)
                d_log = d_state * decay * (before - gated * decay * inverse)
                sum_log = sum_log + d_log * gate_a
                d_gate_a = d_log * rate * gate_a * (1.0 - gate_a)
                d_rooted = d_state * root
                d_conv_rec = d_rooted * gate_i
                d_gate_i = d_rooted * conv_val * gate_i * (1.0 - gate_i)
                d_conv[at, lane] = d_conv_rec
                outs[half] = (d_br, d_gate_a, d_gate_i)
            flow[:, lane] = carried
            sums[0, :, lane] = sum_log
            second = pl.ds(width + lane.start, LANES)
            for target, there, which in ((d_both, lane, 0), (d_gates, lane, 1), (d_gates, second, 2)):
                both = jnp.concatenate([outs[0][which], outs[1][which]], axis=0).astype(bf16)
                target[0, pl.ds(base, 16), there] = both
                if which > 0:
                    wide = both.astype(f32)
                    sums[which, :, lane] += wide[:SUB] + wide[SUB:]
        return 0

    lax.fori_loop(0, pieces, scan_piece, 0)
    d_conv[...] += dot_nt(d_gates[0], w_gates[...])

    def conv_piece(j, _):
        base = pl.multiple_of((pieces - 1 - j) * 16, 16)
        for lane in lanes:
            following = later[:, lane]
            totals = [None, None]
            tap_sums = [sums[3 + k, :, lane] for k in range(5)]
            for half in (1, 0):
                at = pl.ds(base + SUB * half, SUB)
                cur = d_conv[at, lane]
                seen = pre[0, at, lane]
                tap_sums[0] = tap_sums[0] + cur
                tap_sums[1] = tap_sums[1] + cur * seen
                total = taps[0:1, lane] * cur
                for k in range(1, 4):
                    ahead = shift_up(cur, following, k, row)
                    tap_sums[1 + k] = tap_sums[1 + k] + ahead * seen
                    total = total + taps[k : k + 1, lane] * ahead
                totals[half] = total
                following = cur
            later[:, lane] = following
            for k in range(5):
                sums[3 + k, :, lane] = tap_sums[k]
            d_both[0, pl.ds(base, 16), pl.ds(width + lane.start, LANES)] = jnp.concatenate(totals, axis=0).astype(bf16)
        return 0

    lax.fori_loop(0, pieces, conv_piece, 0)
    for at in range(0, x.shape[1], MODEL_TILE):
        column = pl.ds(at, MODEL_TILE)
        part = dot_nt(d_both[0], w_both[column, :])
        seen = part * x[:, column].astype(f32)
        gain_sums[:, column] += jnp.sum(seen.reshape(rows // SUB, SUB, MODEL_TILE), axis=0)
        d_resid[:, column] = part.astype(bf16)
    store_block(parts, layout, block, slice(None), d_resid[...])


def mlp_kernel(layout, *refs):
    many = len(layout)
    x_pieces, cot_pieces, (w_gate, w_up, w_down) = refs[:many], refs[many : 2 * many], refs[2 * many : 2 * many + 3]
    x, cot, mid = refs[-3:]
    hidden, d_gate, d_up, mlp_part = refs[-3 - many - 4 : -3 - many]
    parts = refs[-3 - many : -3]
    r = pl.program_id(0)
    load_block(x_pieces, layout, r, x)
    load_block(cot_pieces, layout, r, cot)
    for at in range(0, hidden.shape[2], UNIT_TILE):
        column = pl.ds(at, UNIT_TILE)
        up = dot_nn(x[...], w_up[:, column])
        back = dot_nt(cot[...], w_down[column, :])
        value, slope = gelu_parts(dot_nn(x[...], w_gate[:, column]))
        hidden[0, :, column] = (value * up).astype(bf16)
        d_gate[0, :, column] = (back * up * slope).astype(bf16)
        d_up[0, :, column] = (back * value).astype(bf16)
    for at in range(0, cot.shape[1], MODEL_TILE):
        column = pl.ds(at, MODEL_TILE)
        mlp_part[0, :, column] = dot_nn(hidden[0], w_down[:, column]).astype(bf16)
        total = dot_nt(d_gate[0], w_gate[column, :]) + dot_nt(d_up[0], w_up[column, :])
        mid[:, column] = total.astype(bf16)
    store_block(parts, layout, r, slice(None), mid[...])


def weight_grad_kernel(by_rows, nlefts, nrights, *refs):
    lefts, rights = refs[:nlefts], refs[nlefts : nlefts + nrights]
    keep, give, left, right = refs[-4:]
    start = (pl.program_id(0) == 0) & (pl.program_id(1) == 0)

    def assemble(target, sources):
        at = 0
        for ref in sources:
            target[at : at + ref.shape[0], :] = ref[...]
            at += ref.shape[0]

    if nlefts == 1:
        left = lefts[0]
    elif by_rows:
        assemble(left, lefts)
    else:
        pl.when(start)(functools.partial(assemble, left, lefts))
    if nrights == 1:
        right = rights[0]
    elif not by_rows:
        assemble(right, rights)
    else:
        pl.when(start)(functools.partial(assemble, right, rights))
    total = lax.dot_general(
        left[...], right[...], (((0,), (0,)), ((), ())), preferred_element_type=f32
    ).astype(bf16)

    @pl.when(pl.program_id(0) == 0)
    def _():
        keep[...] = total

    @pl.when(pl.program_id(0) == 1)
    def _():
        give[...] = total


def join_kernel(info, first, second, third, fourth, *outs):
    for at, ref in enumerate((first, second, third, fourth)):

        @pl.when(pl.program_id(0) == at)
        def _(ref=ref):
            start = 0
            for out in outs:
                out[...] = ref[:, start : start + out.shape[1]].astype(f32)
                start += out.shape[1]


ANY = pl.BlockSpec(memory_space=pl.ANY)
PARAMS = pltpu.CompilerParams(vmem_limit_bytes=VMEM_BYTES)
MESH = pl.DeviceIdType.MESH


def flip(index, mask, size):
    total, bit = 0, 1
    while bit < size:
        total = total + ((index // bit + mask // bit) % 2) * bit
        bit *= 2
    return total


def neighbours():
    me = lax.axis_index("mp")
    return {"mp": flip(me, 1, 4)}, {"mp": flip(me, 2, 4)}


def remote(source, target, send, recv, at, device):
    return pltpu.make_async_remote_copy(
        src_ref=source,
        dst_ref=target,
        send_sem=send.at[at],
        recv_sem=recv.at[at],
        device_id=device,
        device_id_type=MESH,
    )


class GatherHost:
    def __init__(self, shard):
        rows, model = shard.shape
        self.operands = [shard]
        self.outputs = [jax.ShapeDtypeStruct((count, model), bf16) for count in (rows, rows, rows // 2, rows // 2)]
        self.scratch = [pltpu.SemaphoreType.DMA((4,)), pltpu.SemaphoreType.DMA((4,))]

    def copies(self, ins, outs, scratch):
        (shard,), (by_x, by_y, far_a, far_b), (send, recv) = ins, outs, scratch
        half = far_a.shape[0]
        x, y = neighbours()
        return (
            remote(shard, by_x, send, recv, 0, x),
            remote(shard, by_y, send, recv, 1, y),
            remote(by_x.at[pl.ds(0, half)], far_a, send, recv, 2, y),
            remote(by_y.at[pl.ds(half, half)], far_b, send, recv, 3, x),
        )

    def begin(self, *refs):
        for copy in self.copies(*refs)[:2]:
            copy.start()

    def middle(self, *refs):
        copies = self.copies(*refs)
        copies[0].wait_recv()
        copies[1].wait_recv()
        copies[2].start()
        copies[3].start()

    def end(self, *refs):
        copies = self.copies(*refs)
        copies[0].wait_send()
        copies[1].wait_send()
        copies[2].wait()
        copies[3].wait()

    def result(self, outs):
        return (self.operands[0],) + tuple(outs)


class ScatterHost:
    def __init__(self, parts):
        rows, model = parts[1].shape
        half = rows // 2
        self.first = parts[0]
        self.operands = list(parts[1:])
        self.outputs = [jax.ShapeDtypeStruct((rows, model), bf16)] * 2
        self.scratch = [pltpu.VMEM((half, model), bf16)] * 4 + [pltpu.SemaphoreType.DMA((6,))] * 2
        self.scratch += [pltpu.SemaphoreType.DMA((2,))]

    def copies(self, ins, outs, scratch):
        (one, two, far_a, far_b), (from_x, from_y) = ins, outs
        got_x, got_y, own_x, own_y, send, recv, local = scratch
        half = far_a.shape[0]
        low, high = pl.ds(0, half), pl.ds(half, half)
        x, y = neighbours()
        return (
            remote(far_a, got_x, send, recv, 0, x),
            remote(far_b, got_y, send, recv, 1, y),
            remote(one.at[low], from_x.at[low], send, recv, 2, x),
            remote(two.at[high], from_y.at[high], send, recv, 3, y),
            remote(own_x, from_x.at[high], send, recv, 4, x),
            remote(own_y, from_y.at[low], send, recv, 5, y),
        ), (
            pltpu.make_async_copy(one.at[high], own_x, local.at[0]),
            pltpu.make_async_copy(two.at[low], own_y, local.at[1]),
        )

    def begin(self, *refs):
        copies, locals_ = self.copies(*refs)
        for copy in copies[:4] + locals_:
            copy.start()

    def middle(self, ins, outs, scratch):
        copies, locals_ = self.copies(ins, outs, scratch)
        got_x, got_y, own_x, own_y = scratch[:4]
        for copy in locals_:
            copy.wait()
        copies[0].wait_recv()
        copies[1].wait_recv()
        own_x[...] = (own_x[...].astype(f32) + got_y[...].astype(f32)).astype(bf16)
        own_y[...] = (own_y[...].astype(f32) + got_x[...].astype(f32)).astype(bf16)
        copies[4].start()
        copies[5].start()

    def end(self, *refs):
        copies, _ = self.copies(*refs)
        copies[0].wait_send()
        copies[1].wait_send()
        for copy in copies[2:]:
            copy.wait()

    def result(self, outs):
        return self.first.astype(f32) + outs[0].astype(f32) + outs[1].astype(f32)


class SendHost:
    def __init__(self, pairs):
        self.operands = [array for array, _ in pairs]
        self.which = [which for _, which in pairs]
        self.outputs = [jax.ShapeDtypeStruct(array.shape, array.dtype) for array in self.operands]
        self.scratch = [pltpu.SemaphoreType.DMA((len(pairs),))] * 2

    def copies(self, ins, outs, scratch):
        to = neighbours()
        return [
            remote(source, target, scratch[0], scratch[1], at, to[self.which[at]])
            for at, (source, target) in enumerate(zip(ins, outs))
        ]

    def begin(self, *refs):
        for copy in self.copies(*refs):
            copy.start()

    def middle(self, *refs):
        pass

    def end(self, *refs):
        for copy in self.copies(*refs):
            copy.wait()

    def result(self, outs):
        return tuple(outs)


def call(kernel, grid, ins, outs, scratch, name, us, hosts=(), before=(), aliases=None, middle=0, unique=None):
    nins, nouts, nscratch = len(ins), len(outs), len(scratch)
    steps = math.prod(grid)

    def body(*refs):
        refs = list(refs)

        def take(count):
            part = refs[:count]
            del refs[:count]
            return part

        own_ins = take(nins)
        host_ins = [take(len(host.operands)) for host in hosts]
        take(len(before))
        own_outs = take(nouts)
        host_outs = [take(len(host.outputs)) for host in hosts]
        own_scratch = take(nscratch)
        host_refs = [(i, o, take(len(host.scratch))) for host, i, o in zip(hosts, host_ins, host_outs)]
        step = pl.program_id(0)
        if len(grid) == 2:
            step = step * grid[1] + pl.program_id(1)
        if hosts:

            @pl.when(step == 0)
            def _():
                barrier = pltpu.get_barrier_semaphore()
                for device in neighbours():
                    pl.semaphore_signal(barrier, inc=1, device_id=device, device_id_type=MESH)
                pl.semaphore_wait(barrier, 2)
                for host, there in zip(hosts, host_refs):
                    host.begin(*there)

            @pl.when(step == middle)
            def _():
                for host, there in zip(hosts, host_refs):
                    host.middle(*there)

        kernel(*own_ins, *own_outs, *own_scratch)
        if hosts:

            @pl.when(step == steps - 1)
            def _():
                for host, there in zip(hosts, host_refs):
                    host.end(*there)

    host_operands = [v for host in hosts for v in host.operands]
    host_outputs = [v for host in hosts for v in host.outputs]
    params = pltpu.CompilerParams(vmem_limit_bytes=VMEM_BYTES)
    if hosts:
        params = pltpu.CompilerParams(vmem_limit_bytes=VMEM_BYTES, collective_id=unique, has_side_effects=True)
    results = pl.pallas_call(
        body,
        out_shape=tuple(shape for shape, _ in outs) + tuple(host_outputs),
        grid=grid,
        in_specs=[spec for _, spec in ins] + [ANY] * (len(host_operands) + len(before)),
        out_specs=tuple(spec for _, spec in outs) + (ANY,) * len(host_outputs),
        scratch_shapes=list(scratch) + [v for host in hosts for v in host.scratch],
        input_output_aliases=aliases or {},
        compiler_params=params,
        cost_estimate=cost(us),
        name=name,
    )(*[array for array, _ in ins], *host_operands, *before)
    own, rest = results[:nouts], results[nouts:]
    found = []
    for host in hosts:
        found.append(host.result(rest[: len(host.outputs)]))
        rest = rest[len(host.outputs) :]
    return own, found


def cost(us):
    return pl.CostEstimate(flops=int(us * COST_SCALE * 1.15e9), bytes_accessed=1 << 16, transcendentals=0)


def whole(array):
    zeros = (0,) * array.ndim
    return pl.BlockSpec(array.shape, lambda *_: zeros, pipeline_mode=pl.Buffered(1))


def layout_of(blocks, rows):
    if blocks != 4:
        return tuple((r, 0, rows) for r in range(blocks))
    return ((0, 0, rows), (1, 0, rows), (2, 0, rows), (3, 0, rows // 2), (3, rows // 2, rows - rows // 2))


def piece_outputs(layout, model):
    shapes = tuple(jax.ShapeDtypeStruct((count, model), bf16) for _, _, count in layout)
    specs = tuple(pl.BlockSpec(shape.shape, lambda *_: (0, 0)) for shape in shapes)
    return shapes, specs


def rec_forward(length, x, params, **more):
    blocks, (rows, model) = lax.axis_size("mp"), x[0].shape
    layout = layout_of(blocks, rows)
    width = params[0].shape[1] // 2

    def at(step):
        return (flip(step, lax.axis_index("mp"), blocks), 0, 0)

    wide = pl.BlockSpec((1, rows, width), at)
    out = jax.ShapeDtypeStruct((blocks, rows, width), f32)
    low = jax.ShapeDtypeStruct((blocks, rows, width), bf16)
    shapes, specs = piece_outputs(layout, model)
    final = (jax.ShapeDtypeStruct((SUB, width), f32), pl.BlockSpec((SUB, width), lambda step: (0, 0)))
    return call(
        functools.partial(rec_forward_kernel, layout),
        (blocks,),
        [(v, whole(v)) for v in (length,) + tuple(x) + tuple(params)],
        [(shape, wide) for shape in (low, out, out, low, out, out, out)] + [final] + list(zip(shapes, specs)),
        [
            pltpu.VMEM((rows, 2 * width), f32),
            pltpu.VMEM((SUB, width), f32),
            pltpu.VMEM((SUB, width), f32),
            pltpu.VMEM((rows, model), bf16),
        ],
        "rec_forward",
        37,
        **more,
    )


def rec_backward(length, seq, count, d_resid, x, params, saved, shared, **more):
    blocks, (rows, model) = lax.axis_size("mp"), x[0].shape
    layout = layout_of(blocks, rows)
    width = saved[0].shape[2]

    def at(step):
        return (flip(blocks - 1 - step, lax.axis_index("mp"), blocks), 0, 0)

    def placed(step):
        return (seq * blocks + flip(blocks - 1 - step, lax.axis_index("mp"), blocks), 0, 0)

    wide = pl.BlockSpec((1, rows, width), at)
    double = pl.BlockSpec((1, rows, 2 * width), placed)
    low = jax.ShapeDtypeStruct((count * blocks, rows, 2 * width), bf16)
    shapes, specs = piece_outputs(layout, model)
    sums = (jax.ShapeDtypeStruct((8, SUB, width), f32), pl.BlockSpec((8, SUB, width), lambda step: (0, 0, 0)))
    gain_sums = (jax.ShapeDtypeStruct((SUB, model), f32), pl.BlockSpec((SUB, model), lambda step: (0, 0)))
    inputs = [(v, whole(v)) for v in (length,) + tuple(d_resid) + tuple(x) + tuple(params)]
    inputs += [(v, wide) for v in saved] + [(v, ANY) for v in shared]
    return call(
        functools.partial(rec_backward_kernel, layout, len(shared)),
        (blocks,),
        inputs,
        [(low, double), (low, double), sums, gain_sums] + list(zip(shapes, specs)),
        [
            pltpu.VMEM((rows, width), f32),
            pltpu.VMEM((rows, width), f32),
            pltpu.VMEM((SUB, width), f32),
            pltpu.VMEM((SUB, width), f32),
            pltpu.VMEM((rows, model), bf16),
            pltpu.VMEM((rows, model), bf16),
        ],
        "rec_backward",
        43,
        aliases={len(inputs) - len(shared) + at: at for at in range(len(shared))},
        **more,
    )


def largest_tile(total, limit, unit=LANES):
    return max(t for t in range(unit, limit + 1, unit) if total % t == 0)


def mlp_core(seq, count, x, cot, w_gate, w_up, w_down, shared, **more):
    blocks, (rows, model) = lax.axis_size("mp"), x[0].shape
    layout = layout_of(blocks, rows)
    units = w_gate.shape[1]
    low = jax.ShapeDtypeStruct((count * blocks, rows, units), bf16)
    part = pl.BlockSpec((1, rows, units), lambda r: (seq * blocks + r, 0, 0))
    long = pl.BlockSpec((1, rows, model), lambda r: (flip(r, lax.axis_index("mp"), blocks), 0, 0))
    shapes, specs = piece_outputs(layout, model)
    inputs = [(v, whole(v)) for v in tuple(x) + tuple(cot) + (w_gate, w_up, w_down)] + [(v, ANY) for v in shared]
    return call(
        functools.partial(mlp_kernel, layout),
        (blocks,),
        inputs,
        [(low, part)] * 3 + [(jax.ShapeDtypeStruct((blocks, rows, model), bf16), long)] + list(zip(shapes, specs)),
        [pltpu.VMEM((rows, model), bf16)] * 3,
        "mlp_core",
        54,
        aliases={len(inputs) - len(shared) + at: at for at in range(len(shared))},
        **more,
    )


def flat(array):
    return array.reshape(-1, array.shape[-1])


def core_index():
    return lax.axis_index("dp") % 2 if lax.axis_size("dp") == 8 else 0


def weight_grad(lefts, rights, by_rows=True, limit=512, **more):
    lefts, rights = [flat(v) for v in lefts], [flat(v) for v in rights]
    rows, columns = lefts[0].shape[1], rights[0].shape[1]
    tokens = sum(v.shape[0] for v in lefts)
    half = (rows if by_rows else columns) // 2
    tile = largest_tile(half, limit)
    steps = half // tile

    def cut(array, tiled):
        if not tiled:
            return whole(array)
        return pl.BlockSpec((array.shape[0], tile), lambda h, i: (0, (h + core_index()) % 2 * steps + i))

    def kept(h, i):
        at = i + h * (steps - 1 - i)
        return (at, 0) if by_rows else (0, at)

    def given(h, i):
        at = h * i
        return (at, 0) if by_rows else (0, at)

    shape = jax.ShapeDtypeStruct((half, columns) if by_rows else (rows, half), bf16)
    block = (tile, columns) if by_rows else (rows, tile)
    return call(
        functools.partial(weight_grad_kernel, by_rows, len(lefts), len(rights)),
        (2, steps),
        [(v, cut(v, by_rows)) for v in lefts] + [(v, cut(v, not by_rows)) for v in rights],
        [(shape, pl.BlockSpec(block, kept)), (shape, pl.BlockSpec(block, given))],
        [
            pltpu.VMEM((tokens if len(lefts) > 1 else 16, tile if by_rows else rows), bf16),
            pltpu.VMEM((tokens if len(rights) > 1 else 16, columns if by_rows else tile), bf16),
        ],
        "weight_grad",
        20 if columns > 1000 and by_rows else 13,
        **more,
    )


def join_quarters(where, quarters, by_rows, ways):
    rows, columns = quarters[0].shape
    tile = max(t for t in range(16, 256 + 1, 16) if rows % t == 0)
    steps = rows // tile

    def source(at):
        def index(p, i, where):
            return (jnp.where(p == at, i, jnp.where(p < at, 0, steps - 1)), 0)

        return pl.BlockSpec((tile, columns), index)

    def target(p, i, where):
        half, quarter = where[0] ^ (p // 2), where[1] ^ (p % 2)
        if by_rows:
            return ((half * 2 + quarter) * steps + i, 0)
        return (quarter * steps + i, half)

    shape = (4 * rows, columns // ways) if by_rows else (2 * rows, 2 * columns)
    out = jax.ShapeDtypeStruct(shape, f32)
    return pl.pallas_call(
        join_kernel,
        out_shape=(out,) * ways,
        grid_spec=pltpu.PrefetchScalarGridSpec(
            num_scalar_prefetch=1,
            grid=(4, steps),
            in_specs=[source(at) for at in range(4)],
            out_specs=(pl.BlockSpec((tile, columns // ways), target),) * ways,
        ),
        compiler_params=PARAMS,
        cost_estimate=cost(10),
        name="join_quarters",
    )(where, *quarters)


def swap(value, axis, bit):
    size = lax.axis_size(axis)
    return lax.ppermute(value, axis, [(i, i ^ bit) for i in range(size)])


def gather(shard):
    size = lax.axis_size("mp")
    if size != 4:
        return (shard,) + tuple(swap(shard, "mp", r) for r in range(1, size))
    half = shard.shape[0] // 2
    by_x = swap(shard, "mp", 1)
    by_y = swap(shard, "mp", 2)
    return (shard, by_x, by_y, swap(by_x[:half], "mp", 2), swap(by_y[half:], "mp", 1))


def scatter(parts):
    size = lax.axis_size("mp")
    if size != 4:
        total = parts[0].astype(f32)
        for r in range(1, size):
            total = total + swap(parts[r], "mp", r).astype(f32)
        return total
    half = parts[3].shape[0]
    from_x = swap(parts[3], "mp", 1)
    from_y = swap(parts[4], "mp", 2)
    for_y = jnp.concatenate([add_low(parts[2][:half], from_x), parts[2][half:]], axis=0)
    for_x = jnp.concatenate([parts[1][:half], add_low(parts[1][half:], from_y)], axis=0)
    return parts[0].astype(f32) + swap(for_y, "mp", 2).astype(f32) + swap(for_x, "mp", 1).astype(f32)


def add_low(left, right):
    return (left.astype(f32) + right.astype(f32)).astype(bf16)


def split_half(value, mine):
    half = value.shape[0] // 2
    keep = lax.dynamic_slice_in_dim(value, mine * half, half, 0)
    give = lax.dynamic_slice_in_dim(value, (1 - mine) * half, half, 0)
    return keep, give


class SumOverDp:
    def __init__(self, core, keep, give, by_rows=True, ways=1):
        if lax.axis_size("dp") != 8:
            part = jnp.concatenate([keep, give], axis=0 if by_rows else 1)
            self.totals = jnp.split(lax.psum(part, "dp").astype(f32), ways, axis=1)
            self.total = self.totals[0]
            self.pair = self.quad = self.every = part
            return
        chip = lax.axis_index("dp") // 2
        outer = jnp.where((chip == 0) | (chip == 3), 0, 1)
        self.pair = add_low(keep, swap(give, "dp", 1))
        keep, give = split_half(self.pair, outer)
        self.quad = add_low(keep, swap(give, "dp", 2))
        mirrored = lax.ppermute(self.quad, "dp", [(i, (3 - i // 2) * 2 + i % 2) for i in range(8)])
        self.every = add_low(self.quad, mirrored)
        self.paired = swap(self.every, "dp", 2)
        quarters = (self.every, self.paired, swap(self.every, "dp", 1), swap(self.paired, "dp", 1))
        where = jnp.stack([core[0], outer.astype(jnp.int32)])
        self.totals = join_quarters(where, quarters, by_rows, ways)
        self.total = self.totals[0]


def normalize(values, gain):
    return values * lax.rsqrt(jnp.mean(values * values, axis=-1, keepdims=True) + EPS) * gain


def normalize_back(values, gain, grad):
    inverse = lax.rsqrt(jnp.mean(values * values, axis=-1, keepdims=True) + EPS)
    scaled = grad * gain
    unit = values * inverse
    return inverse * (scaled - unit * jnp.mean(scaled * unit, axis=-1, keepdims=True)), unit


def dense_blocks(weight):
    blocks, inner, outer = weight.shape
    rows = [
        jnp.pad(weight[n], ((0, 0), (n * outer, (blocks - 1 - n) * outer))) for n in range(blocks)
    ]
    return jnp.concatenate(rows, axis=0)


def diagonal_blocks(full, blocks, width):
    inner = width // blocks
    return jnp.stack([full[n * inner : (n + 1) * inner, n * inner : (n + 1) * inner] for n in range(blocks)])


def per_device(
    block_in,
    norm1_gain,
    w_branch,
    w_input,
    conv_weight,
    conv_bias,
    gate_a_weight,
    gate_a_bias,
    gate_i_weight,
    gate_i_bias,
    decay_param,
    w_out,
    norm2_gain,
    w_gate,
    w_up,
    w_down,
    lengths,
    cotangent,
):
    count = block_in.shape[0]
    nblocks = gate_a_weight.shape[0]
    true_width = w_branch.shape[1]
    extra = -true_width % LANES
    me = lax.axis_index("mp")

    def pad_last(value):
        return jnp.pad(value, [(0, 0)] * (value.ndim - 1) + [(0, extra)]) if extra else value

    def line(value):
        return pad_last(value)[None, :]

    wb, wi = pad_last(w_branch), pad_last(w_input)
    wo = jnp.pad(w_out, ((0, extra), (0, 0))) if extra else w_out
    w_ga, w_gi = dense_blocks(gate_a_weight), dense_blocks(gate_i_weight)
    if extra:
        w_ga, w_gi = (jnp.pad(v, ((0, extra), (0, extra))) for v in (w_ga, w_gi))
    taps = pad_last(conv_weight)
    decay_line = line(decay_param)
    w_both = jnp.concatenate([wb, wi], axis=1)
    w_gates = jnp.concatenate([w_ga, w_gi], axis=1)
    forward_params = (
        w_both, taps, line(conv_bias), w_gates, line(gate_a_bias), line(gate_i_bias), decay_line, wo
    )
    backward_params = (wo, w_both, taps, w_gates, decay_line)
    seqs = range(count)
    limits = [jnp.full((SUB, LANES), lengths[s], jnp.int32) for s in seqs]
    core = jnp.int32(core_index()).reshape(1)
    blocks = lax.axis_size("mp")
    hosted = blocks == 4 and count == 2
    ids = iter(range(1, 100))

    def tied(value, *deps):
        return lax.optimization_barrier((value,) + deps)[0]

    def run(function, *args, hosts=(), middle=0, **more):
        if hosted and hosts:
            return function(*args, hosts=hosts, middle=middle, unique=next(ids), **more)
        out, _ = function(*args, **more)
        return out, [
            gather(host.operands[0]) if isinstance(host, GatherHost) else scatter((host.first, *host.operands))
            for host in hosts
        ]

    resid = [block_in[s].astype(f32) for s in seqs]
    starts = [normalize(resid[s], norm1_gain).astype(bf16) for s in seqs]
    piece, model = starts[0].shape
    seq_in = [gather(starts[0])]
    out, (second,) = run(rec_forward, limits[0], seq_in[0], forward_params, hosts=[GatherHost(starts[1])], middle=3)
    seq_in.append(second)
    forward = [out]
    out, (branch,) = run(
        rec_forward, limits[1], seq_in[1], forward_params, hosts=[ScatterHost(out[8:])], middle=2, before=(out[7],)
    )
    forward.append(out)
    mixed = [out[0] for out in forward]
    saved = [out[1:7] for out in forward]
    finals = [out[7][:1, :true_width] for out in forward]
    resid_mid = [resid[0] + branch]
    mids = [normalize(resid_mid[0], norm2_gain).astype(bf16)]
    seq_mid = [gather(mids[0])]
    resid_mid.append(resid[1] + scatter(forward[1][8:]))
    mids.append(normalize(resid_mid[1], norm2_gain).astype(bf16))
    cot_seq = [gather(tied(cotangent[0], forward[1][7]))]

    gathers = [GatherHost(mids[1]), GatherHost(cotangent[1])]
    out, found = run(
        mlp_core, 0, count, seq_mid[0], cot_seq[0], w_gate, w_up, w_down, (), hosts=gathers, middle=3, before=(mids[1],)
    )
    seq_mid.append(found[0])
    cot_seq.append(found[1])
    mlp_part = [out[3]]
    out, (d_mid,) = run(
        mlp_core, 1, count, seq_mid[1], cot_seq[1], w_gate, w_up, w_down, out[:3],
        hosts=[ScatterHost(out[4:])], middle=2,
    )
    mlp_part.append(out[3])
    hidden, d_gate, d_up = out[:3]
    last_parts = out[4:]

    def middle_grad(s, d_mid):
        back, unit = normalize_back(resid_mid[s], norm2_gain, d_mid)
        return cotangent[s].astype(f32) + back, jnp.sum(d_mid * unit, axis=0)

    mlp_total = [lax.psum_scatter(flat(v), "mp", scatter_dimension=0, tiled=True) for v in mlp_part]
    first, gain2 = middle_grad(0, d_mid)
    flat_mid = [p for pieces in seq_mid for p in pieces]
    flat_cot = [p for pieces in cot_seq for p in pieces]
    halves, (first_seq,) = run(weight_grad, [hidden], flat_cot, hosts=[GatherHost(first.astype(bf16))], middle=3)
    down = SumOverDp(core, *halves)
    halves, (d_mid,) = run(
        weight_grad, flat_mid, [d_gate], hosts=[ScatterHost(last_parts)], middle=2, before=(halves[0],)
    )
    gate = SumOverDp(core, *halves)
    halves, _ = run(weight_grad, flat_mid, [d_up], before=(halves[0], down.pair))
    up = SumOverDp(core, *halves)
    second, more_gain2 = middle_grad(1, d_mid)
    gain2 = gain2 + more_gain2
    d_resid = [first, second]

    out, (second_seq,) = run(
        rec_backward, limits[0], 0, count, first_seq, seq_in[0], backward_params, saved[0], (),
        hosts=[GatherHost(second.astype(bf16))], middle=3, before=(halves[0], gate.pair),
    )
    d_resid_seq = [first_seq, second_seq]
    sums, gain1 = out[2], jnp.sum(out[3], axis=0)
    out, (d_in,) = run(
        rec_backward, limits[1], 1, count, second_seq, seq_in[1], backward_params, saved[1], out[:2],
        hosts=[ScatterHost(out[4:])], middle=2, before=(down.quad, gate.quad, up.pair),
    )
    sums, gain1 = sums + out[2], gain1 + jnp.sum(out[3], axis=0)
    d_both, d_gates = out[:2]
    input_grad = [(first + normalize_back(resid[0], norm1_gain, d_in)[0]).astype(bf16)]

    flat_in = [p for pieces in seq_in for p in pieces]
    flat_resid = [p for pieces in d_resid_seq for p in pieces]
    halves, (d_in,) = run(
        weight_grad, flat_in, [d_both], hosts=[ScatterHost(out[4:])], middle=3, before=(up.quad,)
    )
    inward = SumOverDp(core, *halves, ways=2)
    halves, _ = run(weight_grad, mixed, flat_resid, False, before=(halves[0],))
    grad_w_out = SumOverDp(core, *halves, by_rows=False).total[:true_width]
    grad_w_branch, grad_w_input = (v[:, :true_width] for v in inward.totals)
    input_grad.append((second + normalize_back(resid[1], norm1_gain, d_in)[0]).astype(bf16))
    input_grad = jnp.stack(input_grad)
    block_out = jnp.stack([(resid_mid[s] + mlp_total[s].astype(f32)).astype(bf16) for s in seqs])

    gains = jnp.stack([gain1 / norm1_gain, gain2])
    for bit in range(blocks.bit_length() - 1):
        gains = gains + swap(gains, "mp", 1 << bit)
    conv = [part[2] for part in saved]
    d_gates = d_gates.reshape(count, blocks, piece, -1)
    width = d_gates.shape[-1] // 2
    full = sum(jnp.einsum("rtd,rtc->dc", conv[s], d_gates[s], preferred_element_type=f32) for s in seqs)
    full_ga = diagonal_blocks(full[:, :width], nblocks, true_width)
    full_gi = diagonal_blocks(full[:, width:], nblocks, true_width)
    vectors = jnp.sum(sums, axis=1)[:, :true_width]
    decay_grad = vectors[0] * DECAY_EXP * jax.nn.sigmoid(-decay_param)
    vectors = jnp.concatenate([decay_grad[None, :], vectors[1:]], axis=0)
    small = jnp.concatenate(
        [full_ga.reshape(-1), full_gi.reshape(-1), vectors.reshape(-1), gains.reshape(-1)]
    ).astype(bf16)
    used = small.shape[0]
    columns = 640
    padded = -(-used // (64 * columns)) * 64 * columns
    small = jnp.pad(small, (0, padded - used)).reshape(-1, columns)
    small = SumOverDp(core, *split_half(small, core[0])).total.reshape(-1)
    many, few = full_ga.size, vectors.size
    grad_gate_a_weight = small[:many].reshape(full_ga.shape)
    grad_gate_i_weight = small[many : 2 * many].reshape(full_gi.shape)
    vectors = small[2 * many : 2 * many + few].reshape(8, true_width)
    gains = small[2 * many + few : used].reshape(2, model)

    return (
        block_out,
        input_grad,
        gains[0],
        grad_w_branch,
        grad_w_input,
        vectors[4:8],
        vectors[3],
        grad_gate_a_weight,
        vectors[1],
        grad_gate_i_weight,
        vectors[2],
        vectors[0],
        grad_w_out,
        gains[1],
        gate.total,
        up.total,
        down.total,
        jnp.concatenate(finals, axis=0),
    )


def solution(mesh):
    placed = (
        P("dp", "mp", None),
        P(),
        P(None, "mp"),
        P(None, "mp"),
        P(None, "mp"),
        P("mp"),
        P("mp", None, None),
        P("mp"),
        P("mp", None, None),
        P("mp"),
        P("mp"),
        P("mp", None),
        P(),
        P(None, "mp"),
        P(None, "mp"),
        P("mp", None),
        P("dp"),
        P("dp", "mp", None),
    )
    return jax.shard_map(
        per_device,
        mesh=mesh,
        in_specs=placed,
        out_specs=(
            P("dp", "mp", None),
            P("dp", "mp", None),
            P(),
            P(None, "mp"),
            P(None, "mp"),
            P(None, "mp"),
            P("mp"),
            P("mp", None, None),
            P("mp"),
            P("mp", None, None),
            P("mp"),
            P("mp"),
            P("mp", None),
            P(),
            P(None, "mp"),
            P(None, "mp"),
            P("mp", None),
            P("dp", "mp"),
        ),
        check_vma=False,
    )
```

```python
import functools
import math

import jax
import jax.numpy as jnp
from jax import lax
from jax.experimental import pallas as pl
from jax.experimental.pallas import tpu as pltpu
from jax.sharding import PartitionSpec as P

DECAY_EXP = 8.0
EPS = 1e-06
GELU_C = math.sqrt(2.0 / math.pi)
GELU_K = 0.044715
LANES = 128
SUB = 8
UNIT_TILE = 256
COST_SCALE = 0.5
MODEL_TILE = 512
VMEM_BYTES = 56 * 1024 * 1024

f32 = jnp.float32
bf16 = jnp.bfloat16


def dot_nn(left, right):
    return lax.dot_general(left, right, (((1,), (0,)), ((), ())), preferred_element_type=f32)


def dot_nt(left, right):
    return lax.dot_general(left, right, (((1,), (1,)), ((), ())), preferred_element_type=f32)


def one_minus_square(log_a, decay):
    x = 2.0 * log_a
    tail = 1.0 + x * (1.0 / 7.0)
    for k in (6.0, 5.0, 4.0, 3.0, 2.0):
        tail = 1.0 + x * (1.0 / k) * tail
    return jnp.where(x > -0.4, -x * tail, 1.0 - decay * decay)


def gelu_parts(x):
    square = x * x
    th = jnp.tanh(GELU_C * x * (1.0 + GELU_K * square))
    half = 0.5 * (1.0 + th)
    value = x * half
    slope = half + 0.5 * x * (1.0 - th * th) * (GELU_C * (1.0 + 3.0 * GELU_K * square))
    return value, slope


def row_index(shape):
    return lax.broadcasted_iota(jnp.int32, shape, 0)


def shift_down(prev, cur, k, row):
    return jnp.where(row < k, pltpu.roll(prev, k, 0), pltpu.roll(cur, k, 0))


def shift_up(cur, following, k, row):
    return jnp.where(row < SUB - k, pltpu.roll(cur, SUB - k, 0), pltpu.roll(following, SUB - k, 0))


def load_block(pieces, layout, block, target):
    for ref, (owner, start, count) in zip(pieces, layout):

        @pl.when(block == owner)
        def _(ref=ref, start=start, count=count):
            target[pl.ds(start, count), :] = ref[...]


def store_block(pieces, layout, block, column, value):
    for ref, (owner, start, count) in zip(pieces, layout):

        @pl.when(block == owner)
        def _(ref=ref, start=start, count=count):
            ref[:, column] = value[start : start + count]


def rec_forward_kernel(layout, length, *refs):
    x_pieces, refs = refs[: len(layout)], refs[len(layout) :]
    w_both, taps, conv_bias, w_gates, ga_bias, gi_bias, decay_param, w_out = refs[:8]
    gates_pre, tail, carry, x = refs[-4:]
    outs = refs[-4 - 8 - len(layout) : -4]
    mixed, pre, branch, conv, ga, gi, prev_state, final = outs[:8]
    parts = outs[8:]
    step = pl.program_id(0)
    block = flip(step, lax.axis_index("mp"), 4 if len(layout) == 5 else len(layout))
    rows, width = mixed.shape[1:]
    load_block(x_pieces, layout, block, x)
    pieces = rows // 16
    lanes = [pl.ds(at, LANES) for at in range(0, width, LANES)]
    row = row_index((SUB, LANES))

    @pl.when(step == 0)
    def _():
        tail[...] = jnp.zeros_like(tail)
        carry[...] = jnp.zeros_like(carry)

    both = dot_nn(x[...], w_both[...])
    branch[0] = both[:, :width]
    pre[0] = both[:, width:]

    def conv_piece(i, _):
        base = pl.multiple_of(i * 16, 16)
        for lane in lanes:
            bias = conv_bias[:, lane]
            before = tail[:, lane]
            parts = []
            for half in range(2):
                cur = pre[0, pl.ds(base + SUB * half, SUB), lane]
                total = bias + taps[0:1, lane] * cur
                for k in range(1, 4):
                    total = total + taps[k : k + 1, lane] * shift_down(before, cur, k, row)
                parts.append(total)
                before = cur
            tail[:, lane] = before
            conv[0, pl.ds(base, 16), lane] = jnp.concatenate(parts, axis=0).astype(bf16)
        return 0

    lax.fori_loop(0, pieces, conv_piece, 0)
    gates_pre[...] = dot_nn(conv[0], w_gates[...])
    limit = length[...]

    def scan_piece(i, _):
        base = pl.multiple_of(i * 16, 16)
        start = step * rows + base
        for lane in lanes:
            second = pl.ds(width + lane.start, LANES)
            rate = -DECAY_EXP * jax.nn.softplus(-decay_param[:, lane])
            conv_two = conv[0, pl.ds(base, 16), lane].astype(f32)
            state = carry[:, lane]
            outs = []
            for half in range(2):
                at = pl.ds(base + SUB * half, SUB)
                live = (row + (start + SUB * half)) < limit
                gate_a = jax.nn.sigmoid(gates_pre[at, lane] + ga_bias[:, lane])
                gate_i = jax.nn.sigmoid(gates_pre[at, second] + gi_bias[:, lane])
                ga[0, at, lane] = gate_a
                gi[0, at, lane] = gate_i
                log_a = rate * gate_a
                decay = jnp.exp(log_a)
                scaled = jnp.sqrt(one_minus_square(log_a, decay)) * gate_i * conv_two[SUB * half : SUB * half + SUB]
                mul = jnp.where(live, decay, 1.0)
                add = jnp.where(live, scaled, 0.0)
                for shift in (1, 2, 4):
                    inside = row >= shift
                    add = add + mul * jnp.where(inside, pltpu.roll(add, shift, 0), 0.0)
                    mul = mul * jnp.where(inside, pltpu.roll(mul, shift, 0), 1.0)
                states = mul * state + add
                prev_state[0, at, lane] = jnp.where(row == 0, state, pltpu.roll(states, 1, 0))
                state = jnp.broadcast_to(states[SUB - 1 : SUB], (SUB, LANES))
                value, _ = gelu_parts(branch[0, at, lane])
                outs.append(states * value)
            carry[:, lane] = state
            mixed[0, pl.ds(base, 16), lane] = jnp.concatenate(outs, axis=0).astype(bf16)
        return 0

    lax.fori_loop(0, pieces, scan_piece, 0)
    final[...] = carry[...]
    for at in range(0, w_out.shape[1], MODEL_TILE):
        column = pl.ds(at, MODEL_TILE)
        x[:, column] = dot_nn(mixed[0], w_out[:, column]).astype(bf16)
    store_block(parts, layout, block, slice(None), x[...])


def rec_backward_kernel(layout, nshared, length, *refs):
    many = len(layout)
    d_resid_pieces, x_pieces, refs = refs[:many], refs[many : 2 * many], refs[2 * many :]
    w_out, w_both, taps, w_gates, decay_param = refs[:5]
    pre, branch, conv, ga, gi, prev_state = refs[5:11]
    d_mixed, d_conv, flow, later, x, d_resid = refs[-6:]
    outs = refs[-6 - 4 - many : -6]
    d_both, d_gates, sums, gain_sums = outs[:4]
    parts = outs[4:]
    step = pl.program_id(0)
    rows, width = pre.shape[1:]
    pieces = rows // 16
    lanes = [pl.ds(at, LANES) for at in range(0, width, LANES)]
    row = row_index((SUB, LANES))
    first = (pl.num_programs(0) - 1 - step) * rows
    limit = length[...]

    @pl.when(step == 0)
    def _():
        flow[...] = jnp.zeros_like(flow)
        later[...] = jnp.zeros_like(later)
        sums[...] = jnp.zeros_like(sums)
        gain_sums[...] = jnp.zeros_like(gain_sums)

    block = flip(pl.num_programs(0) - 1 - step, lax.axis_index("mp"), 4 if len(layout) == 5 else len(layout))
    load_block(d_resid_pieces, layout, block, d_resid)
    load_block(x_pieces, layout, block, x)
    d_mixed[...] = dot_nt(d_resid[...], w_out[...])

    def scan_piece(j, _):
        base = pl.multiple_of((pieces - 1 - j) * 16, 16)
        for lane in lanes:
            rate = -DECAY_EXP * jax.nn.softplus(-decay_param[:, lane])
            conv_two = conv[0, pl.ds(base, 16), lane].astype(f32)
            carried = flow[:, lane]
            outs = [None, None]
            sum_log = sums[0, :, lane]
            for half in (1, 0):
                at = pl.ds(base + SUB * half, SUB)
                live = (row + (first + base + SUB * half)) < limit
                conv_val = conv_two[SUB * half : SUB * half + SUB]
                gate_a = ga[0, at, lane]
                gate_i = gi[0, at, lane]
                before = prev_state[0, at, lane]
                d_mix = d_mixed[at, lane]
                log_a = rate * gate_a
                decay = jnp.exp(log_a)
                space = one_minus_square(log_a, decay)
                inverse = lax.rsqrt(jnp.maximum(space, 1e-37))
                root = space * inverse
                gated = gate_i * conv_val
                mul = jnp.where(live, decay, 1.0)
                states = mul * before + jnp.where(live, root * gated, 0.0)
                value, slope = gelu_parts(branch[0, at, lane])
                d_br = d_mix * states * slope
                direct = d_mix * value
                add = mul * direct
                for shift in (1, 2, 4):
                    inside = row < SUB - shift
                    add = add + mul * jnp.where(inside, pltpu.roll(add, SUB - shift, 0), 0.0)
                    mul = mul * jnp.where(inside, pltpu.roll(mul, SUB - shift, 0), 1.0)
                moved = add + mul * carried
                d_state = direct + jnp.where(row == SUB - 1, carried, pltpu.roll(moved, SUB - 1, 0))
                carried = jnp.broadcast_to(moved[0:1], (SUB, LANES))
                d_state = jnp.where(live, d_state, 0.0)
                d_log = d_state * decay * (before - gated * decay * inverse)
                sum_log = sum_log + d_log * gate_a
                d_gate_a = d_log * rate * gate_a * (1.0 - gate_a)
                d_rooted = d_state * root
                d_conv_rec = d_rooted * gate_i
                d_gate_i = d_rooted * conv_val * gate_i * (1.0 - gate_i)
                d_conv[at, lane] = d_conv_rec
                outs[half] = (d_br, d_gate_a, d_gate_i)
            flow[:, lane] = carried
            sums[0, :, lane] = sum_log
            second = pl.ds(width + lane.start, LANES)
            for target, there, which in ((d_both, lane, 0), (d_gates, lane, 1), (d_gates, second, 2)):
                both = jnp.concatenate([outs[0][which], outs[1][which]], axis=0).astype(bf16)
                target[0, pl.ds(base, 16), there] = both
                if which > 0:
                    wide = both.astype(f32)
                    sums[which, :, lane] += wide[:SUB] + wide[SUB:]
        return 0

    lax.fori_loop(0, pieces, scan_piece, 0)
    d_conv[...] += dot_nt(d_gates[0], w_gates[...])

    def conv_piece(j, _):
        base = pl.multiple_of((pieces - 1 - j) * 16, 16)
        for lane in lanes:
            following = later[:, lane]
            totals = [None, None]
            tap_sums = [sums[3 + k, :, lane] for k in range(5)]
            for half in (1, 0):
                at = pl.ds(base + SUB * half, SUB)
                cur = d_conv[at, lane]
                seen = pre[0, at, lane]
                tap_sums[0] = tap_sums[0] + cur
                tap_sums[1] = tap_sums[1] + cur * seen
                total = taps[0:1, lane] * cur
                for k in range(1, 4):
                    ahead = shift_up(cur, following, k, row)
                    tap_sums[1 + k] = tap_sums[1 + k] + ahead * seen
                    total = total + taps[k : k + 1, lane] * ahead
                totals[half] = total
                following = cur
            later[:, lane] = following
            for k in range(5):
                sums[3 + k, :, lane] = tap_sums[k]
            d_both[0, pl.ds(base, 16), pl.ds(width + lane.start, LANES)] = jnp.concatenate(totals, axis=0).astype(bf16)
        return 0

    lax.fori_loop(0, pieces, conv_piece, 0)
    for at in range(0, x.shape[1], MODEL_TILE):
        column = pl.ds(at, MODEL_TILE)
        part = dot_nt(d_both[0], w_both[column, :])
        seen = part * x[:, column].astype(f32)
        gain_sums[:, column] += jnp.sum(seen.reshape(rows // SUB, SUB, MODEL_TILE), axis=0)
        d_resid[:, column] = part.astype(bf16)
    store_block(parts, layout, block, slice(None), d_resid[...])


def mlp_forward_kernel(layout, *refs):
    many = len(layout)
    x_pieces, (w_gate, w_up, w_down) = refs[:many], refs[many : many + 3]
    hidden, gate, up, mlp_part, x = refs[-5:]
    load_block(x_pieces, layout, pl.program_id(0), x)
    for at in range(0, hidden.shape[2], UNIT_TILE):
        column = pl.ds(at, UNIT_TILE)
        up_pre = dot_nn(x[...], w_up[:, column])
        gate_pre = dot_nn(x[...], w_gate[:, column])
        value, _ = gelu_parts(gate_pre)
        hidden[0, :, column] = (value * up_pre).astype(bf16)
        gate[0, :, column] = gate_pre.astype(bf16)
        up[0, :, column] = up_pre.astype(bf16)
    for at in range(0, x.shape[1], MODEL_TILE):
        column = pl.ds(at, MODEL_TILE)
        mlp_part[0, :, column] = dot_nn(hidden[0], w_down[:, column]).astype(bf16)


def mlp_backward_kernel(layout, *refs):
    many = len(layout)
    cot_pieces, (gate, up, w_gate, w_up, w_down) = refs[:many], refs[many : many + 5]
    cot, mid = refs[-2:]
    d_gate, d_up = refs[-2 - many - 2 : -2 - many]
    parts = refs[-2 - many : -2]
    r = pl.program_id(0)
    load_block(cot_pieces, layout, r, cot)
    for at in range(0, d_gate.shape[2], UNIT_TILE):
        column = pl.ds(at, UNIT_TILE)
        back = dot_nt(cot[...], w_down[column, :])
        value, slope = gelu_parts(gate[0, :, column].astype(f32))
        d_gate[0, :, column] = (back * up[0, :, column].astype(f32) * slope).astype(bf16)
        d_up[0, :, column] = (back * value).astype(bf16)
    for at in range(0, cot.shape[1], MODEL_TILE):
        column = pl.ds(at, MODEL_TILE)
        total = dot_nt(d_gate[0], w_gate[column, :]) + dot_nt(d_up[0], w_up[column, :])
        mid[:, column] = total.astype(bf16)
    store_block(parts, layout, r, slice(None), mid[...])


def weight_grad_kernel(by_rows, nlefts, nrights, exchange, *refs):
    lefts, rights = refs[:nlefts], refs[nlefts : nlefts + nrights]
    if exchange:
        first, second, left, right, sent, got, send, recv = refs[-8:]
    else:
        out, left, right = refs[-3:]
    step = pl.program_id(0)

    def assemble(target, sources):
        at = 0
        for ref in sources:
            target[at : at + ref.shape[0], :] = ref[...]
            at += ref.shape[0]

    if nlefts == 1:
        left = lefts[0]
    elif by_rows:
        assemble(left, lefts)
    else:
        pl.when(step == 0)(functools.partial(assemble, left, lefts))
    if nrights == 1:
        right = rights[0]
    elif not by_rows:
        assemble(right, rights)
    else:
        pl.when(step == 0)(functools.partial(assemble, right, rights))
    total = lax.dot_general(left[...], right[...], (((0,), (0,)), ((), ())), preferred_element_type=f32)
    if not exchange:
        out[...] = total.astype(bf16)
        return

    def copy(at):
        return remote(sent.at[at], got.at[at], send, recv, at, other_core())

    for at in range(2):

        @pl.when(step == at)
        def _(at=at):
            sent[at] = total.astype(bf16)
            copy(at).start()

    for at, target in ((0, first), (1, second)):

        @pl.when(step == 2 + at)
        def _(at=at, target=target):
            copy(at).wait_recv()
            target[...] = (total + got[at].astype(f32)).astype(bf16)
            copy(at).wait_send()


def join_kernel(ways, first, second, third, fourth, *outs):
    for at, ref in enumerate((first, second, third, fourth)):

        @pl.when(pl.program_id(0) == at)
        def _(ref=ref):
            start = 0
            for out in outs:
                out[...] = ref[:, start : start + out.shape[1]].astype(f32)
                start += out.shape[1]


ANY = pl.BlockSpec(memory_space=pl.ANY)
PARAMS = pltpu.CompilerParams(vmem_limit_bytes=VMEM_BYTES)
MESH = pl.DeviceIdType.MESH


def flip(index, mask, size):
    total, bit = 0, 1
    while bit < size:
        total = total + ((index // bit + mask // bit) % 2) * bit
        bit *= 2
    return total


def neighbours():
    me = lax.axis_index("mp")
    return {"mp": flip(me, 1, 4)}, {"mp": flip(me, 2, 4)}


def other_core():
    return {"dp": flip(lax.axis_index("dp"), 1, 8)}


def remote(source, target, send, recv, at, device):
    return pltpu.make_async_remote_copy(
        src_ref=source,
        dst_ref=target,
        send_sem=send.at[at],
        recv_sem=recv.at[at],
        device_id=device,
        device_id_type=MESH,
    )


class GatherHost:
    def __init__(self, shard):
        rows, model = shard.shape
        self.operands = [shard]
        self.outputs = [jax.ShapeDtypeStruct((count, model), bf16) for count in (rows, rows, rows // 2, rows // 2)]
        self.scratch = [pltpu.SemaphoreType.DMA((4,)), pltpu.SemaphoreType.DMA((4,))]

    def copies(self, ins, outs, scratch):
        (shard,), (by_x, by_y, far_a, far_b), (send, recv) = ins, outs, scratch
        half = far_a.shape[0]
        x, y = neighbours()
        return (
            lambda: remote(shard, by_x, send, recv, 0, x),
            lambda: remote(shard, by_y, send, recv, 1, y),
            lambda: remote(by_x.at[pl.ds(0, half)], far_a, send, recv, 2, y),
            lambda: remote(by_y.at[pl.ds(half, half)], far_b, send, recv, 3, x),
        )

    def begin(self, *refs):
        for copy in self.copies(*refs)[:2]:
            copy().start()

    def middle(self, *refs):
        copies = self.copies(*refs)
        copies[0]().wait_recv()
        copies[1]().wait_recv()
        copies[2]().start()
        copies[3]().start()

    def end(self, *refs):
        copies = self.copies(*refs)
        copies[0]().wait_send()
        copies[1]().wait_send()
        copies[2]().wait()
        copies[3]().wait()

    def devices(self):
        return neighbours()

    def result(self, outs):
        return (self.operands[0],) + tuple(outs)


class ScatterHost:
    def __init__(self, parts):
        rows, model = parts[1].shape
        half = rows // 2
        self.first = parts[0]
        self.operands = list(parts[1:])
        self.outputs = [jax.ShapeDtypeStruct((rows, model), bf16)] * 2
        self.scratch = [pltpu.VMEM((half, model), bf16)] * 4 + [pltpu.SemaphoreType.DMA((6,))] * 2
        self.scratch += [pltpu.SemaphoreType.DMA((2,))]

    def copies(self, ins, outs, scratch):
        (one, two, far_a, far_b), (from_x, from_y) = ins, outs
        got_x, got_y, own_x, own_y, send, recv, local = scratch
        half = far_a.shape[0]
        low, high = pl.ds(0, half), pl.ds(half, half)
        x, y = neighbours()
        return (
            lambda: remote(far_a, got_x, send, recv, 0, x),
            lambda: remote(far_b, got_y, send, recv, 1, y),
            lambda: remote(one.at[low], from_x.at[low], send, recv, 2, x),
            lambda: remote(two.at[high], from_y.at[high], send, recv, 3, y),
            lambda: remote(own_x, from_x.at[high], send, recv, 4, x),
            lambda: remote(own_y, from_y.at[low], send, recv, 5, y),
            lambda: pltpu.make_async_copy(one.at[high], own_x, local.at[0]),
            lambda: pltpu.make_async_copy(two.at[low], own_y, local.at[1]),
        )

    def begin(self, *refs):
        copies = self.copies(*refs)
        for at in (0, 1, 2, 3, 6, 7):
            copies[at]().start()

    def middle(self, ins, outs, scratch):
        copies = self.copies(ins, outs, scratch)
        got_x, got_y, own_x, own_y = scratch[:4]
        copies[6]().wait()
        copies[7]().wait()
        copies[0]().wait_recv()
        copies[1]().wait_recv()
        own_x[...] = (own_x[...].astype(f32) + got_y[...].astype(f32)).astype(bf16)
        own_y[...] = (own_y[...].astype(f32) + got_x[...].astype(f32)).astype(bf16)
        copies[4]().start()
        copies[5]().start()

    def end(self, *refs):
        copies = self.copies(*refs)
        copies[0]().wait_send()
        copies[1]().wait_send()
        for at in (2, 3, 4, 5):
            copies[at]().wait()

    def devices(self):
        return neighbours()

    def result(self, outs):
        return self.first.astype(f32) + outs[0].astype(f32) + outs[1].astype(f32)


class PipeHost:
    def __init__(self, inward, between, outward):
        self.counts = len(inward), len(between), len(outward)
        self.operands = [chunk for _, chunk in inward + between + outward]
        self.names = [name for name, _ in inward + between + outward]
        self.outputs = [jax.ShapeDtypeStruct(chunk.shape, bf16) for chunk in self.operands]
        adding = len(inward) + len(between)
        self.scratch = [pltpu.VMEM(chunk.shape, bf16) for chunk in self.operands[:adding] for _ in range(2)]
        self.scratch += [pltpu.VMEM(chunk.shape, bf16) for chunk in self.operands[adding:]]
        self.scratch += [pltpu.SemaphoreType.DMA((len(self.operands),))] * 4

    def devices(self):
        dp = lax.axis_index("dp")
        return {"dp": flip(dp, 2, 8)}, {"dp": (3 - dp // 2) * 2 + dp % 2}

    def parts(self, ins, outs, scratch):
        pair, mirror = self.devices()
        send, recv, local, back = scratch[-4:]
        inward, between, _ = self.counts
        for at, (chunk, out) in enumerate(zip(ins, outs)):
            if at < inward + between:
                own, got = scratch[2 * at], scratch[2 * at + 1]
                way, device = ("in", pair) if at < inward else ("mid", mirror)
                yield (
                    way,
                    lambda chunk=chunk, got=got, at=at, device=device: remote(chunk, got, send, recv, at, device),
                    lambda chunk=chunk, own=own, at=at: pltpu.make_async_copy(chunk, own, local.at[at]),
                    lambda own=own, out=out, at=at: pltpu.make_async_copy(own, out, back.at[at]),
                    own,
                    got,
                )
            else:
                own = scratch[at + inward + between]
                yield (
                    "out",
                    lambda chunk=chunk, out=out, at=at: remote(chunk, out, send, recv, at, pair),
                    lambda chunk=chunk, own=own, at=at: pltpu.make_async_copy(chunk, own, local.at[at]),
                    lambda own=own, out=out, at=at: pltpu.make_async_copy(own, out, back.at[at]),
                    None,
                    None,
                )

    def inner(self):
        chip = lax.axis_index("dp") // 2
        return (chip + 1) // 2 % 2 == 1

    def begin(self, *refs):
        inner = self.inner()
        for way, there, here, _, _, _ in self.parts(*refs):

            @pl.when(inner)
            def _(way=way, there=there, here=here):
                here().start()
                if way != "in":
                    there().start()

            if way == "in":

                @pl.when(jnp.logical_not(inner))
                def _(there=there):
                    there().start()

    def middle(self, *refs):
        pass

    def end(self, *refs):
        inner = self.inner()
        parts = list(self.parts(*refs))
        for way, there, here, back, own, got in parts:

            @pl.when(inner)
            def _(way=way, there=there, here=here, back=back, own=own, got=got):
                here().wait()
                if way != "out":
                    there().wait_recv()
                    own[...] = (own[...].astype(f32) + got[...].astype(f32)).astype(bf16)
                back().start()
                if way != "in":
                    there().wait_send()

            if way != "mid":

                @pl.when(jnp.logical_not(inner))
                def _(way=way, there=there):
                    if way == "in":
                        there().wait_send()
                    else:
                        there().wait_recv()

        for _, _, _, back, _, _ in parts:

            @pl.when(inner)
            def _(back=back):
                back().wait()

    def result(self, outs):
        return dict(zip(self.names, outs))


class TailHost(PipeHost):
    def __init__(self, inward, between, outward):
        chunks = [(chunk, stage) for stage, group in enumerate((inward, between, outward)) for _, chunk in group]
        self.names = [name for name, _ in inward + between + outward]
        self.operands = [chunk for chunk, _ in chunks]
        self.outputs = [jax.ShapeDtypeStruct(chunk.shape, bf16) for chunk in self.operands]
        self.scratch = [pltpu.VMEM(chunk.shape, bf16) for chunk, stage in chunks for _ in range(3 - stage)]
        self.pieces = []
        for at, (chunk, stage) in enumerate(chunks):
            rows = chunk.shape[0]
            first = rows if stage == 2 else (rows // 32 + 1) // 2 * 32
            for start, count in ((0, first), (first, rows - first)):
                if count > 0:
                    self.pieces.append((at, stage, start, count))
        self.scratch += [pltpu.SemaphoreType.DMA((len(self.pieces),))] * 8

    def begin(self, ins, outs, scratch):
        pair, mirror = self.devices()
        p_send, p_recv, q_send, q_recv, f_send, f_recv, local, back = scratch[-8:]
        buffers, given = {}, 0
        for at, stage, start, _ in self.pieces:
            if start == 0:
                buffers[at] = scratch[given : given + 3 - stage]
                given += 3 - stage

        def part(ref, number):
            _, _, start, count = self.pieces[number]
            return ref.at[pl.ds(start, count)]

        def transfers(number):
            at, stage, _, _ = self.pieces[number]
            own, from_pair, from_mirror = (buffers[at] + [None, None])[:3]
            if stage == 1:
                from_mirror = from_pair
            chunk, out = part(ins[at], number), part(outs[at], number)
            done = own if stage == 2 else from_mirror
            return {
                "inward": lambda: remote(chunk, part(from_pair, number), p_send, p_recv, number, pair),
                "load": lambda: pltpu.make_async_copy(chunk, part(own, number), local.at[number]),
                "between": lambda: remote(part(own, number), part(from_mirror, number), q_send, q_recv, number, mirror),
                "outward": lambda: remote(part(done, number), out, f_send, f_recv, number, pair),
                "keep": lambda: pltpu.make_async_copy(part(done, number), out, back.at[number]),
            }

        def add(number, target, other):
            at, _, start, count = self.pieces[number]
            rows = pl.ds(start, count)
            target[rows, :] = (target[rows, :].astype(f32) + other[rows, :].astype(f32)).astype(bf16)

        numbers = range(len(self.pieces))
        moves = [transfers(number) for number in numbers]
        stages = [stage for _, stage, _, _ in self.pieces]
        inner = self.inner()

        def finish(number):
            if stages[number] < 2:
                moves[number]["between"]().wait_recv()
                own, other = buffers[self.pieces[number][0]][0], buffers[self.pieces[number][0]][-1]
                add(number, other, own)
            moves[number]["outward"]().start()
            moves[number]["keep"]().start()

        @pl.when(inner)
        def _():
            for move in moves:
                move["load"]().start()
            for number in numbers:
                if stages[number] == 2:
                    moves[number]["load"]().wait()
                    finish(number)
            for number in numbers:
                if stages[number] == 1:
                    moves[number]["load"]().wait()
                    moves[number]["between"]().start()
            waiting = [number for number in numbers if stages[number] == 1]
            for number in numbers:
                if stages[number] == 0:
                    moves[number]["load"]().wait()
                    moves[number]["inward"]().wait_recv()
                    own, other = buffers[self.pieces[number][0]][:2]
                    add(number, own, other)
                    moves[number]["between"]().start()
                    waiting.append(number)
                    finish(waiting.pop(0))
            for number in waiting:
                finish(number)
            for number in numbers:
                if stages[number] < 2:
                    moves[number]["between"]().wait_send()
                moves[number]["outward"]().wait_send()
                moves[number]["keep"]().wait()

        @pl.when(jnp.logical_not(inner))
        def _():
            for number in numbers:
                if stages[number] == 0:
                    moves[number]["inward"]().start()
            for number in numbers:
                if stages[number] == 0:
                    moves[number]["inward"]().wait_send()
                moves[number]["outward"]().wait_recv()

    def end(self, *refs):
        pass


def call(
    kernel, grid, ins, outs, scratch, name, us, hosts=(), before=(), aliases=None, middle=0, unique=None, pair=False
):
    nins, nouts, nscratch = len(ins), len(outs), len(scratch)
    steps = math.prod(grid)

    def body(*refs):
        refs = list(refs)

        def take(count):
            part = refs[:count]
            del refs[:count]
            return part

        own_ins = take(nins)
        host_ins = [take(len(host.operands)) for host in hosts]
        take(len(before))
        own_outs = take(nouts)
        host_outs = [take(len(host.outputs)) for host in hosts]
        own_scratch = take(nscratch)
        host_refs = [(i, o, take(len(host.scratch))) for host, i, o in zip(hosts, host_ins, host_outs)]
        step = pl.program_id(0)
        if len(grid) == 2:
            step = step * grid[1] + pl.program_id(1)
        if hosts or pair:

            @pl.when(step == 0)
            def _():
                devices = (other_core(),) if pair else ()
                for kind in (GatherHost, ScatterHost, PipeHost):
                    kinds = [host for host in hosts if isinstance(host, kind)]
                    if kinds and not (kind is ScatterHost and any(isinstance(host, GatherHost) for host in hosts)):
                        devices += tuple(kinds[0].devices())
                barrier = pltpu.get_barrier_semaphore()
                for device in devices:
                    pl.semaphore_signal(barrier, inc=1, device_id=device, device_id_type=MESH)
                pl.semaphore_wait(barrier, len(devices))
                for host, there in zip(hosts, host_refs):
                    host.begin(*there)

        if hosts:

            @pl.when(step == middle)
            def _():
                for host, there in zip(hosts, host_refs):
                    host.middle(*there)

        kernel(*own_ins, *own_outs, *own_scratch)
        if hosts:

            @pl.when(step == steps - 1)
            def _():
                for host, there in zip(hosts, host_refs):
                    host.end(*there)

    host_operands = [v for host in hosts for v in host.operands]
    host_outputs = [v for host in hosts for v in host.outputs]
    params = pltpu.CompilerParams(vmem_limit_bytes=VMEM_BYTES)
    if hosts or pair:
        params = pltpu.CompilerParams(vmem_limit_bytes=VMEM_BYTES, collective_id=unique, has_side_effects=True)
    results = pl.pallas_call(
        body,
        out_shape=tuple(shape for shape, _ in outs) + tuple(host_outputs),
        grid=grid,
        in_specs=[spec for _, spec in ins] + [ANY] * (len(host_operands) + len(before)),
        out_specs=tuple(spec for _, spec in outs) + (ANY,) * len(host_outputs),
        scratch_shapes=list(scratch) + [v for host in hosts for v in host.scratch],
        input_output_aliases=aliases or {},
        compiler_params=params,
        cost_estimate=cost(us),
        name=name,
    )(*[array for array, _ in ins], *host_operands, *before)
    own, rest = results[:nouts], results[nouts:]
    found = []
    for host in hosts:
        found.append(host.result(rest[: len(host.outputs)]))
        rest = rest[len(host.outputs) :]
    return own, found


def cost(us):
    return pl.CostEstimate(flops=int(us * COST_SCALE * 1.15e9), bytes_accessed=1 << 16, transcendentals=0)


def whole(array):
    zeros = (0,) * array.ndim
    return pl.BlockSpec(array.shape, lambda *_: zeros, pipeline_mode=pl.Buffered(1))


def layout_of(blocks, rows):
    if blocks != 4:
        return tuple((r, 0, rows) for r in range(blocks))
    return ((0, 0, rows), (1, 0, rows), (2, 0, rows), (3, 0, rows // 2), (3, rows // 2, rows - rows // 2))


def piece_outputs(layout, model):
    shapes = tuple(jax.ShapeDtypeStruct((count, model), bf16) for _, _, count in layout)
    specs = tuple(pl.BlockSpec(shape.shape, lambda *_: (0, 0)) for shape in shapes)
    return shapes, specs


def rec_forward(length, x, params, **more):
    blocks, (rows, model) = lax.axis_size("mp"), x[0].shape
    layout = layout_of(blocks, rows)
    width = params[0].shape[1] // 2

    def at(step):
        return (flip(step, lax.axis_index("mp"), blocks), 0, 0)

    wide = pl.BlockSpec((1, rows, width), at)
    out = jax.ShapeDtypeStruct((blocks, rows, width), f32)
    low = jax.ShapeDtypeStruct((blocks, rows, width), bf16)
    shapes, specs = piece_outputs(layout, model)
    final = (jax.ShapeDtypeStruct((SUB, width), f32), pl.BlockSpec((SUB, width), lambda step: (0, 0)))
    return call(
        functools.partial(rec_forward_kernel, layout),
        (blocks,),
        [(v, whole(v)) for v in (length,) + tuple(x) + tuple(params)],
        [(shape, wide) for shape in (low, out, out, low, out, out, out)] + [final] + list(zip(shapes, specs)),
        [
            pltpu.VMEM((rows, 2 * width), f32),
            pltpu.VMEM((SUB, width), f32),
            pltpu.VMEM((SUB, width), f32),
            pltpu.VMEM((rows, model), bf16),
        ],
        "rec_forward",
        37,
        **more,
    )


def rec_backward(length, seq, count, d_resid, x, params, saved, shared, **more):
    blocks, (rows, model) = lax.axis_size("mp"), x[0].shape
    layout = layout_of(blocks, rows)
    width = saved[0].shape[2]

    def at(step):
        return (flip(blocks - 1 - step, lax.axis_index("mp"), blocks), 0, 0)

    def placed(step):
        return (seq * blocks + flip(blocks - 1 - step, lax.axis_index("mp"), blocks), 0, 0)

    wide = pl.BlockSpec((1, rows, width), at)
    double = pl.BlockSpec((1, rows, 2 * width), placed)
    low = jax.ShapeDtypeStruct((count * blocks, rows, 2 * width), bf16)
    shapes, specs = piece_outputs(layout, model)
    sums = (jax.ShapeDtypeStruct((8, SUB, width), f32), pl.BlockSpec((8, SUB, width), lambda step: (0, 0, 0)))
    gain_sums = (jax.ShapeDtypeStruct((SUB, model), f32), pl.BlockSpec((SUB, model), lambda step: (0, 0)))
    inputs = [(v, whole(v)) for v in (length,) + tuple(d_resid) + tuple(x) + tuple(params)]
    inputs += [(v, wide) for v in saved] + [(v, ANY) for v in shared]
    return call(
        functools.partial(rec_backward_kernel, layout, len(shared)),
        (blocks,),
        inputs,
        [(low, double), (low, double), sums, gain_sums] + list(zip(shapes, specs)),
        [
            pltpu.VMEM((rows, width), f32),
            pltpu.VMEM((rows, width), f32),
            pltpu.VMEM((SUB, width), f32),
            pltpu.VMEM((SUB, width), f32),
            pltpu.VMEM((rows, model), bf16),
            pltpu.VMEM((rows, model), bf16),
        ],
        "rec_backward",
        43,
        aliases={len(inputs) - len(shared) + at: at for at in range(len(shared))},
        **more,
    )


def largest_tile(total, limit, unit=LANES):
    return max(t for t in range(unit, limit + 1, unit) if total % t == 0)


def mlp_forward(seq, count, x, w_gate, w_up, w_down, shared, **more):
    blocks, (rows, model) = lax.axis_size("mp"), x[0].shape
    units = w_gate.shape[1]
    low = jax.ShapeDtypeStruct((count * blocks, rows, units), bf16)
    part = pl.BlockSpec((1, rows, units), lambda r: (seq * blocks + r, 0, 0))
    long = pl.BlockSpec((1, rows, model), lambda r: (flip(r, lax.axis_index("mp"), blocks), 0, 0))
    inputs = [(v, whole(v)) for v in tuple(x) + (w_gate, w_up, w_down)] + [(v, ANY) for v in shared]
    return call(
        functools.partial(mlp_forward_kernel, layout_of(blocks, rows)),
        (blocks,),
        inputs,
        [(low, part)] * 3 + [(jax.ShapeDtypeStruct((blocks, rows, model), bf16), long)],
        [pltpu.VMEM((rows, model), bf16)],
        "mlp_forward",
        30,
        aliases={len(inputs) - len(shared) + at: at for at in range(len(shared))},
        **more,
    )


def mlp_backward(seq, count, cot, gate, up, w_gate, w_up, w_down, shared, **more):
    blocks, (rows, model) = lax.axis_size("mp"), cot[0].shape
    layout = layout_of(blocks, rows)
    units = w_gate.shape[1]
    low = jax.ShapeDtypeStruct((count * blocks, rows, units), bf16)
    part = pl.BlockSpec((1, rows, units), lambda r: (seq * blocks + r, 0, 0))
    shapes, specs = piece_outputs(layout, model)
    inputs = [(v, whole(v)) for v in cot] + [(gate, part), (up, part)]
    inputs += [(v, whole(v)) for v in (w_gate, w_up, w_down)] + [(v, ANY) for v in shared]
    return call(
        functools.partial(mlp_backward_kernel, layout),
        (blocks,),
        inputs,
        [(low, part)] * 2 + list(zip(shapes, specs)),
        [pltpu.VMEM((rows, model), bf16)] * 2,
        "mlp_backward",
        32,
        aliases={len(inputs) - len(shared) + at: at for at in range(len(shared))},
        **more,
    )


def flat(array):
    return array.reshape(-1, array.shape[-1])


def core_index():
    return lax.axis_index("dp") % 2 if lax.axis_size("dp") == 8 else 0


def weight_grad(lefts, rights, by_rows=True, **more):
    lefts, rights = [flat(v) for v in lefts], [flat(v) for v in rights]
    rows, columns = lefts[0].shape[1], rights[0].shape[1]
    tokens = sum(v.shape[0] for v in lefts)
    exchange = lax.axis_size("dp") == 8
    tiled = rows if by_rows else columns
    tile = tiled // 4 if exchange else largest_tile(tiled, 512)

    def place(step):
        if not exchange:
            return step
        return (core_index() + 1 + step // 2) % 2 * 2 + step % 2

    def cut(array, in_tiles):
        if not in_tiles:
            return whole(array)
        return pl.BlockSpec((array.shape[0], tile), lambda step: (0, place(step)))

    scratch = [
        pltpu.VMEM((tokens if len(lefts) > 1 else 16, tile if by_rows else rows), bf16),
        pltpu.VMEM((tokens if len(rights) > 1 else 16, columns if by_rows else tile), bf16),
    ]
    block = (tile, columns) if by_rows else (rows, tile)
    if exchange:
        outs = [(jax.ShapeDtypeStruct(block, bf16), pl.BlockSpec(block, lambda step: (0, 0)))] * 2
        scratch += [pltpu.VMEM((2,) + block, bf16)] * 2 + [pltpu.SemaphoreType.DMA((2,))] * 2
    else:
        whole_out = jax.ShapeDtypeStruct((rows, columns), bf16)
        outs = [(whole_out, pl.BlockSpec(block, lambda step: (step, 0) if by_rows else (0, step)))]
    return call(
        functools.partial(weight_grad_kernel, by_rows, len(lefts), len(rights), exchange),
        (tiled // tile,),
        [(v, cut(v, by_rows)) for v in lefts] + [(v, cut(v, not by_rows)) for v in rights],
        outs,
        scratch,
        "weight_grad",
        20 if columns > 1000 and by_rows else 13,
        pair=exchange,
        **more,
    )


def join_quarters(quarters, by_rows, ways, rows, **more):
    columns = quarters[0].shape[1]
    tile = max(t for t in range(16, 256 + 1, 16) if rows % t == 0)
    steps = rows // tile

    def source(at):
        def index(p, i):
            return (jnp.where(p == at, i, jnp.where(p < at, 0, steps - 1)), 0)

        return pl.BlockSpec((tile, columns), index)

    def target(p, i):
        at = (core_index() + p // 2) % 2 * 2 + p % 2
        return (at * steps + i, 0) if by_rows else (i, at)

    shape = (4 * rows, columns // ways) if by_rows else (rows, 4 * columns)
    out = (jax.ShapeDtypeStruct(shape, f32), pl.BlockSpec((tile, columns // ways), target))
    return call(
        functools.partial(join_kernel, ways),
        (4, steps),
        [(quarter, source(at)) for at, quarter in enumerate(quarters)],
        [out] * ways,
        [],
        "join_quarters",
        10,
        **more,
    )


def swap(value, axis, bit):
    size = lax.axis_size(axis)
    return lax.ppermute(value, axis, [(i, i ^ bit) for i in range(size)])


def gather(shard):
    size = lax.axis_size("mp")
    if size != 4:
        return (shard,) + tuple(swap(shard, "mp", r) for r in range(1, size))
    half = shard.shape[0] // 2
    by_x = swap(shard, "mp", 1)
    by_y = swap(shard, "mp", 2)
    return (shard, by_x, by_y, swap(by_x[:half], "mp", 2), swap(by_y[half:], "mp", 1))


def scatter(parts):
    size = lax.axis_size("mp")
    if size != 4:
        total = parts[0].astype(f32)
        for r in range(1, size):
            total = total + swap(parts[r], "mp", r).astype(f32)
        return total
    half = parts[3].shape[0]
    from_x = swap(parts[3], "mp", 1)
    from_y = swap(parts[4], "mp", 2)
    for_y = jnp.concatenate([add_low(parts[2][:half], from_x), parts[2][half:]], axis=0)
    for_x = jnp.concatenate([parts[1][:half], add_low(parts[1][half:], from_y)], axis=0)
    return parts[0].astype(f32) + swap(for_y, "mp", 2).astype(f32) + swap(for_x, "mp", 1).astype(f32)


def add_low(left, right):
    return (left.astype(f32) + right.astype(f32)).astype(bf16)


class Pipe:
    def __init__(self):
        self.stages = [{}, {}, {}]
        self.done = {}

    def add(self, **chunks):
        self.stages[0].update(chunks)

    def host(self):
        return PipeHost(*[list(stage.items()) for stage in self.stages])

    def took(self, results):
        inward, between, outward = self.stages
        self.done.update({name: results[name] for name in outward})
        self.stages = [{}, {name: results[name] for name in inward}, {name: results[name] for name in between}]


def add_small(quarters, small):
    columns = quarters[0].shape[1]
    small = add_low(small, swap(small, "dp", 1)).reshape(4, -1, columns)
    return [
        jnp.concatenate([quarter, lax.dynamic_index_in_dim(small, core_index() * 2 + at, 0, False)], axis=0)
        for at, quarter in enumerate(quarters)
    ]


def take_small(quarters, start):
    parts = jnp.stack([quarter[start:] for quarter in quarters])
    order = [((half + core_index()) % 2) * 2 + at for half in range(2) for at in range(2)]
    return jnp.concatenate([lax.dynamic_index_in_dim(parts, pick, 0, False) for pick in order], axis=0).astype(f32)


def normalize(values, gain):
    return values * lax.rsqrt(jnp.mean(values * values, axis=-1, keepdims=True) + EPS) * gain


def normalize_back(values, gain, grad):
    inverse = lax.rsqrt(jnp.mean(values * values, axis=-1, keepdims=True) + EPS)
    scaled = grad * gain
    unit = values * inverse
    return inverse * (scaled - unit * jnp.mean(scaled * unit, axis=-1, keepdims=True)), unit


def dense_blocks(weight):
    blocks, inner, outer = weight.shape
    rows = [
        jnp.pad(weight[n], ((0, 0), (n * outer, (blocks - 1 - n) * outer))) for n in range(blocks)
    ]
    return jnp.concatenate(rows, axis=0)


def diagonal_blocks(full, blocks, width):
    inner = width // blocks
    return jnp.stack([full[n * inner : (n + 1) * inner, n * inner : (n + 1) * inner] for n in range(blocks)])


def per_device(
    block_in,
    norm1_gain,
    w_branch,
    w_input,
    conv_weight,
    conv_bias,
    gate_a_weight,
    gate_a_bias,
    gate_i_weight,
    gate_i_bias,
    decay_param,
    w_out,
    norm2_gain,
    w_gate,
    w_up,
    w_down,
    lengths,
    cotangent,
):
    count = block_in.shape[0]
    nblocks = gate_a_weight.shape[0]
    true_width = w_branch.shape[1]
    extra = -true_width % LANES
    me = lax.axis_index("mp")

    def pad_last(value):
        return jnp.pad(value, [(0, 0)] * (value.ndim - 1) + [(0, extra)]) if extra else value

    def line(value):
        return pad_last(value)[None, :]

    wb, wi = pad_last(w_branch), pad_last(w_input)
    wo = jnp.pad(w_out, ((0, extra), (0, 0))) if extra else w_out
    w_ga, w_gi = dense_blocks(gate_a_weight), dense_blocks(gate_i_weight)
    if extra:
        w_ga, w_gi = (jnp.pad(v, ((0, extra), (0, extra))) for v in (w_ga, w_gi))
    taps = pad_last(conv_weight)
    decay_line = line(decay_param)
    w_both = jnp.concatenate([wb, wi], axis=1)
    w_gates = jnp.concatenate([w_ga, w_gi], axis=1)
    forward_params = (
        w_both, taps, line(conv_bias), w_gates, line(gate_a_bias), line(gate_i_bias), decay_line, wo
    )
    backward_params = (wo, w_both, taps, w_gates, decay_line)
    seqs = range(count)
    limits = [jnp.full((SUB, LANES), lengths[s], jnp.int32) for s in seqs]
    blocks = lax.axis_size("mp")
    hosted = blocks == 4 and count == 2
    ids = iter(range(1, 100))

    piped = hosted and lax.axis_size("dp") == 8
    pipe = Pipe()

    def enter(**chunks):
        if piped:
            pipe.add(**chunks)

    def tied(value, *deps):
        return lax.optimization_barrier((value,) + deps)[0]

    def run(function, *args, hosts=(), middle=0, **more):
        if hosted:
            moving = piped and any(pipe.stages)
            out, found = function(
                *args, hosts=list(hosts) + ([pipe.host()] if moving else []), middle=middle, unique=next(ids), **more
            )
            if moving:
                pipe.took(found[-1])
            return out, found[: len(hosts)]
        out, _ = function(*args, **more)
        return out, [
            gather(host.operands[0]) if isinstance(host, GatherHost) else scatter((host.first, *host.operands))
            for host in hosts
        ]

    resid = [block_in[s].astype(f32) for s in seqs]
    starts = [normalize(resid[s], norm1_gain).astype(bf16) for s in seqs]
    piece, model = starts[0].shape
    seq_in = [gather(starts[0])]
    out, (second,) = run(rec_forward, limits[0], seq_in[0], forward_params, hosts=[GatherHost(starts[1])], middle=3)
    seq_in.append(second)
    forward = [out]
    out, (branch,) = run(
        rec_forward, limits[1], seq_in[1], forward_params, hosts=[ScatterHost(out[8:])], middle=2, before=(out[7],)
    )
    forward.append(out)
    mixed = [out[0] for out in forward]
    saved = [out[1:7] for out in forward]
    finals = [out[7][:1, :true_width] for out in forward]
    resid_mid = [resid[0] + branch]
    mid = normalize(resid_mid[0], norm2_gain).astype(bf16)
    seq_mid = [gather(mid)]
    forward_shared, (branch,) = run(
        mlp_forward, 0, count, seq_mid[0], w_gate, w_up, w_down, (), hosts=[ScatterHost(forward[1][8:])], middle=2
    )
    mlp_part = [forward_shared[3]]
    resid_mid.append(resid[1] + branch)
    mid = normalize(resid_mid[1], norm2_gain).astype(bf16)
    seq_mid.append(gather(mid))
    forward_shared, (found,) = run(
        mlp_forward, 1, count, seq_mid[1], w_gate, w_up, w_down, forward_shared[:3],
        hosts=[GatherHost(cotangent[0])], middle=3,
    )
    mlp_part.append(forward_shared[3])
    cot_seq = [found]
    hidden, gate_low, up_low = forward_shared[:3]
    backward, (found,) = run(
        mlp_backward, 0, count, cot_seq[0], gate_low, up_low, w_gate, w_up, w_down, (),
        hosts=[GatherHost(cotangent[1])], middle=3,
    )
    cot_seq.append(found)

    def middle_grad(s, d_mid):
        back, unit = normalize_back(resid_mid[s], norm2_gain, d_mid)
        return cotangent[s].astype(f32) + back, jnp.sum(d_mid * unit, axis=0)

    flat_mid = [p for pieces in seq_mid for p in pieces]
    flat_cot = [p for pieces in cot_seq for p in pieces]
    grad_down, _ = run(weight_grad, [hidden], flat_cot)
    enter(down0=grad_down[0])
    backward, (d_mid,) = run(
        mlp_backward, 1, count, cot_seq[1], gate_low, up_low, w_gate, w_up, w_down, backward[:2],
        hosts=[ScatterHost(backward[2:])], middle=2, before=(grad_down[0],),
    )
    d_gate, d_up = backward[:2]
    first, gain2 = middle_grad(0, d_mid)
    enter(down1=grad_down[-1])
    grad_gate, (first_seq,) = run(weight_grad, flat_mid, [d_gate], hosts=[GatherHost(first.astype(bf16))], middle=3)
    enter(gate0=grad_gate[0])
    grad_up, (d_mid,) = run(
        weight_grad, flat_mid, [d_up], hosts=[ScatterHost(backward[2:])], middle=2, before=(grad_gate[0],)
    )
    second, more_gain2 = middle_grad(1, d_mid)
    gain2 = gain2 + more_gain2
    enter(gate1=grad_gate[-1])
    out, (second_seq,) = run(
        rec_backward, limits[0], 0, count, first_seq, seq_in[0], backward_params, saved[0], (),
        hosts=[GatherHost(second.astype(bf16))], middle=3, before=(grad_up[0],),
    )
    sums, gain1 = out[2], jnp.sum(out[3], axis=0)
    enter(up0=grad_up[0])
    out, (d_in,) = run(
        rec_backward, limits[1], 1, count, second_seq, seq_in[1], backward_params, saved[1], out[:2],
        hosts=[ScatterHost(out[4:])], middle=2,
    )
    sums, gain1 = sums + out[2], gain1 + jnp.sum(out[3], axis=0)
    d_both, d_gates = out[:2]
    input_grad = [(first + normalize_back(resid[0], norm1_gain, d_in)[0]).astype(bf16)]
    enter(up1=grad_up[-1])

    flat_in = [p for pieces in seq_in for p in pieces]
    flat_resid = [p for pieces in (first_seq, second_seq) for p in pieces]
    grad_in, _ = run(weight_grad, flat_in, [d_both])
    enter(in0=grad_in[0])
    grad_out, (d_in,) = run(
        weight_grad, mixed, flat_resid, False, hosts=[ScatterHost(out[4:])], middle=2, before=(grad_in[0],)
    )
    input_grad.append((second + normalize_back(resid[1], norm1_gain, d_in)[0]).astype(bf16))
    input_grad = jnp.stack(input_grad)

    gains = jnp.stack([gain1 / norm1_gain, gain2])
    for bit in range(blocks.bit_length() - 1):
        gains = gains + swap(gains, "mp", 1 << bit)
    conv = [part[2] for part in saved]
    d_gates = d_gates.reshape(count, blocks, piece, -1)
    width = d_gates.shape[-1] // 2
    full = sum(jnp.einsum("rtd,rtc->dc", conv[s], d_gates[s], preferred_element_type=f32) for s in seqs)
    full_ga = diagonal_blocks(full[:, :width], nblocks, true_width)
    full_gi = diagonal_blocks(full[:, width:], nblocks, true_width)
    vectors = jnp.sum(sums, axis=1)[:, :true_width]
    decay_grad = vectors[0] * DECAY_EXP * jax.nn.sigmoid(-decay_param)
    vectors = jnp.concatenate([decay_grad[None, :], vectors[1:]], axis=0)
    small = jnp.concatenate(
        [full_ga.reshape(-1), full_gi.reshape(-1), vectors.reshape(-1), gains.reshape(-1)]
    ).astype(bf16)
    used = small.shape[0]
    unit = 4 * 16 * model // 4
    small = jnp.pad(small, (0, -used % unit)).reshape(4, -1, model // 4)
    if piped:

        def join(name, grad, before=(), by_rows=True, ways=1):
            first, second = (pipe.done[name + at] for at in "01")
            quarters = (first, second, swap(first, "dp", 1), swap(second, "dp", 1))
            return join_quarters(quarters, by_rows, ways, grad[0].shape[0], before=before)[0], quarters

        with_small = add_small(grad_out, small)
        enter(in1=grad_in[-1], out0=with_small[0], out1=with_small[1])
        last = TailHost(*[list(stage.items()) for stage in pipe.stages])
        _, (found,) = call(
            lambda: None, (1,), [], [], [], "sum_tail", 90, hosts=[last], before=(grad_out[0],), unique=next(ids)
        )
        pipe.done.update(found)
        totals_down, _ = join("down", grad_down)
        totals_gate, _ = join("gate", grad_gate)
        totals_up, _ = join("up", grad_up)
        totals_in, _ = join("in", grad_in, ways=2)
        totals_out, quarters = join("out", grad_out, by_rows=False)
        small = take_small(quarters, grad_out[0].shape[0])
    else:
        small = lax.psum(small, "dp").astype(f32)
        totals_down, totals_gate, totals_up, totals_in, totals_out = (
            jnp.split(lax.psum(v[0], "dp").astype(f32), ways, axis=1)
            for v, ways in ((grad_down, 1), (grad_gate, 1), (grad_up, 1), (grad_in, 2), (grad_out, 1))
        )
    grad_w_out = totals_out[0][:true_width]
    grad_w_branch, grad_w_input = (v[:, :true_width] for v in totals_in)
    mlp_total = [
        lax.psum_scatter(flat(tied(v, grad_out[0])), "mp", scatter_dimension=0, tiled=True) for v in mlp_part
    ]
    block_out = jnp.stack([(resid_mid[s] + mlp_total[s].astype(f32)).astype(bf16) for s in seqs])

    small = small.reshape(-1)
    many, few = full_ga.size, vectors.size
    grad_gate_a_weight = small[:many].reshape(full_ga.shape)
    grad_gate_i_weight = small[many : 2 * many].reshape(full_gi.shape)
    vectors = small[2 * many : 2 * many + few].reshape(8, true_width)
    gains = small[2 * many + few : used].reshape(2, model)

    return (
        block_out,
        input_grad,
        gains[0],
        grad_w_branch,
        grad_w_input,
        vectors[4:8],
        vectors[3],
        grad_gate_a_weight,
        vectors[1],
        grad_gate_i_weight,
        vectors[2],
        vectors[0],
        grad_w_out,
        gains[1],
        totals_gate[0],
        totals_up[0],
        totals_down[0],
        jnp.concatenate(finals, axis=0),
    )


def solution(mesh):
    placed = (
        P("dp", "mp", None),
        P(),
        P(None, "mp"),
        P(None, "mp"),
        P(None, "mp"),
        P("mp"),
        P("mp", None, None),
        P("mp"),
        P("mp", None, None),
        P("mp"),
        P("mp"),
        P("mp", None),
        P(),
        P(None, "mp"),
        P(None, "mp"),
        P("mp", None),
        P("dp"),
        P("dp", "mp", None),
    )
    return jax.shard_map(
        per_device,
        mesh=mesh,
        in_specs=placed,
        out_specs=(
            P("dp", "mp", None),
            P("dp", "mp", None),
            P(),
            P(None, "mp"),
            P(None, "mp"),
            P(None, "mp"),
            P("mp"),
            P("mp", None, None),
            P("mp"),
            P("mp", None, None),
            P("mp"),
            P("mp"),
            P("mp", None),
            P(),
            P(None, "mp"),
            P(None, "mp"),
            P("mp", None),
            P("dp", "mp"),
        ),
        check_vma=False,
    )
```

```python
import functools
import math

import jax
import jax.numpy as jnp
from jax import lax
from jax.experimental import pallas as pl
from jax.experimental.pallas import tpu as pltpu
from jax.sharding import PartitionSpec as P

DECAY_EXP = 8.0
EPS = 1e-06
GELU_C = math.sqrt(2.0 / math.pi)
GELU_K = 0.044715
LANES = 128
SUB = 8
UNIT_TILE = 256
COST_SCALE = 0.5
MODEL_TILE = 512
VMEM_BYTES = 56 * 1024 * 1024

f32 = jnp.float32
bf16 = jnp.bfloat16


def dot_nn(left, right):
    return lax.dot_general(left, right, (((1,), (0,)), ((), ())), preferred_element_type=f32)


def dot_nt(left, right):
    return lax.dot_general(left, right, (((1,), (1,)), ((), ())), preferred_element_type=f32)


def one_minus_square(log_a, decay):
    x = 2.0 * log_a
    tail = 1.0 + x * (1.0 / 7.0)
    for k in (6.0, 5.0, 4.0, 3.0, 2.0):
        tail = 1.0 + x * (1.0 / k) * tail
    return jnp.where(x > -0.4, -x * tail, 1.0 - decay * decay)


def gelu_parts(x):
    square = x * x
    th = jnp.tanh(GELU_C * x * (1.0 + GELU_K * square))
    half = 0.5 * (1.0 + th)
    value = x * half
    slope = half + 0.5 * x * (1.0 - th * th) * (GELU_C * (1.0 + 3.0 * GELU_K * square))
    return value, slope


def row_index(shape):
    return lax.broadcasted_iota(jnp.int32, shape, 0)


def shift_down(prev, cur, k, row):
    return jnp.where(row < k, pltpu.roll(prev, k, 0), pltpu.roll(cur, k, 0))


def shift_up(cur, following, k, row):
    return jnp.where(row < SUB - k, pltpu.roll(cur, SUB - k, 0), pltpu.roll(following, SUB - k, 0))


def load_block(pieces, layout, block, target):
    for ref, (owner, start, count) in zip(pieces, layout):

        @pl.when(block == owner)
        def _(ref=ref, start=start, count=count):
            target[pl.ds(start, count), :] = ref[...]


def store_block(pieces, layout, block, column, value):
    for ref, (owner, start, count) in zip(pieces, layout):

        @pl.when(block == owner)
        def _(ref=ref, start=start, count=count):
            ref[:, column] = value[start : start + count]


def rec_forward_kernel(layout, length, *refs):
    x_pieces, refs = refs[: len(layout)], refs[len(layout) :]
    w_both, taps, conv_bias, w_gates, ga_bias, gi_bias, decay_param, w_out = refs[:8]
    gates_pre, tail, carry, x = refs[-4:]
    outs = refs[-4 - 8 - len(layout) : -4]
    mixed, pre, branch, conv, ga, gi, prev_state, final = outs[:8]
    parts = outs[8:]
    step = pl.program_id(0)
    block = flip(step, lax.axis_index("mp"), 4 if len(layout) == 5 else len(layout))
    rows, width = mixed.shape[1:]
    load_block(x_pieces, layout, block, x)
    pieces = rows // 16
    lanes = [pl.ds(at, LANES) for at in range(0, width, LANES)]
    row = row_index((SUB, LANES))

    @pl.when(step == 0)
    def _():
        tail[...] = jnp.zeros_like(tail)
        carry[...] = jnp.zeros_like(carry)

    both = dot_nn(x[...], w_both[...])
    branch[0] = both[:, :width]
    pre[0] = both[:, width:]

    def conv_piece(i, _):
        base = pl.multiple_of(i * 16, 16)
        for lane in lanes:
            bias = conv_bias[:, lane]
            before = tail[:, lane]
            parts = []
            for half in range(2):
                cur = pre[0, pl.ds(base + SUB * half, SUB), lane]
                total = bias + taps[0:1, lane] * cur
                for k in range(1, 4):
                    total = total + taps[k : k + 1, lane] * shift_down(before, cur, k, row)
                parts.append(total)
                before = cur
            tail[:, lane] = before
            conv[0, pl.ds(base, 16), lane] = jnp.concatenate(parts, axis=0).astype(bf16)
        return 0

    lax.fori_loop(0, pieces, conv_piece, 0)
    gates_pre[...] = dot_nn(conv[0], w_gates[...])
    limit = length[...]

    def scan_piece(i, _):
        base = pl.multiple_of(i * 16, 16)
        start = step * rows + base
        for lane in lanes:
            second = pl.ds(width + lane.start, LANES)
            rate = -DECAY_EXP * jax.nn.softplus(-decay_param[:, lane])
            conv_two = conv[0, pl.ds(base, 16), lane].astype(f32)
            state = carry[:, lane]
            outs = []
            for half in range(2):
                at = pl.ds(base + SUB * half, SUB)
                live = (row + (start + SUB * half)) < limit
                gate_a = jax.nn.sigmoid(gates_pre[at, lane] + ga_bias[:, lane])
                gate_i = jax.nn.sigmoid(gates_pre[at, second] + gi_bias[:, lane])
                ga[0, at, lane] = gate_a
                gi[0, at, lane] = gate_i
                log_a = rate * gate_a
                decay = jnp.exp(log_a)
                scaled = jnp.sqrt(one_minus_square(log_a, decay)) * gate_i * conv_two[SUB * half : SUB * half + SUB]
                mul = jnp.where(live, decay, 1.0)
                add = jnp.where(live, scaled, 0.0)
                for shift in (1, 2, 4):
                    inside = row >= shift
                    add = add + mul * jnp.where(inside, pltpu.roll(add, shift, 0), 0.0)
                    mul = mul * jnp.where(inside, pltpu.roll(mul, shift, 0), 1.0)
                states = mul * state + add
                prev_state[0, at, lane] = jnp.where(row == 0, state, pltpu.roll(states, 1, 0))
                state = jnp.broadcast_to(states[SUB - 1 : SUB], (SUB, LANES))
                value, _ = gelu_parts(branch[0, at, lane])
                outs.append(states * value)
            carry[:, lane] = state
            mixed[0, pl.ds(base, 16), lane] = jnp.concatenate(outs, axis=0).astype(bf16)
        return 0

    lax.fori_loop(0, pieces, scan_piece, 0)
    final[...] = carry[...]
    for at in range(0, w_out.shape[1], MODEL_TILE):
        column = pl.ds(at, MODEL_TILE)
        x[:, column] = dot_nn(mixed[0], w_out[:, column]).astype(bf16)
    store_block(parts, layout, block, slice(None), x[...])


def rec_backward_kernel(layout, nshared, length, *refs):
    many = len(layout)
    d_resid_pieces, x_pieces, refs = refs[:many], refs[many : 2 * many], refs[2 * many :]
    w_out, w_both, taps, w_gates, decay_param = refs[:5]
    pre, branch, conv, ga, gi, prev_state = refs[5:11]
    d_mixed, d_conv, flow, later, x, d_resid = refs[-6:]
    outs = refs[-6 - 4 - many : -6]
    d_both, d_gates, sums, gain_sums = outs[:4]
    parts = outs[4:]
    step = pl.program_id(0)
    rows, width = pre.shape[1:]
    pieces = rows // 16
    lanes = [pl.ds(at, LANES) for at in range(0, width, LANES)]
    row = row_index((SUB, LANES))
    first = (pl.num_programs(0) - 1 - step) * rows
    limit = length[...]

    @pl.when(step == 0)
    def _():
        flow[...] = jnp.zeros_like(flow)
        later[...] = jnp.zeros_like(later)
        sums[...] = jnp.zeros_like(sums)
        gain_sums[...] = jnp.zeros_like(gain_sums)

    block = flip(pl.num_programs(0) - 1 - step, lax.axis_index("mp"), 4 if len(layout) == 5 else len(layout))
    load_block(d_resid_pieces, layout, block, d_resid)
    load_block(x_pieces, layout, block, x)
    d_mixed[...] = dot_nt(d_resid[...], w_out[...])

    def scan_piece(j, _):
        base = pl.multiple_of((pieces - 1 - j) * 16, 16)
        for lane in lanes:
            rate = -DECAY_EXP * jax.nn.softplus(-decay_param[:, lane])
            conv_two = conv[0, pl.ds(base, 16), lane].astype(f32)
            carried = flow[:, lane]
            outs = [None, None]
            sum_log = sums[0, :, lane]
            for half in (1, 0):
                at = pl.ds(base + SUB * half, SUB)
                live = (row + (first + base + SUB * half)) < limit
                conv_val = conv_two[SUB * half : SUB * half + SUB]
                gate_a = ga[0, at, lane]
                gate_i = gi[0, at, lane]
                before = prev_state[0, at, lane]
                d_mix = d_mixed[at, lane]
                log_a = rate * gate_a
                decay = jnp.exp(log_a)
                space = one_minus_square(log_a, decay)
                inverse = lax.rsqrt(jnp.maximum(space, 1e-37))
                root = space * inverse
                gated = gate_i * conv_val
                mul = jnp.where(live, decay, 1.0)
                states = mul * before + jnp.where(live, root * gated, 0.0)
                value, slope = gelu_parts(branch[0, at, lane])
                d_br = d_mix * states * slope
                direct = d_mix * value
                add = mul * direct
                for shift in (1, 2, 4):
                    inside = row < SUB - shift
                    add = add + mul * jnp.where(inside, pltpu.roll(add, SUB - shift, 0), 0.0)
                    mul = mul * jnp.where(inside, pltpu.roll(mul, SUB - shift, 0), 1.0)
                moved = add + mul * carried
                d_state = direct + jnp.where(row == SUB - 1, carried, pltpu.roll(moved, SUB - 1, 0))
                carried = jnp.broadcast_to(moved[0:1], (SUB, LANES))
                d_state = jnp.where(live, d_state, 0.0)
                d_log = d_state * decay * (before - gated * decay * inverse)
                sum_log = sum_log + d_log * gate_a
                d_gate_a = d_log * rate * gate_a * (1.0 - gate_a)
                d_rooted = d_state * root
                d_conv_rec = d_rooted * gate_i
                d_gate_i = d_rooted * conv_val * gate_i * (1.0 - gate_i)
                d_conv[at, lane] = d_conv_rec
                outs[half] = (d_br, d_gate_a, d_gate_i)
            flow[:, lane] = carried
            sums[0, :, lane] = sum_log
            second = pl.ds(width + lane.start, LANES)
            for target, there, which in ((d_both, lane, 0), (d_gates, lane, 1), (d_gates, second, 2)):
                both = jnp.concatenate([outs[0][which], outs[1][which]], axis=0).astype(bf16)
                target[0, pl.ds(base, 16), there] = both
                if which > 0:
                    wide = both.astype(f32)
                    sums[which, :, lane] += wide[:SUB] + wide[SUB:]
        return 0

    lax.fori_loop(0, pieces, scan_piece, 0)
    d_conv[...] += dot_nt(d_gates[0], w_gates[...])

    def conv_piece(j, _):
        base = pl.multiple_of((pieces - 1 - j) * 16, 16)
        for lane in lanes:
            following = later[:, lane]
            totals = [None, None]
            tap_sums = [sums[3 + k, :, lane] for k in range(5)]
            for half in (1, 0):
                at = pl.ds(base + SUB * half, SUB)
                cur = d_conv[at, lane]
                seen = pre[0, at, lane]
                tap_sums[0] = tap_sums[0] + cur
                tap_sums[1] = tap_sums[1] + cur * seen
                total = taps[0:1, lane] * cur
                for k in range(1, 4):
                    ahead = shift_up(cur, following, k, row)
                    tap_sums[1 + k] = tap_sums[1 + k] + ahead * seen
                    total = total + taps[k : k + 1, lane] * ahead
                totals[half] = total
                following = cur
            later[:, lane] = following
            for k in range(5):
                sums[3 + k, :, lane] = tap_sums[k]
            d_both[0, pl.ds(base, 16), pl.ds(width + lane.start, LANES)] = jnp.concatenate(totals, axis=0).astype(bf16)
        return 0

    lax.fori_loop(0, pieces, conv_piece, 0)
    for at in range(0, x.shape[1], MODEL_TILE):
        column = pl.ds(at, MODEL_TILE)
        part = dot_nt(d_both[0], w_both[column, :])
        seen = part * x[:, column].astype(f32)
        gain_sums[:, column] += jnp.sum(seen.reshape(rows // SUB, SUB, MODEL_TILE), axis=0)
        d_resid[:, column] = part.astype(bf16)
    store_block(parts, layout, block, slice(None), d_resid[...])


def mlp_forward_kernel(layout, *refs):
    many = len(layout)
    x_pieces, (w_gate, w_up, w_down) = refs[:many], refs[many : many + 3]
    hidden, gate, up, mlp_part, x = refs[-5:]
    load_block(x_pieces, layout, pl.program_id(0), x)
    for at in range(0, hidden.shape[2], UNIT_TILE):
        column = pl.ds(at, UNIT_TILE)
        up_pre = dot_nn(x[...], w_up[:, column])
        gate_pre = dot_nn(x[...], w_gate[:, column])
        value, _ = gelu_parts(gate_pre)
        hidden[0, :, column] = (value * up_pre).astype(bf16)
        gate[0, :, column] = gate_pre.astype(bf16)
        up[0, :, column] = up_pre.astype(bf16)
    for at in range(0, x.shape[1], MODEL_TILE):
        column = pl.ds(at, MODEL_TILE)
        mlp_part[0, :, column] = dot_nn(hidden[0], w_down[:, column]).astype(bf16)


def mlp_backward_kernel(layout, *refs):
    many = len(layout)
    cot_pieces, (gate, up, w_gate, w_up, w_down) = refs[:many], refs[many : many + 5]
    cot, mid = refs[-2:]
    d_gate, d_up = refs[-2 - many - 2 : -2 - many]
    parts = refs[-2 - many : -2]
    r = pl.program_id(0)
    load_block(cot_pieces, layout, r, cot)
    for at in range(0, d_gate.shape[2], UNIT_TILE):
        column = pl.ds(at, UNIT_TILE)
        back = dot_nt(cot[...], w_down[column, :])
        value, slope = gelu_parts(gate[0, :, column].astype(f32))
        d_gate[0, :, column] = (back * up[0, :, column].astype(f32) * slope).astype(bf16)
        d_up[0, :, column] = (back * value).astype(bf16)
    for at in range(0, cot.shape[1], MODEL_TILE):
        column = pl.ds(at, MODEL_TILE)
        total = dot_nt(d_gate[0], w_gate[column, :]) + dot_nt(d_up[0], w_up[column, :])
        mid[:, column] = total.astype(bf16)
    store_block(parts, layout, r, slice(None), mid[...])


def weight_grad_kernel(by_rows, nlefts, nrights, exchange, *refs):
    lefts, rights = refs[:nlefts], refs[nlefts : nlefts + nrights]
    if exchange:
        first, second, left, right, sent, got, send, recv = refs[-8:]
    else:
        out, left, right = refs[-3:]
    step = pl.program_id(0)

    def assemble(target, sources):
        at = 0
        for ref in sources:
            target[at : at + ref.shape[0], :] = ref[...]
            at += ref.shape[0]

    if nlefts == 1:
        left = lefts[0]
    elif by_rows:
        assemble(left, lefts)
    else:
        pl.when(step == 0)(functools.partial(assemble, left, lefts))
    if nrights == 1:
        right = rights[0]
    elif not by_rows:
        assemble(right, rights)
    else:
        pl.when(step == 0)(functools.partial(assemble, right, rights))
    total = lax.dot_general(left[...], right[...], (((0,), (0,)), ((), ())), preferred_element_type=f32)
    if not exchange:
        out[...] = total.astype(bf16)
        return

    def copy(at):
        return remote(sent.at[at], got.at[at], send, recv, at, other_core())

    for at in range(2):

        @pl.when(step == at)
        def _(at=at):
            sent[at] = total.astype(bf16)
            copy(at).start()

    for at, target in ((0, first), (1, second)):

        @pl.when(step == 2 + at)
        def _(at=at, target=target):
            copy(at).wait_recv()
            target[...] = (total + got[at].astype(f32)).astype(bf16)
            copy(at).wait_send()


def join_kernel(starts, *refs):
    step = pl.program_id(0)
    outs = refs[len(starts) - 1 :]
    for ref, first, after in zip(refs, starts, starts[1:]):

        @pl.when((step >= first) & (step < after))
        def _(ref=ref):
            start = 0
            for out in outs:
                out[...] = ref[:, start : start + out.shape[1]].astype(f32)
                start += out.shape[1]


ANY = pl.BlockSpec(memory_space=pl.ANY)
PARAMS = pltpu.CompilerParams(vmem_limit_bytes=VMEM_BYTES)
MESH = pl.DeviceIdType.MESH


def flip(index, mask, size):
    total, bit = 0, 1
    while bit < size:
        total = total + ((index // bit + mask // bit) % 2) * bit
        bit *= 2
    return total


def neighbours():
    me = lax.axis_index("mp")
    return {"mp": flip(me, 1, 4)}, {"mp": flip(me, 2, 4)}


def other_core():
    return {"dp": flip(lax.axis_index("dp"), 1, 8)}


def remote(source, target, send, recv, at, device):
    return pltpu.make_async_remote_copy(
        src_ref=source,
        dst_ref=target,
        send_sem=send.at[at],
        recv_sem=recv.at[at],
        device_id=device,
        device_id_type=MESH,
    )


class GatherHost:
    def __init__(self, shard):
        rows, model = shard.shape
        self.operands = [shard]
        self.outputs = [jax.ShapeDtypeStruct((count, model), bf16) for count in (rows, rows, rows // 2, rows // 2)]
        self.scratch = [pltpu.SemaphoreType.DMA((4,)), pltpu.SemaphoreType.DMA((4,))]

    def copies(self, ins, outs, scratch):
        (shard,), (by_x, by_y, far_a, far_b), (send, recv) = ins, outs, scratch
        half = far_a.shape[0]
        x, y = neighbours()
        return (
            lambda: remote(shard, by_x, send, recv, 0, x),
            lambda: remote(shard, by_y, send, recv, 1, y),
            lambda: remote(by_x.at[pl.ds(0, half)], far_a, send, recv, 2, y),
            lambda: remote(by_y.at[pl.ds(half, half)], far_b, send, recv, 3, x),
        )

    def begin(self, *refs):
        for copy in self.copies(*refs)[:2]:
            copy().start()

    def middle(self, *refs):
        copies = self.copies(*refs)
        copies[0]().wait_recv()
        copies[1]().wait_recv()
        copies[2]().start()
        copies[3]().start()

    def end(self, *refs):
        copies = self.copies(*refs)
        copies[0]().wait_send()
        copies[1]().wait_send()
        copies[2]().wait()
        copies[3]().wait()

    def devices(self):
        return neighbours()

    def result(self, outs):
        return (self.operands[0],) + tuple(outs)


class ScatterHost:
    def __init__(self, parts):
        rows, model = parts[1].shape
        half = rows // 2
        self.first = parts[0]
        self.operands = list(parts[1:])
        self.outputs = [jax.ShapeDtypeStruct((rows, model), bf16)] * 2
        self.scratch = [pltpu.VMEM((half, model), bf16)] * 4 + [pltpu.SemaphoreType.DMA((6,))] * 2
        self.scratch += [pltpu.SemaphoreType.DMA((2,))]

    def copies(self, ins, outs, scratch):
        (one, two, far_a, far_b), (from_x, from_y) = ins, outs
        got_x, got_y, own_x, own_y, send, recv, local = scratch
        half = far_a.shape[0]
        low, high = pl.ds(0, half), pl.ds(half, half)
        x, y = neighbours()
        return (
            lambda: remote(far_a, got_x, send, recv, 0, x),
            lambda: remote(far_b, got_y, send, recv, 1, y),
            lambda: remote(one.at[low], from_x.at[low], send, recv, 2, x),
            lambda: remote(two.at[high], from_y.at[high], send, recv, 3, y),
            lambda: remote(own_x, from_x.at[high], send, recv, 4, x),
            lambda: remote(own_y, from_y.at[low], send, recv, 5, y),
            lambda: pltpu.make_async_copy(one.at[high], own_x, local.at[0]),
            lambda: pltpu.make_async_copy(two.at[low], own_y, local.at[1]),
        )

    def begin(self, *refs):
        copies = self.copies(*refs)
        for at in (0, 1, 2, 3, 6, 7):
            copies[at]().start()

    def middle(self, ins, outs, scratch):
        copies = self.copies(ins, outs, scratch)
        got_x, got_y, own_x, own_y = scratch[:4]
        copies[6]().wait()
        copies[7]().wait()
        copies[0]().wait_recv()
        copies[1]().wait_recv()
        own_x[...] = (own_x[...].astype(f32) + got_y[...].astype(f32)).astype(bf16)
        own_y[...] = (own_y[...].astype(f32) + got_x[...].astype(f32)).astype(bf16)
        copies[4]().start()
        copies[5]().start()

    def end(self, *refs):
        copies = self.copies(*refs)
        copies[0]().wait_send()
        copies[1]().wait_send()
        for at in (2, 3, 4, 5):
            copies[at]().wait()

    def devices(self):
        return neighbours()

    def result(self, outs):
        return self.first.astype(f32) + outs[0].astype(f32) + outs[1].astype(f32)


def chip_partners():
    dp = lax.axis_index("dp")
    return {"dp": flip(dp, 2, 8)}, {"dp": (3 - dp // 2) * 2 + dp % 2}


def chip_is_inner():
    return (lax.axis_index("dp") // 2 + 1) // 2 % 2 == 1


class PipeHost:
    def __init__(self, pieces):
        self.pieces = pieces
        self.names = [piece[0] for piece in pieces]
        self.operands = [piece[1] for piece in pieces]
        self.outputs = [jax.ShapeDtypeStruct((piece[3], piece[1].shape[1]), bf16) for piece in pieces]
        self.scratch = []
        for (_, _, _, _, stage, hops), out in zip(pieces, self.outputs):
            self.scratch += [pltpu.VMEM(out.shape, bf16)] * (1 + min(hops, 2 - stage))
        self.scratch += [pltpu.SemaphoreType.DMA((len(pieces),))] * 6

    def devices(self):
        return chip_partners()

    def parts(self, ins, outs, scratch):
        pair, mirror = chip_partners()
        send, recv, send_on, recv_on, local, back = scratch[-6:]
        given = 0
        for at, ((_, _, start, count, stage, hops), array, out) in enumerate(zip(self.pieces, ins, outs)):
            many = 1 + min(hops, 2 - stage)
            buffers = list(scratch[given : given + many])
            given += many
            source = array.at[pl.ds(start, count)]

            def hop(number, at=at, stage=stage, source=source, buffers=buffers, out=out):
                way = stage + number
                target = out if way == 2 else buffers[number + 1]
                sems = (send, recv) if number == 0 else (send_on, recv_on)
                return remote(source if number == 0 else buffers[number], target, *sems, at, mirror if way == 1 else pair)

            def load(at=at, source=source, buffers=buffers):
                return pltpu.make_async_copy(source, buffers[0], local.at[at])

            def keep(at=at, buffers=buffers, out=out):
                return pltpu.make_async_copy(buffers[-1], out, back.at[at])

            yield stage, hops, buffers, hop, load, keep

    def add(self, target, other):
        target[...] = (target[...].astype(f32) + other[...].astype(f32)).astype(bf16)

    def begin(self, *refs):
        inner = chip_is_inner()
        for stage, _, _, hop, load, _ in self.parts(*refs):

            @pl.when(inner)
            def _(stage=stage, hop=hop, load=load):
                load().start()
                if stage > 0:
                    hop(0).start()

            if stage == 0:

                @pl.when(jnp.logical_not(inner))
                def _(hop=hop):
                    hop(0).start()

    def middle(self, *refs):
        inner = chip_is_inner()
        for stage, hops, buffers, hop, load, keep in self.parts(*refs):

            @pl.when(inner)
            def _(stage=stage, hops=hops, buffers=buffers, hop=hop, load=load, keep=keep):
                load().wait()
                if stage == 2:
                    keep().start()
                elif hops == 2:
                    hop(0).wait_recv()
                    self.add(buffers[1], buffers[0])
                    hop(1).start()
                    if stage == 1:
                        keep().start()

    def end(self, *refs):
        inner = chip_is_inner()
        parts = list(self.parts(*refs))
        for stage, hops, buffers, hop, load, keep in parts:

            @pl.when(inner)
            def _(stage=stage, hops=hops, buffers=buffers, hop=hop, load=load, keep=keep):
                if stage > 0:
                    hop(0).wait_send()
                if hops == 2:
                    hop(1).wait_send()
                if stage + hops < 3:
                    hop(hops - 1).wait_recv()
                    self.add(buffers[-1], buffers[-2])
                    keep().start()

            @pl.when(jnp.logical_not(inner))
            def _(stage=stage, hops=hops, hop=hop):
                if stage == 0:
                    hop(0).wait_send()
                if stage + hops == 3:
                    hop(hops - 1).wait_recv()

        for _, _, _, _, _, keep in parts:

            @pl.when(inner)
            def _(keep=keep):
                keep().wait()

    def result(self, outs):
        return dict(zip(self.names, outs))


class Tail:
    def __init__(self, chunks):
        self.chunks = chunks
        self.pieces = []
        for at, (shape, stage, _, _) in enumerate(chunks):
            rows = shape[0]
            first = rows if stage == 2 or rows < 64 else (rows // 32 + 1) // 2 * 32
            self.pieces += [(at, start, count) for start, count in ((0, first), (first, rows - first)) if count > 0]
        self.scratch = []
        for shape, stage, late, _ in chunks:
            self.scratch += [pltpu.VMEM(shape, bf16)] * (3 - stage - (1 if late else 0))
        self.scratch += [pltpu.SemaphoreType.DMA((len(self.pieces),))] * 8

    def setup(self, refs, outs, scratch):
        pair, mirror = chip_partners()
        p_send, p_recv, q_send, q_recv, f_send, f_recv, local, back = scratch[-8:]
        buffers, given = [], 0
        for ref, (_, stage, late, _) in zip(refs, self.chunks):
            count = 3 - stage - (1 if late else 0)
            mine = ([ref] if late else []) + list(scratch[given : given + count])
            given += count
            buffers.append(mine if stage == 0 else [mine[0], None, mine[-1]])

        def transfers(number):
            at, start, count = self.pieces[number]
            rows = pl.ds(start, count)
            own, from_pair, from_mirror = buffers[at]
            early = self.chunks[at][1]
            source, out = refs[at].at[rows], outs[at].at[rows]
            sent = source if early == 1 else own.at[rows]
            done = own if early == 2 else from_mirror
            given_out = source if early == 2 else done.at[rows]
            return {
                "inward": lambda: remote(source, from_pair.at[rows], p_send, p_recv, number, pair),
                "load": lambda: pltpu.make_async_copy(source, own.at[rows], local.at[number]),
                "between": lambda: remote(sent, from_mirror.at[rows], q_send, q_recv, number, mirror),
                "outward": lambda: remote(given_out, out, f_send, f_recv, number, pair),
                "keep": lambda: pltpu.make_async_copy(done.at[rows], out, back.at[number]),
            }

        self.buffers = buffers
        self.moves = [transfers(number) for number in range(len(self.pieces))]
        self.stages = [self.chunks[at][1] for at, _, _ in self.pieces]
        self.late = [self.chunks[at][2] for at, _, _ in self.pieces]
        self.out = [self.chunks[at][3] for at, _, _ in self.pieces]
        self.inner = chip_is_inner()

    def start(self):
        @pl.when(self.inner)
        def _():
            for move, stage, late in zip(self.moves, self.stages, self.late):
                if stage == 2:
                    move["outward"]().start()
                if stage == 1:
                    move["between"]().start()
                if not late:
                    move["load"]().start()

        @pl.when(jnp.logical_not(self.inner))
        def _():
            for move, stage, late in zip(self.moves, self.stages, self.late):
                if stage == 0 and not late:
                    move["inward"]().start()

    def add(self, number, target, other):
        _, start, count = self.pieces[number]
        rows = pl.ds(start, count)
        target[rows, :] = (target[rows, :].astype(f32) + other[rows, :].astype(f32)).astype(bf16)

    def finish(self):
        numbers = range(len(self.pieces))

        def on(number):
            self.moves[number]["between"]().wait_recv()
            own, _, other = self.buffers[self.pieces[number][0]]
            self.add(number, other, own)
            if self.out[number]:
                self.moves[number]["outward"]().start()
            self.moves[number]["keep"]().start()

        @pl.when(self.inner)
        def _():
            for number in numbers:
                if not self.late[number]:
                    self.moves[number]["load"]().wait()
                if self.stages[number] == 2:
                    self.moves[number]["keep"]().start()
            waiting = [number for number in numbers if self.stages[number] == 1]
            for number in numbers:
                if self.stages[number] == 0:
                    self.moves[number]["inward"]().wait_recv()
                    own, other, _ = self.buffers[self.pieces[number][0]]
                    self.add(number, own, other)
                    self.moves[number]["between"]().start()
                    waiting.append(number)
                    on(waiting.pop(0))
            for number in waiting:
                on(number)
            for number in numbers:
                if self.stages[number] < 2:
                    self.moves[number]["between"]().wait_send()
                if self.out[number]:
                    self.moves[number]["outward"]().wait_send()
                self.moves[number]["keep"]().wait()

        @pl.when(jnp.logical_not(self.inner))
        def _():
            for number in numbers:
                if self.stages[number] == 0 and self.late[number]:
                    self.moves[number]["inward"]().start()
            for number in numbers:
                if self.stages[number] == 0:
                    self.moves[number]["inward"]().wait_send()
                if self.out[number]:
                    self.moves[number]["outward"]().wait_recv()


def call(
    kernel, grid, ins, outs, scratch, name, us, hosts=(), before=(), aliases=None, middle=0, unique=None, pair=False, chips=False,
    pipe_middle=0
):
    nins, nouts, nscratch = len(ins), len(outs), len(scratch)
    steps = math.prod(grid)
    loaded = [at for at, (_, spec) in enumerate(ins) if spec is WHOLE]

    def body(*refs):
        refs = list(refs)

        def take(count):
            part = refs[:count]
            del refs[:count]
            return part

        own_ins = take(nins)
        host_ins = [take(len(host.operands)) for host in hosts]
        take(len(before))
        own_outs = take(nouts)
        host_outs = [take(len(host.outputs)) for host in hosts]
        own_scratch = take(nscratch)
        host_refs = [(i, o, take(len(host.scratch))) for host, i, o in zip(hosts, host_ins, host_outs)]
        buffers = take(len(loaded))
        step = pl.program_id(0)
        if len(grid) == 2:
            step = step * grid[1] + pl.program_id(1)
        if hosts or pair:

            @pl.when(step == 0)
            def _():
                devices = (other_core(),) if pair else ()
                for kind in (GatherHost, ScatterHost, PipeHost):
                    kinds = [host for host in hosts if isinstance(host, kind)]
                    if kinds and not (kind is ScatterHost and any(isinstance(host, GatherHost) for host in hosts)):
                        devices += tuple(kinds[0].devices())
                if chips:
                    devices += tuple(chip_partners())
                barrier = pltpu.get_barrier_semaphore()
                for device in devices:
                    pl.semaphore_signal(barrier, inc=1, device_id=device, device_id_type=MESH)
                pl.semaphore_wait(barrier, len(devices))
                for host, there in zip(hosts, host_refs):
                    host.begin(*there)

        if loaded:
            arrived = take(1)[0]
            loads = [(own_ins[at], buffer, arrived.at[k]) for k, (at, buffer) in enumerate(zip(loaded, buffers))]

            @pl.when(step == 0)
            def _():
                for load in loads:
                    pltpu.make_async_copy(*load).start()
                for load in loads:
                    pltpu.make_async_copy(*load).wait()

            for at, buffer in zip(loaded, buffers):
                own_ins[at] = buffer
        if hosts:

            for host, there in list(zip(hosts, host_refs))[::-1]:
                at = pipe_middle if isinstance(host, PipeHost) else middle

                @pl.when(step == at)
                def _(host=host, there=there):
                    host.middle(*there)

        kernel(*own_ins, *own_outs, *own_scratch)
        if hosts:

            @pl.when(step == steps - 1)
            def _():
                for host, there in zip(hosts, host_refs):
                    host.end(*there)

    host_operands = [v for host in hosts for v in host.operands]
    host_outputs = [v for host in hosts for v in host.outputs]
    params = pltpu.CompilerParams(vmem_limit_bytes=VMEM_BYTES)
    if hosts or pair:
        params = pltpu.CompilerParams(vmem_limit_bytes=VMEM_BYTES, collective_id=unique, has_side_effects=True)
    results = pl.pallas_call(
        body,
        out_shape=tuple(shape for shape, _ in outs) + tuple(host_outputs),
        grid=grid,
        in_specs=[ANY if spec is WHOLE else spec for _, spec in ins] + [ANY] * (len(host_operands) + len(before)),
        out_specs=tuple(spec for _, spec in outs) + (ANY,) * len(host_outputs),
        scratch_shapes=list(scratch)
        + [v for host in hosts for v in host.scratch]
        + [pltpu.VMEM(ins[at][0].shape, ins[at][0].dtype) for at in loaded]
        + ([pltpu.SemaphoreType.DMA((len(loaded),))] if loaded else []),
        input_output_aliases=aliases or {},
        compiler_params=params,
        cost_estimate=cost(us),
        name=name,
    )(*[array for array, _ in ins], *host_operands, *before)
    own, rest = results[:nouts], results[nouts:]
    found = []
    for host in hosts:
        found.append(host.result(rest[: len(host.outputs)]))
        rest = rest[len(host.outputs) :]
    return own, found


def cost(us):
    return pl.CostEstimate(flops=int(us * COST_SCALE * 1.15e9), bytes_accessed=1 << 16, transcendentals=0)


WHOLE = "whole"


def whole(array):
    return WHOLE


def layout_of(blocks, rows):
    if blocks != 4:
        return tuple((r, 0, rows) for r in range(blocks))
    return ((0, 0, rows), (1, 0, rows), (2, 0, rows), (3, 0, rows // 2), (3, rows // 2, rows - rows // 2))


def piece_outputs(layout, model):
    shapes = tuple(jax.ShapeDtypeStruct((count, model), bf16) for _, _, count in layout)
    specs = tuple(pl.BlockSpec(shape.shape, lambda *_: (0, 0)) for shape in shapes)
    return shapes, specs


def rec_forward(length, x, params, **more):
    blocks, (rows, model) = lax.axis_size("mp"), x[0].shape
    layout = layout_of(blocks, rows)
    width = params[0].shape[1] // 2

    def at(step):
        return (flip(step, lax.axis_index("mp"), blocks), 0, 0)

    wide = pl.BlockSpec((1, rows, width), at)
    out = jax.ShapeDtypeStruct((blocks, rows, width), f32)
    low = jax.ShapeDtypeStruct((blocks, rows, width), bf16)
    shapes, specs = piece_outputs(layout, model)
    final = (jax.ShapeDtypeStruct((SUB, width), f32), pl.BlockSpec((SUB, width), lambda step: (0, 0)))
    return call(
        functools.partial(rec_forward_kernel, layout),
        (blocks,),
        [(v, whole(v)) for v in (length,) + tuple(x) + tuple(params)],
        [(shape, wide) for shape in (low, out, out, low, out, out, out)] + [final] + list(zip(shapes, specs)),
        [
            pltpu.VMEM((rows, 2 * width), f32),
            pltpu.VMEM((SUB, width), f32),
            pltpu.VMEM((SUB, width), f32),
            pltpu.VMEM((rows, model), bf16),
        ],
        "rec_forward",
        37,
        **more,
    )


def rec_backward(length, seq, count, d_resid, x, params, saved, shared, **more):
    blocks, (rows, model) = lax.axis_size("mp"), x[0].shape
    layout = layout_of(blocks, rows)
    width = saved[0].shape[2]

    def at(step):
        return (flip(blocks - 1 - step, lax.axis_index("mp"), blocks), 0, 0)

    def placed(step):
        return (seq * blocks + flip(blocks - 1 - step, lax.axis_index("mp"), blocks), 0, 0)

    wide = pl.BlockSpec((1, rows, width), at)
    double = pl.BlockSpec((1, rows, 2 * width), placed)
    low = jax.ShapeDtypeStruct((count * blocks, rows, 2 * width), bf16)
    shapes, specs = piece_outputs(layout, model)
    sums = (jax.ShapeDtypeStruct((8, SUB, width), f32), pl.BlockSpec((8, SUB, width), lambda step: (0, 0, 0)))
    gain_sums = (jax.ShapeDtypeStruct((SUB, model), f32), pl.BlockSpec((SUB, model), lambda step: (0, 0)))
    inputs = [(v, whole(v)) for v in (length,) + tuple(d_resid) + tuple(x) + tuple(params)]
    inputs += [(v, wide) for v in saved] + [(v, ANY) for v in shared]
    return call(
        functools.partial(rec_backward_kernel, layout, len(shared)),
        (blocks,),
        inputs,
        [(low, double), (low, double), sums, gain_sums] + list(zip(shapes, specs)),
        [
            pltpu.VMEM((rows, width), f32),
            pltpu.VMEM((rows, width), f32),
            pltpu.VMEM((SUB, width), f32),
            pltpu.VMEM((SUB, width), f32),
            pltpu.VMEM((rows, model), bf16),
            pltpu.VMEM((rows, model), bf16),
        ],
        "rec_backward",
        43,
        aliases={len(inputs) - len(shared) + at: at for at in range(len(shared))},
        **more,
    )


def largest_tile(total, limit, unit=LANES):
    return max(t for t in range(unit, limit + 1, unit) if total % t == 0)


def mlp_forward(seq, count, x, w_gate, w_up, w_down, shared, **more):
    blocks, (rows, model) = lax.axis_size("mp"), x[0].shape
    units = w_gate.shape[1]
    low = jax.ShapeDtypeStruct((count * blocks, rows, units), bf16)
    part = pl.BlockSpec((1, rows, units), lambda r: (seq * blocks + r, 0, 0))
    long = pl.BlockSpec((1, rows, model), lambda r: (flip(r, lax.axis_index("mp"), blocks), 0, 0))
    inputs = [(v, whole(v)) for v in tuple(x) + (w_gate, w_up, w_down)] + [(v, ANY) for v in shared]
    return call(
        functools.partial(mlp_forward_kernel, layout_of(blocks, rows)),
        (blocks,),
        inputs,
        [(low, part)] * 3 + [(jax.ShapeDtypeStruct((blocks, rows, model), bf16), long)],
        [pltpu.VMEM((rows, model), bf16)],
        "mlp_forward",
        30,
        aliases={len(inputs) - len(shared) + at: at for at in range(len(shared))},
        **more,
    )


def mlp_backward(seq, count, cot, gate, up, w_gate, w_up, w_down, shared, **more):
    blocks, (rows, model) = lax.axis_size("mp"), cot[0].shape
    layout = layout_of(blocks, rows)
    units = w_gate.shape[1]
    low = jax.ShapeDtypeStruct((count * blocks, rows, units), bf16)
    part = pl.BlockSpec((1, rows, units), lambda r: (seq * blocks + r, 0, 0))
    shapes, specs = piece_outputs(layout, model)
    inputs = [(v, whole(v)) for v in cot] + [(gate, part), (up, part)]
    inputs += [(v, whole(v)) for v in (w_gate, w_up, w_down)] + [(v, ANY) for v in shared]
    return call(
        functools.partial(mlp_backward_kernel, layout),
        (blocks,),
        inputs,
        [(low, part)] * 2 + list(zip(shapes, specs)),
        [pltpu.VMEM((rows, model), bf16)] * 2,
        "mlp_backward",
        32,
        aliases={len(inputs) - len(shared) + at: at for at in range(len(shared))},
        **more,
    )


def flat(array):
    return array.reshape(-1, array.shape[-1])


def core_index():
    return lax.axis_index("dp") % 2 if lax.axis_size("dp") == 8 else 0


def weight_grad(lefts, rights, by_rows=True, **more):
    lefts, rights = [flat(v) for v in lefts], [flat(v) for v in rights]
    rows, columns = lefts[0].shape[1], rights[0].shape[1]
    tokens = sum(v.shape[0] for v in lefts)
    exchange = lax.axis_size("dp") == 8
    tiled = rows if by_rows else columns
    tile = tiled // 4 if exchange else largest_tile(tiled, 512)

    def place(step):
        if not exchange:
            return step
        return (core_index() + 1 + step // 2) % 2 * 2 + step % 2

    def cut(array, in_tiles):
        if not in_tiles:
            return whole(array)
        return pl.BlockSpec((array.shape[0], tile), lambda step: (0, place(step)))

    scratch = [
        pltpu.VMEM((tokens if len(lefts) > 1 else 16, tile if by_rows else rows), bf16),
        pltpu.VMEM((tokens if len(rights) > 1 else 16, columns if by_rows else tile), bf16),
    ]
    block = (tile, columns) if by_rows else (rows, tile)
    if exchange:
        outs = [(jax.ShapeDtypeStruct(block, bf16), pl.BlockSpec(block, lambda step: (0, 0)))] * 2
        scratch += [pltpu.VMEM((2,) + block, bf16)] * 2 + [pltpu.SemaphoreType.DMA((2,))] * 2
    else:
        whole_out = jax.ShapeDtypeStruct((rows, columns), bf16)
        outs = [(whole_out, pl.BlockSpec(block, lambda step: (step, 0) if by_rows else (0, step)))]
    return call(
        functools.partial(weight_grad_kernel, by_rows, len(lefts), len(rights), exchange),
        (tiled // tile,),
        [(v, cut(v, by_rows)) for v in lefts] + [(v, cut(v, not by_rows)) for v in rights],
        outs,
        scratch,
        "weight_grad",
        20 if columns > 1000 and by_rows else 13,
        pair=exchange,
        **more,
    )


def last_kernel(nlefts, nrights, nchunks, nblocks, tail, *refs):
    lefts, refs = refs[:nlefts], refs[nlefts:]
    rights, refs = refs[:nrights], refs[nrights:]
    convs, refs = refs[:nlefts], refs[nlefts:]
    d_gates, sums_a, sums_b, gain_a, gain_b, gain_c, gain_d = refs[:7]
    chunks, refs = refs[7 : 7 + nchunks], refs[7 + nchunks :]
    outs, scratch = refs[: nchunks + 4], refs[nchunks + 4 :]
    pack, gains, first, second, whole_pack, got_pack, left, right, dense, sent, got, send, recv = scratch[:13]
    step = pl.program_id(0)
    tail.setup(list(chunks) + [pack, gains, first, second], outs, scratch[13:])
    pl.when(step == 0)(tail.start)

    def copy(at):
        return remote(sent.at[at], got.at[at], send, recv, at, other_core())

    def pack_copy():
        return remote(whole_pack, got_pack, send, recv, 2, other_core())

    @pl.when(step < 4)
    def _():
        at = 0
        for ref in rights:
            right[at : at + ref.shape[0], :] = ref[...]
            at += ref.shape[0]

    @pl.when(step == 0)
    def _():
        at = 0
        for ref in lefts:
            left[at : at + ref.shape[0], :] = ref[...]
            at += ref.shape[0]

    for at in range(4):

        @pl.when(step == at)
        def _(at=at):
            total = lax.dot_general(left[...], right[...], (((0,), (0,)), ((), ())), preferred_element_type=f32)
            if at < 2:
                sent[at] = total.astype(bf16)
                copy(at).start()
            else:
                copy(at - 2).wait_recv()
                (first, second)[at - 2][...] = (total + got[at - 2].astype(f32)).astype(bf16)
                copy(at - 2).wait_send()

    @pl.when(step == 3)
    def _():
        at = 0
        for ref in convs:
            rows = ref.shape[0]
            term = lax.dot_general(
                ref[...], d_gates[at : at + rows, :], (((0,), (0,)), ((), ())), preferred_element_type=f32
            )
            dense[...] = term if at == 0 else dense[...] + term
            at += rows
        width = dense.shape[0]
        inner = width // nblocks
        lane = lax.broadcasted_iota(jnp.int32, (inner, width), 1)
        for gate in range(2):
            total = jnp.zeros((inner, width), f32)
            for n in range(nblocks):
                here = (lane >= n * inner) & (lane < (n + 1) * inner)
                block = dense[n * inner : (n + 1) * inner, gate * width : (gate + 1) * width]
                total = total + jnp.where(here, block, 0.0)
            whole_pack[gate * inner : (gate + 1) * inner, :] = total.astype(bf16)
        vectors = jnp.sum(sums_a[...] + sums_b[...], axis=1)
        rest = whole_pack.shape[0] - 2 * inner
        vectors = jnp.concatenate([vectors, jnp.zeros((rest - 8, width), f32)], axis=0)
        whole_pack[2 * inner :, :] = vectors.astype(bf16)
        pack_copy().start()
        one = jnp.sum(gain_a[...] + gain_b[...], axis=0, keepdims=True)
        two = gain_c[...] + gain_d[...]
        row = lax.broadcasted_iota(jnp.int32, (16, one.shape[1]), 0)
        gains[...] = jnp.where(row == 0, one, jnp.where(row == 1, two, 0.0)).astype(bf16)

    @pl.when(step == 4)
    def _():
        pack_copy().wait()
        mine = pl.ds(pl.multiple_of(core_index() * pack.shape[0], 16), pack.shape[0])
        pack[...] = (whole_pack[mine, :].astype(f32) + got_pack[mine, :].astype(f32)).astype(bf16)
        tail.finish()


def last_grad(lefts, rights, convs, d_gates, vectors, moving, nblocks, **more):
    lefts, rights, convs = ([flat(v) for v in group] for group in (lefts, rights, convs))
    rows, columns = lefts[0].shape[1], rights[0].shape[1]
    tokens = sum(v.shape[0] for v in lefts)
    tile = columns // 4

    def place(step):
        step = step - step // 4
        return (core_index() + 1 + step // 2) % 2 * 2 + step % 2

    chunks = [(chunk, stage) for stage, group in enumerate(moving) for _, chunk in group.items()]
    names = [name for group in moving for name in group]
    block = (rows, tile)
    packed = -(-(2 * rows // nblocks + 16) // 32) * 32
    made = [((packed // 2, rows), True), ((16, columns), True), (block, False), (block, False)]
    tail = Tail(
        [(chunk.shape, stage, False, True) for chunk, stage in chunks] + [(shape, 0, True, out) for shape, out in made]
    )
    outs = [jax.ShapeDtypeStruct(chunk[0], bf16) for chunk in tail.chunks]
    out, found = call(
        functools.partial(last_kernel, len(lefts), len(rights), len(chunks), nblocks, tail),
        (5,),
        [(v, whole(v)) for v in lefts]
        + [(v, pl.BlockSpec((v.shape[0], tile), lambda step: (0, place(step)))) for v in rights]
        + [(v, whole(v)) for v in convs + [flat(d_gates)] + list(vectors)]
        + [(chunk, ANY) for chunk, _ in chunks],
        [(shape, ANY) for shape in outs],
        [pltpu.VMEM(shape, bf16) for shape, _ in made]
        + [
            pltpu.VMEM((packed, rows), bf16),
            pltpu.VMEM((packed, rows), bf16),
            pltpu.VMEM((tokens, rows), bf16),
            pltpu.VMEM((tokens, tile), bf16),
            pltpu.VMEM((rows, 2 * rows), f32),
            pltpu.VMEM((2,) + block, bf16),
            pltpu.VMEM((2,) + block, bf16),
            pltpu.SemaphoreType.DMA((3,)),
            pltpu.SemaphoreType.DMA((3,)),
        ]
        + tail.scratch,
        "last_grad",
        120,
        pair=True,
        chips=True,
        **more,
    )
    return dict(zip(names + ["pack", "gains", "out0", "out1"], out)), found


def join_pieces(pieces, by_rows, ways, **more):
    columns = pieces[0].shape[1]
    half = len(pieces) // 2
    rows = pieces[0].shape[0] if not by_rows else sum(piece.shape[0] for piece in pieces[:half])
    unit = math.gcd(*[piece.shape[0] for piece in pieces])
    tile = max(t for t in range(16, 256 + 1, 16) if unit % t == 0)
    counts = [piece.shape[0] // tile for piece in pieces]
    starts = [sum(counts[:at]) for at in range(len(counts))]
    steps = sum(counts)

    def source(at):
        def index(i):
            return (jnp.clip(i - starts[at], 0, counts[at] - 1), 0)

        return pl.BlockSpec((tile, columns), index)

    def target(i):
        at = (i + core_index() * (steps // 2)) % steps
        return (at, 0) if by_rows else (at % counts[0], at // counts[0])

    shape = (2 * rows, columns // ways) if by_rows else (rows, len(pieces) * columns)
    out = (jax.ShapeDtypeStruct(shape, f32), pl.BlockSpec((tile, columns // ways), target))
    return call(
        functools.partial(join_kernel, tuple(starts) + (steps,)),
        (steps,),
        [(piece, source(at)) for at, piece in enumerate(pieces)],
        [out] * ways,
        [],
        "join_pieces",
        0.05,
        **more,
    )


def swap(value, axis, bit):
    size = lax.axis_size(axis)
    return lax.ppermute(value, axis, [(i, i ^ bit) for i in range(size)])


def gather(shard):
    size = lax.axis_size("mp")
    if size != 4:
        return (shard,) + tuple(swap(shard, "mp", r) for r in range(1, size))
    half = shard.shape[0] // 2
    by_x = swap(shard, "mp", 1)
    by_y = swap(shard, "mp", 2)
    return (shard, by_x, by_y, swap(by_x[:half], "mp", 2), swap(by_y[half:], "mp", 1))


def scatter(parts):
    size = lax.axis_size("mp")
    if size != 4:
        total = parts[0].astype(f32)
        for r in range(1, size):
            total = total + swap(parts[r], "mp", r).astype(f32)
        return total
    half = parts[3].shape[0]
    from_x = swap(parts[3], "mp", 1)
    from_y = swap(parts[4], "mp", 2)
    for_y = jnp.concatenate([add_low(parts[2][:half], from_x), parts[2][half:]], axis=0)
    for_x = jnp.concatenate([parts[1][:half], add_low(parts[1][half:], from_y)], axis=0)
    return parts[0].astype(f32) + swap(for_y, "mp", 2).astype(f32) + swap(for_x, "mp", 1).astype(f32)


def add_low(left, right):
    return (left.astype(f32) + right.astype(f32)).astype(bf16)


class Pipe:
    def __init__(self):
        self.queue, self.moving, self.done = [], [], {}

    def enter(self, name, quarters):
        self.queue += [[name + str(at), quarter, 0] for at, quarter in enumerate(quarters)]

    def host(self, budget):
        pieces = [(name, array, 0, array.shape[0], stage, 3 - stage) for name, array, stage in self.moving]
        cuts, left = [], budget
        while self.queue and left > 0:
            name, array, start = self.queue[0]
            unit = array.shape[0] // 4
            units = min((array.shape[0] - start) // unit, left)
            cuts.append((name, array, start, units))
            left -= units
            self.queue[0][2] += units * unit
            if self.queue[0][2] == array.shape[0]:
                self.queue.pop(0)
        early = sum(units for _, _, _, units in cuts) // 2
        for name, array, start, units in cuts:
            unit = array.shape[0] // 4
            first = min(units, early)
            early -= first
            for at, count, hops in ((start, first * unit, 2), (start + first * unit, (units - first) * unit, 1)):
                if count > 0:
                    pieces.append((name + "_" + str(at).zfill(4), array, at, count, 0, hops))
        return PipeHost(pieces) if pieces else None

    def took(self, host, results):
        self.moving = []
        for name, _, _, _, stage, hops in host.pieces:
            if stage + hops == 3:
                self.done[name] = results[name]
            else:
                self.moving.append((name, results[name], stage + hops))

    def left(self):
        groups = ({}, {}, {})
        for name, array, stage in self.moving:
            groups[stage][name] = array
        for name, array, start in self.queue:
            groups[0][name + "_" + str(start).zfill(4)] = array[start:]
        return groups


def normalize(values, gain):
    return values * lax.rsqrt(jnp.mean(values * values, axis=-1, keepdims=True) + EPS) * gain


def normalize_back(values, gain, grad):
    inverse = lax.rsqrt(jnp.mean(values * values, axis=-1, keepdims=True) + EPS)
    scaled = grad * gain
    unit = values * inverse
    return inverse * (scaled - unit * jnp.mean(scaled * unit, axis=-1, keepdims=True)), unit


def dense_blocks(weight):
    blocks, inner, outer = weight.shape
    rows = [
        jnp.pad(weight[n], ((0, 0), (n * outer, (blocks - 1 - n) * outer))) for n in range(blocks)
    ]
    return jnp.concatenate(rows, axis=0)


def diagonal_blocks(full, blocks, width):
    inner = width // blocks
    return jnp.stack([full[n * inner : (n + 1) * inner, n * inner : (n + 1) * inner] for n in range(blocks)])


def per_device(
    block_in,
    norm1_gain,
    w_branch,
    w_input,
    conv_weight,
    conv_bias,
    gate_a_weight,
    gate_a_bias,
    gate_i_weight,
    gate_i_bias,
    decay_param,
    w_out,
    norm2_gain,
    w_gate,
    w_up,
    w_down,
    lengths,
    cotangent,
):
    count = block_in.shape[0]
    nblocks = gate_a_weight.shape[0]
    true_width = w_branch.shape[1]
    extra = -true_width % LANES
    me = lax.axis_index("mp")

    def pad_last(value):
        return jnp.pad(value, [(0, 0)] * (value.ndim - 1) + [(0, extra)]) if extra else value

    def line(value):
        return pad_last(value)[None, :]

    wb, wi = pad_last(w_branch), pad_last(w_input)
    wo = jnp.pad(w_out, ((0, extra), (0, 0))) if extra else w_out
    w_ga, w_gi = dense_blocks(gate_a_weight), dense_blocks(gate_i_weight)
    if extra:
        w_ga, w_gi = (jnp.pad(v, ((0, extra), (0, extra))) for v in (w_ga, w_gi))
    taps = pad_last(conv_weight)
    decay_line = line(decay_param)
    w_both = jnp.concatenate([wb, wi], axis=1)
    w_gates = jnp.concatenate([w_ga, w_gi], axis=1)
    forward_params = (
        w_both, taps, line(conv_bias), w_gates, line(gate_a_bias), line(gate_i_bias), decay_line, wo
    )
    backward_params = (wo, w_both, taps, w_gates, decay_line)
    seqs = range(count)
    limits = [jnp.full((SUB, LANES), lengths[s], jnp.int32) for s in seqs]
    blocks = lax.axis_size("mp")
    hosted = blocks == 4 and count == 2
    ids = iter(range(1, 100))

    piped = hosted and lax.axis_size("dp") == 8 and not extra
    pipe = Pipe()

    def enter(name, quarters):
        if piped:
            pipe.enter(name, quarters)

    def tied(value, *deps):
        return lax.optimization_barrier((value,) + deps)[0]

    def run(function, *args, hosts=(), middle=0, budget=4, **more):
        if hosted:
            window = pipe.host(budget) if piped else None
            out, found = function(
                *args, hosts=list(hosts) + ([window] if window else []), middle=middle, unique=next(ids),
                pipe_middle=3 if function is weight_grad else 2, **more
            )
            if window:
                pipe.took(window, found[-1])
            return out, found[: len(hosts)]
        out, _ = function(*args, **more)
        return out, [
            gather(host.operands[0]) if isinstance(host, GatherHost) else scatter((host.first, *host.operands))
            for host in hosts
        ]

    resid = [block_in[s].astype(f32) for s in seqs]
    starts = [normalize(resid[s], norm1_gain).astype(bf16) for s in seqs]
    piece, model = starts[0].shape
    seq_in = [gather(starts[0])]
    out, (second,) = run(rec_forward, limits[0], seq_in[0], forward_params, hosts=[GatherHost(starts[1])], middle=3)
    seq_in.append(second)
    forward = [out]
    out, (branch,) = run(
        rec_forward, limits[1], seq_in[1], forward_params, hosts=[ScatterHost(out[8:])], middle=2, before=(out[7],)
    )
    forward.append(out)
    mixed = [out[0] for out in forward]
    saved = [out[1:7] for out in forward]
    finals = [out[7][:1, :true_width] for out in forward]
    resid_mid = [resid[0] + branch]
    mid = normalize(resid_mid[0], norm2_gain).astype(bf16)
    seq_mid = [gather(mid)]
    forward_shared, (branch,) = run(
        mlp_forward, 0, count, seq_mid[0], w_gate, w_up, w_down, (), hosts=[ScatterHost(forward[1][8:])], middle=2
    )
    mlp_part = [forward_shared[3]]
    resid_mid.append(resid[1] + branch)
    mid = normalize(resid_mid[1], norm2_gain).astype(bf16)
    seq_mid.append(gather(mid))
    forward_shared, (found,) = run(
        mlp_forward, 1, count, seq_mid[1], w_gate, w_up, w_down, forward_shared[:3],
        hosts=[GatherHost(cotangent[0])], middle=3,
    )
    mlp_part.append(forward_shared[3])
    cot_seq = [found]
    hidden, gate_low, up_low = forward_shared[:3]
    backward, (found,) = run(
        mlp_backward, 0, count, cot_seq[0], gate_low, up_low, w_gate, w_up, w_down, (),
        hosts=[GatherHost(cotangent[1])], middle=3,
    )
    cot_seq.append(found)

    def middle_grad(s, d_mid):
        back, unit = normalize_back(resid_mid[s], norm2_gain, d_mid)
        return cotangent[s].astype(f32) + back, jnp.sum(d_mid * unit, axis=0, keepdims=True)

    flat_mid = [p for pieces in seq_mid for p in pieces]
    flat_cot = [p for pieces in cot_seq for p in pieces]
    grad_down, _ = run(weight_grad, [hidden], flat_cot)
    enter("down", grad_down)
    backward, (d_mid,) = run(
        mlp_backward, 1, count, cot_seq[1], gate_low, up_low, w_gate, w_up, w_down, backward[:2],
        hosts=[ScatterHost(backward[2:])], middle=2, before=(grad_down[0],),
    )
    d_gate, d_up = backward[:2]
    first, gain2 = middle_grad(0, d_mid)
    grad_gate, (first_seq,) = run(weight_grad, flat_mid, [d_gate], hosts=[GatherHost(first.astype(bf16))], middle=3)
    enter("gate", grad_gate)
    grad_up, (d_mid,) = run(
        weight_grad, flat_mid, [d_up], hosts=[ScatterHost(backward[2:])], middle=2, before=(grad_gate[0],)
    )
    second, more_gain2 = middle_grad(1, d_mid)
    enter("up", grad_up)
    out, (second_seq,) = run(
        rec_backward, limits[0], 0, count, first_seq, seq_in[0], backward_params, saved[0], (),
        hosts=[GatherHost(second.astype(bf16))], middle=3, before=(grad_up[0],), budget=4,
    )
    sums, gain1 = out[2], out[3]
    out, (d_in,) = run(
        rec_backward, limits[1], 1, count, second_seq, seq_in[1], backward_params, saved[1], out[:2],
        hosts=[ScatterHost(out[4:])], middle=2, budget=4,
    )
    d_both, d_gates = out[:2]
    input_grad = [(first + normalize_back(resid[0], norm1_gain, d_in)[0]).astype(bf16)]

    flat_in = [p for pieces in seq_in for p in pieces]
    flat_resid = [p for pieces in (first_seq, second_seq) for p in pieces]
    grad_in, _ = run(weight_grad, flat_in, [d_both])
    conv = [part[2] for part in saved]
    if piped:

        def join(prefix, by_rows=True, ways=1):
            mine = [pipe.done[name] for name in sorted(pipe.done) if name.startswith(prefix)]
            return join_pieces(mine + [swap(piece, "dp", 1) for piece in mine], by_rows, ways)[0]

        moving = pipe.left()
        moving[0].update(in0=grad_in[0], in1=grad_in[1])
        found, (d_in,) = last_grad(
            mixed, flat_resid, conv, d_gates, (sums, out[2], gain1, out[3], gain2, more_gain2), moving, nblocks,
            hosts=[ScatterHost(out[4:])], middle=4, unique=next(ids), before=(grad_in[0],),
        )
        pipe.done.update({name: found[name] for name in found if name not in ("out0", "out1")})
        pairs = [(2 * a + core, 2 * b + core) for a, b in ((1, 0), (2, 3)) for core in range(2)]
        came = {name: lax.ppermute(found[name], "dp", pairs) for name in ("out0", "out1")}
        totals_down, totals_gate, totals_up = (join(name) for name in ("down", "gate", "up"))
        totals_in = join("in", ways=2)
        came = dict(zip(came, lax.optimization_barrier((*came.values(), totals_gate, totals_up, totals_in[0]))))
        for name in came:
            found[name] = jnp.where(chip_is_inner(), found[name], came[name])
        pipe.done.update(out0=found["out0"], out1=found["out1"])
        totals_out = join("out", by_rows=False)
        pack, other = found["pack"].astype(f32), swap(found["pack"], "dp", 1).astype(f32)
        mine = core_index() == 0
        pack = jnp.concatenate([jnp.where(mine, pack, other), jnp.where(mine, other, pack)], axis=0)
        inner = true_width // nblocks
        full_ga, full_gi = (
            jnp.transpose(pack[at * inner : (at + 1) * inner].reshape(inner, nblocks, inner), (1, 0, 2)) for at in range(2)
        )
        vectors = pack[2 * inner : 2 * inner + 8]
        gains = found["gains"][:2].astype(f32)
        gains = gains + swap(gains, "dp", 1)
        for bit in (1, 2):
            gains = gains + swap(gains, "mp", bit)
    else:
        grad_out, _ = run(weight_grad, mixed, flat_resid, False, before=(grad_in[0],))
        d_in = scatter(out[4:])
        totals_down, totals_gate, totals_up, totals_in, totals_out = (
            jnp.split(lax.psum(v[0], "dp").astype(f32), ways, axis=1)
            for v, ways in ((grad_down, 1), (grad_gate, 1), (grad_up, 1), (grad_in, 2), (grad_out, 1))
        )
        d_gates = d_gates.reshape(count, blocks, piece, -1)
        width = d_gates.shape[-1] // 2
        full = sum(jnp.einsum("rtd,rtc->dc", conv[s], d_gates[s], preferred_element_type=f32) for s in seqs)
        gains = jnp.stack([jnp.sum(gain1 + out[3], axis=0), (gain2 + more_gain2)[0]])
        vectors = jnp.sum(sums + out[2], axis=1)[:, :true_width]
        full_ga, full_gi, vectors, gains = lax.psum(
            (
                diagonal_blocks(full[:, :width], nblocks, true_width).astype(bf16),
                diagonal_blocks(full[:, width:], nblocks, true_width).astype(bf16),
                vectors.astype(bf16),
                lax.psum(gains, "mp").astype(bf16),
            ),
            "dp",
        )
    input_grad.append((second + normalize_back(resid[1], norm1_gain, d_in)[0]).astype(bf16))
    input_grad = jnp.stack(input_grad)
    grad_gate_a_weight, grad_gate_i_weight, vectors, gains = (
        v.astype(f32) for v in (full_ga, full_gi, vectors, gains)
    )
    gains = jnp.stack([gains[0] / norm1_gain, gains[1]])
    vectors = jnp.concatenate(
        [(vectors[0] * DECAY_EXP * jax.nn.sigmoid(-decay_param))[None, :], vectors[1:]], axis=0
    )
    grad_w_out = totals_out[0][:true_width]
    grad_w_branch, grad_w_input = (v[:, :true_width] for v in totals_in)
    mlp_total = [
        lax.psum_scatter(flat(tied(v, grad_in[0])), "mp", scatter_dimension=0, tiled=True) for v in mlp_part
    ]
    block_out = jnp.stack([(resid_mid[s] + mlp_total[s].astype(f32)).astype(bf16) for s in seqs])

    return (
        block_out,
        input_grad,
        gains[0],
        grad_w_branch,
        grad_w_input,
        vectors[4:8],
        vectors[3],
        grad_gate_a_weight,
        vectors[1],
        grad_gate_i_weight,
        vectors[2],
        vectors[0],
        grad_w_out,
        gains[1],
        totals_gate[0],
        totals_up[0],
        totals_down[0],
        jnp.concatenate(finals, axis=0),
    )


def solution(mesh):
    placed = (
        P("dp", "mp", None),
        P(),
        P(None, "mp"),
        P(None, "mp"),
        P(None, "mp"),
        P("mp"),
        P("mp", None, None),
        P("mp"),
        P("mp", None, None),
        P("mp"),
        P("mp"),
        P("mp", None),
        P(),
        P(None, "mp"),
        P(None, "mp"),
        P("mp", None),
        P("dp"),
        P("dp", "mp", None),
    )
    return jax.shard_map(
        per_device,
        mesh=mesh,
        in_specs=placed,
        out_specs=(
            P("dp", "mp", None),
            P("dp", "mp", None),
            P(),
            P(None, "mp"),
            P(None, "mp"),
            P(None, "mp"),
            P("mp"),
            P("mp", None, None),
            P("mp"),
            P("mp", None, None),
            P("mp"),
            P("mp"),
            P("mp", None),
            P(),
            P(None, "mp"),
            P(None, "mp"),
            P("mp", None),
            P("dp", "mp"),
        ),
        check_vma=False,
    )
```

```python
import functools
import math

import jax
import jax.numpy as jnp
from jax import lax
from jax.experimental import pallas as pl
from jax.experimental.pallas import tpu as pltpu
from jax.sharding import PartitionSpec as P

DECAY_EXP = 8.0
EPS = 1e-06
GELU_C = math.sqrt(2.0 / math.pi)
GELU_K = 0.044715
LANES = 128
SUB = 8
UNIT_TILE = 256
COST_SCALE = 0.5
MODEL_TILE = 512
VMEM_BYTES = 56 * 1024 * 1024

f32 = jnp.float32
bf16 = jnp.bfloat16


def dot_nn(left, right):
    return lax.dot_general(left, right, (((1,), (0,)), ((), ())), preferred_element_type=f32)


def dot_nt(left, right):
    return lax.dot_general(left, right, (((1,), (1,)), ((), ())), preferred_element_type=f32)


def one_minus_square(log_a, decay):
    x = 2.0 * log_a
    tail = 1.0 + x * (1.0 / 7.0)
    for k in (6.0, 5.0, 4.0, 3.0, 2.0):
        tail = 1.0 + x * (1.0 / k) * tail
    return jnp.where(x > -0.4, -x * tail, 1.0 - decay * decay)


def gelu_parts(x):
    square = x * x
    th = jnp.tanh(GELU_C * x * (1.0 + GELU_K * square))
    half = 0.5 * (1.0 + th)
    value = x * half
    slope = half + 0.5 * x * (1.0 - th * th) * (GELU_C * (1.0 + 3.0 * GELU_K * square))
    return value, slope


def row_index(shape):
    return lax.broadcasted_iota(jnp.int32, shape, 0)


def shift_down(prev, cur, k, row):
    return jnp.where(row < k, pltpu.roll(prev, k, 0), pltpu.roll(cur, k, 0))


def shift_up(cur, following, k, row):
    return jnp.where(row < SUB - k, pltpu.roll(cur, SUB - k, 0), pltpu.roll(following, SUB - k, 0))


def load_block(pieces, layout, block, target):
    for ref, (owner, start, count) in zip(pieces, layout):

        @pl.when(block == owner)
        def _(ref=ref, start=start, count=count):
            target[pl.ds(start, count), :] = ref[...]


def store_block(pieces, layout, block, column, value):
    for ref, (owner, start, count) in zip(pieces, layout):

        @pl.when(block == owner)
        def _(ref=ref, start=start, count=count):
            ref[:, column] = value[start : start + count]


def rec_forward_kernel(layout, length, *refs):
    x_pieces, refs = refs[: len(layout)], refs[len(layout) :]
    w_both, taps, conv_bias, w_gates, ga_bias, gi_bias, decay_param, w_out = refs[:8]
    branch = refs[-1]
    gates_pre, tail, carry, x = refs[-5:-1]
    outs = refs[-5 - 10 - len(layout) : -5]
    mixed, pre, value_out, slope_out, space_out, conv, ga, gi, prev_state, final = outs[:10]
    parts = outs[10:]
    step = pl.program_id(0)
    block = flip(step, lax.axis_index("mp"), 4 if len(layout) == 5 else len(layout))
    rows, width = mixed.shape[1:]
    load_block(x_pieces, layout, block, x)
    pieces = rows // 16
    lanes = [pl.ds(at, LANES) for at in range(0, width, LANES)]
    row = row_index((SUB, LANES))

    @pl.when(step == 0)
    def _():
        tail[...] = jnp.zeros_like(tail)
        carry[...] = jnp.zeros_like(carry)

    both = dot_nn(x[...], w_both[...])
    branch[...] = both[:, :width]
    pre[0] = both[:, width:]

    def conv_piece(i, _):
        base = pl.multiple_of(i * 16, 16)
        for lane in lanes:
            bias = conv_bias[:, lane]
            before = tail[:, lane]
            parts = []
            for half in range(2):
                cur = pre[0, pl.ds(base + SUB * half, SUB), lane]
                total = bias + taps[0:1, lane] * cur
                for k in range(1, 4):
                    total = total + taps[k : k + 1, lane] * shift_down(before, cur, k, row)
                parts.append(total)
                before = cur
            tail[:, lane] = before
            conv[0, pl.ds(base, 16), lane] = jnp.concatenate(parts, axis=0).astype(bf16)
        return 0

    lax.fori_loop(0, pieces, conv_piece, 0)
    gates_pre[...] = dot_nn(conv[0], w_gates[...])
    limit = length[...]

    def scan_piece(i, _):
        base = pl.multiple_of(i * 16, 16)
        start = step * rows + base
        for lane in lanes:
            second = pl.ds(width + lane.start, LANES)
            rate = -DECAY_EXP * jax.nn.softplus(-decay_param[:, lane])
            conv_two = conv[0, pl.ds(base, 16), lane].astype(f32)
            state = carry[:, lane]
            outs = []
            for half in range(2):
                at = pl.ds(base + SUB * half, SUB)
                live = (row + (start + SUB * half)) < limit
                gate_a = jax.nn.sigmoid(gates_pre[at, lane] + ga_bias[:, lane])
                gate_i = jax.nn.sigmoid(gates_pre[at, second] + gi_bias[:, lane])
                ga[0, at, lane] = gate_a
                gi[0, at, lane] = gate_i
                log_a = rate * gate_a
                decay = jnp.exp(log_a)
                space = one_minus_square(log_a, decay)
                space_out[0, at, lane] = space
                scaled = jnp.sqrt(space) * gate_i * conv_two[SUB * half : SUB * half + SUB]
                mul = jnp.where(live, decay, 1.0)
                add = jnp.where(live, scaled, 0.0)
                for shift in (1, 2, 4):
                    inside = row >= shift
                    add = add + mul * jnp.where(inside, pltpu.roll(add, shift, 0), 0.0)
                    mul = mul * jnp.where(inside, pltpu.roll(mul, shift, 0), 1.0)
                states = mul * state + add
                prev_state[0, at, lane] = jnp.where(row == 0, state, pltpu.roll(states, 1, 0))
                state = jnp.broadcast_to(states[SUB - 1 : SUB], (SUB, LANES))
                value, slope = gelu_parts(branch[at, lane])
                value_out[0, at, lane] = value
                slope_out[0, at, lane] = slope
                outs.append(states * value)
            carry[:, lane] = state
            mixed[0, pl.ds(base, 16), lane] = jnp.concatenate(outs, axis=0).astype(bf16)
        return 0

    lax.fori_loop(0, pieces, scan_piece, 0)
    final[...] = carry[...]
    for at in range(0, w_out.shape[1], MODEL_TILE):
        column = pl.ds(at, MODEL_TILE)
        x[:, column] = dot_nn(mixed[0], w_out[:, column]).astype(bf16)
    store_block(parts, layout, block, slice(None), x[...])


def rec_backward_kernel(layout, nshared, wait_late, length, *refs):
    many = len(layout)
    d_resid_pieces, x_pieces, refs = refs[:many], refs[many : 2 * many], refs[2 * many :]
    w_out, w_both, taps, w_gates, decay_param = refs[:5]
    pre, value_in, slope_in, space_in, conv, ga, gi, prev_state = refs[5:13]
    d_mixed, d_conv, flow, later, x, d_resid = refs[-6:]
    outs = refs[-6 - 4 - many : -6]
    d_both, d_gates, sums, gain_sums = outs[:4]
    parts = outs[4:]
    step = pl.program_id(0)
    rows, width = pre.shape[1:]
    pieces = rows // 16
    lanes = [pl.ds(at, LANES) for at in range(0, width, LANES)]
    row = row_index((SUB, LANES))
    first = (pl.num_programs(0) - 1 - step) * rows
    limit = length[...]

    @pl.when(step == 0)
    def _():
        flow[...] = jnp.zeros_like(flow)
        later[...] = jnp.zeros_like(later)
        sums[...] = jnp.zeros_like(sums)
        gain_sums[...] = jnp.zeros_like(gain_sums)

    block = flip(pl.num_programs(0) - 1 - step, lax.axis_index("mp"), 4 if len(layout) == 5 else len(layout))
    load_block(d_resid_pieces, layout, block, d_resid)
    d_mixed[...] = dot_nt(d_resid[...], w_out[...])

    def scan_piece(j, _):
        base = pl.multiple_of((pieces - 1 - j) * 16, 16)
        for lane in lanes:
            rate = -DECAY_EXP * jax.nn.softplus(-decay_param[:, lane])
            conv_two = conv[0, pl.ds(base, 16), lane].astype(f32)
            carried = flow[:, lane]
            outs = [None, None]
            sum_log = sums[0, :, lane]
            for half in (1, 0):
                at = pl.ds(base + SUB * half, SUB)
                live = (row + (first + base + SUB * half)) < limit
                conv_val = conv_two[SUB * half : SUB * half + SUB]
                gate_a = ga[0, at, lane]
                gate_i = gi[0, at, lane]
                before = prev_state[0, at, lane]
                d_mix = d_mixed[at, lane]
                log_a = rate * gate_a
                decay = jnp.exp(log_a)
                space = space_in[0, at, lane]
                inverse = lax.rsqrt(jnp.maximum(space, 1e-37))
                root = space * inverse
                gated = gate_i * conv_val
                mul = jnp.where(live, decay, 1.0)
                states = mul * before + jnp.where(live, root * gated, 0.0)
                d_br = d_mix * states * slope_in[0, at, lane]
                direct = d_mix * value_in[0, at, lane]
                add = mul * direct
                for shift in (1, 2, 4):
                    inside = row < SUB - shift
                    add = add + mul * jnp.where(inside, pltpu.roll(add, SUB - shift, 0), 0.0)
                    mul = mul * jnp.where(inside, pltpu.roll(mul, SUB - shift, 0), 1.0)
                moved = add + mul * carried
                d_state = direct + jnp.where(row == SUB - 1, carried, pltpu.roll(moved, SUB - 1, 0))
                carried = jnp.broadcast_to(moved[0:1], (SUB, LANES))
                d_state = jnp.where(live, d_state, 0.0)
                d_log = d_state * decay * (before - gated * decay * inverse)
                sum_log = sum_log + d_log * gate_a
                d_gate_a = d_log * rate * gate_a * (1.0 - gate_a)
                d_rooted = d_state * root
                d_conv_rec = d_rooted * gate_i
                d_gate_i = d_rooted * conv_val * gate_i * (1.0 - gate_i)
                d_conv[at, lane] = d_conv_rec
                outs[half] = (d_br, d_gate_a, d_gate_i)
            flow[:, lane] = carried
            sums[0, :, lane] = sum_log
            second = pl.ds(width + lane.start, LANES)
            for target, there, which in ((d_both, lane, 0), (d_gates, lane, 1), (d_gates, second, 2)):
                both = jnp.concatenate([outs[0][which], outs[1][which]], axis=0).astype(bf16)
                target[0, pl.ds(base, 16), there] = both
                if which > 0:
                    wide = both.astype(f32)
                    sums[which, :, lane] += wide[:SUB] + wide[SUB:]
        return 0

    lax.fori_loop(0, pieces, scan_piece, 0)
    wait_late()
    load_block(x_pieces, layout, block, x)
    d_conv[...] += dot_nt(d_gates[0], w_gates[...])

    def conv_piece(j, _):
        base = pl.multiple_of((pieces - 1 - j) * 16, 16)
        for lane in lanes:
            following = later[:, lane]
            totals = [None, None]
            tap_sums = [sums[3 + k, :, lane] for k in range(5)]
            for half in (1, 0):
                at = pl.ds(base + SUB * half, SUB)
                cur = d_conv[at, lane]
                seen = pre[0, at, lane]
                tap_sums[0] = tap_sums[0] + cur
                tap_sums[1] = tap_sums[1] + cur * seen
                total = taps[0:1, lane] * cur
                for k in range(1, 4):
                    ahead = shift_up(cur, following, k, row)
                    tap_sums[1 + k] = tap_sums[1 + k] + ahead * seen
                    total = total + taps[k : k + 1, lane] * ahead
                totals[half] = total
                following = cur
            later[:, lane] = following
            for k in range(5):
                sums[3 + k, :, lane] = tap_sums[k]
            d_both[0, pl.ds(base, 16), pl.ds(width + lane.start, LANES)] = jnp.concatenate(totals, axis=0).astype(bf16)
        return 0

    lax.fori_loop(0, pieces, conv_piece, 0)
    for at in range(0, x.shape[1], MODEL_TILE):
        column = pl.ds(at, MODEL_TILE)
        part = dot_nt(d_both[0], w_both[column, :])
        seen = part * x[:, column].astype(f32)
        gain_sums[:, column] += jnp.sum(seen.reshape(rows // SUB, SUB, MODEL_TILE), axis=0)
        d_resid[:, column] = part.astype(bf16)
    store_block(parts, layout, block, slice(None), d_resid[...])


def mlp_forward_kernel(layout, *refs):
    many = len(layout)
    x_pieces, (w_gate, w_up, w_down) = refs[:many], refs[many : many + 3]
    hidden, gate, up, mlp_part, x = refs[-5:]
    load_block(x_pieces, layout, pl.program_id(0), x)
    for at in range(0, hidden.shape[2], UNIT_TILE):
        column = pl.ds(at, UNIT_TILE)
        up_pre = dot_nn(x[...], w_up[:, column])
        gate_pre = dot_nn(x[...], w_gate[:, column])
        value, _ = gelu_parts(gate_pre)
        hidden[0, :, column] = (value * up_pre).astype(bf16)
        gate[0, :, column] = gate_pre.astype(bf16)
        up[0, :, column] = up_pre.astype(bf16)
    for at in range(0, x.shape[1], MODEL_TILE):
        column = pl.ds(at, MODEL_TILE)
        mlp_part[0, :, column] = dot_nn(hidden[0], w_down[:, column]).astype(bf16)


def mlp_backward_kernel(layout, *refs):
    many = len(layout)
    cot_pieces, (gate, up, w_gate, w_up, w_down) = refs[:many], refs[many : many + 5]
    cot, mid = refs[-2:]
    d_gate, d_up = refs[-2 - many - 2 : -2 - many]
    parts = refs[-2 - many : -2]
    r = pl.program_id(0)
    load_block(cot_pieces, layout, r, cot)
    for at in range(0, d_gate.shape[2], UNIT_TILE):
        column = pl.ds(at, UNIT_TILE)
        back = dot_nt(cot[...], w_down[column, :])
        value, slope = gelu_parts(gate[0, :, column].astype(f32))
        d_gate[0, :, column] = (back * up[0, :, column].astype(f32) * slope).astype(bf16)
        d_up[0, :, column] = (back * value).astype(bf16)
    for at in range(0, cot.shape[1], MODEL_TILE):
        column = pl.ds(at, MODEL_TILE)
        total = dot_nt(d_gate[0], w_gate[column, :]) + dot_nt(d_up[0], w_up[column, :])
        mid[:, column] = total.astype(bf16)
    store_block(parts, layout, r, slice(None), mid[...])


def weight_grad_kernel(by_rows, nlefts, nrights, exchange, *refs):
    lefts, rights = refs[:nlefts], refs[nlefts : nlefts + nrights]
    if exchange:
        first, second, left, right, sent, got, send, recv = refs[-8:]
    else:
        out, left, right = refs[-3:]
    step = pl.program_id(0)

    def assemble(target, sources):
        at = 0
        for ref in sources:
            target[at : at + ref.shape[0], :] = ref[...]
            at += ref.shape[0]

    if nlefts == 1:
        left = lefts[0]
    elif by_rows:
        assemble(left, lefts)
    else:
        pl.when(step == 0)(functools.partial(assemble, left, lefts))
    if nrights == 1:
        right = rights[0]
    elif not by_rows:
        assemble(right, rights)
    else:
        pl.when(step == 0)(functools.partial(assemble, right, rights))
    total = lax.dot_general(left[...], right[...], (((0,), (0,)), ((), ())), preferred_element_type=f32)
    if not exchange:
        out[...] = total.astype(bf16)
        return

    def copy(at):
        return remote(sent.at[at], got.at[at], send, recv, at, other_core())

    for at in range(2):

        @pl.when(step == at)
        def _(at=at):
            sent[at] = total.astype(bf16)
            copy(at).start()

    for at, target in ((0, first), (1, second)):

        @pl.when(step == 2 + at)
        def _(at=at, target=target):
            copy(at).wait_recv()
            target[...] = (total + got[at].astype(f32)).astype(bf16)
            copy(at).wait_send()


def join_kernel(npieces, by_rows, ways, *refs):
    pieces, outs = refs[:npieces], refs[npieces : npieces + ways]
    held, wide = refs[npieces + ways : 2 * npieces + ways], refs[2 * npieces + ways : 3 * npieces + ways]
    arrive, leave = refs[-2:]
    half = npieces // 2
    core = core_index()
    loads = [pltpu.make_async_copy(piece, vmem, arrive.at[at]) for at, (piece, vmem) in enumerate(zip(pieces, held))]
    for load in loads:
        load.start()
    stores, start = [], 0

    def store(source, target):
        stores.append(pltpu.make_async_copy(source, target, leave.at[len(stores)]))
        stores[-1].start()

    span = sum(piece.shape[0] for piece in pieces[:half])
    for at, (load, vmem, big) in enumerate(zip(loads, held, wide)):
        start = 0 if at == half else start
        mine = core if at < half else 1 - core
        load.wait()
        big[...] = vmem[...].astype(f32)
        if by_rows:
            place = pl.ds(pl.multiple_of(mine * span + start, 16), vmem.shape[0])
            start += vmem.shape[0]
            for way, out in enumerate(outs):
                store(big.at[:, pl.ds(way * out.shape[1], out.shape[1])], out.at[place, :])
        else:
            rows, columns = outs[0].shape[0], vmem.shape[1]
            for block in range(2):
                place = pl.ds(pl.multiple_of((mine * 2 + block) * columns, LANES), columns)
                store(big.at[pl.ds(block * rows, rows), :], outs[0].at[:, place])
    for store in stores:
        store.wait()


ANY = pl.BlockSpec(memory_space=pl.ANY)
PARAMS = pltpu.CompilerParams(vmem_limit_bytes=VMEM_BYTES)
MESH = pl.DeviceIdType.MESH


def flip(index, mask, size):
    total, bit = 0, 1
    while bit < size:
        total = total + ((index // bit + mask // bit) % 2) * bit
        bit *= 2
    return total


def neighbours():
    me = lax.axis_index("mp")
    return {"mp": flip(me, 1, 4)}, {"mp": flip(me, 2, 4)}


def other_core():
    return {"dp": flip(lax.axis_index("dp"), 1, 8)}


def remote(source, target, send, recv, at, device):
    return pltpu.make_async_remote_copy(
        src_ref=source,
        dst_ref=target,
        send_sem=send.at[at],
        recv_sem=recv.at[at],
        device_id=device,
        device_id_type=MESH,
    )


class GatherHost:
    def __init__(self, shard):
        rows, model = shard.shape
        self.operands = [shard]
        self.outputs = [jax.ShapeDtypeStruct((count, model), bf16) for count in (rows, rows, rows // 2, rows // 2)]
        self.scratch = [pltpu.SemaphoreType.DMA((4,)), pltpu.SemaphoreType.DMA((4,))]

    def copies(self, ins, outs, scratch):
        (shard,), (by_x, by_y, far_a, far_b), (send, recv) = ins, outs, scratch
        half = far_a.shape[0]
        x, y = neighbours()
        return (
            lambda: remote(shard, by_x, send, recv, 0, x),
            lambda: remote(shard, by_y, send, recv, 1, y),
            lambda: remote(by_x.at[pl.ds(0, half)], far_a, send, recv, 2, y),
            lambda: remote(by_y.at[pl.ds(half, half)], far_b, send, recv, 3, x),
        )

    def begin(self, *refs):
        for copy in self.copies(*refs)[:2]:
            copy().start()

    def middle(self, *refs):
        copies = self.copies(*refs)
        copies[0]().wait_recv()
        copies[1]().wait_recv()
        copies[2]().start()
        copies[3]().start()

    def end(self, *refs):
        copies = self.copies(*refs)
        copies[0]().wait_send()
        copies[1]().wait_send()
        copies[2]().wait()
        copies[3]().wait()

    def devices(self):
        return neighbours()

    def result(self, outs):
        return (self.operands[0],) + tuple(outs)


class ScatterHost:
    def __init__(self, parts):
        rows, model = parts[1].shape
        half = rows // 2
        self.first = parts[0]
        self.operands = list(parts[1:])
        self.outputs = [jax.ShapeDtypeStruct((rows, model), bf16)] * 2
        self.scratch = [pltpu.VMEM((half, model), bf16)] * 4 + [pltpu.SemaphoreType.DMA((6,))] * 2
        self.scratch += [pltpu.SemaphoreType.DMA((2,))]

    def copies(self, ins, outs, scratch):
        (one, two, far_a, far_b), (from_x, from_y) = ins, outs
        got_x, got_y, own_x, own_y, send, recv, local = scratch
        half = far_a.shape[0]
        low, high = pl.ds(0, half), pl.ds(half, half)
        x, y = neighbours()
        return (
            lambda: remote(far_a, got_x, send, recv, 0, x),
            lambda: remote(far_b, got_y, send, recv, 1, y),
            lambda: remote(one.at[low], from_x.at[low], send, recv, 2, x),
            lambda: remote(two.at[high], from_y.at[high], send, recv, 3, y),
            lambda: remote(own_x, from_x.at[high], send, recv, 4, x),
            lambda: remote(own_y, from_y.at[low], send, recv, 5, y),
            lambda: pltpu.make_async_copy(one.at[high], own_x, local.at[0]),
            lambda: pltpu.make_async_copy(two.at[low], own_y, local.at[1]),
        )

    def begin(self, *refs):
        copies = self.copies(*refs)
        for at in (0, 1, 2, 3, 6, 7):
            copies[at]().start()

    def middle(self, ins, outs, scratch):
        copies = self.copies(ins, outs, scratch)
        got_x, got_y, own_x, own_y = scratch[:4]
        copies[6]().wait()
        copies[7]().wait()
        copies[0]().wait_recv()
        copies[1]().wait_recv()
        own_x[...] = (own_x[...].astype(f32) + got_y[...].astype(f32)).astype(bf16)
        own_y[...] = (own_y[...].astype(f32) + got_x[...].astype(f32)).astype(bf16)
        copies[4]().start()
        copies[5]().start()

    def end(self, *refs):
        copies = self.copies(*refs)
        copies[0]().wait_send()
        copies[1]().wait_send()
        for at in (2, 3, 4, 5):
            copies[at]().wait()

    def devices(self):
        return neighbours()

    def result(self, outs):
        return self.first.astype(f32) + outs[0].astype(f32) + outs[1].astype(f32)


def chip_partners():
    dp = lax.axis_index("dp")
    return {"dp": flip(dp, 2, 8)}, {"dp": (3 - dp // 2) * 2 + dp % 2}


def chip_is_inner():
    return (lax.axis_index("dp") // 2 + 1) // 2 % 2 == 1


class PipeHost:
    def __init__(self, pieces):
        self.pieces = pieces
        self.names = [piece[0] for piece in pieces]
        self.operands = [piece[1] for piece in pieces]
        self.outputs = [jax.ShapeDtypeStruct((piece[3], piece[1].shape[1]), bf16) for piece in pieces]
        self.scratch = []
        for (_, _, _, _, stage, hops, _), out in zip(pieces, self.outputs):
            self.scratch += [pltpu.VMEM(out.shape, bf16)] * (1 + min(hops, 2 - stage))
        self.scratch += [pltpu.SemaphoreType.DMA((len(pieces),))] * 6

    def devices(self):
        return chip_partners()

    def parts(self, ins, outs, scratch):
        pair, mirror = chip_partners()
        send, recv, send_on, recv_on, local, back = scratch[-6:]
        given = 0
        for at, ((_, _, start, count, stage, hops, slot), array, out) in enumerate(zip(self.pieces, ins, outs)):
            many = 1 + min(hops, 2 - stage)
            buffers = list(scratch[given : given + many])
            given += many
            source = array.at[pl.ds(start, count)]

            def hop(number, at=at, stage=stage, source=source, buffers=buffers, out=out):
                way = stage + number
                target = out if way == 2 else buffers[number + 1]
                sems = (send, recv) if number == 0 else (send_on, recv_on)
                return remote(source if number == 0 else buffers[number], target, *sems, at, mirror if way == 1 else pair)

            def load(at=at, source=source, buffers=buffers):
                return pltpu.make_async_copy(source, buffers[0], local.at[at])

            def keep(at=at, buffers=buffers, out=out):
                return pltpu.make_async_copy(buffers[-1], out, back.at[at])

            yield stage, hops, slot, buffers, hop, load, keep

    def add(self, target, other):
        target[...] = (target[...].astype(f32) + other[...].astype(f32)).astype(bf16)

    def begin(self, *refs):
        inner = chip_is_inner()
        for stage, _, _, _, hop, load, _ in self.parts(*refs):

            @pl.when(inner)
            def _(stage=stage, hop=hop, load=load):
                load().start()
                if stage > 0:
                    hop(0).start()

            if stage == 0:

                @pl.when(jnp.logical_not(inner))
                def _(hop=hop):
                    hop(0).start()

    def middle(self, at, *refs):
        inner = chip_is_inner()
        for stage, hops, slot, buffers, hop, load, keep in self.parts(*refs):
            if slot == at:

                @pl.when(inner)
                def _(stage=stage, hops=hops, buffers=buffers, hop=hop, load=load, keep=keep):
                    load().wait()
                    if hops == 2:
                        hop(0).wait_recv()
                        self.add(buffers[1], buffers[0])
                        hop(1).start()
                    if stage + hops == 3:
                        keep().start()

    def slots(self):
        return sorted(set(piece[6] for piece in self.pieces) - {END, None})

    def end(self, *refs):
        inner = chip_is_inner()
        self.middle(END, *refs)
        parts = list(self.parts(*refs))
        for stage, hops, slot, buffers, hop, load, keep in parts:

            @pl.when(inner)
            def _(stage=stage, hops=hops, slot=slot, buffers=buffers, hop=hop, load=load, keep=keep):
                if slot is None:
                    load().wait()
                if stage > 0:
                    hop(0).wait_send()
                if hops == 2:
                    hop(1).wait_send()
                if stage + hops < 3:
                    hop(hops - 1).wait_recv()
                    self.add(buffers[-1], buffers[-2])
                    keep().start()

            @pl.when(jnp.logical_not(inner))
            def _(stage=stage, hops=hops, hop=hop):
                if stage == 0:
                    hop(0).wait_send()
                if stage + hops == 3:
                    hop(hops - 1).wait_recv()

        for _, _, _, _, _, _, keep in parts:

            @pl.when(inner)
            def _(keep=keep):
                keep().wait()

    def result(self, outs):
        return dict(zip(self.names, outs))


class Tail:
    def __init__(self, chunks):
        self.chunks = chunks
        self.pieces = []
        for at, (shape, stage, _, _) in enumerate(chunks):
            rows = shape[0]
            parts = 1 if stage == 2 or rows < 64 else 2 if rows < 256 else 4
            size = -(-rows // parts // 16) * 16
            self.pieces += [(at, start, min(size, rows - start)) for start in range(0, rows, size)]
        self.scratch = []
        for shape, stage, late, _ in chunks:
            self.scratch += [pltpu.VMEM(shape, bf16)] * (3 - stage - (1 if late else 0))
        self.scratch += [pltpu.SemaphoreType.DMA((len(self.pieces),))] * 8

    def setup(self, refs, outs, scratch):
        pair, mirror = chip_partners()
        p_send, p_recv, q_send, q_recv, f_send, f_recv, local, back = scratch[-8:]
        buffers, given = [], 0
        for ref, (_, stage, late, _) in zip(refs, self.chunks):
            count = 3 - stage - (1 if late else 0)
            mine = ([ref] if late else []) + list(scratch[given : given + count])
            given += count
            buffers.append(mine if stage == 0 else [mine[0], None, mine[-1]])

        def transfers(number):
            at, start, count = self.pieces[number]
            rows = pl.ds(start, count)
            own, from_pair, from_mirror = buffers[at]
            early = self.chunks[at][1]
            source, out = refs[at].at[rows], outs[at].at[rows]
            sent = source if early == 1 else own.at[rows]
            done = own if early == 2 else from_mirror
            given_out = source if early == 2 else done.at[rows]
            return {
                "inward": lambda: remote(source, from_pair.at[rows], p_send, p_recv, number, pair),
                "load": lambda: pltpu.make_async_copy(source, own.at[rows], local.at[number]),
                "between": lambda: remote(sent, from_mirror.at[rows], q_send, q_recv, number, mirror),
                "outward": lambda: remote(given_out, out, f_send, f_recv, number, pair),
                "keep": lambda: pltpu.make_async_copy(done.at[rows], out, back.at[number]),
            }

        self.buffers = buffers
        self.moves = [transfers(number) for number in range(len(self.pieces))]
        self.stages = [self.chunks[at][1] for at, _, _ in self.pieces]
        self.late = [self.chunks[at][2] for at, _, _ in self.pieces]
        self.out = [self.chunks[at][3] for at, _, _ in self.pieces]
        self.inner = chip_is_inner()

    def start(self):
        @pl.when(self.inner)
        def _():
            for move, stage, late in zip(self.moves, self.stages, self.late):
                if stage == 2:
                    move["outward"]().start()
                if stage == 1:
                    move["between"]().start()
                if not late:
                    move["load"]().start()

        @pl.when(jnp.logical_not(self.inner))
        def _():
            for move, stage, late in zip(self.moves, self.stages, self.late):
                if stage == 0 and not late:
                    move["inward"]().start()

    def add(self, number, target, other):
        _, start, count = self.pieces[number]
        rows = pl.ds(start, count)
        target[rows, :] = (target[rows, :].astype(f32) + other[rows, :].astype(f32)).astype(bf16)

    def finish(self):
        numbers = range(len(self.pieces))

        def on(number):
            self.moves[number]["between"]().wait_recv()
            own, _, other = self.buffers[self.pieces[number][0]]
            self.add(number, other, own)
            if self.out[number]:
                self.moves[number]["outward"]().start()
            self.moves[number]["keep"]().start()

        @pl.when(self.inner)
        def _():
            for number in numbers:
                if not self.late[number]:
                    self.moves[number]["load"]().wait()
                if self.stages[number] == 2:
                    self.moves[number]["keep"]().start()
            waiting = [number for number in numbers if self.stages[number] == 1]
            for number in numbers:
                if self.stages[number] == 0:
                    self.moves[number]["inward"]().wait_recv()
                    own, other, _ = self.buffers[self.pieces[number][0]]
                    self.add(number, own, other)
                    self.moves[number]["between"]().start()
                    waiting.append(number)
                    on(waiting.pop(0))
            for number in waiting:
                on(number)
            for number in numbers:
                if self.stages[number] < 2:
                    self.moves[number]["between"]().wait_send()
                if self.out[number]:
                    self.moves[number]["outward"]().wait_send()
                self.moves[number]["keep"]().wait()

        @pl.when(jnp.logical_not(self.inner))
        def _():
            for number in numbers:
                if self.stages[number] == 0 and self.late[number]:
                    self.moves[number]["inward"]().start()
            for number in numbers:
                if self.stages[number] == 0:
                    self.moves[number]["inward"]().wait_send()
                if self.out[number]:
                    self.moves[number]["outward"]().wait_recv()


def call(
    kernel, grid, ins, outs, scratch, name, us, hosts=(), before=(), aliases=None, middle=0, unique=None, pair=False, chips=False, late=()
):
    nins, nouts, nscratch = len(ins), len(outs), len(scratch)
    steps = math.prod(grid)
    loaded = [at for at, (_, spec) in enumerate(ins) if spec is WHOLE]

    def body(*refs):
        refs = list(refs)

        def take(count):
            part = refs[:count]
            del refs[:count]
            return part

        own_ins = take(nins)
        host_ins = [take(len(host.operands)) for host in hosts]
        take(len(before))
        own_outs = take(nouts)
        host_outs = [take(len(host.outputs)) for host in hosts]
        own_scratch = take(nscratch)
        host_refs = [(i, o, take(len(host.scratch))) for host, i, o in zip(hosts, host_ins, host_outs)]
        buffers = take(len(loaded))
        step = pl.program_id(0)
        if len(grid) == 2:
            step = step * grid[1] + pl.program_id(1)
        if hosts or pair:

            @pl.when(step == 0)
            def _():
                devices = (other_core(),) if pair else ()
                for kind in (GatherHost, ScatterHost, PipeHost):
                    kinds = [host for host in hosts if isinstance(host, kind)]
                    if kinds and not (kind is ScatterHost and any(isinstance(host, GatherHost) for host in hosts)):
                        devices += tuple(kinds[0].devices())
                if chips:
                    devices += tuple(chip_partners())
                barrier = pltpu.get_barrier_semaphore()
                for device in devices:
                    pl.semaphore_signal(barrier, inc=1, device_id=device, device_id_type=MESH)
                pl.semaphore_wait(barrier, len(devices))
                for host, there in zip(hosts, host_refs):
                    host.begin(*there)

        if loaded:
            arrived = take(1)[0]
            loads = [(own_ins[at], buffer, arrived.at[k]) for k, (at, buffer) in enumerate(zip(loaded, buffers))]

            second = [load for load, at in zip(loads, loaded) if at in late]
            first = [load for load, at in zip(loads, loaded) if at not in late]

            @pl.when(step == 0)
            def _():
                for load in first + second:
                    pltpu.make_async_copy(*load).start()
                for load in first:
                    pltpu.make_async_copy(*load).wait()

            for at, buffer in zip(loaded, buffers):
                own_ins[at] = buffer
        if hosts:

            for host, there in list(zip(hosts, host_refs))[::-1]:
                for at in host.slots() if isinstance(host, PipeHost) else (middle,):

                    @pl.when(step == at)
                    def _(host=host, there=there, at=at):
                        host.middle(*((at,) if isinstance(host, PipeHost) else ()), *there)

        def wait_late():
            @pl.when(step == 0)
            def _():
                for load in second:
                    pltpu.make_async_copy(*load).wait()

        kernel(*([wait_late] if late else []), *own_ins, *own_outs, *own_scratch)
        if hosts:

            @pl.when(step == steps - 1)
            def _():
                for host, there in zip(hosts, host_refs):
                    host.end(*there)

    host_operands = [v for host in hosts for v in host.operands]
    host_outputs = [v for host in hosts for v in host.outputs]
    params = pltpu.CompilerParams(vmem_limit_bytes=VMEM_BYTES)
    if hosts or pair:
        params = pltpu.CompilerParams(vmem_limit_bytes=VMEM_BYTES, collective_id=unique, has_side_effects=True)
    results = pl.pallas_call(
        body,
        out_shape=tuple(shape for shape, _ in outs) + tuple(host_outputs),
        grid=grid,
        in_specs=[ANY if spec is WHOLE else spec for _, spec in ins] + [ANY] * (len(host_operands) + len(before)),
        out_specs=tuple(spec for _, spec in outs) + (ANY,) * len(host_outputs),
        scratch_shapes=list(scratch)
        + [v for host in hosts for v in host.scratch]
        + [pltpu.VMEM(ins[at][0].shape, ins[at][0].dtype) for at in loaded]
        + ([pltpu.SemaphoreType.DMA((len(loaded),))] if loaded else []),
        input_output_aliases=aliases or {},
        compiler_params=params,
        cost_estimate=cost(us),
        name=name,
    )(*[array for array, _ in ins], *host_operands, *before)
    own, rest = results[:nouts], results[nouts:]
    found = []
    for host in hosts:
        found.append(host.result(rest[: len(host.outputs)]))
        rest = rest[len(host.outputs) :]
    return own, found


def cost(us):
    return pl.CostEstimate(flops=int(us * COST_SCALE * 1.15e9), bytes_accessed=1 << 16, transcendentals=0)


WHOLE = "whole"
END = 99


def whole(array):
    return WHOLE


def layout_of(blocks, rows):
    if blocks != 4:
        return tuple((r, 0, rows) for r in range(blocks))
    return ((0, 0, rows), (1, 0, rows), (2, 0, rows), (3, 0, rows // 2), (3, rows // 2, rows - rows // 2))


def piece_outputs(layout, model):
    shapes = tuple(jax.ShapeDtypeStruct((count, model), bf16) for _, _, count in layout)
    specs = tuple(pl.BlockSpec(shape.shape, lambda *_: (0, 0)) for shape in shapes)
    return shapes, specs


def rec_forward(length, x, params, **more):
    blocks, (rows, model) = lax.axis_size("mp"), x[0].shape
    layout = layout_of(blocks, rows)
    width = params[0].shape[1] // 2

    def at(step):
        return (flip(step, lax.axis_index("mp"), blocks), 0, 0)

    wide = pl.BlockSpec((1, rows, width), at)
    out = jax.ShapeDtypeStruct((blocks, rows, width), f32)
    low = jax.ShapeDtypeStruct((blocks, rows, width), bf16)
    shapes, specs = piece_outputs(layout, model)
    final = (jax.ShapeDtypeStruct((SUB, width), f32), pl.BlockSpec((SUB, width), lambda step: (0, 0)))
    return call(
        functools.partial(rec_forward_kernel, layout),
        (blocks,),
        [(v, whole(v)) for v in (length,) + tuple(x) + tuple(params)],
        [(shape, wide) for shape in (low, out, out, out, out, low, out, out, out)] + [final] + list(zip(shapes, specs)),
        [
            pltpu.VMEM((rows, 2 * width), f32),
            pltpu.VMEM((SUB, width), f32),
            pltpu.VMEM((SUB, width), f32),
            pltpu.VMEM((rows, model), bf16),
            pltpu.VMEM((rows, width), f32),
        ],
        "rec_forward",
        37,
        **more,
    )


def rec_backward(length, seq, count, d_resid, x, params, saved, shared, **more):
    blocks, (rows, model) = lax.axis_size("mp"), x[0].shape
    layout = layout_of(blocks, rows)
    width = saved[0].shape[2]

    def at(step):
        return (flip(blocks - 1 - step, lax.axis_index("mp"), blocks), 0, 0)

    def placed(step):
        return (seq * blocks + flip(blocks - 1 - step, lax.axis_index("mp"), blocks), 0, 0)

    wide = pl.BlockSpec((1, rows, width), at)
    double = pl.BlockSpec((1, rows, 2 * width), placed)
    low = jax.ShapeDtypeStruct((count * blocks, rows, 2 * width), bf16)
    shapes, specs = piece_outputs(layout, model)
    sums = (jax.ShapeDtypeStruct((8, SUB, width), f32), pl.BlockSpec((8, SUB, width), lambda step: (0, 0, 0)))
    gain_sums = (jax.ShapeDtypeStruct((SUB, model), f32), pl.BlockSpec((SUB, model), lambda step: (0, 0)))
    inputs = [(v, whole(v)) for v in (length,) + tuple(d_resid) + tuple(x) + tuple(params)]
    before_x, before_params = 1 + len(d_resid), 1 + len(d_resid) + len(x)
    late = tuple(range(before_x, before_params)) + tuple(before_params + at for at in (1, 2, 3))
    inputs += [(v, wide) for v in saved] + [(v, ANY) for v in shared]
    return call(
        functools.partial(rec_backward_kernel, layout, len(shared)),
        (blocks,),
        inputs,
        [(low, double), (low, double), sums, gain_sums] + list(zip(shapes, specs)),
        [
            pltpu.VMEM((rows, width), f32),
            pltpu.VMEM((rows, width), f32),
            pltpu.VMEM((SUB, width), f32),
            pltpu.VMEM((SUB, width), f32),
            pltpu.VMEM((rows, model), bf16),
            pltpu.VMEM((rows, model), bf16),
        ],
        "rec_backward",
        43,
        aliases={len(inputs) - len(shared) + at: at for at in range(len(shared))},
        late=late,
        **more,
    )


def largest_tile(total, limit, unit=LANES):
    return max(t for t in range(unit, limit + 1, unit) if total % t == 0)


def mlp_forward(seq, count, x, w_gate, w_up, w_down, shared, **more):
    blocks, (rows, model) = lax.axis_size("mp"), x[0].shape
    units = w_gate.shape[1]
    low = jax.ShapeDtypeStruct((count * blocks, rows, units), bf16)
    part = pl.BlockSpec((1, rows, units), lambda r: (seq * blocks + r, 0, 0))
    long = pl.BlockSpec((1, rows, model), lambda r: (flip(r, lax.axis_index("mp"), blocks), 0, 0))
    inputs = [(v, whole(v)) for v in tuple(x) + (w_gate, w_up, w_down)] + [(v, ANY) for v in shared]
    return call(
        functools.partial(mlp_forward_kernel, layout_of(blocks, rows)),
        (blocks,),
        inputs,
        [(low, part)] * 3 + [(jax.ShapeDtypeStruct((blocks, rows, model), bf16), long)],
        [pltpu.VMEM((rows, model), bf16)],
        "mlp_forward",
        30,
        aliases={len(inputs) - len(shared) + at: at for at in range(len(shared))},
        **more,
    )


def mlp_backward(seq, count, cot, gate, up, w_gate, w_up, w_down, shared, **more):
    blocks, (rows, model) = lax.axis_size("mp"), cot[0].shape
    layout = layout_of(blocks, rows)
    units = w_gate.shape[1]
    low = jax.ShapeDtypeStruct((count * blocks, rows, units), bf16)
    part = pl.BlockSpec((1, rows, units), lambda r: (seq * blocks + r, 0, 0))
    shapes, specs = piece_outputs(layout, model)
    inputs = [(v, whole(v)) for v in cot] + [(gate, part), (up, part)]
    inputs += [(v, whole(v)) for v in (w_gate, w_up, w_down)] + [(v, ANY) for v in shared]
    return call(
        functools.partial(mlp_backward_kernel, layout),
        (blocks,),
        inputs,
        [(low, part)] * 2 + list(zip(shapes, specs)),
        [pltpu.VMEM((rows, model), bf16)] * 2,
        "mlp_backward",
        32,
        aliases={len(inputs) - len(shared) + at: at for at in range(len(shared))},
        **more,
    )


def flat(array):
    return array.reshape(-1, array.shape[-1])


def core_index():
    return lax.axis_index("dp") % 2 if lax.axis_size("dp") == 8 else 0


def weight_grad(lefts, rights, by_rows=True, **more):
    lefts, rights = [flat(v) for v in lefts], [flat(v) for v in rights]
    rows, columns = lefts[0].shape[1], rights[0].shape[1]
    tokens = sum(v.shape[0] for v in lefts)
    exchange = lax.axis_size("dp") == 8
    tiled = rows if by_rows else columns
    tile = tiled // 4 if exchange else largest_tile(tiled, 512)

    def place(step):
        if not exchange:
            return step
        return (core_index() + 1 + step // 2) % 2 * 2 + step % 2

    def cut(array, in_tiles):
        if not in_tiles:
            return whole(array)
        return pl.BlockSpec((array.shape[0], tile), lambda step: (0, place(step)))

    scratch = [
        pltpu.VMEM((tokens if len(lefts) > 1 else 16, tile if by_rows else rows), bf16),
        pltpu.VMEM((tokens if len(rights) > 1 else 16, columns if by_rows else tile), bf16),
    ]
    block = (tile, columns) if by_rows else (rows, tile)
    if exchange:
        outs = [(jax.ShapeDtypeStruct(block, bf16), pl.BlockSpec(block, lambda step: (0, 0)))] * 2
        scratch += [pltpu.VMEM((2,) + block, bf16)] * 2 + [pltpu.SemaphoreType.DMA((2,))] * 2
    else:
        whole_out = jax.ShapeDtypeStruct((rows, columns), bf16)
        outs = [(whole_out, pl.BlockSpec(block, lambda step: (step, 0) if by_rows else (0, step)))]
    return call(
        functools.partial(weight_grad_kernel, by_rows, len(lefts), len(rights), exchange),
        (tiled // tile,),
        [(v, cut(v, by_rows)) for v in lefts] + [(v, cut(v, not by_rows)) for v in rights],
        outs,
        scratch,
        "weight_grad",
        20 if columns > 1000 and by_rows else 13,
        pair=exchange,
        **more,
    )


def last_kernel(nlefts, nrights, nchunks, nblocks, nfinals, tail, *refs):
    lefts, refs = refs[:nlefts], refs[nlefts:]
    rights, refs = refs[:nrights], refs[nrights:]
    convs, refs = refs[:nlefts], refs[nlefts:]
    d_gates, sums_a, sums_b, gain_a, gain_b, gain_c, gain_d = refs[:7]
    chunks, refs = refs[7 : 7 + nchunks], refs[7 + nchunks :]
    finals, refs = refs[:nfinals], refs[nfinals:]
    outs, refs = refs[: nchunks + 3], refs[nchunks + 3 :]
    others, scratch = refs[:nfinals], refs[nfinals:]
    pack, gains, both, whole_pack, got_pack, got_gains, left, right, dense, sent, got, send, recv = scratch[:13]
    finals_send, finals_recv = scratch[13:15]
    step = pl.program_id(0)
    tail.setup(list(chunks) + [pack, gains, both], outs, scratch[15:])
    pl.when(step == 0)(tail.start)

    def swap_final(at):
        return remote(finals[at], others[at], finals_send, finals_recv, at, other_core())

    def swap_gains():
        return remote(gains, got_gains, send, recv, 3, other_core())

    @pl.when(step == 0)
    def _():
        one = jnp.sum(gain_a[...] + gain_b[...], axis=0, keepdims=True)
        two = gain_c[...] + gain_d[...]
        row = lax.broadcasted_iota(jnp.int32, (16, one.shape[1]), 0)
        gains[...] = jnp.where(row == 0, one, jnp.where(row == 1, two, 0.0)).astype(bf16)
        swap_gains().start()

    @pl.when(step == 1)
    def _():
        swap_gains().wait()
        gains[...] = (gains[...].astype(f32) + got_gains[...].astype(f32)).astype(bf16)

    def copy(at):
        return remote(sent.at[at], got.at[at], send, recv, at, other_core())

    def pack_copy():
        return remote(whole_pack, got_pack, send, recv, 2, other_core())

    @pl.when(step < 4)
    def _():
        at = 0
        for ref in rights:
            right[at : at + ref.shape[0], :] = ref[...]
            at += ref.shape[0]

    @pl.when(step == 0)
    def _():
        at = 0
        for ref in lefts:
            left[at : at + ref.shape[0], :] = ref[...]
            at += ref.shape[0]

    for at in range(4):

        @pl.when(step == at)
        def _(at=at):
            total = lax.dot_general(left[...], right[...], (((0,), (0,)), ((), ())), preferred_element_type=f32)
            if at < 2:
                sent[at] = total.astype(bf16)
                copy(at).start()
            else:
                copy(at - 2).wait_recv()
                rows = total.shape[0]
                both[(at - 2) * rows : (at - 1) * rows, :] = (total + got[at - 2].astype(f32)).astype(bf16)
                copy(at - 2).wait_send()

    @pl.when(step == 3)
    def _():
        at = 0
        for ref in convs:
            rows = ref.shape[0]
            term = lax.dot_general(
                ref[...], d_gates[at : at + rows, :], (((0,), (0,)), ((), ())), preferred_element_type=f32
            )
            dense[...] = term if at == 0 else dense[...] + term
            at += rows
        width = dense.shape[0]
        inner = width // nblocks
        lane = lax.broadcasted_iota(jnp.int32, (inner, width), 1)
        for gate in range(2):
            total = jnp.zeros((inner, width), f32)
            for n in range(nblocks):
                here = (lane >= n * inner) & (lane < (n + 1) * inner)
                block = dense[n * inner : (n + 1) * inner, gate * width : (gate + 1) * width]
                total = total + jnp.where(here, block, 0.0)
            whole_pack[gate * inner : (gate + 1) * inner, :] = total.astype(bf16)
        vectors = jnp.sum(sums_a[...] + sums_b[...], axis=1)
        rest = whole_pack.shape[0] - 2 * inner
        vectors = jnp.concatenate([vectors, jnp.zeros((rest - 8, width), f32)], axis=0)
        whole_pack[2 * inner :, :] = vectors.astype(bf16)
        pack_copy().start()

    @pl.when(step == 4)
    def _():
        pack_copy().wait()
        for at in range(nfinals):
            swap_final(at).start()
        mine = pl.ds(pl.multiple_of(core_index() * pack.shape[0], 16), pack.shape[0])
        pack[...] = (whole_pack[mine, :].astype(f32) + got_pack[mine, :].astype(f32)).astype(bf16)
        tail.finish()
        for at in range(nfinals):
            swap_final(at).wait()


def last_grad(lefts, rights, convs, d_gates, vectors, moving, finals, nblocks, **more):
    lefts, rights, convs = ([flat(v) for v in group] for group in (lefts, rights, convs))
    rows, columns = lefts[0].shape[1], rights[0].shape[1]
    tokens = sum(v.shape[0] for v in lefts)
    tile = columns // 4

    def place(step):
        step = step - step // 4
        return (core_index() + 1 + step // 2) % 2 * 2 + step % 2

    chunks = [(chunk, stage) for stage, group in enumerate(moving) for _, chunk in group.items()]
    names = [name for group in moving for name in group]
    block = (rows, tile)
    packed = -(-(2 * rows // nblocks + 16) // 32) * 32
    made = [((packed // 2, rows), True), ((16, columns), True), ((2 * rows, tile), False)]
    tail = Tail(
        [(chunk.shape, stage, False, True) for chunk, stage in chunks] + [(shape, 0, True, out) for shape, out in made]
    )
    outs = [jax.ShapeDtypeStruct(chunk[0], bf16) for chunk in tail.chunks]
    out, found = call(
        functools.partial(last_kernel, len(lefts), len(rights), len(chunks), nblocks, len(finals), tail),
        (5,),
        [(v, whole(v)) for v in lefts]
        + [(v, pl.BlockSpec((v.shape[0], tile), lambda step: (0, place(step)))) for v in rights]
        + [(v, whole(v)) for v in convs + [flat(d_gates)] + list(vectors)]
        + [(chunk, ANY) for chunk, _ in chunks]
        + [(piece, ANY) for piece in finals.values()],
        [(shape, ANY) for shape in outs]
        + [(jax.ShapeDtypeStruct(piece.shape, bf16), ANY) for piece in finals.values()],
        [pltpu.VMEM(shape, bf16) for shape, _ in made]
        + [
            pltpu.VMEM((packed, rows), bf16),
            pltpu.VMEM((packed, rows), bf16),
            pltpu.VMEM((16, columns), bf16),
            pltpu.VMEM((tokens, rows), bf16),
            pltpu.VMEM((tokens, tile), bf16),
            pltpu.VMEM((rows, 2 * rows), f32),
            pltpu.VMEM((2,) + block, bf16),
            pltpu.VMEM((2,) + block, bf16),
            pltpu.SemaphoreType.DMA((4,)),
            pltpu.SemaphoreType.DMA((4,)),
            pltpu.SemaphoreType.DMA((len(finals),)),
            pltpu.SemaphoreType.DMA((len(finals),)),
        ]
        + tail.scratch,
        "last_grad",
        120,
        pair=True,
        chips=True,
        **more,
    )
    names += ["pack", "gains", "out"]
    return dict(zip(names, out)), dict(zip(finals, out[len(names) :])), found


def join_pieces(pieces, by_rows, ways):
    rows, columns = sum(v.shape[0] for v in pieces), pieces[0].shape[1]
    shape = (rows, columns // ways) if by_rows else (rows // 4, 4 * columns)
    out = (jax.ShapeDtypeStruct(shape, f32), ANY)
    return call(
        functools.partial(join_kernel, len(pieces), by_rows, ways),
        (1,),
        [(piece, ANY) for piece in pieces],
        [out] * ways,
        [pltpu.VMEM(piece.shape, bf16) for piece in pieces]
        + [pltpu.VMEM(piece.shape, f32) for piece in pieces]
        + [pltpu.SemaphoreType.DMA((len(pieces),)), pltpu.SemaphoreType.DMA((len(pieces) * max(2, ways),))],
        "join_pieces",
        0.05,
    )[0]


def swap(value, axis, bit):
    size = lax.axis_size(axis)
    return lax.ppermute(value, axis, [(i, i ^ bit) for i in range(size)])


def gather(shard):
    size = lax.axis_size("mp")
    if size != 4:
        return (shard,) + tuple(swap(shard, "mp", r) for r in range(1, size))
    half = shard.shape[0] // 2
    by_x = swap(shard, "mp", 1)
    by_y = swap(shard, "mp", 2)
    return (shard, by_x, by_y, swap(by_x[:half], "mp", 2), swap(by_y[half:], "mp", 1))


def scatter(parts):
    size = lax.axis_size("mp")
    if size != 4:
        total = parts[0].astype(f32)
        for r in range(1, size):
            total = total + swap(parts[r], "mp", r).astype(f32)
        return total
    half = parts[3].shape[0]
    from_x = swap(parts[3], "mp", 1)
    from_y = swap(parts[4], "mp", 2)
    for_y = jnp.concatenate([add_low(parts[2][:half], from_x), parts[2][half:]], axis=0)
    for_x = jnp.concatenate([parts[1][:half], add_low(parts[1][half:], from_y)], axis=0)
    return parts[0].astype(f32) + swap(for_y, "mp", 2).astype(f32) + swap(for_x, "mp", 1).astype(f32)


def add_low(left, right):
    return (left.astype(f32) + right.astype(f32)).astype(bf16)


class Pipe:
    def __init__(self):
        self.queue, self.moving, self.done = [], [], {}

    def enter(self, name, quarters):
        self.queue += [[name + str(at), quarter, 0] for at, quarter in enumerate(quarters)]

    def host(self, budget, slots):
        pieces, old = [], list(slots)
        for name, array, stage in self.moving:
            slot = slots[0] if stage == 2 else old.pop(0)
            pieces.append((name, array, 0, array.shape[0], stage, 3 - stage, slot))
        ahead = list(slots)
        while self.queue and budget > 0:
            name, array, start = self.queue[0]
            unit = array.shape[0] // 4
            slot = ahead.pop(0) if ahead else None
            pieces.append((name + "_" + str(start).zfill(4), array, start, unit, 0, 2 if slot else 1, slot))
            budget -= 1
            self.queue[0][2] += unit
            if self.queue[0][2] == array.shape[0]:
                self.queue.pop(0)
        return PipeHost(pieces) if pieces else None

    def took(self, host, results):
        self.moving = []
        for name, _, _, _, stage, hops, _ in host.pieces:
            if stage + hops == 3:
                self.done[name] = results[name]
            else:
                self.moving.append((name, results[name], stage + hops))

    def left(self):
        groups = ({}, {}, {})
        for name, array, stage in self.moving:
            groups[stage][name] = array
        for name, array, start in self.queue:
            groups[0][name + "_" + str(start).zfill(4)] = array[start:]
        return groups


def normalize(values, gain):
    return values * lax.rsqrt(jnp.mean(values * values, axis=-1, keepdims=True) + EPS) * gain


def normalize_back(values, gain, grad):
    inverse = lax.rsqrt(jnp.mean(values * values, axis=-1, keepdims=True) + EPS)
    scaled = grad * gain
    unit = values * inverse
    return inverse * (scaled - unit * jnp.mean(scaled * unit, axis=-1, keepdims=True)), unit


def dense_blocks(weight):
    blocks, inner, outer = weight.shape
    rows = [
        jnp.pad(weight[n], ((0, 0), (n * outer, (blocks - 1 - n) * outer))) for n in range(blocks)
    ]
    return jnp.concatenate(rows, axis=0)


def diagonal_blocks(full, blocks, width):
    inner = width // blocks
    return jnp.stack([full[n * inner : (n + 1) * inner, n * inner : (n + 1) * inner] for n in range(blocks)])


def per_device(
    block_in,
    norm1_gain,
    w_branch,
    w_input,
    conv_weight,
    conv_bias,
    gate_a_weight,
    gate_a_bias,
    gate_i_weight,
    gate_i_bias,
    decay_param,
    w_out,
    norm2_gain,
    w_gate,
    w_up,
    w_down,
    lengths,
    cotangent,
):
    count = block_in.shape[0]
    nblocks = gate_a_weight.shape[0]
    true_width = w_branch.shape[1]
    extra = -true_width % LANES
    me = lax.axis_index("mp")

    def pad_last(value):
        return jnp.pad(value, [(0, 0)] * (value.ndim - 1) + [(0, extra)]) if extra else value

    def line(value):
        return pad_last(value)[None, :]

    wb, wi = pad_last(w_branch), pad_last(w_input)
    wo = jnp.pad(w_out, ((0, extra), (0, 0))) if extra else w_out
    w_ga, w_gi = dense_blocks(gate_a_weight), dense_blocks(gate_i_weight)
    if extra:
        w_ga, w_gi = (jnp.pad(v, ((0, extra), (0, extra))) for v in (w_ga, w_gi))
    taps = pad_last(conv_weight)
    decay_line = line(decay_param)
    w_both = jnp.concatenate([wb, wi], axis=1)
    w_gates = jnp.concatenate([w_ga, w_gi], axis=1)
    forward_params = (
        w_both, taps, line(conv_bias), w_gates, line(gate_a_bias), line(gate_i_bias), decay_line, wo
    )
    backward_params = (wo, w_both, taps, w_gates, decay_line)
    seqs = range(count)
    limits = [jnp.full((SUB, LANES), lengths[s], jnp.int32) for s in seqs]
    blocks = lax.axis_size("mp")
    hosted = blocks == 4 and count == 2
    ids = iter(range(1, 100))

    piped = hosted and lax.axis_size("dp") == 8 and not extra
    pipe = Pipe()

    def enter(name, quarters):
        if piped:
            pipe.enter(name, quarters)

    def tied(value, *deps):
        return lax.optimization_barrier((value,) + deps)[0]

    def run(function, *args, hosts=(), middle=0, budget=4, **more):
        if hosted:
            window = pipe.host(budget, (2, 3) if function is weight_grad else (1, 2)) if piped else None
            out, found = function(
                *args, hosts=list(hosts) + ([window] if window else []), middle=middle, unique=next(ids), **more
            )
            if window:
                pipe.took(window, found[-1])
            return out, found[: len(hosts)]
        out, _ = function(*args, **more)
        return out, [
            gather(host.operands[0]) if isinstance(host, GatherHost) else scatter((host.first, *host.operands))
            for host in hosts
        ]

    resid = [block_in[s].astype(f32) for s in seqs]
    starts = [normalize(resid[s], norm1_gain).astype(bf16) for s in seqs]
    piece, model = starts[0].shape
    seq_in = [gather(starts[0])]
    out, (second,) = run(rec_forward, limits[0], seq_in[0], forward_params, hosts=[GatherHost(starts[1])], middle=3)
    seq_in.append(second)
    forward = [out]
    out, (branch,) = run(
        rec_forward, limits[1], seq_in[1], forward_params, hosts=[ScatterHost(out[10:])], middle=2, before=(out[9],)
    )
    forward.append(out)
    mixed = [out[0] for out in forward]
    saved = [out[1:9] for out in forward]
    finals = [out[9][:1, :true_width] for out in forward]
    resid_mid = [resid[0] + branch]
    mid = normalize(resid_mid[0], norm2_gain).astype(bf16)
    seq_mid = [gather(mid)]
    forward_shared, (branch,) = run(
        mlp_forward, 0, count, seq_mid[0], w_gate, w_up, w_down, (), hosts=[ScatterHost(forward[1][10:])], middle=2
    )
    mlp_part = [forward_shared[3]]
    resid_mid.append(resid[1] + branch)
    mid = normalize(resid_mid[1], norm2_gain).astype(bf16)
    seq_mid.append(gather(mid))
    forward_shared, (found,) = run(
        mlp_forward, 1, count, seq_mid[1], w_gate, w_up, w_down, forward_shared[:3],
        hosts=[GatherHost(cotangent[0])], middle=3,
    )
    mlp_part.append(forward_shared[3])
    cot_seq = [found]
    hidden, gate_low, up_low = forward_shared[:3]
    backward, (found,) = run(
        mlp_backward, 0, count, cot_seq[0], gate_low, up_low, w_gate, w_up, w_down, (),
        hosts=[GatherHost(cotangent[1])], middle=3,
    )
    cot_seq.append(found)

    def middle_grad(s, d_mid):
        back, unit = normalize_back(resid_mid[s], norm2_gain, d_mid)
        return cotangent[s].astype(f32) + back, jnp.sum(d_mid * unit, axis=0, keepdims=True)

    flat_mid = [p for pieces in seq_mid for p in pieces]
    flat_cot = [p for pieces in cot_seq for p in pieces]
    grad_down, _ = run(weight_grad, [hidden], flat_cot)
    enter("down", grad_down)
    backward, (d_mid,) = run(
        mlp_backward, 1, count, cot_seq[1], gate_low, up_low, w_gate, w_up, w_down, backward[:2],
        hosts=[ScatterHost(backward[2:])], middle=2, before=(grad_down[0],),
    )
    d_gate, d_up = backward[:2]
    first, gain2 = middle_grad(0, d_mid)
    grad_gate, (first_seq,) = run(weight_grad, flat_mid, [d_gate], hosts=[GatherHost(first.astype(bf16))], middle=3)
    enter("gate", grad_gate)
    grad_up, (d_mid,) = run(
        weight_grad, flat_mid, [d_up], hosts=[ScatterHost(backward[2:])], middle=2, before=(grad_gate[0],)
    )
    second, more_gain2 = middle_grad(1, d_mid)
    enter("up", grad_up)
    out, (second_seq,) = run(
        rec_backward, limits[0], 0, count, first_seq, seq_in[0], backward_params, saved[0], (),
        hosts=[GatherHost(second.astype(bf16))], middle=3, before=(grad_up[0],), budget=4,
    )
    sums, gain1 = out[2], out[3]
    out, (d_in,) = run(
        rec_backward, limits[1], 1, count, second_seq, seq_in[1], backward_params, saved[1], out[:2],
        hosts=[ScatterHost(out[4:])], middle=2, budget=4,
    )
    d_both, d_gates = out[:2]
    input_grad = [(first + normalize_back(resid[0], norm1_gain, d_in)[0]).astype(bf16)]

    flat_in = [p for pieces in seq_in for p in pieces]
    flat_resid = [p for pieces in (first_seq, second_seq) for p in pieces]
    grad_in, _ = run(weight_grad, flat_in, [d_both])
    conv = [part[4] for part in saved]
    if piped:

        def join(prefix, by_rows=True, ways=1):
            names = [name for name in sorted(pipe.done) if name.startswith(prefix)]
            mine = [pipe.done[name] for name in names]
            other = [others[name] if name in others else swap(pipe.done[name], "dp", 1) for name in names]
            return join_pieces(mine + other, by_rows, ways)

        moving = pipe.left()
        moving[0].update(in0=grad_in[0], in1=grad_in[1])
        found, others, (d_in,) = last_grad(
            mixed, flat_resid, conv, d_gates, (sums, out[2], gain1, out[3], gain2, more_gain2), moving, dict(pipe.done),
            nblocks,
            hosts=[ScatterHost(out[4:])], middle=4, unique=next(ids), before=(grad_in[0],),
        )
        pipe.done.update({name: found[name] for name in found if name != "out"})
        pairs = [(2 * a + core, 2 * b + core) for a, b in ((1, 0), (2, 3)) for core in range(2)]
        came = lax.ppermute(found["out"], "dp", pairs)
        totals_down, totals_gate, totals_up = (join(name) for name in ("down", "gate", "up"))
        totals_in = join("in", ways=2)
        came = lax.optimization_barrier((came, totals_down, totals_gate, totals_up, totals_in[0]))[0]
        pipe.done["out"] = jnp.where(chip_is_inner(), found["out"], came)
        totals_out = join("out", by_rows=False)
        pack, other = found["pack"].astype(f32), swap(found["pack"], "dp", 1).astype(f32)
        mine = core_index() == 0
        pack = jnp.concatenate([jnp.where(mine, pack, other), jnp.where(mine, other, pack)], axis=0)
        inner = true_width // nblocks
        full_ga, full_gi = (
            jnp.transpose(pack[at * inner : (at + 1) * inner].reshape(inner, nblocks, inner), (1, 0, 2)) for at in range(2)
        )
        vectors = pack[2 * inner : 2 * inner + 8]
        gains = found["gains"][:2].astype(f32)
        for bit in (1, 2):
            gains = gains + swap(gains, "mp", bit)
    else:
        grad_out, _ = run(weight_grad, mixed, flat_resid, False, before=(grad_in[0],))
        d_in = scatter(out[4:])
        totals_down, totals_gate, totals_up, totals_in, totals_out = (
            jnp.split(lax.psum(v[0], "dp").astype(f32), ways, axis=1)
            for v, ways in ((grad_down, 1), (grad_gate, 1), (grad_up, 1), (grad_in, 2), (grad_out, 1))
        )
        d_gates = d_gates.reshape(count, blocks, piece, -1)
        width = d_gates.shape[-1] // 2
        full = sum(jnp.einsum("rtd,rtc->dc", conv[s], d_gates[s], preferred_element_type=f32) for s in seqs)
        gains = jnp.stack([jnp.sum(gain1 + out[3], axis=0), (gain2 + more_gain2)[0]])
        vectors = jnp.sum(sums + out[2], axis=1)[:, :true_width]
        full_ga, full_gi, vectors, gains = lax.psum(
            (
                diagonal_blocks(full[:, :width], nblocks, true_width).astype(bf16),
                diagonal_blocks(full[:, width:], nblocks, true_width).astype(bf16),
                vectors.astype(bf16),
                lax.psum(gains, "mp").astype(bf16),
            ),
            "dp",
        )
    input_grad.append((second + normalize_back(resid[1], norm1_gain, d_in)[0]).astype(bf16))
    input_grad = jnp.stack(input_grad)
    grad_gate_a_weight, grad_gate_i_weight, vectors, gains = (
        v.astype(f32) for v in (full_ga, full_gi, vectors, gains)
    )
    gains = jnp.stack([gains[0] / norm1_gain, gains[1]])
    vectors = jnp.concatenate(
        [(vectors[0] * DECAY_EXP * jax.nn.sigmoid(-decay_param))[None, :], vectors[1:]], axis=0
    )
    grad_w_out = totals_out[0][:true_width]
    grad_w_branch, grad_w_input = (v[:, :true_width] for v in totals_in)
    mlp_total = [
        lax.psum_scatter(flat(tied(v, grad_in[0])), "mp", scatter_dimension=0, tiled=True) for v in mlp_part
    ]
    block_out = jnp.stack([(resid_mid[s] + mlp_total[s].astype(f32)).astype(bf16) for s in seqs])

    return (
        block_out,
        input_grad,
        gains[0],
        grad_w_branch,
        grad_w_input,
        vectors[4:8],
        vectors[3],
        grad_gate_a_weight,
        vectors[1],
        grad_gate_i_weight,
        vectors[2],
        vectors[0],
        grad_w_out,
        gains[1],
        totals_gate[0],
        totals_up[0],
        totals_down[0],
        jnp.concatenate(finals, axis=0),
    )


def solution(mesh):
    placed = (
        P("dp", "mp", None),
        P(),
        P(None, "mp"),
        P(None, "mp"),
        P(None, "mp"),
        P("mp"),
        P("mp", None, None),
        P("mp"),
        P("mp", None, None),
        P("mp"),
        P("mp"),
        P("mp", None),
        P(),
        P(None, "mp"),
        P(None, "mp"),
        P("mp", None),
        P("dp"),
        P("dp", "mp", None),
    )
    return jax.shard_map(
        per_device,
        mesh=mesh,
        in_specs=placed,
        out_specs=(
            P("dp", "mp", None),
            P("dp", "mp", None),
            P(),
            P(None, "mp"),
            P(None, "mp"),
            P(None, "mp"),
            P("mp"),
            P("mp", None, None),
            P("mp"),
            P("mp", None, None),
            P("mp"),
            P("mp"),
            P("mp", None),
            P(),
            P(None, "mp"),
            P(None, "mp"),
            P("mp", None),
            P("dp", "mp"),
        ),
        check_vma=False,
    )
```

```python
import functools
import math

import jax
import jax.numpy as jnp
from jax import lax
from jax.experimental import pallas as pl
from jax.experimental.pallas import tpu as pltpu
from jax.sharding import PartitionSpec as P

DECAY_EXP = 8.0
EPS = 1e-06
GELU_C = math.sqrt(2.0 / math.pi)
GELU_K = 0.044715
LANES = 128
SUB = 8
UNIT_TILE = 256
COST_SCALE = 0.5
MODEL_TILE = 512
VMEM_BYTES = 56 * 1024 * 1024

f32 = jnp.float32
bf16 = jnp.bfloat16


def dot_nn(left, right):
    return lax.dot_general(left, right, (((1,), (0,)), ((), ())), preferred_element_type=f32)


def dot_nt(left, right):
    return lax.dot_general(left, right, (((1,), (1,)), ((), ())), preferred_element_type=f32)


def one_minus_square(log_a, decay):
    x = 2.0 * log_a
    tail = 1.0 + x * (1.0 / 7.0)
    for k in (6.0, 5.0, 4.0, 3.0, 2.0):
        tail = 1.0 + x * (1.0 / k) * tail
    return jnp.where(x > -0.4, -x * tail, 1.0 - decay * decay)


def gelu_parts(x):
    square = x * x
    th = jnp.tanh(GELU_C * x * (1.0 + GELU_K * square))
    half = 0.5 * (1.0 + th)
    value = x * half
    slope = half + 0.5 * x * (1.0 - th * th) * (GELU_C * (1.0 + 3.0 * GELU_K * square))
    return value, slope


def row_index(shape):
    return lax.broadcasted_iota(jnp.int32, shape, 0)


def shift_down(prev, cur, k, row):
    return jnp.where(row < k, pltpu.roll(prev, k, 0), pltpu.roll(cur, k, 0))


def shift_up(cur, following, k, row):
    return jnp.where(row < SUB - k, pltpu.roll(cur, SUB - k, 0), pltpu.roll(following, SUB - k, 0))


def load_block(pieces, layout, block, target):
    for ref, (owner, start, count) in zip(pieces, layout):

        @pl.when(block == owner)
        def _(ref=ref, start=start, count=count):
            target[pl.ds(start, count), :] = ref[...]


def store_block(pieces, layout, block, column, value):
    for ref, (owner, start, count) in zip(pieces, layout):

        @pl.when(block == owner)
        def _(ref=ref, start=start, count=count):
            ref[:, column] = value[start : start + count]


def rec_forward_kernel(layout, wait_late, length, *refs):
    x_pieces, refs = refs[: len(layout)], refs[len(layout) :]
    w_both, taps, conv_bias, w_gates, ga_bias, gi_bias, decay_param, w_out = refs[:8]
    branch = refs[-1]
    gates_pre, tail, carry, x = refs[-5:-1]
    outs = refs[-5 - 10 - len(layout) : -5]
    mixed, pre, value_out, slope_out, space_out, conv, ga, gi, prev_state, final = outs[:10]
    parts = outs[10:]
    step = pl.program_id(0)
    block = flip(step, lax.axis_index("mp"), 4 if len(layout) == 5 else len(layout))
    rows, width = mixed.shape[1:]
    load_block(x_pieces, layout, block, x)
    pieces = rows // 16
    lanes = [pl.ds(at, LANES) for at in range(0, width, LANES)]
    row = row_index((SUB, LANES))

    @pl.when(step == 0)
    def _():
        tail[...] = jnp.zeros_like(tail)
        carry[...] = jnp.zeros_like(carry)

    both = dot_nn(x[...], w_both[...])
    branch[...] = both[:, :width]
    pre[0] = both[:, width:]

    def conv_piece(i, _):
        base = pl.multiple_of(i * 16, 16)
        for lane in lanes:
            bias = conv_bias[:, lane]
            before = tail[:, lane]
            parts = []
            for half in range(2):
                cur = pre[0, pl.ds(base + SUB * half, SUB), lane]
                total = bias + taps[0:1, lane] * cur
                for k in range(1, 4):
                    total = total + taps[k : k + 1, lane] * shift_down(before, cur, k, row)
                parts.append(total)
                before = cur
            tail[:, lane] = before
            conv[0, pl.ds(base, 16), lane] = jnp.concatenate(parts, axis=0).astype(bf16)
        return 0

    lax.fori_loop(0, pieces, conv_piece, 0)
    wait_late()
    gates_pre[...] = dot_nn(conv[0], w_gates[...])
    limit = length[...]

    def scan_piece(i, _):
        base = pl.multiple_of(i * 16, 16)
        start = step * rows + base
        for lane in lanes:
            second = pl.ds(width + lane.start, LANES)
            rate = -DECAY_EXP * jax.nn.softplus(-decay_param[:, lane])
            conv_two = conv[0, pl.ds(base, 16), lane].astype(f32)
            state = carry[:, lane]
            outs = []
            for half in range(2):
                at = pl.ds(base + SUB * half, SUB)
                live = (row + (start + SUB * half)) < limit
                gate_a = jax.nn.sigmoid(gates_pre[at, lane] + ga_bias[:, lane])
                gate_i = jax.nn.sigmoid(gates_pre[at, second] + gi_bias[:, lane])
                ga[0, at, lane] = gate_a
                gi[0, at, lane] = gate_i
                log_a = rate * gate_a
                decay = jnp.exp(log_a)
                space = one_minus_square(log_a, decay)
                space_out[0, at, lane] = space
                scaled = jnp.sqrt(space) * gate_i * conv_two[SUB * half : SUB * half + SUB]
                mul = jnp.where(live, decay, 1.0)
                add = jnp.where(live, scaled, 0.0)
                for shift in (1, 2, 4):
                    inside = row >= shift
                    add = add + mul * jnp.where(inside, pltpu.roll(add, shift, 0), 0.0)
                    mul = mul * jnp.where(inside, pltpu.roll(mul, shift, 0), 1.0)
                states = mul * state + add
                prev_state[0, at, lane] = jnp.where(row == 0, state, pltpu.roll(states, 1, 0))
                state = jnp.broadcast_to(states[SUB - 1 : SUB], (SUB, LANES))
                value, slope = gelu_parts(branch[at, lane])
                value_out[0, at, lane] = value
                slope_out[0, at, lane] = slope
                outs.append(states * value)
            carry[:, lane] = state
            mixed[0, pl.ds(base, 16), lane] = jnp.concatenate(outs, axis=0).astype(bf16)
        return 0

    lax.fori_loop(0, pieces, scan_piece, 0)
    final[...] = carry[...]
    for at in range(0, w_out.shape[1], MODEL_TILE):
        column = pl.ds(at, MODEL_TILE)
        x[:, column] = dot_nn(mixed[0], w_out[:, column]).astype(bf16)
    store_block(parts, layout, block, slice(None), x[...])


def rec_backward_kernel(layout, nshared, wait_late, length, *refs):
    many = len(layout)
    d_resid_pieces, x_pieces, refs = refs[:many], refs[many : 2 * many], refs[2 * many :]
    w_out, w_both, taps, w_gates, decay_param = refs[:5]
    pre, value_in, slope_in, space_in, conv, ga, gi, prev_state = refs[5:13]
    d_mixed, d_conv, flow, later, x, d_resid = refs[-6:]
    outs = refs[-6 - 4 - many : -6]
    d_both, d_gates, sums, gain_sums = outs[:4]
    parts = outs[4:]
    step = pl.program_id(0)
    rows, width = pre.shape[1:]
    pieces = rows // 16
    lanes = [pl.ds(at, LANES) for at in range(0, width, LANES)]
    row = row_index((SUB, LANES))
    first = (pl.num_programs(0) - 1 - step) * rows
    limit = length[...]

    @pl.when(step == 0)
    def _():
        flow[...] = jnp.zeros_like(flow)
        later[...] = jnp.zeros_like(later)
        sums[...] = jnp.zeros_like(sums)
        gain_sums[...] = jnp.zeros_like(gain_sums)

    block = flip(pl.num_programs(0) - 1 - step, lax.axis_index("mp"), 4 if len(layout) == 5 else len(layout))
    load_block(d_resid_pieces, layout, block, d_resid)
    d_mixed[...] = dot_nt(d_resid[...], w_out[...])

    def scan_piece(j, _):
        base = pl.multiple_of((pieces - 1 - j) * 16, 16)
        for lane in lanes:
            rate = -DECAY_EXP * jax.nn.softplus(-decay_param[:, lane])
            conv_two = conv[0, pl.ds(base, 16), lane].astype(f32)
            carried = flow[:, lane]
            outs = [None, None]
            sum_log = sums[0, :, lane]
            for half in (1, 0):
                at = pl.ds(base + SUB * half, SUB)
                live = (row + (first + base + SUB * half)) < limit
                conv_val = conv_two[SUB * half : SUB * half + SUB]
                gate_a = ga[0, at, lane]
                gate_i = gi[0, at, lane]
                before = prev_state[0, at, lane]
                d_mix = d_mixed[at, lane]
                log_a = rate * gate_a
                decay = jnp.exp(log_a)
                space = space_in[0, at, lane]
                inverse = lax.rsqrt(jnp.maximum(space, 1e-37))
                root = space * inverse
                gated = gate_i * conv_val
                mul = jnp.where(live, decay, 1.0)
                states = mul * before + jnp.where(live, root * gated, 0.0)
                d_br = d_mix * states * slope_in[0, at, lane]
                direct = d_mix * value_in[0, at, lane]
                add = mul * direct
                for shift in (1, 2, 4):
                    inside = row < SUB - shift
                    add = add + mul * jnp.where(inside, pltpu.roll(add, SUB - shift, 0), 0.0)
                    mul = mul * jnp.where(inside, pltpu.roll(mul, SUB - shift, 0), 1.0)
                moved = add + mul * carried
                d_state = direct + jnp.where(row == SUB - 1, carried, pltpu.roll(moved, SUB - 1, 0))
                carried = jnp.broadcast_to(moved[0:1], (SUB, LANES))
                d_state = jnp.where(live, d_state, 0.0)
                d_log = d_state * decay * (before - gated * decay * inverse)
                sum_log = sum_log + d_log * gate_a
                d_gate_a = d_log * rate * gate_a * (1.0 - gate_a)
                d_rooted = d_state * root
                d_conv_rec = d_rooted * gate_i
                d_gate_i = d_rooted * conv_val * gate_i * (1.0 - gate_i)
                d_conv[at, lane] = d_conv_rec
                outs[half] = (d_br, d_gate_a, d_gate_i)
            flow[:, lane] = carried
            sums[0, :, lane] = sum_log
            second = pl.ds(width + lane.start, LANES)
            for target, there, which in ((d_both, lane, 0), (d_gates, lane, 1), (d_gates, second, 2)):
                both = jnp.concatenate([outs[0][which], outs[1][which]], axis=0).astype(bf16)
                target[0, pl.ds(base, 16), there] = both
                if which > 0:
                    wide = both.astype(f32)
                    sums[which, :, lane] += wide[:SUB] + wide[SUB:]
        return 0

    lax.fori_loop(0, pieces, scan_piece, 0)
    wait_late()
    load_block(x_pieces, layout, block, x)
    d_conv[...] += dot_nt(d_gates[0], w_gates[...])

    def conv_piece(j, _):
        base = pl.multiple_of((pieces - 1 - j) * 16, 16)
        for lane in lanes:
            following = later[:, lane]
            totals = [None, None]
            tap_sums = [sums[3 + k, :, lane] for k in range(5)]
            for half in (1, 0):
                at = pl.ds(base + SUB * half, SUB)
                cur = d_conv[at, lane]
                seen = pre[0, at, lane]
                tap_sums[0] = tap_sums[0] + cur
                tap_sums[1] = tap_sums[1] + cur * seen
                total = taps[0:1, lane] * cur
                for k in range(1, 4):
                    ahead = shift_up(cur, following, k, row)
                    tap_sums[1 + k] = tap_sums[1 + k] + ahead * seen
                    total = total + taps[k : k + 1, lane] * ahead
                totals[half] = total
                following = cur
            later[:, lane] = following
            for k in range(5):
                sums[3 + k, :, lane] = tap_sums[k]
            d_both[0, pl.ds(base, 16), pl.ds(width + lane.start, LANES)] = jnp.concatenate(totals, axis=0).astype(bf16)
        return 0

    lax.fori_loop(0, pieces, conv_piece, 0)
    for at in range(0, x.shape[1], MODEL_TILE):
        column = pl.ds(at, MODEL_TILE)
        part = dot_nt(d_both[0], w_both[column, :])
        seen = part * x[:, column].astype(f32)
        gain_sums[:, column] += jnp.sum(seen.reshape(rows // SUB, SUB, MODEL_TILE), axis=0)
        d_resid[:, column] = part.astype(bf16)
    store_block(parts, layout, block, slice(None), d_resid[...])


def mlp_forward_kernel(layout, *refs):
    many = len(layout)
    x_pieces, (w_gate, w_up, w_down) = refs[:many], refs[many : many + 3]
    hidden, gate, up, mlp_part, x = refs[-5:]
    load_block(x_pieces, layout, pl.program_id(0), x)
    for at in range(0, hidden.shape[2], UNIT_TILE):
        column = pl.ds(at, UNIT_TILE)
        up_pre = dot_nn(x[...], w_up[:, column])
        gate_pre = dot_nn(x[...], w_gate[:, column])
        value, _ = gelu_parts(gate_pre)
        hidden[0, :, column] = (value * up_pre).astype(bf16)
        gate[0, :, column] = gate_pre.astype(bf16)
        up[0, :, column] = up_pre.astype(bf16)
    for at in range(0, x.shape[1], MODEL_TILE):
        column = pl.ds(at, MODEL_TILE)
        mlp_part[0, :, column] = dot_nn(hidden[0], w_down[:, column]).astype(bf16)


def mlp_backward_kernel(layout, *refs):
    many = len(layout)
    cot_pieces, (gate, up, w_gate, w_up, w_down) = refs[:many], refs[many : many + 5]
    cot, mid = refs[-2:]
    d_gate, d_up = refs[-2 - many - 2 : -2 - many]
    parts = refs[-2 - many : -2]
    r = pl.program_id(0)
    load_block(cot_pieces, layout, r, cot)
    for at in range(0, d_gate.shape[2], UNIT_TILE):
        column = pl.ds(at, UNIT_TILE)
        back = dot_nt(cot[...], w_down[column, :])
        value, slope = gelu_parts(gate[0, :, column].astype(f32))
        d_gate[0, :, column] = (back * up[0, :, column].astype(f32) * slope).astype(bf16)
        d_up[0, :, column] = (back * value).astype(bf16)
    for at in range(0, cot.shape[1], MODEL_TILE):
        column = pl.ds(at, MODEL_TILE)
        total = dot_nt(d_gate[0], w_gate[column, :]) + dot_nt(d_up[0], w_up[column, :])
        mid[:, column] = total.astype(bf16)
    store_block(parts, layout, r, slice(None), mid[...])


def weight_grad_kernel(by_rows, nlefts, nrights, exchange, *refs):
    lefts, rights = refs[:nlefts], refs[nlefts : nlefts + nrights]
    arrived, refs = refs[-1], refs[:-1]
    if exchange:
        first, second, left, right, sent, got, send, recv = refs[-8:]
    else:
        out, left, right = refs[-3:]
    step = pl.program_id(0)

    def assemble(target, sources):
        at = 0
        for ref in sources:
            target[at : at + ref.shape[0], :] = ref[...]
            at += ref.shape[0]

    if nlefts == 1:
        left = lefts[0]
    elif by_rows:
        assemble(left, lefts)
    else:
        pl.when(step == 0)(functools.partial(assemble, left, lefts))
    if nrights == 1:
        right = rights[0]
    elif not by_rows:
        assemble(right, rights)
    else:

        @pl.when(step == 0)
        def _():
            at, loads = 0, []
            for ref in rights:
                place = right.at[pl.ds(at, ref.shape[0])]
                loads.append(pltpu.make_async_copy(ref, place, arrived.at[len(loads)]))
                loads[-1].start()
                at += ref.shape[0]
            for load in loads:
                load.wait()

    total = lax.dot_general(left[...], right[...], (((0,), (0,)), ((), ())), preferred_element_type=f32)
    if not exchange:
        out[...] = total.astype(bf16)
        return

    def copy(at):
        return remote(sent.at[at], got.at[at], send, recv, at, other_core())

    for at in range(2):

        @pl.when(step == at)
        def _(at=at):
            sent[at] = total.astype(bf16)
            copy(at).start()

    for at, target in ((0, first), (1, second)):

        @pl.when(step == 2 + at)
        def _(at=at, target=target):
            copy(at).wait_recv()
            target[...] = (total + got[at].astype(f32)).astype(bf16)
            copy(at).wait_send()


def join_kernel(npieces, by_rows, ways, *refs):
    pieces, outs = refs[:npieces], refs[npieces : npieces + ways]
    held, wide = refs[npieces + ways : 2 * npieces + ways], refs[2 * npieces + ways : 3 * npieces + ways]
    arrive, leave = refs[-2:]
    half = npieces // 2
    core = core_index()
    loads = [pltpu.make_async_copy(piece, vmem, arrive.at[at]) for at, (piece, vmem) in enumerate(zip(pieces, held))]
    for load in loads:
        load.start()
    stores, start = [], 0

    def store(source, target):
        stores.append(pltpu.make_async_copy(source, target, leave.at[len(stores)]))
        stores[-1].start()

    span = sum(piece.shape[0] for piece in pieces[:half])
    for at, (load, vmem, big) in enumerate(zip(loads, held, wide)):
        start = 0 if at == half else start
        mine = core if at < half else 1 - core
        load.wait()
        big[...] = vmem[...].astype(f32)
        if by_rows:
            place = pl.ds(pl.multiple_of(mine * span + start, 16), vmem.shape[0])
            start += vmem.shape[0]
            for way, out in enumerate(outs):
                store(big.at[:, pl.ds(way * out.shape[1], out.shape[1])], out.at[place, :])
        else:
            rows, columns = outs[0].shape[0], vmem.shape[1]
            for block in range(2):
                place = pl.ds(pl.multiple_of((mine * 2 + block) * columns, LANES), columns)
                store(big.at[pl.ds(block * rows, rows), :], outs[0].at[:, place])
    for store in stores:
        store.wait()


ANY = pl.BlockSpec(memory_space=pl.ANY)
PARAMS = pltpu.CompilerParams(vmem_limit_bytes=VMEM_BYTES)
MESH = pl.DeviceIdType.MESH


def flip(index, mask, size):
    total, bit = 0, 1
    while bit < size:
        total = total + ((index // bit + mask // bit) % 2) * bit
        bit *= 2
    return total


def neighbours():
    me = lax.axis_index("mp")
    return {"mp": flip(me, 1, 4)}, {"mp": flip(me, 2, 4)}


def other_core():
    return {"dp": flip(lax.axis_index("dp"), 1, 8)}


def remote(source, target, send, recv, at, device):
    return pltpu.make_async_remote_copy(
        src_ref=source,
        dst_ref=target,
        send_sem=send.at[at],
        recv_sem=recv.at[at],
        device_id=device,
        device_id_type=MESH,
    )


class GatherHost:
    def __init__(self, shard):
        rows, model = shard.shape
        self.operands = [shard]
        self.outputs = [jax.ShapeDtypeStruct((count, model), bf16) for count in (rows, rows, rows // 2, rows // 2)]
        self.scratch = [pltpu.SemaphoreType.DMA((6,)), pltpu.SemaphoreType.DMA((6,))]

    def copies(self, ins, outs, scratch):
        (shard,), (by_x, by_y, far_a, far_b), (send, recv) = ins, outs, scratch
        half = far_a.shape[0]
        low, high = pl.ds(0, half), pl.ds(half, half)
        x, y = neighbours()
        return (
            lambda: remote(shard.at[low], by_x.at[low], send, recv, 0, x),
            lambda: remote(shard.at[high], by_y.at[high], send, recv, 1, y),
            lambda: remote(shard.at[high], by_x.at[high], send, recv, 2, x),
            lambda: remote(shard.at[low], by_y.at[low], send, recv, 3, y),
            lambda: remote(by_x.at[low], far_a, send, recv, 4, y),
            lambda: remote(by_y.at[high], far_b, send, recv, 5, x),
        )

    def begin(self, *refs):
        for copy in self.copies(*refs)[:4]:
            copy().start()

    def middle(self, *refs):
        copies = self.copies(*refs)
        copies[0]().wait_recv()
        copies[1]().wait_recv()
        copies[4]().start()
        copies[5]().start()

    def end(self, *refs):
        copies = self.copies(*refs)
        copies[0]().wait_send()
        copies[1]().wait_send()
        for at in (2, 3, 4, 5):
            copies[at]().wait()

    def devices(self):
        return neighbours()

    def result(self, outs):
        return (self.operands[0],) + tuple(outs)


class ScatterHost:
    def __init__(self, parts):
        rows, model = parts[1].shape
        half = rows // 2
        self.first = parts[0]
        self.operands = list(parts[1:])
        self.outputs = [jax.ShapeDtypeStruct((rows, model), bf16)] * 2
        self.scratch = [pltpu.VMEM((half, model), bf16)] * 4 + [pltpu.SemaphoreType.DMA((6,))] * 2
        self.scratch += [pltpu.SemaphoreType.DMA((2,))]

    def copies(self, ins, outs, scratch):
        (one, two, far_a, far_b), (from_x, from_y) = ins, outs
        got_x, got_y, own_x, own_y, send, recv, local = scratch
        half = far_a.shape[0]
        low, high = pl.ds(0, half), pl.ds(half, half)
        x, y = neighbours()
        return (
            lambda: remote(far_a, got_x, send, recv, 0, x),
            lambda: remote(far_b, got_y, send, recv, 1, y),
            lambda: remote(one.at[low], from_x.at[low], send, recv, 2, x),
            lambda: remote(two.at[high], from_y.at[high], send, recv, 3, y),
            lambda: remote(own_x, from_x.at[high], send, recv, 4, x),
            lambda: remote(own_y, from_y.at[low], send, recv, 5, y),
            lambda: pltpu.make_async_copy(one.at[high], own_x, local.at[0]),
            lambda: pltpu.make_async_copy(two.at[low], own_y, local.at[1]),
        )

    def begin(self, *refs):
        copies = self.copies(*refs)
        for at in (0, 1, 2, 3, 6, 7):
            copies[at]().start()

    def middle(self, ins, outs, scratch):
        copies = self.copies(ins, outs, scratch)
        got_x, got_y, own_x, own_y = scratch[:4]
        copies[6]().wait()
        copies[7]().wait()
        copies[0]().wait_recv()
        copies[1]().wait_recv()
        own_x[...] = (own_x[...].astype(f32) + got_y[...].astype(f32)).astype(bf16)
        own_y[...] = (own_y[...].astype(f32) + got_x[...].astype(f32)).astype(bf16)
        copies[4]().start()
        copies[5]().start()

    def end(self, *refs):
        copies = self.copies(*refs)
        copies[0]().wait_send()
        copies[1]().wait_send()
        for at in (2, 3, 4, 5):
            copies[at]().wait()

    def devices(self):
        return neighbours()

    def result(self, outs):
        return self.first.astype(f32) + outs[0].astype(f32) + outs[1].astype(f32)


def chip_partners():
    dp = lax.axis_index("dp")
    return {"dp": flip(dp, 2, 8)}, {"dp": (3 - dp // 2) * 2 + dp % 2}


def chip_is_inner():
    return (lax.axis_index("dp") // 2 + 1) // 2 % 2 == 1


class PipeHost:
    def __init__(self, pieces):
        self.pieces = pieces
        self.names = [piece[0] for piece in pieces]
        self.operands = [piece[1] for piece in pieces]
        self.outputs = [jax.ShapeDtypeStruct((piece[3], piece[1].shape[1]), bf16) for piece in pieces]
        self.scratch = []
        for (_, _, _, _, stage, hops, _), out in zip(pieces, self.outputs):
            self.scratch += [pltpu.VMEM(out.shape, bf16)] * (1 + min(hops, 2 - stage))
        self.scratch += [pltpu.SemaphoreType.DMA((len(pieces),))] * 6

    def devices(self):
        return chip_partners()

    def parts(self, ins, outs, scratch):
        pair, mirror = chip_partners()
        send, recv, send_on, recv_on, local, back = scratch[-6:]
        given = 0
        for at, ((_, _, start, count, stage, hops, slot), array, out) in enumerate(zip(self.pieces, ins, outs)):
            many = 1 + min(hops, 2 - stage)
            buffers = list(scratch[given : given + many])
            given += many
            source = array.at[pl.ds(start, count)]

            def hop(number, at=at, stage=stage, source=source, buffers=buffers, out=out):
                way = stage + number
                target = out if way == 2 else buffers[number + 1]
                sems = (send, recv) if number == 0 else (send_on, recv_on)
                return remote(source if number == 0 else buffers[number], target, *sems, at, mirror if way == 1 else pair)

            def load(at=at, source=source, buffers=buffers):
                return pltpu.make_async_copy(source, buffers[0], local.at[at])

            def keep(at=at, buffers=buffers, out=out):
                return pltpu.make_async_copy(buffers[-1], out, back.at[at])

            yield stage, hops, slot, buffers, hop, load, keep

    def add(self, target, other):
        target[...] = (target[...].astype(f32) + other[...].astype(f32)).astype(bf16)

    def begin(self, *refs):
        inner = chip_is_inner()
        for stage, _, _, _, hop, load, _ in self.parts(*refs):

            @pl.when(inner)
            def _(stage=stage, hop=hop, load=load):
                load().start()
                if stage > 0:
                    hop(0).start()

            if stage == 0:

                @pl.when(jnp.logical_not(inner))
                def _(hop=hop):
                    hop(0).start()

    def middle(self, at, *refs):
        inner = chip_is_inner()
        for stage, hops, slot, buffers, hop, load, keep in self.parts(*refs):
            if slot == at:

                @pl.when(inner)
                def _(stage=stage, hops=hops, buffers=buffers, hop=hop, load=load, keep=keep):
                    load().wait()
                    if hops == 2:
                        hop(0).wait_recv()
                        self.add(buffers[1], buffers[0])
                        hop(1).start()
                    if stage + hops == 3:
                        keep().start()

    def slots(self):
        return sorted(set(piece[6] for piece in self.pieces) - {END, None})

    def end(self, *refs):
        inner = chip_is_inner()
        self.middle(END, *refs)
        parts = list(self.parts(*refs))
        for stage, hops, slot, buffers, hop, load, keep in parts:

            @pl.when(inner)
            def _(stage=stage, hops=hops, slot=slot, buffers=buffers, hop=hop, load=load, keep=keep):
                if slot is None:
                    load().wait()
                if stage > 0:
                    hop(0).wait_send()
                if hops == 2:
                    hop(1).wait_send()
                if stage + hops < 3:
                    hop(hops - 1).wait_recv()
                    self.add(buffers[-1], buffers[-2])
                    keep().start()

            @pl.when(jnp.logical_not(inner))
            def _(stage=stage, hops=hops, hop=hop):
                if stage == 0:
                    hop(0).wait_send()
                if stage + hops == 3:
                    hop(hops - 1).wait_recv()

        for _, _, _, _, _, _, keep in parts:

            @pl.when(inner)
            def _(keep=keep):
                keep().wait()

    def result(self, outs):
        return dict(zip(self.names, outs))


class Tail:
    def __init__(self, chunks):
        self.chunks = chunks
        self.pieces = []
        for at, (shape, stage, _, _) in enumerate(chunks):
            rows = shape[0]
            parts = 1 if stage == 2 or rows < 64 else 2 if rows < 256 else 4
            size = -(-rows // parts // 16) * 16
            self.pieces += [(at, start, min(size, rows - start)) for start in range(0, rows, size)]
        self.scratch = []
        for shape, stage, late, _ in chunks:
            self.scratch += [pltpu.VMEM(shape, bf16)] * (3 - stage - (1 if late else 0))
        self.scratch += [pltpu.SemaphoreType.DMA((len(self.pieces),))] * 8

    def setup(self, refs, outs, scratch):
        pair, mirror = chip_partners()
        p_send, p_recv, q_send, q_recv, f_send, f_recv, local, back = scratch[-8:]
        buffers, given = [], 0
        for ref, (_, stage, late, _) in zip(refs, self.chunks):
            count = 3 - stage - (1 if late else 0)
            mine = ([ref] if late else []) + list(scratch[given : given + count])
            given += count
            buffers.append(mine if stage == 0 else [mine[0], None, mine[-1]])

        def transfers(number):
            at, start, count = self.pieces[number]
            rows = pl.ds(start, count)
            own, from_pair, from_mirror = buffers[at]
            early = self.chunks[at][1]
            source, out = refs[at].at[rows], outs[at].at[rows]
            sent = source if early == 1 else own.at[rows]
            done = own if early == 2 else from_mirror
            given_out = source if early == 2 else done.at[rows]
            return {
                "inward": lambda: remote(source, from_pair.at[rows], p_send, p_recv, number, pair),
                "load": lambda: pltpu.make_async_copy(source, own.at[rows], local.at[number]),
                "between": lambda: remote(sent, from_mirror.at[rows], q_send, q_recv, number, mirror),
                "outward": lambda: remote(given_out, out, f_send, f_recv, number, pair),
                "keep": lambda: pltpu.make_async_copy(done.at[rows], out, back.at[number]),
            }

        self.buffers = buffers
        self.moves = [transfers(number) for number in range(len(self.pieces))]
        self.stages = [self.chunks[at][1] for at, _, _ in self.pieces]
        self.late = [self.chunks[at][2] for at, _, _ in self.pieces]
        self.out = [self.chunks[at][3] for at, _, _ in self.pieces]
        self.inner = chip_is_inner()

    def start(self):
        @pl.when(self.inner)
        def _():
            for move, stage, late in zip(self.moves, self.stages, self.late):
                if stage == 2:
                    move["outward"]().start()
                if stage == 1:
                    move["between"]().start()
                if not late:
                    move["load"]().start()

        @pl.when(jnp.logical_not(self.inner))
        def _():
            for move, stage, late in zip(self.moves, self.stages, self.late):
                if stage == 0 and not late:
                    move["inward"]().start()

    def add(self, number, target, other):
        _, start, count = self.pieces[number]
        rows = pl.ds(start, count)
        target[rows, :] = (target[rows, :].astype(f32) + other[rows, :].astype(f32)).astype(bf16)

    def finish(self):
        numbers = range(len(self.pieces))

        def on(number):
            self.moves[number]["between"]().wait_recv()
            own, _, other = self.buffers[self.pieces[number][0]]
            self.add(number, other, own)
            if self.out[number]:
                self.moves[number]["outward"]().start()
            self.moves[number]["keep"]().start()

        @pl.when(self.inner)
        def _():
            for number in numbers:
                if not self.late[number]:
                    self.moves[number]["load"]().wait()
                if self.stages[number] == 2:
                    self.moves[number]["keep"]().start()
            waiting = [number for number in numbers if self.stages[number] == 1]
            for number in numbers:
                if self.stages[number] == 0:
                    self.moves[number]["inward"]().wait_recv()
                    own, other, _ = self.buffers[self.pieces[number][0]]
                    self.add(number, own, other)
                    self.moves[number]["between"]().start()
                    waiting.append(number)
                    on(waiting.pop(0))
            for number in waiting:
                on(number)
            for number in numbers:
                if self.stages[number] < 2:
                    self.moves[number]["between"]().wait_send()
                if self.out[number]:
                    self.moves[number]["outward"]().wait_send()
                self.moves[number]["keep"]().wait()

        @pl.when(jnp.logical_not(self.inner))
        def _():
            for number in numbers:
                if self.stages[number] == 0 and self.late[number]:
                    self.moves[number]["inward"]().start()
            for number in numbers:
                if self.stages[number] == 0:
                    self.moves[number]["inward"]().wait_send()
                if self.out[number]:
                    self.moves[number]["outward"]().wait_recv()


def call(
    kernel, grid, ins, outs, scratch, name, us, hosts=(), before=(), aliases=None, middle=0, unique=None, pair=False, chips=False, late=()
):
    nins, nouts, nscratch = len(ins), len(outs), len(scratch)
    steps = math.prod(grid)
    loaded = [at for at, (_, spec) in enumerate(ins) if spec is WHOLE]

    def body(*refs):
        refs = list(refs)

        def take(count):
            part = refs[:count]
            del refs[:count]
            return part

        own_ins = take(nins)
        host_ins = [take(len(host.operands)) for host in hosts]
        take(len(before))
        own_outs = take(nouts)
        host_outs = [take(len(host.outputs)) for host in hosts]
        own_scratch = take(nscratch)
        host_refs = [(i, o, take(len(host.scratch))) for host, i, o in zip(hosts, host_ins, host_outs)]
        buffers = take(len(loaded))
        step = pl.program_id(0)
        if len(grid) == 2:
            step = step * grid[1] + pl.program_id(1)
        if hosts or pair:

            @pl.when(step == 0)
            def _():
                devices = (other_core(),) if pair else ()
                if any(isinstance(host, (GatherHost, ScatterHost)) for host in hosts):
                    devices += tuple(neighbours())
                between = chips or any(isinstance(host, PipeHost) for host in hosts)
                if between:
                    devices += chip_partners()[:1]
                barrier = pltpu.get_barrier_semaphore()
                for device in devices:
                    pl.semaphore_signal(barrier, inc=1, device_id=device, device_id_type=MESH)
                if between:

                    @pl.when(chip_is_inner())
                    def _():
                        pl.semaphore_signal(barrier, inc=1, device_id=chip_partners()[1], device_id_type=MESH)
                        pl.semaphore_wait(barrier, len(devices) + 1)

                    @pl.when(jnp.logical_not(chip_is_inner()))
                    def _():
                        pl.semaphore_wait(barrier, len(devices))
                else:
                    pl.semaphore_wait(barrier, len(devices))
                for host, there in zip(hosts, host_refs):
                    host.begin(*there)

        if loaded:
            arrived = take(1)[0]
            loads = [(own_ins[at], buffer, arrived.at[k]) for k, (at, buffer) in enumerate(zip(loaded, buffers))]

            second = [load for load, at in zip(loads, loaded) if at in late]
            first = [load for load, at in zip(loads, loaded) if at not in late]

            @pl.when(step == 0)
            def _():
                for load in first + second:
                    pltpu.make_async_copy(*load).start()
                for load in first:
                    pltpu.make_async_copy(*load).wait()

            for at, buffer in zip(loaded, buffers):
                own_ins[at] = buffer
        if hosts:

            for host, there in list(zip(hosts, host_refs))[::-1]:
                if late and not isinstance(host, PipeHost):
                    continue
                for at in host.slots() if isinstance(host, PipeHost) else (middle,):

                    @pl.when(step == at)
                    def _(host=host, there=there, at=at):
                        host.middle(*((at,) if isinstance(host, PipeHost) else ()), *there)

        def wait_late():
            @pl.when(step == 0)
            def _():
                for load in second:
                    pltpu.make_async_copy(*load).wait()

            for host, there in zip(hosts, host_refs):
                if not isinstance(host, PipeHost):

                    @pl.when(step == middle)
                    def _(host=host, there=there):
                        host.middle(*there)

        kernel(*([wait_late] if late else []), *own_ins, *own_outs, *own_scratch)
        if hosts:

            @pl.when(step == steps - 1)
            def _():
                for host, there in zip(hosts, host_refs):
                    host.end(*there)

    host_operands = [v for host in hosts for v in host.operands]
    host_outputs = [v for host in hosts for v in host.outputs]
    params = pltpu.CompilerParams(vmem_limit_bytes=VMEM_BYTES)
    if hosts or pair:
        params = pltpu.CompilerParams(vmem_limit_bytes=VMEM_BYTES, collective_id=unique, has_side_effects=True)
    results = pl.pallas_call(
        body,
        out_shape=tuple(shape for shape, _ in outs) + tuple(host_outputs),
        grid=grid,
        in_specs=[ANY if spec is WHOLE else spec for _, spec in ins] + [ANY] * (len(host_operands) + len(before)),
        out_specs=tuple(spec for _, spec in outs) + (ANY,) * len(host_outputs),
        scratch_shapes=list(scratch)
        + [v for host in hosts for v in host.scratch]
        + [pltpu.VMEM(ins[at][0].shape, ins[at][0].dtype) for at in loaded]
        + ([pltpu.SemaphoreType.DMA((len(loaded),))] if loaded else []),
        input_output_aliases=aliases or {},
        compiler_params=params,
        cost_estimate=cost(us),
        name=name,
    )(*[array for array, _ in ins], *host_operands, *before)
    own, rest = results[:nouts], results[nouts:]
    found = []
    for host in hosts:
        found.append(host.result(rest[: len(host.outputs)]))
        rest = rest[len(host.outputs) :]
    return own, found


def cost(us):
    return pl.CostEstimate(flops=int(us * COST_SCALE * 1.15e9), bytes_accessed=1 << 16, transcendentals=0)


WHOLE = "whole"
END = 99


def whole(array):
    return WHOLE


def layout_of(blocks, rows):
    if blocks != 4:
        return tuple((r, 0, rows) for r in range(blocks))
    return ((0, 0, rows), (1, 0, rows), (2, 0, rows), (3, 0, rows // 2), (3, rows // 2, rows - rows // 2))


def piece_outputs(layout, model):
    shapes = tuple(jax.ShapeDtypeStruct((count, model), bf16) for _, _, count in layout)
    specs = tuple(pl.BlockSpec(shape.shape, lambda *_: (0, 0)) for shape in shapes)
    return shapes, specs


def rec_forward(length, x, params, **more):
    blocks, (rows, model) = lax.axis_size("mp"), x[0].shape
    layout = layout_of(blocks, rows)
    width = params[0].shape[1] // 2

    def at(step):
        return (flip(step, lax.axis_index("mp"), blocks), 0, 0)

    wide = pl.BlockSpec((1, rows, width), at)
    out = jax.ShapeDtypeStruct((blocks, rows, width), f32)
    low = jax.ShapeDtypeStruct((blocks, rows, width), bf16)
    shapes, specs = piece_outputs(layout, model)
    final = (jax.ShapeDtypeStruct((SUB, width), f32), pl.BlockSpec((SUB, width), lambda step: (0, 0)))
    return call(
        functools.partial(rec_forward_kernel, layout),
        (blocks,),
        [(v, whole(v)) for v in (length,) + tuple(x) + tuple(params)],
        [(shape, wide) for shape in (low, out, out, out, out, low, out, out, out)] + [final] + list(zip(shapes, specs)),
        [
            pltpu.VMEM((rows, 2 * width), f32),
            pltpu.VMEM((SUB, width), f32),
            pltpu.VMEM((SUB, width), f32),
            pltpu.VMEM((rows, model), bf16),
            pltpu.VMEM((rows, width), f32),
        ],
        "rec_forward",
        37,
        late=tuple(1 + len(x) + at for at in (3, 7)),
        **more,
    )


def rec_backward(length, seq, count, d_resid, x, params, saved, shared, **more):
    blocks, (rows, model) = lax.axis_size("mp"), x[0].shape
    layout = layout_of(blocks, rows)
    width = saved[0].shape[2]

    def at(step):
        return (flip(blocks - 1 - step, lax.axis_index("mp"), blocks), 0, 0)

    def placed(step):
        return (seq * blocks + flip(blocks - 1 - step, lax.axis_index("mp"), blocks), 0, 0)

    wide = pl.BlockSpec((1, rows, width), at)
    double = pl.BlockSpec((1, rows, 2 * width), placed)
    low = jax.ShapeDtypeStruct((count * blocks, rows, 2 * width), bf16)
    shapes, specs = piece_outputs(layout, model)
    sums = (jax.ShapeDtypeStruct((8, SUB, width), f32), pl.BlockSpec((8, SUB, width), lambda step: (0, 0, 0)))
    gain_sums = (jax.ShapeDtypeStruct((SUB, model), f32), pl.BlockSpec((SUB, model), lambda step: (0, 0)))
    inputs = [(v, whole(v)) for v in (length,) + tuple(d_resid) + tuple(x) + tuple(params)]
    before_x, before_params = 1 + len(d_resid), 1 + len(d_resid) + len(x)
    late = tuple(range(before_x, before_params)) + tuple(before_params + at for at in (1, 2, 3))
    inputs += [(v, wide) for v in saved] + [(v, ANY) for v in shared]
    return call(
        functools.partial(rec_backward_kernel, layout, len(shared)),
        (blocks,),
        inputs,
        [(low, double), (low, double), sums, gain_sums] + list(zip(shapes, specs)),
        [
            pltpu.VMEM((rows, width), f32),
            pltpu.VMEM((rows, width), f32),
            pltpu.VMEM((SUB, width), f32),
            pltpu.VMEM((SUB, width), f32),
            pltpu.VMEM((rows, model), bf16),
            pltpu.VMEM((rows, model), bf16),
        ],
        "rec_backward",
        43,
        aliases={len(inputs) - len(shared) + at: at for at in range(len(shared))},
        late=late,
        **more,
    )


def largest_tile(total, limit, unit=LANES):
    return max(t for t in range(unit, limit + 1, unit) if total % t == 0)


def mlp_forward(seq, count, x, w_gate, w_up, w_down, shared, **more):
    blocks, (rows, model) = lax.axis_size("mp"), x[0].shape
    units = w_gate.shape[1]
    low = jax.ShapeDtypeStruct((count * blocks, rows, units), bf16)
    part = pl.BlockSpec((1, rows, units), lambda r: (seq * blocks + r, 0, 0))
    long = pl.BlockSpec((1, rows, model), lambda r: (flip(r, lax.axis_index("mp"), blocks), 0, 0))
    inputs = [(v, whole(v)) for v in tuple(x) + (w_gate, w_up, w_down)] + [(v, ANY) for v in shared]
    return call(
        functools.partial(mlp_forward_kernel, layout_of(blocks, rows)),
        (blocks,),
        inputs,
        [(low, part)] * 3 + [(jax.ShapeDtypeStruct((blocks, rows, model), bf16), long)],
        [pltpu.VMEM((rows, model), bf16)],
        "mlp_forward",
        30,
        aliases={len(inputs) - len(shared) + at: at for at in range(len(shared))},
        **more,
    )


def mlp_backward(seq, count, cot, gate, up, w_gate, w_up, w_down, shared, **more):
    blocks, (rows, model) = lax.axis_size("mp"), cot[0].shape
    layout = layout_of(blocks, rows)
    units = w_gate.shape[1]
    low = jax.ShapeDtypeStruct((count * blocks, rows, units), bf16)
    part = pl.BlockSpec((1, rows, units), lambda r: (seq * blocks + r, 0, 0))
    shapes, specs = piece_outputs(layout, model)
    inputs = [(v, whole(v)) for v in cot] + [(gate, part), (up, part)]
    inputs += [(v, whole(v)) for v in (w_gate, w_up, w_down)] + [(v, ANY) for v in shared]
    return call(
        functools.partial(mlp_backward_kernel, layout),
        (blocks,),
        inputs,
        [(low, part)] * 2 + list(zip(shapes, specs)),
        [pltpu.VMEM((rows, model), bf16)] * 2,
        "mlp_backward",
        32,
        aliases={len(inputs) - len(shared) + at: at for at in range(len(shared))},
        **more,
    )


def flat(array):
    return array.reshape(-1, array.shape[-1])


def core_index():
    return lax.axis_index("dp") % 2 if lax.axis_size("dp") == 8 else 0


def weight_grad(lefts, rights, by_rows=True, **more):
    lefts, rights = [flat(v) for v in lefts], [flat(v) for v in rights]
    rows, columns = lefts[0].shape[1], rights[0].shape[1]
    tokens = sum(v.shape[0] for v in lefts)
    exchange = lax.axis_size("dp") == 8
    tiled = rows if by_rows else columns
    tile = tiled // 4 if exchange else largest_tile(tiled, 512)

    def place(step):
        if not exchange:
            return step
        return (core_index() + 1 + step // 2) % 2 * 2 + step % 2

    def cut(array, in_tiles):
        if not in_tiles:
            return whole(array)
        return pl.BlockSpec((array.shape[0], tile), lambda step: (0, place(step)))

    scratch = [
        pltpu.VMEM((tokens if len(lefts) > 1 else 16, tile if by_rows else rows), bf16),
        pltpu.VMEM((tokens if len(rights) > 1 else 16, columns if by_rows else tile), bf16),
    ]
    block = (tile, columns) if by_rows else (rows, tile)
    if exchange:
        outs = [(jax.ShapeDtypeStruct(block, bf16), pl.BlockSpec(block, lambda step: (0, 0)))] * 2
        scratch += [pltpu.VMEM((2,) + block, bf16)] * 2 + [pltpu.SemaphoreType.DMA((2,))] * 2
        scratch.append(pltpu.SemaphoreType.DMA((len(rights),)))
    else:
        scratch.append(pltpu.SemaphoreType.DMA((len(rights),)))
        whole_out = jax.ShapeDtypeStruct((rows, columns), bf16)
        outs = [(whole_out, pl.BlockSpec(block, lambda step: (step, 0) if by_rows else (0, step)))]
    return call(
        functools.partial(weight_grad_kernel, by_rows, len(lefts), len(rights), exchange),
        (tiled // tile,),
        [(v, cut(v, by_rows)) for v in lefts]
        + [(v, ANY if by_rows and len(rights) > 1 else cut(v, not by_rows)) for v in rights],
        outs,
        scratch,
        "weight_grad",
        20 if columns > 1000 and by_rows else 13,
        pair=exchange,
        **more,
    )


def last_kernel(nlefts, nrights, nchunks, nblocks, nfinals, tail, *refs):
    lefts, refs = refs[:nlefts], refs[nlefts:]
    rights, refs = refs[:nrights], refs[nrights:]
    convs, refs = refs[:nlefts], refs[nlefts:]
    d_gates, sums_a, sums_b, gain_a, gain_b, gain_c, gain_d = refs[:7]
    chunks, refs = refs[7 : 7 + nchunks], refs[7 + nchunks :]
    finals, refs = refs[:nfinals], refs[nfinals:]
    outs, refs = refs[: nchunks + 3], refs[nchunks + 3 :]
    others, scratch = refs[:nfinals], refs[nfinals:]
    pack, gains, both, whole_pack, got_pack, got_gains, left, right, dense, sent, got, send, recv = scratch[:13]
    finals_send, finals_recv = scratch[13:15]
    step = pl.program_id(0)
    tail.setup(list(chunks) + [pack, gains, both], outs, scratch[15:])
    pl.when(step == 0)(tail.start)

    def swap_final(at):
        return remote(finals[at], others[at], finals_send, finals_recv, at, other_core())

    def swap_gains():
        return remote(gains, got_gains, send, recv, 3, other_core())

    @pl.when(step == 0)
    def _():
        one = jnp.sum(gain_a[...] + gain_b[...], axis=0, keepdims=True)
        two = gain_c[...] + gain_d[...]
        row = lax.broadcasted_iota(jnp.int32, (16, one.shape[1]), 0)
        gains[...] = jnp.where(row == 0, one, jnp.where(row == 1, two, 0.0)).astype(bf16)
        swap_gains().start()

    @pl.when(step == 1)
    def _():
        swap_gains().wait()
        gains[...] = (gains[...].astype(f32) + got_gains[...].astype(f32)).astype(bf16)

    def copy(at):
        return remote(sent.at[at], got.at[at], send, recv, at, other_core())

    def pack_copy():
        return remote(whole_pack, got_pack, send, recv, 2, other_core())

    @pl.when(step < 4)
    def _():
        at = 0
        for ref in rights:
            right[at : at + ref.shape[0], :] = ref[...]
            at += ref.shape[0]

    @pl.when(step == 0)
    def _():
        at = 0
        for ref in lefts:
            left[at : at + ref.shape[0], :] = ref[...]
            at += ref.shape[0]

    for at in range(4):

        @pl.when(step == at)
        def _(at=at):
            total = lax.dot_general(left[...], right[...], (((0,), (0,)), ((), ())), preferred_element_type=f32)
            if at < 2:
                sent[at] = total.astype(bf16)
                copy(at).start()
            else:
                copy(at - 2).wait_recv()
                rows = total.shape[0]
                both[(at - 2) * rows : (at - 1) * rows, :] = (total + got[at - 2].astype(f32)).astype(bf16)
                copy(at - 2).wait_send()

    @pl.when(step == 3)
    def _():
        at = 0
        for ref in convs:
            rows = ref.shape[0]
            term = lax.dot_general(
                ref[...], d_gates[at : at + rows, :], (((0,), (0,)), ((), ())), preferred_element_type=f32
            )
            dense[...] = term if at == 0 else dense[...] + term
            at += rows
        width = dense.shape[0]
        inner = width // nblocks
        lane = lax.broadcasted_iota(jnp.int32, (inner, width), 1)
        for gate in range(2):
            total = jnp.zeros((inner, width), f32)
            for n in range(nblocks):
                here = (lane >= n * inner) & (lane < (n + 1) * inner)
                block = dense[n * inner : (n + 1) * inner, gate * width : (gate + 1) * width]
                total = total + jnp.where(here, block, 0.0)
            whole_pack[gate * inner : (gate + 1) * inner, :] = total.astype(bf16)
        vectors = jnp.sum(sums_a[...] + sums_b[...], axis=1)
        rest = whole_pack.shape[0] - 2 * inner
        vectors = jnp.concatenate([vectors, jnp.zeros((rest - 8, width), f32)], axis=0)
        whole_pack[2 * inner :, :] = vectors.astype(bf16)
        pack_copy().start()

    @pl.when(step == 4)
    def _():
        pack_copy().wait()
        for at in range(nfinals):
            swap_final(at).start()
        mine = pl.ds(pl.multiple_of(core_index() * pack.shape[0], 16), pack.shape[0])
        pack[...] = (whole_pack[mine, :].astype(f32) + got_pack[mine, :].astype(f32)).astype(bf16)
        tail.finish()
        for at in range(nfinals):
            swap_final(at).wait()


def last_grad(lefts, rights, convs, d_gates, vectors, moving, finals, nblocks, **more):
    lefts, rights, convs = ([flat(v) for v in group] for group in (lefts, rights, convs))
    rows, columns = lefts[0].shape[1], rights[0].shape[1]
    tokens = sum(v.shape[0] for v in lefts)
    tile = columns // 4

    def place(step):
        step = step - step // 4
        return (core_index() + 1 + step // 2) % 2 * 2 + step % 2

    chunks = [(chunk, stage) for stage, group in enumerate(moving) for _, chunk in group.items()]
    names = [name for group in moving for name in group]
    block = (rows, tile)
    packed = -(-(2 * rows // nblocks + 16) // 32) * 32
    made = [((packed // 2, rows), True), ((16, columns), True), ((2 * rows, tile), False)]
    tail = Tail(
        [(chunk.shape, stage, False, True) for chunk, stage in chunks] + [(shape, 0, True, out) for shape, out in made]
    )
    outs = [jax.ShapeDtypeStruct(chunk[0], bf16) for chunk in tail.chunks]
    out, found = call(
        functools.partial(last_kernel, len(lefts), len(rights), len(chunks), nblocks, len(finals), tail),
        (5,),
        [(v, whole(v)) for v in lefts]
        + [(v, pl.BlockSpec((v.shape[0], tile), lambda step: (0, place(step)))) for v in rights]
        + [(v, whole(v)) for v in convs + [flat(d_gates)] + list(vectors)]
        + [(chunk, ANY) for chunk, _ in chunks]
        + [(piece, ANY) for piece in finals.values()],
        [(shape, ANY) for shape in outs]
        + [(jax.ShapeDtypeStruct(piece.shape, bf16), ANY) for piece in finals.values()],
        [pltpu.VMEM(shape, bf16) for shape, _ in made]
        + [
            pltpu.VMEM((packed, rows), bf16),
            pltpu.VMEM((packed, rows), bf16),
            pltpu.VMEM((16, columns), bf16),
            pltpu.VMEM((tokens, rows), bf16),
            pltpu.VMEM((tokens, tile), bf16),
            pltpu.VMEM((rows, 2 * rows), f32),
            pltpu.VMEM((2,) + block, bf16),
            pltpu.VMEM((2,) + block, bf16),
            pltpu.SemaphoreType.DMA((4,)),
            pltpu.SemaphoreType.DMA((4,)),
            pltpu.SemaphoreType.DMA((len(finals),)),
            pltpu.SemaphoreType.DMA((len(finals),)),
        ]
        + tail.scratch,
        "last_grad",
        120,
        pair=True,
        chips=True,
        **more,
    )
    names += ["pack", "gains", "out"]
    return dict(zip(names, out)), dict(zip(finals, out[len(names) :])), found


def join_pieces(pieces, by_rows, ways):
    rows, columns = sum(v.shape[0] for v in pieces), pieces[0].shape[1]
    shape = (rows, columns // ways) if by_rows else (rows // 4, 4 * columns)
    out = (jax.ShapeDtypeStruct(shape, f32), ANY)
    return call(
        functools.partial(join_kernel, len(pieces), by_rows, ways),
        (1,),
        [(piece, ANY) for piece in pieces],
        [out] * ways,
        [pltpu.VMEM(piece.shape, bf16) for piece in pieces]
        + [pltpu.VMEM(piece.shape, f32) for piece in pieces]
        + [pltpu.SemaphoreType.DMA((len(pieces),)), pltpu.SemaphoreType.DMA((len(pieces) * max(2, ways),))],
        "join_pieces",
        0.05,
    )[0]


def swap(value, axis, bit):
    size = lax.axis_size(axis)
    return lax.ppermute(value, axis, [(i, i ^ bit) for i in range(size)])


def gather(shard):
    size = lax.axis_size("mp")
    if size != 4:
        return (shard,) + tuple(swap(shard, "mp", r) for r in range(1, size))
    half = shard.shape[0] // 2
    by_x = swap(shard, "mp", 1)
    by_y = swap(shard, "mp", 2)
    return (shard, by_x, by_y, swap(by_x[:half], "mp", 2), swap(by_y[half:], "mp", 1))


def scatter(parts):
    size = lax.axis_size("mp")
    if size != 4:
        total = parts[0].astype(f32)
        for r in range(1, size):
            total = total + swap(parts[r], "mp", r).astype(f32)
        return total
    half = parts[3].shape[0]
    from_x = swap(parts[3], "mp", 1)
    from_y = swap(parts[4], "mp", 2)
    for_y = jnp.concatenate([add_low(parts[2][:half], from_x), parts[2][half:]], axis=0)
    for_x = jnp.concatenate([parts[1][:half], add_low(parts[1][half:], from_y)], axis=0)
    return parts[0].astype(f32) + swap(for_y, "mp", 2).astype(f32) + swap(for_x, "mp", 1).astype(f32)


def add_low(left, right):
    return (left.astype(f32) + right.astype(f32)).astype(bf16)


class Pipe:
    def __init__(self):
        self.queue, self.moving, self.done = [], [], {}

    def enter(self, name, quarters):
        self.queue += [[name + str(at), quarter, 0] for at, quarter in enumerate(quarters)]

    def host(self, budget, slots):
        pieces, old = [], list(slots)
        for name, array, stage in self.moving:
            slot = slots[0] if stage == 2 else old.pop(0)
            pieces.append((name, array, 0, array.shape[0], stage, 3 - stage, slot))
        ahead = list(slots)
        while self.queue and budget > 0:
            name, array, start = self.queue[0]
            unit = array.shape[0] // 4
            slot = ahead.pop(0) if ahead else None
            pieces.append((name + "_" + str(start).zfill(4), array, start, unit, 0, 2 if slot else 1, slot))
            budget -= 1
            self.queue[0][2] += unit
            if self.queue[0][2] == array.shape[0]:
                self.queue.pop(0)
        return PipeHost(pieces) if pieces else None

    def took(self, host, results):
        self.moving = []
        for name, _, _, _, stage, hops, _ in host.pieces:
            if stage + hops == 3:
                self.done[name] = results[name]
            else:
                self.moving.append((name, results[name], stage + hops))

    def left(self):
        groups = ({}, {}, {})
        for name, array, stage in self.moving:
            groups[stage][name] = array
        for name, array, start in self.queue:
            groups[0][name + "_" + str(start).zfill(4)] = array[start:]
        return groups


def normalize(values, gain):
    return values * lax.rsqrt(jnp.mean(values * values, axis=-1, keepdims=True) + EPS) * gain


def normalize_back(values, gain, grad):
    inverse = lax.rsqrt(jnp.mean(values * values, axis=-1, keepdims=True) + EPS)
    scaled = grad * gain
    unit = values * inverse
    return inverse * (scaled - unit * jnp.mean(scaled * unit, axis=-1, keepdims=True)), unit


def dense_blocks(weight):
    blocks, inner, outer = weight.shape
    rows = [
        jnp.pad(weight[n], ((0, 0), (n * outer, (blocks - 1 - n) * outer))) for n in range(blocks)
    ]
    return jnp.concatenate(rows, axis=0)


def diagonal_blocks(full, blocks, width):
    inner = width // blocks
    return jnp.stack([full[n * inner : (n + 1) * inner, n * inner : (n + 1) * inner] for n in range(blocks)])


def per_device(
    block_in,
    norm1_gain,
    w_branch,
    w_input,
    conv_weight,
    conv_bias,
    gate_a_weight,
    gate_a_bias,
    gate_i_weight,
    gate_i_bias,
    decay_param,
    w_out,
    norm2_gain,
    w_gate,
    w_up,
    w_down,
    lengths,
    cotangent,
):
    count = block_in.shape[0]
    nblocks = gate_a_weight.shape[0]
    true_width = w_branch.shape[1]
    extra = -true_width % LANES
    me = lax.axis_index("mp")

    def pad_last(value):
        return jnp.pad(value, [(0, 0)] * (value.ndim - 1) + [(0, extra)]) if extra else value

    def line(value):
        return pad_last(value)[None, :]

    wb, wi = pad_last(w_branch), pad_last(w_input)
    wo = jnp.pad(w_out, ((0, extra), (0, 0))) if extra else w_out
    w_ga, w_gi = dense_blocks(gate_a_weight), dense_blocks(gate_i_weight)
    if extra:
        w_ga, w_gi = (jnp.pad(v, ((0, extra), (0, extra))) for v in (w_ga, w_gi))
    taps = pad_last(conv_weight)
    decay_line = line(decay_param)
    w_both = jnp.concatenate([wb, wi], axis=1)
    w_gates = jnp.concatenate([w_ga, w_gi], axis=1)
    forward_params = (
        w_both, taps, line(conv_bias), w_gates, line(gate_a_bias), line(gate_i_bias), decay_line, wo
    )
    backward_params = (wo, w_both, taps, w_gates, decay_line)
    seqs = range(count)
    limits = [jnp.full((SUB, LANES), lengths[s], jnp.int32) for s in seqs]
    blocks = lax.axis_size("mp")
    hosted = blocks == 4 and count == 2
    ids = iter(range(1, 100))

    piped = hosted and lax.axis_size("dp") == 8 and not extra
    pipe = Pipe()

    def enter(name, quarters):
        if piped:
            pipe.enter(name, quarters)

    def tied(value, *deps):
        return lax.optimization_barrier((value,) + deps)[0]

    def run(function, *args, hosts=(), middle=0, budget=4, **more):
        if hosted:
            window = pipe.host(budget, (2, 3) if function is weight_grad else (1, 2)) if piped else None
            out, found = function(
                *args, hosts=list(hosts) + ([window] if window else []), middle=middle, unique=next(ids), **more
            )
            if window:
                pipe.took(window, found[-1])
            return out, found[: len(hosts)]
        out, _ = function(*args, **more)
        return out, [
            gather(host.operands[0]) if isinstance(host, GatherHost) else scatter((host.first, *host.operands))
            for host in hosts
        ]

    resid = [block_in[s].astype(f32) for s in seqs]
    starts = [normalize(resid[s], norm1_gain).astype(bf16) for s in seqs]
    piece, model = starts[0].shape
    seq_in = [gather(starts[0])]
    out, (second,) = run(rec_forward, limits[0], seq_in[0], forward_params, hosts=[GatherHost(starts[1])], middle=1)
    seq_in.append(second)
    forward = [out]
    out, (branch,) = run(
        rec_forward, limits[1], seq_in[1], forward_params, hosts=[ScatterHost(out[10:])], middle=1, before=(out[9],)
    )
    forward.append(out)
    mixed = [out[0] for out in forward]
    saved = [out[1:9] for out in forward]
    finals = [out[9][:1, :true_width] for out in forward]
    resid_mid = [resid[0] + branch]
    mid = normalize(resid_mid[0], norm2_gain).astype(bf16)
    seq_mid = [gather(mid)]
    forward_shared, (branch,) = run(
        mlp_forward, 0, count, seq_mid[0], w_gate, w_up, w_down, (), hosts=[ScatterHost(forward[1][10:])], middle=2
    )
    mlp_part = [forward_shared[3]]
    resid_mid.append(resid[1] + branch)
    mid = normalize(resid_mid[1], norm2_gain).astype(bf16)
    seq_mid.append(gather(mid))
    forward_shared, (found,) = run(
        mlp_forward, 1, count, seq_mid[1], w_gate, w_up, w_down, forward_shared[:3],
        hosts=[GatherHost(cotangent[0])], middle=2,
    )
    mlp_part.append(forward_shared[3])
    cot_seq = [found]
    hidden, gate_low, up_low = forward_shared[:3]
    backward, (found,) = run(
        mlp_backward, 0, count, cot_seq[0], gate_low, up_low, w_gate, w_up, w_down, (),
        hosts=[GatherHost(cotangent[1])], middle=2,
    )
    cot_seq.append(found)

    def middle_grad(s, d_mid):
        back, unit = normalize_back(resid_mid[s], norm2_gain, d_mid)
        return cotangent[s].astype(f32) + back, jnp.sum(d_mid * unit, axis=0, keepdims=True)

    flat_mid = [p for pieces in seq_mid for p in pieces]
    flat_cot = [p for pieces in cot_seq for p in pieces]
    grad_down, _ = run(weight_grad, [hidden], flat_cot)
    enter("down", grad_down)
    backward, (d_mid,) = run(
        mlp_backward, 1, count, cot_seq[1], gate_low, up_low, w_gate, w_up, w_down, backward[:2],
        hosts=[ScatterHost(backward[2:])], middle=2, before=(grad_down[0],),
    )
    d_gate, d_up = backward[:2]
    first, gain2 = middle_grad(0, d_mid)
    grad_gate, (first_seq,) = run(weight_grad, flat_mid, [d_gate], hosts=[GatherHost(first.astype(bf16))], middle=3)
    enter("gate", grad_gate)
    grad_up, (d_mid,) = run(
        weight_grad, flat_mid, [d_up], hosts=[ScatterHost(backward[2:])], middle=2, before=(grad_gate[0],)
    )
    second, more_gain2 = middle_grad(1, d_mid)
    enter("up", grad_up)
    out, (second_seq,) = run(
        rec_backward, limits[0], 0, count, first_seq, seq_in[0], backward_params, saved[0], (),
        hosts=[GatherHost(second.astype(bf16))], middle=1, before=(grad_up[0],), budget=4,
    )
    sums, gain1 = out[2], out[3]
    out, (d_in,) = run(
        rec_backward, limits[1], 1, count, second_seq, seq_in[1], backward_params, saved[1], out[:2],
        hosts=[ScatterHost(out[4:])], middle=1, budget=4,
    )
    d_both, d_gates = out[:2]
    input_grad = [(first + normalize_back(resid[0], norm1_gain, d_in)[0]).astype(bf16)]

    flat_in = [p for pieces in seq_in for p in pieces]
    flat_resid = [p for pieces in (first_seq, second_seq) for p in pieces]
    grad_in, _ = run(weight_grad, flat_in, [d_both])
    conv = [part[4] for part in saved]
    mlp_total = [
        lax.psum_scatter(flat(tied(v, grad_in[0])), "mp", scatter_dimension=0, tiled=True) for v in mlp_part
    ]

    def finish_output(*after):
        totals = lax.optimization_barrier((*mlp_total, *after))[:count]
        return jnp.stack([(resid_mid[s] + totals[s].astype(f32)).astype(bf16) for s in seqs])

    def finish_input(d_in):
        last = (second + normalize_back(resid[1], norm1_gain, d_in)[0]).astype(bf16)
        return jnp.stack(input_grad + [last])

    if piped:

        def join(prefix, by_rows=True, ways=1):
            names = [name for name in sorted(pipe.done) if name.startswith(prefix)]
            mine = [pipe.done[name] for name in names]
            other = [others[name] if name in others else swap(pipe.done[name], "dp", 1) for name in names]
            return join_pieces(mine + other, by_rows, ways)

        moving = pipe.left()
        moving[0].update(in0=grad_in[0], in1=grad_in[1])
        found, others, (d_in,) = last_grad(
            mixed, flat_resid, conv, d_gates, (sums, out[2], gain1, out[3], gain2, more_gain2), moving, dict(pipe.done),
            nblocks,
            hosts=[ScatterHost(out[4:])], middle=4, unique=next(ids), before=(grad_in[0],),
        )
        pipe.done.update({name: found[name] for name in found if name != "out"})
        pairs = [(2 * a + core, 2 * b + core) for a, b in ((1, 0), (2, 3)) for core in range(2)]
        came = lax.ppermute(found["out"], "dp", pairs)
        totals_down, totals_gate, totals_up = (join(name) for name in ("down", "gate", "up"))
        totals_in = join("in", ways=2)
        input_grad = finish_input(d_in)
        came = lax.optimization_barrier((came, totals_down, totals_gate, totals_up, totals_in[0]))[0]
        pipe.done["out"] = jnp.where(chip_is_inner(), found["out"], came)
        block_out = finish_output(pipe.done["out"])
        totals_out = join("out", by_rows=False)
        pack, other = found["pack"].astype(f32), swap(found["pack"], "dp", 1).astype(f32)
        mine = core_index() == 0
        pack = jnp.concatenate([jnp.where(mine, pack, other), jnp.where(mine, other, pack)], axis=0)
        inner = true_width // nblocks
        full_ga, full_gi = (
            jnp.transpose(pack[at * inner : (at + 1) * inner].reshape(inner, nblocks, inner), (1, 0, 2)) for at in range(2)
        )
        vectors = pack[2 * inner : 2 * inner + 8]
        gains = found["gains"][:2].astype(f32)
        for bit in (1, 2):
            gains = gains + swap(gains, "mp", bit)
    else:
        grad_out, _ = run(weight_grad, mixed, flat_resid, False, before=(grad_in[0],))
        input_grad, block_out = finish_input(scatter(out[4:])), finish_output()
        totals_down, totals_gate, totals_up, totals_in, totals_out = (
            jnp.split(lax.psum(v[0], "dp").astype(f32), ways, axis=1)
            for v, ways in ((grad_down, 1), (grad_gate, 1), (grad_up, 1), (grad_in, 2), (grad_out, 1))
        )
        d_gates = d_gates.reshape(count, blocks, piece, -1)
        width = d_gates.shape[-1] // 2
        full = sum(jnp.einsum("rtd,rtc->dc", conv[s], d_gates[s], preferred_element_type=f32) for s in seqs)
        gains = jnp.stack([jnp.sum(gain1 + out[3], axis=0), (gain2 + more_gain2)[0]])
        vectors = jnp.sum(sums + out[2], axis=1)[:, :true_width]
        full_ga, full_gi, vectors, gains = lax.psum(
            (
                diagonal_blocks(full[:, :width], nblocks, true_width).astype(bf16),
                diagonal_blocks(full[:, width:], nblocks, true_width).astype(bf16),
                vectors.astype(bf16),
                lax.psum(gains, "mp").astype(bf16),
            ),
            "dp",
        )
    grad_gate_a_weight, grad_gate_i_weight, vectors, gains = (
        v.astype(f32) for v in (full_ga, full_gi, vectors, gains)
    )
    gains = jnp.stack([gains[0] / norm1_gain, gains[1]])
    vectors = jnp.concatenate(
        [(vectors[0] * DECAY_EXP * jax.nn.sigmoid(-decay_param))[None, :], vectors[1:]], axis=0
    )
    grad_w_out = totals_out[0][:true_width]
    grad_w_branch, grad_w_input = (v[:, :true_width] for v in totals_in)
    return (
        block_out,
        input_grad,
        gains[0],
        grad_w_branch,
        grad_w_input,
        vectors[4:8],
        vectors[3],
        grad_gate_a_weight,
        vectors[1],
        grad_gate_i_weight,
        vectors[2],
        vectors[0],
        grad_w_out,
        gains[1],
        totals_gate[0],
        totals_up[0],
        totals_down[0],
        jnp.concatenate(finals, axis=0),
    )


def solution(mesh):
    placed = (
        P("dp", "mp", None),
        P(),
        P(None, "mp"),
        P(None, "mp"),
        P(None, "mp"),
        P("mp"),
        P("mp", None, None),
        P("mp"),
        P("mp", None, None),
        P("mp"),
        P("mp"),
        P("mp", None),
        P(),
        P(None, "mp"),
        P(None, "mp"),
        P("mp", None),
        P("dp"),
        P("dp", "mp", None),
    )
    return jax.shard_map(
        per_device,
        mesh=mesh,
        in_specs=placed,
        out_specs=(
            P("dp", "mp", None),
            P("dp", "mp", None),
            P(),
            P(None, "mp"),
            P(None, "mp"),
            P(None, "mp"),
            P("mp"),
            P("mp", None, None),
            P("mp"),
            P("mp", None, None),
            P("mp"),
            P("mp"),
            P("mp", None),
            P(),
            P(None, "mp"),
            P(None, "mp"),
            P("mp", None),
            P("dp", "mp"),
        ),
        check_vma=False,
    )
```

```python
import functools
import math

import jax
import jax.numpy as jnp
from jax import lax
from jax.experimental import pallas as pl
from jax.experimental.pallas import tpu as pltpu
from jax.sharding import PartitionSpec as P

DECAY_EXP = 8.0
EPS = 1e-06
GELU_C = math.sqrt(2.0 / math.pi)
GELU_K = 0.044715
LANES = 128
SUB = 8
UNIT_TILE = 256
COST_SCALE = 0.5
MODEL_TILE = 512
VMEM_BYTES = 56 * 1024 * 1024

f32 = jnp.float32
bf16 = jnp.bfloat16


def dot_nn(left, right):
    return lax.dot_general(left, right, (((1,), (0,)), ((), ())), preferred_element_type=f32)


def dot_nt(left, right):
    return lax.dot_general(left, right, (((1,), (1,)), ((), ())), preferred_element_type=f32)


def one_minus_square(log_a, decay):
    x = 2.0 * log_a
    tail = 1.0 + x * (1.0 / 7.0)
    for k in (6.0, 5.0, 4.0, 3.0, 2.0):
        tail = 1.0 + x * (1.0 / k) * tail
    return jnp.where(x > -0.4, -x * tail, 1.0 - decay * decay)


def gelu_parts(x):
    square = x * x
    th = jnp.tanh(GELU_C * x * (1.0 + GELU_K * square))
    half = 0.5 * (1.0 + th)
    value = x * half
    slope = half + 0.5 * x * (1.0 - th * th) * (GELU_C * (1.0 + 3.0 * GELU_K * square))
    return value, slope


def row_index(shape):
    return lax.broadcasted_iota(jnp.int32, shape, 0)


def shift_down(prev, cur, k, row):
    return jnp.where(row < k, pltpu.roll(prev, k, 0), pltpu.roll(cur, k, 0))


def shift_up(cur, following, k, row):
    return jnp.where(row < SUB - k, pltpu.roll(cur, SUB - k, 0), pltpu.roll(following, SUB - k, 0))


def load_block(pieces, layout, block, target):
    for ref, (owner, start, count) in zip(pieces, layout):

        @pl.when(block == owner)
        def _(ref=ref, start=start, count=count):
            target[pl.ds(start, count), :] = ref[...]


def store_block(pieces, layout, block, column, value):
    for ref, (owner, start, count) in zip(pieces, layout):

        @pl.when(block == owner)
        def _(ref=ref, start=start, count=count):
            ref[:, column] = value[start : start + count]


def rec_forward_kernel(layout, seq, wait_late, length, *refs):
    x_pieces, refs = refs[: len(layout)], refs[len(layout) :]
    w_both, taps, conv_bias, w_gates, ga_bias, gi_bias, decay_param, w_out = refs[:8]
    branch = refs[-1]
    gates_pre, tail, carry, x = refs[-5:-1]
    outs = refs[-5 - 10 - len(layout) : -5]
    mixed, pre, value_out, slope_out, space_out, conv, ga, gi, prev_state, final = outs[:10]
    parts = outs[10:]
    step = pl.program_id(0)
    block = flip(step, lax.axis_index("mp"), 4 if len(layout) == 5 else len(layout))
    rows, width = mixed.shape[1:]
    load_block(x_pieces, layout, block, x)
    pieces = rows // 16
    lanes = [pl.ds(at, LANES) for at in range(0, width, LANES)]
    row = row_index((SUB, LANES))

    @pl.when(step == 0)
    def _():
        tail[...] = jnp.zeros_like(tail)
        carry[...] = jnp.zeros_like(carry)

    both = dot_nn(x[...], w_both[...])
    branch[...] = both[:, :width]
    pre[0] = both[:, width:]

    def conv_piece(i, _):
        base = pl.multiple_of(i * 16, 16)
        for lane in lanes:
            bias = conv_bias[:, lane]
            before = tail[:, lane]
            parts = []
            for half in range(2):
                cur = pre[0, pl.ds(base + SUB * half, SUB), lane]
                total = bias + taps[0:1, lane] * cur
                for k in range(1, 4):
                    total = total + taps[k : k + 1, lane] * shift_down(before, cur, k, row)
                parts.append(total)
                before = cur
            tail[:, lane] = before
            conv[0, pl.ds(base, 16), lane] = jnp.concatenate(parts, axis=0).astype(bf16)
        return 0

    lax.fori_loop(0, pieces, conv_piece, 0)
    wait_late()
    gates_pre[...] = dot_nn(conv[0], w_gates[...])
    limit = length[seq]

    def scan_piece(i, _):
        base = pl.multiple_of(i * 16, 16)
        start = step * rows + base
        for lane in lanes:
            second = pl.ds(width + lane.start, LANES)
            rate = -DECAY_EXP * jax.nn.softplus(-decay_param[:, lane])
            conv_two = conv[0, pl.ds(base, 16), lane].astype(f32)
            state = carry[:, lane]
            outs = []
            for half in range(2):
                at = pl.ds(base + SUB * half, SUB)
                live = (row + (start + SUB * half)) < limit
                gate_a = jax.nn.sigmoid(gates_pre[at, lane] + ga_bias[:, lane])
                gate_i = jax.nn.sigmoid(gates_pre[at, second] + gi_bias[:, lane])
                ga[0, at, lane] = gate_a
                gi[0, at, lane] = gate_i
                log_a = rate * gate_a
                decay = jnp.exp(log_a)
                space = one_minus_square(log_a, decay)
                space_out[0, at, lane] = space
                scaled = jnp.sqrt(space) * gate_i * conv_two[SUB * half : SUB * half + SUB]
                mul = jnp.where(live, decay, 1.0)
                add = jnp.where(live, scaled, 0.0)
                for shift in (1, 2, 4):
                    inside = row >= shift
                    add = add + mul * jnp.where(inside, pltpu.roll(add, shift, 0), 0.0)
                    mul = mul * jnp.where(inside, pltpu.roll(mul, shift, 0), 1.0)
                states = mul * state + add
                prev_state[0, at, lane] = jnp.where(row == 0, state, pltpu.roll(states, 1, 0))
                state = jnp.broadcast_to(states[SUB - 1 : SUB], (SUB, LANES))
                value, slope = gelu_parts(branch[at, lane])
                value_out[0, at, lane] = value
                slope_out[0, at, lane] = slope
                outs.append(states * value)
            carry[:, lane] = state
            mixed[0, pl.ds(base, 16), lane] = jnp.concatenate(outs, axis=0).astype(bf16)
        return 0

    lax.fori_loop(0, pieces, scan_piece, 0)
    final[...] = carry[...]
    for at in range(0, w_out.shape[1], MODEL_TILE):
        column = pl.ds(at, MODEL_TILE)
        x[:, column] = dot_nn(mixed[0], w_out[:, column]).astype(bf16)
    store_block(parts, layout, block, slice(None), x[...])


def rec_backward_kernel(layout, seq, wait_late, length, *refs):
    many = len(layout)
    d_resid_pieces, x_pieces, refs = refs[:many], refs[many : 2 * many], refs[2 * many :]
    w_out, w_both, taps, w_gates, decay_param = refs[:5]
    pre, value_in, slope_in, space_in, conv, ga, gi, prev_state = refs[5:13]
    d_mixed, d_conv, flow, later, x, d_resid = refs[-6:]
    outs = refs[-6 - 4 - many : -6]
    d_both, d_gates, sums, gain_sums = outs[:4]
    parts = outs[4:]
    step = pl.program_id(0)
    rows, width = pre.shape[1:]
    pieces = rows // 16
    lanes = [pl.ds(at, LANES) for at in range(0, width, LANES)]
    row = row_index((SUB, LANES))
    first = (pl.num_programs(0) - 1 - step) * rows
    limit = length[seq]

    @pl.when(step == 0)
    def _():
        flow[...] = jnp.zeros_like(flow)
        later[...] = jnp.zeros_like(later)
        sums[...] = jnp.zeros_like(sums)
        gain_sums[...] = jnp.zeros_like(gain_sums)

    block = flip(pl.num_programs(0) - 1 - step, lax.axis_index("mp"), 4 if len(layout) == 5 else len(layout))
    load_block(d_resid_pieces, layout, block, d_resid)
    d_mixed[...] = dot_nt(d_resid[...], w_out[...])

    def scan_piece(j, _):
        base = pl.multiple_of((pieces - 1 - j) * 16, 16)
        for lane in lanes:
            rate = -DECAY_EXP * jax.nn.softplus(-decay_param[:, lane])
            conv_two = conv[0, pl.ds(base, 16), lane].astype(f32)
            carried = flow[:, lane]
            outs = [None, None]
            sum_log = sums[0, :, lane]
            for half in (1, 0):
                at = pl.ds(base + SUB * half, SUB)
                live = (row + (first + base + SUB * half)) < limit
                conv_val = conv_two[SUB * half : SUB * half + SUB]
                gate_a = ga[0, at, lane]
                gate_i = gi[0, at, lane]
                before = prev_state[0, at, lane]
                d_mix = d_mixed[at, lane]
                log_a = rate * gate_a
                decay = jnp.exp(log_a)
                space = space_in[0, at, lane]
                inverse = lax.rsqrt(jnp.maximum(space, 1e-37))
                root = space * inverse
                gated = gate_i * conv_val
                mul = jnp.where(live, decay, 1.0)
                states = mul * before + jnp.where(live, root * gated, 0.0)
                d_br = d_mix * states * slope_in[0, at, lane]
                direct = d_mix * value_in[0, at, lane]
                add = mul * direct
                for shift in (1, 2, 4):
                    inside = row < SUB - shift
                    add = add + mul * jnp.where(inside, pltpu.roll(add, SUB - shift, 0), 0.0)
                    mul = mul * jnp.where(inside, pltpu.roll(mul, SUB - shift, 0), 1.0)
                moved = add + mul * carried
                d_state = direct + jnp.where(row == SUB - 1, carried, pltpu.roll(moved, SUB - 1, 0))
                carried = jnp.broadcast_to(moved[0:1], (SUB, LANES))
                d_state = jnp.where(live, d_state, 0.0)
                d_log = d_state * decay * (before - gated * decay * inverse)
                sum_log = sum_log + d_log * gate_a
                d_gate_a = d_log * rate * gate_a * (1.0 - gate_a)
                d_rooted = d_state * root
                d_conv_rec = d_rooted * gate_i
                d_gate_i = d_rooted * conv_val * gate_i * (1.0 - gate_i)
                d_conv[at, lane] = d_conv_rec
                outs[half] = (d_br, d_gate_a, d_gate_i)
            flow[:, lane] = carried
            sums[0, :, lane] = sum_log
            second = pl.ds(width + lane.start, LANES)
            for target, there, which in ((d_both, lane, 0), (d_gates, lane, 1), (d_gates, second, 2)):
                both = jnp.concatenate([outs[0][which], outs[1][which]], axis=0).astype(bf16)
                target[0, pl.ds(base, 16), there] = both
                if which > 0:
                    wide = both.astype(f32)
                    sums[which, :, lane] += wide[:SUB] + wide[SUB:]
        return 0

    lax.fori_loop(0, pieces, scan_piece, 0)
    wait_late()
    load_block(x_pieces, layout, block, x)
    d_conv[...] += dot_nt(d_gates[0], w_gates[...])

    def conv_piece(j, _):
        base = pl.multiple_of((pieces - 1 - j) * 16, 16)
        for lane in lanes:
            following = later[:, lane]
            totals = [None, None]
            tap_sums = [sums[3 + k, :, lane] for k in range(5)]
            for half in (1, 0):
                at = pl.ds(base + SUB * half, SUB)
                cur = d_conv[at, lane]
                seen = pre[0, at, lane]
                tap_sums[0] = tap_sums[0] + cur
                tap_sums[1] = tap_sums[1] + cur * seen
                total = taps[0:1, lane] * cur
                for k in range(1, 4):
                    ahead = shift_up(cur, following, k, row)
                    tap_sums[1 + k] = tap_sums[1 + k] + ahead * seen
                    total = total + taps[k : k + 1, lane] * ahead
                totals[half] = total
                following = cur
            later[:, lane] = following
            for k in range(5):
                sums[3 + k, :, lane] = tap_sums[k]
            d_both[0, pl.ds(base, 16), pl.ds(width + lane.start, LANES)] = jnp.concatenate(totals, axis=0).astype(bf16)
        return 0

    lax.fori_loop(0, pieces, conv_piece, 0)
    for at in range(0, x.shape[1], MODEL_TILE):
        column = pl.ds(at, MODEL_TILE)
        part = dot_nt(d_both[0], w_both[column, :])
        seen = part * x[:, column].astype(f32)
        gain_sums[:, column] += jnp.sum(seen.reshape(rows // SUB, SUB, MODEL_TILE), axis=0)
        d_resid[:, column] = part.astype(bf16)
    store_block(parts, layout, block, slice(None), d_resid[...])


def mlp_forward_kernel(layout, *refs):
    many = len(layout)
    x_pieces, (w_gate, w_up, w_down) = refs[:many], refs[many : many + 3]
    hidden, gate, up, mlp_part, x = refs[-5:]
    load_block(x_pieces, layout, pl.program_id(0), x)
    for at in range(0, hidden.shape[2], UNIT_TILE):
        column = pl.ds(at, UNIT_TILE)
        up_pre = dot_nn(x[...], w_up[:, column])
        gate_pre = dot_nn(x[...], w_gate[:, column])
        value, _ = gelu_parts(gate_pre)
        hidden[0, :, column] = (value * up_pre).astype(bf16)
        gate[0, :, column] = gate_pre.astype(bf16)
        up[0, :, column] = up_pre.astype(bf16)
    for at in range(0, x.shape[1], MODEL_TILE):
        column = pl.ds(at, MODEL_TILE)
        mlp_part[0, :, column] = dot_nn(hidden[0], w_down[:, column]).astype(bf16)


def mlp_backward_kernel(layout, *refs):
    many = len(layout)
    cot_pieces, (gate, up, w_gate, w_up, w_down) = refs[:many], refs[many : many + 5]
    cot, mid = refs[-2:]
    d_gate, d_up = refs[-2 - many - 2 : -2 - many]
    parts = refs[-2 - many : -2]
    r = pl.program_id(0)
    load_block(cot_pieces, layout, r, cot)
    for at in range(0, d_gate.shape[2], UNIT_TILE):
        column = pl.ds(at, UNIT_TILE)
        back = dot_nt(cot[...], w_down[column, :])
        value, slope = gelu_parts(gate[0, :, column].astype(f32))
        d_gate[0, :, column] = (back * up[0, :, column].astype(f32) * slope).astype(bf16)
        d_up[0, :, column] = (back * value).astype(bf16)
    for at in range(0, cot.shape[1], MODEL_TILE):
        column = pl.ds(at, MODEL_TILE)
        total = dot_nt(d_gate[0], w_gate[column, :]) + dot_nt(d_up[0], w_up[column, :])
        mid[:, column] = total.astype(bf16)
    store_block(parts, layout, r, slice(None), mid[...])


def weight_grad_kernel(by_rows, nlefts, nrights, exchange, *refs):
    lefts, rights = refs[:nlefts], refs[nlefts : nlefts + nrights]
    arrived, refs = refs[-1], refs[:-1]
    if exchange:
        first, second, left, right, sent, got, send, recv = refs[-8:]
    else:
        out, left, right = refs[-3:]
    step = pl.program_id(0)

    def assemble(target, sources):
        at = 0
        for ref in sources:
            target[at : at + ref.shape[0], :] = ref[...]
            at += ref.shape[0]

    if nlefts == 1:
        left = lefts[0]
    elif by_rows:
        assemble(left, lefts)
    else:
        pl.when(step == 0)(functools.partial(assemble, left, lefts))
    if nrights == 1:
        right = rights[0]
    elif not by_rows:
        assemble(right, rights)
    else:

        @pl.when(step == 0)
        def _():
            at, loads = 0, []
            for ref in rights:
                place = right.at[pl.ds(at, ref.shape[0])]
                loads.append(pltpu.make_async_copy(ref, place, arrived.at[len(loads)]))
                loads[-1].start()
                at += ref.shape[0]
            for load in loads:
                load.wait()

    total = lax.dot_general(left[...], right[...], (((0,), (0,)), ((), ())), preferred_element_type=f32)
    if not exchange:
        out[...] = total.astype(bf16)
        return

    def copy(at):
        return remote(sent.at[at], got.at[at], send, recv, at, other_core())

    for at in range(2):

        @pl.when(step == at)
        def _(at=at):
            sent[at] = total.astype(bf16)
            copy(at).start()

    for at, target in ((0, first), (1, second)):

        @pl.when(step == 2 + at)
        def _(at=at, target=target):
            copy(at).wait_recv()
            target[...] = (total + got[at].astype(f32)).astype(bf16)
            copy(at).wait_send()


def join_kernel(npieces, by_rows, ways, *refs):
    pieces, outs = refs[:npieces], refs[npieces : npieces + ways]
    held, wide = refs[npieces + ways : 2 * npieces + ways], refs[2 * npieces + ways : 3 * npieces + ways]
    arrive, leave = refs[-2:]
    half = npieces // 2
    core = core_index()
    loads = [pltpu.make_async_copy(piece, vmem, arrive.at[at]) for at, (piece, vmem) in enumerate(zip(pieces, held))]
    for load in loads:
        load.start()
    stores, start = [], 0

    def store(source, target):
        stores.append(pltpu.make_async_copy(source, target, leave.at[len(stores)]))
        stores[-1].start()

    span = sum(piece.shape[0] for piece in pieces[:half])
    for at, (load, vmem, big) in enumerate(zip(loads, held, wide)):
        start = 0 if at == half else start
        mine = core if at < half else 1 - core
        load.wait()
        big[...] = vmem[...].astype(f32)
        if by_rows:
            place = pl.ds(pl.multiple_of(mine * span + start, 16), vmem.shape[0])
            start += vmem.shape[0]
            for way, out in enumerate(outs):
                store(big.at[:, pl.ds(way * out.shape[1], out.shape[1])], out.at[place, :])
        else:
            rows, columns = outs[0].shape[0], vmem.shape[1]
            for block in range(2):
                place = pl.ds(pl.multiple_of((mine * 2 + block) * columns, LANES), columns)
                store(big.at[pl.ds(block * rows, rows), :], outs[0].at[:, place])
    for store in stores:
        store.wait()


ANY = pl.BlockSpec(memory_space=pl.ANY)
PARAMS = pltpu.CompilerParams(vmem_limit_bytes=VMEM_BYTES)
MESH = pl.DeviceIdType.MESH


def flip(index, mask, size):
    total, bit = 0, 1
    while bit < size:
        total = total + ((index // bit + mask // bit) % 2) * bit
        bit *= 2
    return total


def neighbours():
    me = lax.axis_index("mp")
    return {"mp": flip(me, 1, 4)}, {"mp": flip(me, 2, 4)}


def other_core():
    return {"dp": flip(lax.axis_index("dp"), 1, 8)}


def remote(source, target, send, recv, at, device):
    return pltpu.make_async_remote_copy(
        src_ref=source,
        dst_ref=target,
        send_sem=send.at[at],
        recv_sem=recv.at[at],
        device_id=device,
        device_id_type=MESH,
    )


class GatherHost:
    def __init__(self, shard):
        rows, model = shard.shape
        self.operands = [shard]
        self.outputs = [jax.ShapeDtypeStruct((count, model), bf16) for count in (rows, rows, rows // 2, rows // 2)]
        self.scratch = [pltpu.SemaphoreType.DMA((6,)), pltpu.SemaphoreType.DMA((6,))]

    def copies(self, ins, outs, scratch):
        (shard,), (by_x, by_y, far_a, far_b), (send, recv) = ins, outs, scratch
        half = far_a.shape[0]
        low, high = pl.ds(0, half), pl.ds(half, half)
        x, y = neighbours()
        return (
            lambda: remote(shard.at[low], by_x.at[low], send, recv, 0, x),
            lambda: remote(shard.at[high], by_y.at[high], send, recv, 1, y),
            lambda: remote(shard.at[high], by_x.at[high], send, recv, 2, x),
            lambda: remote(shard.at[low], by_y.at[low], send, recv, 3, y),
            lambda: remote(by_x.at[low], far_a, send, recv, 4, y),
            lambda: remote(by_y.at[high], far_b, send, recv, 5, x),
        )

    def begin(self, *refs):
        for copy in self.copies(*refs)[:4]:
            copy().start()

    def middle(self, *refs):
        copies = self.copies(*refs)
        copies[0]().wait_recv()
        copies[1]().wait_recv()
        copies[4]().start()
        copies[5]().start()

    def end(self, *refs):
        copies = self.copies(*refs)
        copies[0]().wait_send()
        copies[1]().wait_send()
        for at in (2, 3, 4, 5):
            copies[at]().wait()

    def devices(self):
        return neighbours()

    def result(self, outs):
        return (self.operands[0],) + tuple(outs)


class ScatterHost:
    def __init__(self, parts):
        rows, model = parts[1].shape
        half = rows // 2
        self.first = parts[0]
        self.operands = list(parts[1:])
        self.outputs = [jax.ShapeDtypeStruct((rows, model), bf16)] * 2
        self.scratch = [pltpu.VMEM((half, model), bf16)] * 4 + [pltpu.SemaphoreType.DMA((6,))] * 2
        self.scratch += [pltpu.SemaphoreType.DMA((2,))]

    def copies(self, ins, outs, scratch):
        (one, two, far_a, far_b), (from_x, from_y) = ins, outs
        got_x, got_y, own_x, own_y, send, recv, local = scratch
        half = far_a.shape[0]
        low, high = pl.ds(0, half), pl.ds(half, half)
        x, y = neighbours()
        return (
            lambda: remote(far_a, got_x, send, recv, 0, x),
            lambda: remote(far_b, got_y, send, recv, 1, y),
            lambda: remote(one.at[low], from_x.at[low], send, recv, 2, x),
            lambda: remote(two.at[high], from_y.at[high], send, recv, 3, y),
            lambda: remote(own_x, from_x.at[high], send, recv, 4, x),
            lambda: remote(own_y, from_y.at[low], send, recv, 5, y),
            lambda: pltpu.make_async_copy(one.at[high], own_x, local.at[0]),
            lambda: pltpu.make_async_copy(two.at[low], own_y, local.at[1]),
        )

    def begin(self, *refs):
        copies = self.copies(*refs)
        for at in (0, 1, 2, 3, 6, 7):
            copies[at]().start()

    def middle(self, ins, outs, scratch):
        copies = self.copies(ins, outs, scratch)
        got_x, got_y, own_x, own_y = scratch[:4]
        copies[6]().wait()
        copies[7]().wait()
        copies[0]().wait_recv()
        copies[1]().wait_recv()
        own_x[...] = (own_x[...].astype(f32) + got_y[...].astype(f32)).astype(bf16)
        own_y[...] = (own_y[...].astype(f32) + got_x[...].astype(f32)).astype(bf16)
        copies[4]().start()
        copies[5]().start()

    def end(self, *refs):
        copies = self.copies(*refs)
        copies[0]().wait_send()
        copies[1]().wait_send()
        for at in (2, 3, 4, 5):
            copies[at]().wait()

    def devices(self):
        return neighbours()

    def result(self, outs):
        return self.first.astype(f32) + outs[0].astype(f32) + outs[1].astype(f32)


def chip_partners():
    dp = lax.axis_index("dp")
    return {"dp": flip(dp, 2, 8)}, {"dp": (3 - dp // 2) * 2 + dp % 2}


def chip_is_inner():
    return (lax.axis_index("dp") // 2 + 1) // 2 % 2 == 1


class PipeHost:
    def __init__(self, pieces):
        self.pieces = pieces
        self.names = [piece[0] for piece in pieces]
        self.operands = [piece[1] for piece in pieces]
        self.outputs = [jax.ShapeDtypeStruct((piece[3], piece[1].shape[1]), bf16) for piece in pieces]
        self.scratch = []
        for (_, _, _, _, stage, hops, _), out in zip(pieces, self.outputs):
            self.scratch += [pltpu.VMEM(out.shape, bf16)] * (1 + min(hops, 2 - stage))
        self.scratch += [pltpu.SemaphoreType.DMA((len(pieces),))] * 6

    def devices(self):
        return chip_partners()

    def parts(self, ins, outs, scratch):
        pair, mirror = chip_partners()
        send, recv, send_on, recv_on, local, back = scratch[-6:]
        given = 0
        for at, ((_, _, start, count, stage, hops, slot), array, out) in enumerate(zip(self.pieces, ins, outs)):
            many = 1 + min(hops, 2 - stage)
            buffers = list(scratch[given : given + many])
            given += many
            source = array.at[pl.ds(start, count)]

            def hop(number, at=at, stage=stage, source=source, buffers=buffers, out=out):
                way = stage + number
                target = out if way == 2 else buffers[number + 1]
                sems = (send, recv) if number == 0 else (send_on, recv_on)
                return remote(source if number == 0 else buffers[number], target, *sems, at, mirror if way == 1 else pair)

            def load(at=at, source=source, buffers=buffers):
                return pltpu.make_async_copy(source, buffers[0], local.at[at])

            def keep(at=at, buffers=buffers, out=out):
                return pltpu.make_async_copy(buffers[-1], out, back.at[at])

            yield stage, hops, slot, buffers, hop, load, keep

    def add(self, target, other):
        target[...] = (target[...].astype(f32) + other[...].astype(f32)).astype(bf16)

    def begin(self, *refs):
        inner = chip_is_inner()
        for stage, _, _, _, hop, load, _ in self.parts(*refs):

            @pl.when(inner)
            def _(stage=stage, hop=hop, load=load):
                load().start()
                if stage > 0:
                    hop(0).start()

            if stage == 0:

                @pl.when(jnp.logical_not(inner))
                def _(hop=hop):
                    hop(0).start()

    def middle(self, at, *refs):
        inner = chip_is_inner()
        for stage, hops, slot, buffers, hop, load, keep in self.parts(*refs):
            if slot == at:

                @pl.when(inner)
                def _(stage=stage, hops=hops, buffers=buffers, hop=hop, load=load, keep=keep):
                    load().wait()
                    if hops == 2:
                        hop(0).wait_recv()
                        self.add(buffers[1], buffers[0])
                        hop(1).start()
                    if stage + hops == 3:
                        keep().start()

    def slots(self):
        return sorted(set(piece[6] for piece in self.pieces) - {END, None})

    def end(self, *refs):
        inner = chip_is_inner()
        self.middle(END, *refs)
        parts = list(self.parts(*refs))
        for stage, hops, slot, buffers, hop, load, keep in parts:

            @pl.when(inner)
            def _(stage=stage, hops=hops, slot=slot, buffers=buffers, hop=hop, load=load, keep=keep):
                if slot is None:
                    load().wait()
                if stage > 0:
                    hop(0).wait_send()
                if hops == 2:
                    hop(1).wait_send()
                if stage + hops < 3:
                    hop(hops - 1).wait_recv()
                    self.add(buffers[-1], buffers[-2])
                    keep().start()

            @pl.when(jnp.logical_not(inner))
            def _(stage=stage, hops=hops, hop=hop):
                if stage == 0:
                    hop(0).wait_send()
                if stage + hops == 3:
                    hop(hops - 1).wait_recv()

        for _, _, _, _, _, _, keep in parts:

            @pl.when(inner)
            def _(keep=keep):
                keep().wait()

    def result(self, outs):
        return dict(zip(self.names, outs))


class Tail:
    def __init__(self, chunks):
        self.chunks = chunks
        self.pieces = []
        for at, (shape, stage, _, _) in enumerate(chunks):
            rows = shape[0]
            parts = 1 if stage == 2 or rows < 64 else 2 if rows < 256 else 4
            size = -(-rows // parts // 16) * 16
            self.pieces += [(at, start, min(size, rows - start)) for start in range(0, rows, size)]
        self.scratch = []
        for shape, stage, late, _ in chunks:
            self.scratch += [pltpu.VMEM(shape, bf16)] * (3 - stage - (1 if late else 0))
        self.scratch += [pltpu.SemaphoreType.DMA((len(self.pieces),))] * 8

    def setup(self, refs, outs, scratch):
        pair, mirror = chip_partners()
        p_send, p_recv, q_send, q_recv, f_send, f_recv, local, back = scratch[-8:]
        buffers, given = [], 0
        for ref, (_, stage, late, _) in zip(refs, self.chunks):
            count = 3 - stage - (1 if late else 0)
            mine = ([ref] if late else []) + list(scratch[given : given + count])
            given += count
            buffers.append(mine if stage == 0 else [mine[0], None, mine[-1]])

        def transfers(number):
            at, start, count = self.pieces[number]
            rows = pl.ds(start, count)
            own, from_pair, from_mirror = buffers[at]
            early = self.chunks[at][1]
            source, out = refs[at].at[rows], outs[at].at[rows]
            sent = source if early == 1 else own.at[rows]
            done = own if early == 2 else from_mirror
            given_out = source if early == 2 else done.at[rows]
            return {
                "inward": lambda: remote(source, from_pair.at[rows], p_send, p_recv, number, pair),
                "load": lambda: pltpu.make_async_copy(source, own.at[rows], local.at[number]),
                "between": lambda: remote(sent, from_mirror.at[rows], q_send, q_recv, number, mirror),
                "outward": lambda: remote(given_out, out, f_send, f_recv, number, pair),
                "keep": lambda: pltpu.make_async_copy(done.at[rows], out, back.at[number]),
            }

        self.buffers = buffers
        self.moves = [transfers(number) for number in range(len(self.pieces))]
        self.stages = [self.chunks[at][1] for at, _, _ in self.pieces]
        self.late = [self.chunks[at][2] for at, _, _ in self.pieces]
        self.out = [self.chunks[at][3] for at, _, _ in self.pieces]
        self.inner = chip_is_inner()

    def start(self):
        @pl.when(self.inner)
        def _():
            for move, stage, late in zip(self.moves, self.stages, self.late):
                if stage == 2:
                    move["outward"]().start()
                if stage == 1:
                    move["between"]().start()
                if not late:
                    move["load"]().start()

        @pl.when(jnp.logical_not(self.inner))
        def _():
            for move, stage, late in zip(self.moves, self.stages, self.late):
                if stage == 0 and not late:
                    move["inward"]().start()

    def add(self, number, target, other):
        _, start, count = self.pieces[number]
        rows = pl.ds(start, count)
        target[rows, :] = (target[rows, :].astype(f32) + other[rows, :].astype(f32)).astype(bf16)

    def finish(self):
        numbers = range(len(self.pieces))

        def on(number):
            self.moves[number]["between"]().wait_recv()
            own, _, other = self.buffers[self.pieces[number][0]]
            self.add(number, other, own)
            if self.out[number]:
                self.moves[number]["outward"]().start()
            self.moves[number]["keep"]().start()

        @pl.when(self.inner)
        def _():
            for number in numbers:
                if not self.late[number]:
                    self.moves[number]["load"]().wait()
                if self.stages[number] == 2:
                    self.moves[number]["keep"]().start()
            waiting = [number for number in numbers if self.stages[number] == 1]
            for number in numbers:
                if self.stages[number] == 0:
                    self.moves[number]["inward"]().wait_recv()
                    own, other, _ = self.buffers[self.pieces[number][0]]
                    self.add(number, own, other)
                    self.moves[number]["between"]().start()
                    waiting.append(number)
                    on(waiting.pop(0))
            for number in waiting:
                on(number)
            for number in numbers:
                if self.stages[number] < 2:
                    self.moves[number]["between"]().wait_send()
                if self.out[number]:
                    self.moves[number]["outward"]().wait_send()
                self.moves[number]["keep"]().wait()

        @pl.when(jnp.logical_not(self.inner))
        def _():
            for number in numbers:
                if self.stages[number] == 0 and self.late[number]:
                    self.moves[number]["inward"]().start()
            for number in numbers:
                if self.stages[number] == 0:
                    self.moves[number]["inward"]().wait_send()
                if self.out[number]:
                    self.moves[number]["outward"]().wait_recv()


def call(
    kernel, grid, ins, outs, scratch, name, us, hosts=(), before=(), aliases=None, middle=0, unique=None, pair=False, chips=False, late=()
):
    nins, nouts, nscratch = len(ins), len(outs), len(scratch)
    steps = math.prod(grid)
    loaded = [at for at, (_, spec) in enumerate(ins) if spec is WHOLE]

    def body(*refs):
        refs = list(refs)

        def take(count):
            part = refs[:count]
            del refs[:count]
            return part

        own_ins = take(nins)
        host_ins = [take(len(host.operands)) for host in hosts]
        take(len(before))
        own_outs = take(nouts)
        host_outs = [take(len(host.outputs)) for host in hosts]
        own_scratch = take(nscratch)
        host_refs = [(i, o, take(len(host.scratch))) for host, i, o in zip(hosts, host_ins, host_outs)]
        buffers = take(len(loaded))
        step = pl.program_id(0)
        if len(grid) == 2:
            step = step * grid[1] + pl.program_id(1)
        if hosts or pair:

            @pl.when(step == 0)
            def _():
                devices = (other_core(),) if pair else ()
                if any(isinstance(host, (GatherHost, ScatterHost)) for host in hosts):
                    devices += tuple(neighbours())
                between = chips or any(isinstance(host, PipeHost) for host in hosts)
                if between:
                    devices += chip_partners()[:1]
                barrier = pltpu.get_barrier_semaphore()
                for device in devices:
                    pl.semaphore_signal(barrier, inc=1, device_id=device, device_id_type=MESH)
                if between:

                    @pl.when(chip_is_inner())
                    def _():
                        pl.semaphore_signal(barrier, inc=1, device_id=chip_partners()[1], device_id_type=MESH)
                        pl.semaphore_wait(barrier, len(devices) + 1)

                    @pl.when(jnp.logical_not(chip_is_inner()))
                    def _():
                        pl.semaphore_wait(barrier, len(devices))
                else:
                    pl.semaphore_wait(barrier, len(devices))
                for host, there in zip(hosts, host_refs):
                    host.begin(*there)

        if loaded:
            arrived = take(1)[0]
            loads = [(own_ins[at], buffer, arrived.at[k]) for k, (at, buffer) in enumerate(zip(loaded, buffers))]

            second = [load for load, at in zip(loads, loaded) if at in late]
            first = [load for load, at in zip(loads, loaded) if at not in late]

            @pl.when(step == 0)
            def _():
                for load in first + second:
                    pltpu.make_async_copy(*load).start()
                for load in first:
                    pltpu.make_async_copy(*load).wait()

            for at, buffer in zip(loaded, buffers):
                own_ins[at] = buffer
        if hosts:

            for host, there in list(zip(hosts, host_refs))[::-1]:
                if late and not isinstance(host, PipeHost):
                    continue
                for at in host.slots() if isinstance(host, PipeHost) else (middle,):

                    @pl.when(step == at)
                    def _(host=host, there=there, at=at):
                        host.middle(*((at,) if isinstance(host, PipeHost) else ()), *there)

        def wait_late():
            @pl.when(step == 0)
            def _():
                for load in second:
                    pltpu.make_async_copy(*load).wait()

            for host, there in zip(hosts, host_refs):
                if not isinstance(host, PipeHost):

                    @pl.when(step == middle)
                    def _(host=host, there=there):
                        host.middle(*there)

        kernel(*([wait_late] if late else []), *own_ins, *own_outs, *own_scratch)
        if hosts:

            @pl.when(step == steps - 1)
            def _():
                for host, there in list(zip(hosts, host_refs))[::-1]:
                    host.end(*there)

    host_operands = [v for host in hosts for v in host.operands]
    host_outputs = [v for host in hosts for v in host.outputs]
    params = pltpu.CompilerParams(vmem_limit_bytes=VMEM_BYTES)
    if hosts or pair:
        params = pltpu.CompilerParams(vmem_limit_bytes=VMEM_BYTES, collective_id=unique, has_side_effects=True)
    results = pl.pallas_call(
        body,
        out_shape=tuple(shape for shape, _ in outs) + tuple(host_outputs),
        grid=grid,
        in_specs=[ANY if spec is WHOLE else spec for _, spec in ins] + [ANY] * (len(host_operands) + len(before)),
        out_specs=tuple(spec for _, spec in outs) + (ANY,) * len(host_outputs),
        scratch_shapes=list(scratch)
        + [v for host in hosts for v in host.scratch]
        + [pltpu.VMEM(ins[at][0].shape, ins[at][0].dtype) for at in loaded]
        + ([pltpu.SemaphoreType.DMA((len(loaded),))] if loaded else []),
        input_output_aliases=aliases or {},
        compiler_params=params,
        cost_estimate=cost(us),
        name=name,
    )(*[array for array, _ in ins], *host_operands, *before)
    own, rest = results[:nouts], results[nouts:]
    found = []
    for host in hosts:
        found.append(host.result(rest[: len(host.outputs)]))
        rest = rest[len(host.outputs) :]
    return own, found


def cost(us):
    return pl.CostEstimate(flops=int(us * COST_SCALE * 1.15e9), bytes_accessed=1 << 16, transcendentals=0)


WHOLE = "whole"
END = 99


def whole(array):
    return WHOLE


def layout_of(blocks, rows):
    if blocks != 4:
        return tuple((r, 0, rows) for r in range(blocks))
    return ((0, 0, rows), (1, 0, rows), (2, 0, rows), (3, 0, rows // 2), (3, rows // 2, rows - rows // 2))


def piece_outputs(layout, model):
    shapes = tuple(jax.ShapeDtypeStruct((count, model), bf16) for _, _, count in layout)
    specs = tuple(pl.BlockSpec(shape.shape, lambda *_: (0, 0)) for shape in shapes)
    return shapes, specs


def rec_forward(length, seq, x, params, **more):
    blocks, (rows, model) = lax.axis_size("mp"), x[0].shape
    layout = layout_of(blocks, rows)
    width = params[0].shape[1] // 2

    def at(step):
        return (flip(step, lax.axis_index("mp"), blocks), 0, 0)

    wide = pl.BlockSpec((1, rows, width), at)
    out = jax.ShapeDtypeStruct((blocks, rows, width), f32)
    low = jax.ShapeDtypeStruct((blocks, rows, width), bf16)
    shapes, specs = piece_outputs(layout, model)
    final = (jax.ShapeDtypeStruct((SUB, width), f32), pl.BlockSpec((SUB, width), lambda step: (0, 0)))
    return call(
        functools.partial(rec_forward_kernel, layout, seq),
        (blocks,),
        [(v, whole(v)) for v in (length,) + tuple(x) + tuple(params)],
        [(shape, wide) for shape in (low, out, out, out, out, low, out, out, out)] + [final] + list(zip(shapes, specs)),
        [
            pltpu.VMEM((rows, 2 * width), f32),
            pltpu.VMEM((SUB, width), f32),
            pltpu.VMEM((SUB, width), f32),
            pltpu.VMEM((rows, model), bf16),
            pltpu.VMEM((rows, width), f32),
        ],
        "rec_forward",
        37,
        late=tuple(1 + len(x) + at for at in (3, 7)),
        **more,
    )


def rec_backward(length, seq, count, d_resid, x, params, saved, shared, **more):
    blocks, (rows, model) = lax.axis_size("mp"), x[0].shape
    layout = layout_of(blocks, rows)
    width = saved[0].shape[2]

    def at(step):
        return (flip(blocks - 1 - step, lax.axis_index("mp"), blocks), 0, 0)

    def placed(step):
        return (seq * blocks + flip(blocks - 1 - step, lax.axis_index("mp"), blocks), 0, 0)

    wide = pl.BlockSpec((1, rows, width), at)
    double = pl.BlockSpec((1, rows, 2 * width), placed)
    low = jax.ShapeDtypeStruct((count * blocks, rows, 2 * width), bf16)
    shapes, specs = piece_outputs(layout, model)
    sums = (jax.ShapeDtypeStruct((8, SUB, width), f32), pl.BlockSpec((8, SUB, width), lambda step: (0, 0, 0)))
    gain_sums = (jax.ShapeDtypeStruct((SUB, model), f32), pl.BlockSpec((SUB, model), lambda step: (0, 0)))
    inputs = [(v, whole(v)) for v in (length,) + tuple(d_resid) + tuple(x) + tuple(params)]
    before_x, before_params = 1 + len(d_resid), 1 + len(d_resid) + len(x)
    late = tuple(range(before_x, before_params)) + tuple(before_params + at for at in (1, 2, 3))
    inputs += [(v, wide) for v in saved] + [(v, ANY) for v in shared]
    return call(
        functools.partial(rec_backward_kernel, layout, seq),
        (blocks,),
        inputs,
        [(low, double), (low, double), sums, gain_sums] + list(zip(shapes, specs)),
        [
            pltpu.VMEM((rows, width), f32),
            pltpu.VMEM((rows, width), f32),
            pltpu.VMEM((SUB, width), f32),
            pltpu.VMEM((SUB, width), f32),
            pltpu.VMEM((rows, model), bf16),
            pltpu.VMEM((rows, model), bf16),
        ],
        "rec_backward",
        43,
        aliases={len(inputs) - len(shared) + at: at for at in range(len(shared))},
        late=late,
        **more,
    )


def largest_tile(total, limit, unit=LANES):
    return max(t for t in range(unit, limit + 1, unit) if total % t == 0)


def mlp_forward(seq, count, x, w_gate, w_up, w_down, shared, **more):
    blocks, (rows, model) = lax.axis_size("mp"), x[0].shape
    units = w_gate.shape[1]
    low = jax.ShapeDtypeStruct((count * blocks, rows, units), bf16)
    part = pl.BlockSpec((1, rows, units), lambda r: (seq * blocks + r, 0, 0))
    long = pl.BlockSpec((1, rows, model), lambda r: (flip(r, lax.axis_index("mp"), blocks), 0, 0))
    inputs = [(v, whole(v)) for v in tuple(x) + (w_gate, w_up, w_down)] + [(v, ANY) for v in shared]
    return call(
        functools.partial(mlp_forward_kernel, layout_of(blocks, rows)),
        (blocks,),
        inputs,
        [(low, part)] * 3 + [(jax.ShapeDtypeStruct((blocks, rows, model), bf16), long)],
        [pltpu.VMEM((rows, model), bf16)],
        "mlp_forward",
        30,
        aliases={len(inputs) - len(shared) + at: at for at in range(len(shared))},
        **more,
    )


def mlp_backward(seq, count, cot, gate, up, w_gate, w_up, w_down, shared, **more):
    blocks, (rows, model) = lax.axis_size("mp"), cot[0].shape
    layout = layout_of(blocks, rows)
    units = w_gate.shape[1]
    low = jax.ShapeDtypeStruct((count * blocks, rows, units), bf16)
    part = pl.BlockSpec((1, rows, units), lambda r: (seq * blocks + r, 0, 0))
    shapes, specs = piece_outputs(layout, model)
    inputs = [(v, whole(v)) for v in cot] + [(gate, part), (up, part)]
    inputs += [(v, whole(v)) for v in (w_gate, w_up, w_down)] + [(v, ANY) for v in shared]
    return call(
        functools.partial(mlp_backward_kernel, layout),
        (blocks,),
        inputs,
        [(low, part)] * 2 + list(zip(shapes, specs)),
        [pltpu.VMEM((rows, model), bf16)] * 2,
        "mlp_backward",
        32,
        aliases={len(inputs) - len(shared) + at: at for at in range(len(shared))},
        **more,
    )


def flat(array):
    return array.reshape(-1, array.shape[-1])


def core_index():
    return lax.axis_index("dp") % 2 if lax.axis_size("dp") == 8 else 0


def weight_grad(lefts, rights, by_rows=True, **more):
    lefts, rights = [flat(v) for v in lefts], [flat(v) for v in rights]
    rows, columns = lefts[0].shape[1], rights[0].shape[1]
    tokens = sum(v.shape[0] for v in lefts)
    exchange = lax.axis_size("dp") == 8
    tiled = rows if by_rows else columns
    tile = tiled // 4 if exchange else largest_tile(tiled, 512)

    def place(step):
        if not exchange:
            return step
        return (core_index() + 1 + step // 2) % 2 * 2 + step % 2

    def cut(array, in_tiles):
        if not in_tiles:
            return whole(array)
        return pl.BlockSpec((array.shape[0], tile), lambda step: (0, place(step)))

    scratch = [
        pltpu.VMEM((tokens if len(lefts) > 1 else 16, tile if by_rows else rows), bf16),
        pltpu.VMEM((tokens if len(rights) > 1 else 16, columns if by_rows else tile), bf16),
    ]
    block = (tile, columns) if by_rows else (rows, tile)
    if exchange:
        outs = [(jax.ShapeDtypeStruct(block, bf16), pl.BlockSpec(block, lambda step: (0, 0)))] * 2
        scratch += [pltpu.VMEM((2,) + block, bf16)] * 2 + [pltpu.SemaphoreType.DMA((2,))] * 2
        scratch.append(pltpu.SemaphoreType.DMA((len(rights),)))
    else:
        scratch.append(pltpu.SemaphoreType.DMA((len(rights),)))
        whole_out = jax.ShapeDtypeStruct((rows, columns), bf16)
        outs = [(whole_out, pl.BlockSpec(block, lambda step: (step, 0) if by_rows else (0, step)))]
    return call(
        functools.partial(weight_grad_kernel, by_rows, len(lefts), len(rights), exchange),
        (tiled // tile,),
        [(v, cut(v, by_rows)) for v in lefts]
        + [(v, ANY if by_rows and len(rights) > 1 else cut(v, not by_rows)) for v in rights],
        outs,
        scratch,
        "weight_grad",
        20 if columns > 1000 and by_rows else 13,
        pair=exchange,
        **more,
    )


def last_kernel(nlefts, nrights, nchunks, nblocks, nfinals, tail, *refs):
    lefts, refs = refs[:nlefts], refs[nlefts:]
    rights, refs = refs[:nrights], refs[nrights:]
    convs, refs = refs[:nlefts], refs[nlefts:]
    d_gates, sums_a, sums_b, gain_a, gain_b, gain_c, gain_d = refs[:7]
    chunks, refs = refs[7 : 7 + nchunks], refs[7 + nchunks :]
    finals, refs = refs[:nfinals], refs[nfinals:]
    outs, refs = refs[: nchunks + 3], refs[nchunks + 3 :]
    others, scratch = refs[:nfinals], refs[nfinals:]
    pack, gains, both, whole_pack, got_pack, got_gains, left, right, dense, sent, got, send, recv = scratch[:13]
    finals_send, finals_recv = scratch[13:15]
    step = pl.program_id(0)
    tail.setup(list(chunks) + [pack, gains, both], outs, scratch[15:])
    pl.when(step == 0)(tail.start)

    def swap_final(at):
        return remote(finals[at], others[at], finals_send, finals_recv, at, other_core())

    def swap_gains():
        return remote(gains, got_gains, send, recv, 3, other_core())

    @pl.when(step == 0)
    def _():
        one = jnp.sum(gain_a[...] + gain_b[...], axis=0, keepdims=True)
        two = gain_c[...] + gain_d[...]
        row = lax.broadcasted_iota(jnp.int32, (16, one.shape[1]), 0)
        gains[...] = jnp.where(row == 0, one, jnp.where(row == 1, two, 0.0)).astype(bf16)
        swap_gains().start()

    @pl.when(step == 1)
    def _():
        swap_gains().wait()
        gains[...] = (gains[...].astype(f32) + got_gains[...].astype(f32)).astype(bf16)

    def copy(at):
        return remote(sent.at[at], got.at[at], send, recv, at, other_core())

    def pack_copy():
        return remote(whole_pack, got_pack, send, recv, 2, other_core())

    @pl.when(step < 4)
    def _():
        at = 0
        for ref in rights:
            right[at : at + ref.shape[0], :] = ref[...]
            at += ref.shape[0]

    @pl.when(step == 0)
    def _():
        at = 0
        for ref in lefts:
            left[at : at + ref.shape[0], :] = ref[...]
            at += ref.shape[0]

    for at in range(4):

        @pl.when(step == at)
        def _(at=at):
            total = lax.dot_general(left[...], right[...], (((0,), (0,)), ((), ())), preferred_element_type=f32)
            if at < 2:
                sent[at] = total.astype(bf16)
                copy(at).start()
            else:
                copy(at - 2).wait_recv()
                rows = total.shape[0]
                both[(at - 2) * rows : (at - 1) * rows, :] = (total + got[at - 2].astype(f32)).astype(bf16)
                copy(at - 2).wait_send()

    @pl.when(step == 3)
    def _():
        at = 0
        for ref in convs:
            rows = ref.shape[0]
            term = lax.dot_general(
                ref[...], d_gates[at : at + rows, :], (((0,), (0,)), ((), ())), preferred_element_type=f32
            )
            dense[...] = term if at == 0 else dense[...] + term
            at += rows
        width = dense.shape[0]
        inner = width // nblocks
        lane = lax.broadcasted_iota(jnp.int32, (inner, width), 1)
        for gate in range(2):
            total = jnp.zeros((inner, width), f32)
            for n in range(nblocks):
                here = (lane >= n * inner) & (lane < (n + 1) * inner)
                block = dense[n * inner : (n + 1) * inner, gate * width : (gate + 1) * width]
                total = total + jnp.where(here, block, 0.0)
            whole_pack[gate * inner : (gate + 1) * inner, :] = total.astype(bf16)
        vectors = jnp.sum(sums_a[...] + sums_b[...], axis=1)
        rest = whole_pack.shape[0] - 2 * inner
        vectors = jnp.concatenate([vectors, jnp.zeros((rest - 8, width), f32)], axis=0)
        whole_pack[2 * inner :, :] = vectors.astype(bf16)
        pack_copy().start()

    @pl.when(step == 4)
    def _():
        pack_copy().wait()
        for at in range(nfinals):
            swap_final(at).start()
        mine = pl.ds(pl.multiple_of(core_index() * pack.shape[0], 16), pack.shape[0])
        pack[...] = (whole_pack[mine, :].astype(f32) + got_pack[mine, :].astype(f32)).astype(bf16)
        tail.finish()
        for at in range(nfinals):
            swap_final(at).wait()


def last_grad(lefts, rights, convs, d_gates, vectors, moving, finals, nblocks, **more):
    lefts, rights, convs = ([flat(v) for v in group] for group in (lefts, rights, convs))
    rows, columns = lefts[0].shape[1], rights[0].shape[1]
    tokens = sum(v.shape[0] for v in lefts)
    tile = columns // 4

    def place(step):
        step = step - step // 4
        return (core_index() + 1 + step // 2) % 2 * 2 + step % 2

    chunks = [(chunk, stage) for stage, group in enumerate(moving) for _, chunk in group.items()]
    names = [name for group in moving for name in group]
    block = (rows, tile)
    packed = -(-(2 * rows // nblocks + 16) // 32) * 32
    made = [((packed // 2, rows), True), ((16, columns), True), ((2 * rows, tile), False)]
    tail = Tail(
        [(chunk.shape, stage, False, True) for chunk, stage in chunks] + [(shape, 0, True, out) for shape, out in made]
    )
    outs = [jax.ShapeDtypeStruct(chunk[0], bf16) for chunk in tail.chunks]
    out, found = call(
        functools.partial(last_kernel, len(lefts), len(rights), len(chunks), nblocks, len(finals), tail),
        (5,),
        [(v, whole(v)) for v in lefts]
        + [(v, pl.BlockSpec((v.shape[0], tile), lambda step: (0, place(step)))) for v in rights]
        + [(v, whole(v)) for v in convs + [flat(d_gates)] + list(vectors)]
        + [(chunk, ANY) for chunk, _ in chunks]
        + [(piece, ANY) for piece in finals.values()],
        [(shape, ANY) for shape in outs]
        + [(jax.ShapeDtypeStruct(piece.shape, bf16), ANY) for piece in finals.values()],
        [pltpu.VMEM(shape, bf16) for shape, _ in made]
        + [
            pltpu.VMEM((packed, rows), bf16),
            pltpu.VMEM((packed, rows), bf16),
            pltpu.VMEM((16, columns), bf16),
            pltpu.VMEM((tokens, rows), bf16),
            pltpu.VMEM((tokens, tile), bf16),
            pltpu.VMEM((rows, 2 * rows), f32),
            pltpu.VMEM((2,) + block, bf16),
            pltpu.VMEM((2,) + block, bf16),
            pltpu.SemaphoreType.DMA((4,)),
            pltpu.SemaphoreType.DMA((4,)),
            pltpu.SemaphoreType.DMA((len(finals),)),
            pltpu.SemaphoreType.DMA((len(finals),)),
        ]
        + tail.scratch,
        "last_grad",
        120,
        pair=True,
        chips=True,
        **more,
    )
    names += ["pack", "gains", "out"]
    return dict(zip(names, out)), dict(zip(finals, out[len(names) :])), found


def join_pieces(pieces, by_rows, ways):
    rows, columns = sum(v.shape[0] for v in pieces), pieces[0].shape[1]
    shape = (rows, columns // ways) if by_rows else (rows // 4, 4 * columns)
    out = (jax.ShapeDtypeStruct(shape, f32), ANY)
    return call(
        functools.partial(join_kernel, len(pieces), by_rows, ways),
        (1,),
        [(piece, ANY) for piece in pieces],
        [out] * ways,
        [pltpu.VMEM(piece.shape, bf16) for piece in pieces]
        + [pltpu.VMEM(piece.shape, f32) for piece in pieces]
        + [pltpu.SemaphoreType.DMA((len(pieces),)), pltpu.SemaphoreType.DMA((len(pieces) * max(2, ways),))],
        "join_pieces",
        0.05,
    )[0]


def swap(value, axis, bit):
    size = lax.axis_size(axis)
    return lax.ppermute(value, axis, [(i, i ^ bit) for i in range(size)])


def gather(shard):
    size = lax.axis_size("mp")
    if size != 4:
        return (shard,) + tuple(swap(shard, "mp", r) for r in range(1, size))
    half = shard.shape[0] // 2
    by_x = swap(shard, "mp", 1)
    by_y = swap(shard, "mp", 2)
    return (shard, by_x, by_y, swap(by_x[:half], "mp", 2), swap(by_y[half:], "mp", 1))


def scatter(parts):
    size = lax.axis_size("mp")
    if size != 4:
        total = parts[0].astype(f32)
        for r in range(1, size):
            total = total + swap(parts[r], "mp", r).astype(f32)
        return total
    half = parts[3].shape[0]
    from_x = swap(parts[3], "mp", 1)
    from_y = swap(parts[4], "mp", 2)
    for_y = jnp.concatenate([add_low(parts[2][:half], from_x), parts[2][half:]], axis=0)
    for_x = jnp.concatenate([parts[1][:half], add_low(parts[1][half:], from_y)], axis=0)
    return parts[0].astype(f32) + swap(for_y, "mp", 2).astype(f32) + swap(for_x, "mp", 1).astype(f32)


def add_low(left, right):
    return (left.astype(f32) + right.astype(f32)).astype(bf16)


class Pipe:
    def __init__(self):
        self.queue, self.moving, self.done = [], [], {}

    def enter(self, name, quarters):
        self.queue += [[name + str(at), quarter, 0] for at, quarter in enumerate(quarters)]

    def host(self, budget, slots):
        pieces, old = [], list(slots)
        for name, array, stage in self.moving:
            slot = slots[0] if stage == 2 else old.pop(0)
            pieces.append((name, array, 0, array.shape[0], stage, 3 - stage, slot))
        ahead = list(slots)
        while self.queue and budget > 0:
            name, array, start = self.queue[0]
            unit = array.shape[0] // 4
            slot = ahead.pop(0) if ahead else None
            pieces.append((name + "_" + str(start).zfill(4), array, start, unit, 0, 2 if slot else 1, slot))
            budget -= 1
            self.queue[0][2] += unit
            if self.queue[0][2] == array.shape[0]:
                self.queue.pop(0)
        return PipeHost(pieces) if pieces else None

    def took(self, host, results):
        self.moving = []
        for name, _, _, _, stage, hops, _ in host.pieces:
            if stage + hops == 3:
                self.done[name] = results[name]
            else:
                self.moving.append((name, results[name], stage + hops))

    def left(self):
        groups = ({}, {}, {})
        for name, array, stage in self.moving:
            groups[stage][name] = array
        for name, array, start in self.queue:
            groups[0][name + "_" + str(start).zfill(4)] = array[start:]
        return groups


def normalize(values, gain):
    return values * lax.rsqrt(jnp.mean(values * values, axis=-1, keepdims=True) + EPS) * gain


def normalize_back(values, gain, grad):
    inverse = lax.rsqrt(jnp.mean(values * values, axis=-1, keepdims=True) + EPS)
    scaled = grad * gain
    unit = values * inverse
    return inverse * (scaled - unit * jnp.mean(scaled * unit, axis=-1, keepdims=True)), unit


def dense_blocks(weight):
    blocks, inner, outer = weight.shape
    rows = [
        jnp.pad(weight[n], ((0, 0), (n * outer, (blocks - 1 - n) * outer))) for n in range(blocks)
    ]
    return jnp.concatenate(rows, axis=0)


def diagonal_blocks(full, blocks, width):
    inner = width // blocks
    return jnp.stack([full[n * inner : (n + 1) * inner, n * inner : (n + 1) * inner] for n in range(blocks)])


def per_device(
    block_in,
    norm1_gain,
    w_branch,
    w_input,
    conv_weight,
    conv_bias,
    gate_a_weight,
    gate_a_bias,
    gate_i_weight,
    gate_i_bias,
    decay_param,
    w_out,
    norm2_gain,
    w_gate,
    w_up,
    w_down,
    lengths,
    cotangent,
):
    count = block_in.shape[0]
    nblocks = gate_a_weight.shape[0]
    true_width = w_branch.shape[1]
    extra = -true_width % LANES
    me = lax.axis_index("mp")

    def pad_last(value):
        return jnp.pad(value, [(0, 0)] * (value.ndim - 1) + [(0, extra)]) if extra else value

    def line(value):
        return pad_last(value)[None, :]

    wb, wi = pad_last(w_branch), pad_last(w_input)
    wo = jnp.pad(w_out, ((0, extra), (0, 0))) if extra else w_out
    w_ga, w_gi = dense_blocks(gate_a_weight), dense_blocks(gate_i_weight)
    if extra:
        w_ga, w_gi = (jnp.pad(v, ((0, extra), (0, extra))) for v in (w_ga, w_gi))
    taps = pad_last(conv_weight)
    decay_line = line(decay_param)
    w_both = jnp.concatenate([wb, wi], axis=1)
    w_gates = jnp.concatenate([w_ga, w_gi], axis=1)
    forward_params = (
        w_both, taps, line(conv_bias), w_gates, line(gate_a_bias), line(gate_i_bias), decay_line, wo
    )
    backward_params = (wo, w_both, taps, w_gates, decay_line)
    seqs = range(count)
    limits = jnp.broadcast_to(lengths[:, None, None], (count, SUB, LANES))
    blocks = lax.axis_size("mp")
    hosted = blocks == 4 and count == 2
    ids = iter(range(1, 100))

    piped = hosted and lax.axis_size("dp") == 8 and not extra
    pipe = Pipe()

    def enter(name, quarters):
        if piped:
            pipe.enter(name, quarters)

    def tied(value, *deps):
        return lax.optimization_barrier((value,) + deps)[0]

    def run(function, *args, hosts=(), middle=0, budget=4, **more):
        if hosted:
            window = pipe.host(budget, (2, 3) if function is weight_grad else (1, 2)) if piped else None
            out, found = function(
                *args, hosts=list(hosts) + ([window] if window else []), middle=middle, unique=next(ids), **more
            )
            if window:
                pipe.took(window, found[-1])
            return out, found[: len(hosts)]
        out, _ = function(*args, **more)
        return out, [
            gather(host.operands[0]) if isinstance(host, GatherHost) else scatter((host.first, *host.operands))
            for host in hosts
        ]

    resid = [block_in[s].astype(f32) for s in seqs]
    starts = [normalize(resid[s], norm1_gain).astype(bf16) for s in seqs]
    piece, model = starts[0].shape
    seq_in = [gather(starts[0])]
    out, (second,) = run(rec_forward, limits, 0, seq_in[0], forward_params, hosts=[GatherHost(starts[1])], middle=1)
    seq_in.append(second)
    forward = [out]
    out, (branch,) = run(
        rec_forward, limits, 1, seq_in[1], forward_params, hosts=[ScatterHost(out[10:])], middle=1, before=(out[9],)
    )
    forward.append(out)
    mixed = [out[0] for out in forward]
    saved = [out[1:9] for out in forward]
    finals = [out[9][:1, :true_width] for out in forward]
    resid_mid = [resid[0] + branch]
    mid = normalize(resid_mid[0], norm2_gain).astype(bf16)
    seq_mid = [gather(mid)]
    forward_shared, (branch,) = run(
        mlp_forward, 0, count, seq_mid[0], w_gate, w_up, w_down, (), hosts=[ScatterHost(forward[1][10:])], middle=2
    )
    mlp_part = [forward_shared[3]]
    resid_mid.append(resid[1] + branch)
    mid = normalize(resid_mid[1], norm2_gain).astype(bf16)
    seq_mid.append(gather(mid))
    forward_shared, (found,) = run(
        mlp_forward, 1, count, seq_mid[1], w_gate, w_up, w_down, forward_shared[:3],
        hosts=[GatherHost(cotangent[0])], middle=2,
    )
    mlp_part.append(forward_shared[3])
    cot_seq = [found]
    hidden, gate_low, up_low = forward_shared[:3]
    backward, (found,) = run(
        mlp_backward, 0, count, cot_seq[0], gate_low, up_low, w_gate, w_up, w_down, (),
        hosts=[GatherHost(cotangent[1])], middle=2,
    )
    cot_seq.append(found)

    def middle_grad(s, d_mid):
        back, unit = normalize_back(resid_mid[s], norm2_gain, d_mid)
        return cotangent[s].astype(f32) + back, jnp.sum(d_mid * unit, axis=0, keepdims=True)

    flat_mid = [p for pieces in seq_mid for p in pieces]
    flat_cot = [p for pieces in cot_seq for p in pieces]
    grad_down, _ = run(weight_grad, [hidden], flat_cot)
    enter("down", grad_down)
    backward, (d_mid,) = run(
        mlp_backward, 1, count, cot_seq[1], gate_low, up_low, w_gate, w_up, w_down, backward[:2],
        hosts=[ScatterHost(backward[2:])], middle=2, before=(grad_down[0],),
    )
    d_gate, d_up = backward[:2]
    first, gain2 = middle_grad(0, d_mid)
    grad_gate, (first_seq,) = run(weight_grad, flat_mid, [d_gate], hosts=[GatherHost(first.astype(bf16))], middle=3)
    enter("gate", grad_gate)
    grad_up, (d_mid,) = run(
        weight_grad, flat_mid, [d_up], hosts=[ScatterHost(backward[2:])], middle=2, before=(grad_gate[0],)
    )
    second, more_gain2 = middle_grad(1, d_mid)
    enter("up", grad_up)
    out, (second_seq,) = run(
        rec_backward, limits, 0, count, first_seq, seq_in[0], backward_params, saved[0], (),
        hosts=[GatherHost(second.astype(bf16))], middle=1, before=(grad_up[0],), budget=4,
    )
    sums, gain1 = out[2], out[3]
    out, (d_in,) = run(
        rec_backward, limits, 1, count, second_seq, seq_in[1], backward_params, saved[1], out[:2],
        hosts=[ScatterHost(out[4:])], middle=1, budget=4,
    )
    d_both, d_gates = out[:2]
    input_grad = [(first + normalize_back(resid[0], norm1_gain, d_in)[0]).astype(bf16)]

    flat_in = [p for pieces in seq_in for p in pieces]
    flat_resid = [p for pieces in (first_seq, second_seq) for p in pieces]
    grad_in, _ = run(weight_grad, flat_in, [d_both])
    conv = [part[4] for part in saved]
    mlp_total = [
        lax.psum_scatter(flat(tied(v, grad_in[0])), "mp", scatter_dimension=0, tiled=True) for v in mlp_part
    ]

    def finish_output(*after):
        totals = lax.optimization_barrier((*mlp_total, *after))[:count]
        return jnp.stack([(resid_mid[s] + totals[s].astype(f32)).astype(bf16) for s in seqs])

    def finish_input(d_in):
        last = (second + normalize_back(resid[1], norm1_gain, d_in)[0]).astype(bf16)
        return jnp.stack(input_grad + [last])

    if piped:

        def join(prefix, by_rows=True, ways=1):
            names = [name for name in sorted(pipe.done) if name.startswith(prefix)]
            mine = [pipe.done[name] for name in names]
            other = [others[name] if name in others else swap(pipe.done[name], "dp", 1) for name in names]
            return join_pieces(mine + other, by_rows, ways)

        moving = pipe.left()
        moving[0].update(in0=grad_in[0], in1=grad_in[1])
        found, others, (d_in,) = last_grad(
            mixed, flat_resid, conv, d_gates, (sums, out[2], gain1, out[3], gain2, more_gain2), moving, dict(pipe.done),
            nblocks,
            hosts=[ScatterHost(out[4:])], middle=4, unique=next(ids), before=(grad_in[0],),
        )
        pipe.done.update({name: found[name] for name in found if name != "out"})
        pairs = [(2 * a + core, 2 * b + core) for a, b in ((1, 0), (2, 3)) for core in range(2)]
        came = lax.ppermute(found["out"], "dp", pairs)
        totals_down, totals_gate, totals_up = (join(name) for name in ("down", "gate", "up"))
        totals_in = join("in", ways=2)
        input_grad = finish_input(d_in)
        came = lax.optimization_barrier((came, totals_down, totals_gate, totals_up, totals_in[0]))[0]
        pipe.done["out"] = jnp.where(chip_is_inner(), found["out"], came)
        block_out = finish_output(pipe.done["out"])
        totals_out = join("out", by_rows=False)
        pack, other = found["pack"].astype(f32), swap(found["pack"], "dp", 1).astype(f32)
        mine = core_index() == 0
        pack = jnp.concatenate([jnp.where(mine, pack, other), jnp.where(mine, other, pack)], axis=0)
        inner = true_width // nblocks
        full_ga, full_gi = (
            jnp.transpose(pack[at * inner : (at + 1) * inner].reshape(inner, nblocks, inner), (1, 0, 2)) for at in range(2)
        )
        vectors = pack[2 * inner : 2 * inner + 8]
        gains = found["gains"][:2].astype(f32)
        for bit in (1, 2):
            gains = gains + swap(gains, "mp", bit)
    else:
        grad_out, _ = run(weight_grad, mixed, flat_resid, False, before=(grad_in[0],))
        input_grad, block_out = finish_input(scatter(out[4:])), finish_output()
        totals_down, totals_gate, totals_up, totals_in, totals_out = (
            jnp.split(lax.psum(v[0], "dp").astype(f32), ways, axis=1)
            for v, ways in ((grad_down, 1), (grad_gate, 1), (grad_up, 1), (grad_in, 2), (grad_out, 1))
        )
        d_gates = d_gates.reshape(count, blocks, piece, -1)
        width = d_gates.shape[-1] // 2
        full = sum(jnp.einsum("rtd,rtc->dc", conv[s], d_gates[s], preferred_element_type=f32) for s in seqs)
        gains = jnp.stack([jnp.sum(gain1 + out[3], axis=0), (gain2 + more_gain2)[0]])
        vectors = jnp.sum(sums + out[2], axis=1)[:, :true_width]
        full_ga, full_gi, vectors, gains = lax.psum(
            (
                diagonal_blocks(full[:, :width], nblocks, true_width).astype(bf16),
                diagonal_blocks(full[:, width:], nblocks, true_width).astype(bf16),
                vectors.astype(bf16),
                lax.psum(gains, "mp").astype(bf16),
            ),
            "dp",
        )
    grad_gate_a_weight, grad_gate_i_weight, vectors, gains = (
        v.astype(f32) for v in (full_ga, full_gi, vectors, gains)
    )
    gains = jnp.stack([gains[0] / norm1_gain, gains[1]])
    vectors = jnp.concatenate(
        [(vectors[0] * DECAY_EXP * jax.nn.sigmoid(-decay_param))[None, :], vectors[1:]], axis=0
    )
    grad_w_out = totals_out[0][:true_width]
    grad_w_branch, grad_w_input = (v[:, :true_width] for v in totals_in)
    return (
        block_out,
        input_grad,
        gains[0],
        grad_w_branch,
        grad_w_input,
        vectors[4:8],
        vectors[3],
        grad_gate_a_weight,
        vectors[1],
        grad_gate_i_weight,
        vectors[2],
        vectors[0],
        grad_w_out,
        gains[1],
        totals_gate[0],
        totals_up[0],
        totals_down[0],
        jnp.concatenate(finals, axis=0),
    )


def solution(mesh):
    placed = (
        P("dp", "mp", None),
        P(),
        P(None, "mp"),
        P(None, "mp"),
        P(None, "mp"),
        P("mp"),
        P("mp", None, None),
        P("mp"),
        P("mp", None, None),
        P("mp"),
        P("mp"),
        P("mp", None),
        P(),
        P(None, "mp"),
        P(None, "mp"),
        P("mp", None),
        P("dp"),
        P("dp", "mp", None),
    )
    return jax.shard_map(
        per_device,
        mesh=mesh,
        in_specs=placed,
        out_specs=(
            P("dp", "mp", None),
            P("dp", "mp", None),
            P(),
            P(None, "mp"),
            P(None, "mp"),
            P(None, "mp"),
            P("mp"),
            P("mp", None, None),
            P("mp"),
            P("mp", None, None),
            P("mp"),
            P("mp"),
            P("mp", None),
            P(),
            P(None, "mp"),
            P(None, "mp"),
            P("mp", None),
            P("dp", "mp"),
        ),
        check_vma=False,
    )
```
